128 devices in a mesh: lon: 32 (over x, z, core), lat: 4 (over y).
Axes of the slice: x: 4, y: 4, z: 4, core: 2. Of those that a mesh axis runs over, the one named last changes fastest.
Arguments:
- obs_value: float32 [1310720], P(('lon', 'lat')), may hold values from -6 to 6
- send_list: int32 [16384, 80], P(('lon', 'lat')), may hold values from -1 to 10239, as said below
- recv_cell: int32 [16384, 80], P(('lon', 'lat')), may hold values from -1 to 767999, as said below
- column_depth: int32 [160, 4096], P('lat', 'lon'), may hold values from 0 to 75
- zonal_weight: float32 [2, 160, 4096], P(None, 'lat', 'lon'), may hold values from 1000 to 30000
- merid_weight: float32 [2, 160, 4096], P(None, 'lat', 'lon'), may hold values from 400 to 6400
- vert_inverse: float32 [2, 75, 75], replicated, may hold values from 0 to 2
- norm_scale: float32 [2, 75, 160, 4096], P(None, None, 'lat', 'lon'), may hold values from 20 to 200
Outputs:
- increment: float32 [2, 75, 160, 4096], P(None, None, 'lat', 'lon')
- obs_result: float32 [1310720], P(('lon', 'lat'))
The draws below stay inside these ranges and needn't reach their ends.
Inputs may be any that keep to these rules, and one draw needn't show every extreme that they name: `send_list`: row q * 128 + r names, in its first slots, the positions among device q's 10240 observations that device q sends to device r, and -1 in the rest; no position appears twice among device q's rows. Some device receives 80 observations from every device. `recv_cell`: row r * 128 + q, slot k, is the cell of owner r that receives slot k of row q * 128 + r of send_list, and -1 exactly where that slot is -1.
All inputs are finite; a program needn't handle non-finite values.
Results may differ from the reference program's by a relative error of at most 0.0007.
Values sent between devices are 32-bit elements; how exact they have to be, the bound alone decides.
A program may use at most 128 MiB of HBM per device.

```python
import math
import jax
import jax.numpy as jnp
from jax import lax

NZ = 75
CLON = 128
CLAT = 40
CAP = 80
RANKS = 128
NOBS_DEV = 10240
NOBS = 1310720
NLON = 4096
NLAT = 160
N_LON = 32
N_LAT = 4


def obs_tables(key):
    base = jax.random.fold_in(key, 7)
    kind_key, level_key, busy_key, cut_key, perm_key, cell_key = jax.random.split(base, 6)
    sparse = jax.random.randint(kind_key, (RANKS,), 0, 2) == 0
    density = jnp.where(sparse, 1, jax.random.randint(level_key, (RANKS,), 1, 5))
    busiest = jax.random.randint(busy_key, (), 0, RANKS)
    owners = jnp.arange(RANKS)
    cut = jax.random.randint(cut_key, (RANKS, RANKS), 0, CAP // 16 + 1)
    counts = CAP * density[None, :] // 4 - cut
    counts = jnp.where(owners[None, :] == busiest, CAP, counts)
    slot_index = jnp.arange(CAP)
    live = slot_index[None, None, :] < counts[:, :, None]
    orders = jax.vmap(lambda sub_key: jax.random.permutation(sub_key, RANKS * CAP))(jax.random.split(perm_key, RANKS))
    sends = jnp.where(live, orders.reshape(RANKS, RANKS, CAP), -1)
    cells = jax.random.randint(cell_key, (RANKS, RANKS, CAP), 0, 2 * NZ * CLAT * CLON)
    cells = jnp.where(live, cells, -1)
    return (sends, cells)


def draw_send_list(key, part):
    sends, cells = obs_tables(key)
    return sends.reshape(RANKS * RANKS, CAP).astype(jnp.int32)


def draw_recv_cell(key, part):
    sends, cells = obs_tables(key)
    return jnp.transpose(cells, (1, 0, 2)).reshape(RANKS * RANKS, CAP).astype(jnp.int32)


def draw_column_depth(key, part):
    land_key, depth_key = jax.random.split(jax.random.fold_in(key, 11))
    land = jax.random.randint(land_key, (NLAT, NLON), 0, 4) == 0
    depth = jax.random.randint(depth_key, (NLAT, NLON), 1, NZ + 1)
    return jnp.where(land, 0, depth).astype(jnp.int32)


def draw_vert_inverse(key, part):
    diag_key, off_key = jax.random.split(jax.random.fold_in(key, 13))
    main_part = jax.random.uniform(diag_key, (2, NZ), jnp.float32, 0.5, 1.5)
    off_part = jax.random.uniform(off_key, (2, NZ, NZ), jnp.float32, 0.0, 2.0 / NZ)
    return off_part + main_part[:, :, None] * jnp.eye(NZ, dtype=jnp.float32)[None]


def block_levels(rng, shape, shards, low, top_value):
    gain = 1.0
    for axis_at, blocks in shards:
        steps = jax.random.uniform(jax.random.fold_in(jax.random.fold_in(rng, 6), axis_at), (blocks,), jnp.float32, low / len(shards), top_value / len(shards))
        gain = gain * jnp.repeat(jnp.exp(steps), shape[axis_at] // blocks).reshape((-1,) + (1,) * (len(shape) - 1 - axis_at))
    return gain


def centred(stream_key, extent, deviation, most, pieces=(), kind=jnp.bfloat16):
    drawn = deviation * jax.random.normal(stream_key, extent, jnp.float32)
    if pieces:
        drawn = drawn * block_levels(stream_key, extent, pieces, -0.22, 0.18)
    return jnp.clip(drawn, -most, most).astype(kind)


def setup_inputs(seed: int = 0) -> dict:
    key_list = jax.random.split(jax.random.key(seed), 9)
    return {
        "obs_value": centred(key_list[0], (NOBS,), 1.0, 6.0, ((0, 128),), jnp.float32),
        "send_list": draw_send_list(jax.random.fold_in(key_list[8], 71), 0),
        "recv_cell": draw_recv_cell(jax.random.fold_in(key_list[8], 71), 0),
        "column_depth": draw_column_depth(jax.random.fold_in(key_list[8], 71), 0),
        "zonal_weight": jnp.clip(jnp.exp(math.log(30000.0) - 3.4011974 * jax.random.uniform(key_list[4], (2, NLAT, NLON), jnp.float32) ** block_levels(key_list[4], (2, NLAT, NLON), ((1, 4), (2, 32)), -0.2, 0.2)), 1000.0, 30000.0),
        "merid_weight": jnp.clip(jnp.exp(math.log(6400.0) - 2.7725887 * jax.random.uniform(key_list[5], (2, NLAT, NLON), jnp.float32) ** block_levels(key_list[5], (2, NLAT, NLON), ((1, 4), (2, 32)), -0.2, 0.2)), 400.0, 6400.0),
        "vert_inverse": draw_vert_inverse(jax.random.fold_in(key_list[8], 71), 0),
        "norm_scale": jnp.clip(jnp.exp(math.log(200.0) - 2.3025851 * jax.random.uniform(key_list[7], (2, NZ, NLAT, NLON), jnp.float32) ** block_levels(key_list[7], (2, NZ, NLAT, NLON), ((2, 4), (3, 32)), -0.2, 0.2)), 20.0, 200.0),
    }


def zonal_line(data_field, weight):
    left_face = jnp.roll(weight, 1, axis=-1)
    main_diag = 1.0 + left_face + weight
    corner = -weight[:, -1]
    first_diag = main_diag[:, 0]
    factor = -first_diag
    main_diag = main_diag.at[:, 0].set(first_diag - factor)
    main_diag = main_diag.at[:, -1].set(main_diag[:, -1] - corner * corner / factor)
    zero_edge = jnp.zeros_like(weight[:, :1])
    sub_diag = jnp.concatenate([zero_edge, -weight[:, :-1]], axis=1)
    super_diag = jnp.concatenate([-weight[:, :-1], zero_edge], axis=1)
    extra = jnp.zeros_like(weight).at[:, 0].set(factor).at[:, -1].set(corner)
    right_side = jnp.concatenate([jnp.transpose(data_field, (1, 2, 0)), extra[:, :, None]], axis=2)
    solved = lax.linalg.tridiagonal_solve(sub_diag, main_diag, super_diag, right_side)
    plain = solved[:, :, :NZ]
    helper = solved[:, :, NZ]
    ratio = corner / factor
    top_plain = plain[:, 0, :] + ratio[:, None] * plain[:, -1, :]
    top_helper = helper[:, 0] + ratio * helper[:, -1]
    result = plain - helper[:, :, None] * (top_plain / (1.0 + top_helper)[:, None])[:, None, :]
    return jnp.transpose(result, (2, 0, 1))

def merid_line(data_field, weight):
    weight = weight.at[-1, :].set(0.0)
    south_face = jnp.concatenate([jnp.zeros_like(weight[:1]), weight[:-1]], axis=0)
    main_diag = (1.0 + south_face + weight).T
    sub_diag = -south_face.T
    super_diag = -weight.T
    right_side = jnp.transpose(data_field, (2, 1, 0))
    solved = lax.linalg.tridiagonal_solve(sub_diag, main_diag, super_diag, right_side)
    return jnp.transpose(solved, (2, 1, 0))

def fieldwise(solver, data_field, weight):
    return jnp.stack([solver(data_field[index], weight[index]) for index in range(2)])

def reference(obs_value, send_list, recv_cell, column_depth, zonal_weight, merid_weight, vert_inverse, norm_scale):
    n_dev = N_LON * N_LAT
    sends = send_list.reshape(n_dev, n_dev, CAP)
    cells = jnp.transpose(recv_cell.reshape(n_dev, n_dev, CAP), (1, 0, 2))
    live = sends >= 0
    observed = obs_value.reshape(n_dev, NOBS_DEV)
    picked = jnp.take_along_axis(observed, jnp.maximum(sends, 0).reshape(n_dev, n_dev * CAP), axis=1)
    values = jnp.where(live, picked.reshape(n_dev, n_dev, CAP), 0.0)
    owner = jnp.arange(n_dev, dtype=jnp.int32)[None, :, None]
    owner_lon = owner // N_LAT
    owner_lat = owner % N_LAT
    local = jnp.maximum(cells, 0)
    lon_cell = local % CLON
    remain = local // CLON
    lat_cell = remain % CLAT
    remain = remain // CLAT
    level = remain % NZ
    field_id = remain // NZ
    flat = ((field_id * NZ + level) * NLAT + owner_lat * CLAT + lat_cell) * NLON + owner_lon * CLON + lon_cell
    flat = flat.astype(jnp.int32)
    gridded = jnp.zeros((2 * NZ * NLAT * NLON,), jnp.float32).at[flat.reshape(-1)].add(values.reshape(-1))
    gridded = gridded.reshape(2, NZ, NLAT, NLON)
    ocean_mask = (jnp.arange(NZ, dtype=jnp.int32)[:, None, None] < column_depth[None]).astype(jnp.float32)
    scaling = norm_scale * ocean_mask[None]
    smoothed = fieldwise(merid_line, fieldwise(zonal_line, scaling * gridded, zonal_weight), merid_weight)
    mixed = jnp.einsum('fkz,fkab->fzab', vert_inverse, smoothed, precision=lax.Precision.HIGHEST)
    remixed = jnp.einsum('fzk,fkab->fzab', vert_inverse, mixed, precision=lax.Precision.HIGHEST)
    increment = scaling * fieldwise(zonal_line, fieldwise(merid_line, remixed, merid_weight), zonal_weight)
    at_cells = jnp.where(live, increment.reshape(-1)[flat], 0.0)
    target = jnp.where(live, sends, NOBS_DEV)
    result = jnp.zeros((n_dev, NOBS_DEV + 1), jnp.float32)
    result = result.at[jnp.arange(n_dev, dtype=jnp.int32)[:, None, None], target].set(at_cells)
    return (increment, result[:, :NOBS_DEV].reshape(-1))
```

```python
import jax
import jax.numpy as jnp
from jax import lax
from jax.experimental import pallas as pl
from jax.experimental.pallas import tpu as pltpu
from jax.sharding import PartitionSpec as P

F32 = jnp.float32
BF16 = jnp.bfloat16
MESH = pl.DeviceIdType.MESH
NF, NZ, NLAT, NLON = 2, 75, 40, 128
ZP = 80
RANKS, CAP = 128, 80
N_LON, N_LAT = 32, 4
SOLVERS = 19
LANES = 128
CHUNK = 4
GRIDS = 4
ROWS = NF * NLAT * ZP
VMEM_SPEC = pl.BlockSpec(memory_space=pltpu.VMEM)
SMEM_SPEC = pl.BlockSpec(memory_space=pltpu.SMEM)
ANY_SPEC = pl.BlockSpec(memory_space=pl.ANY)


def lane_iota(rows):
    return lax.broadcasted_iota(jnp.int32, (rows, LANES), 1)


def split(value):
    high = value.astype(BF16)
    return high, (value - high.astype(F32)).astype(BF16)


def lane_pick(table, index):
    return jnp.take_along_axis(table, index, axis=1, mode="promise_in_bounds")


def prepare_kernel(
    obs_ref, send_ref, zw_ref, mw_ref, north_ref, vert_in,
    out_ref, zs_ref, zr_ref, zco_ref, ms_ref, mr_ref, mco_ref, vert_ref,
    idx_ref, iw_ref, st_ref, rt_ref, miw_ref,
):
    for field in range(NF):
        product = lax.dot_general(
            vert_in[field], vert_in[field], (((1,), (1,)), ((), ())),
            precision=lax.Precision.HIGHEST, preferred_element_type=F32,
        )
        high, low = split(product)
        vert_ref[field] = jnp.concatenate([high, low, high], axis=1)
    idx_ref[...] = jnp.full((RANKS, LANES), -1, jnp.int32)
    idx_ref[:, :CAP] = send_ref[...]
    part = 64
    for start in range(0, RANKS, part):
        index = idx_ref[start : start + part, :]
        low = index & 127
        high = index >> 7

        def gather_row(row, acc, low=low, high=high):
            line = jnp.broadcast_to(obs_ref[pl.ds(row, 1), :], (part, LANES))
            return jnp.where(high == row, lane_pick(line, low), acc)

        picked = lax.fori_loop(0, CAP, gather_row, jnp.zeros((part, LANES), F32), unroll=4)
        out_ref[start : start + part, :] = picked[:, :CAP]

    iw_ref[...] = jnp.full((LANES, LANES), 1e-3, F32)
    iw_ref[: NF * NLAT, :] = 1.0 / zw_ref[...]
    iw_ref[...] = jnp.transpose(iw_ref[...])
    zero = north_ref[...] * 0.0
    one = zero + 1.0

    def zonal_step(step, carry):
        s_val, s_flux, s_sum, r_val, r_flux, r_sum = carry
        back = LANES - 1 - step
        st_ref[pl.ds(step, 1), :] = s_val[0:1]
        s_sum = s_sum + s_val
        s_val = s_val + s_flux * iw_ref[pl.ds(step, 1), :]
        s_flux = s_flux + s_val
        r_sum = r_sum + r_val
        r_val = r_val + r_flux * iw_ref[pl.ds(back, 1), :]
        rt_ref[pl.ds(back, 1), :] = r_val[0:1]
        r_flux = r_flux + r_val
        return s_val, s_flux, s_sum, r_val, r_flux, r_sum

    _, _, s_sum, r_first, _, r_sum = lax.fori_loop(
        0, LANES, zonal_step, (zero, one, zero, zero, one, zero), unroll=8
    )
    coupling = 1.0 / r_first[0:1]
    zco_ref[...] = jnp.zeros((8, LANES), F32)
    zco_ref[0:1, :] = coupling
    zco_ref[1:2, :] = r_sum[0:1] * coupling
    zco_ref[2:3, :] = s_sum[0:1] * coupling
    zs_ref[...] = jnp.transpose(st_ref[...])[: NF * NLAT, :]
    zr_ref[...] = jnp.transpose(rt_ref[...] * coupling)[: NF * NLAT, :]

    north = north_ref[...]
    miw_ref[...] = 1.0 / mw_ref[...]
    mco_ref[...] = jnp.zeros((NF, 8, LANES), F32)
    for field in range(NF):
        s_val, s_flux, s_sum = zero, one, zero
        for row in range(NLAT):
            ms_ref[field, row : row + 1, :] = s_val[0:1]
            s_sum = s_sum + s_val
            s_val = s_val + s_flux * miw_ref[field, row : row + 1, :]
            s_flux = s_flux + s_val
        r_val = jnp.where(north > 0.5, 1.0, miw_ref[field, NLAT - 1 : NLAT, :] + zero)
        r_flux = jnp.where(north > 0.5, 0.0, one)
        r_sum = zero
        mr_ref[field, NLAT - 1 : NLAT, :] = r_val[0:1]
        for row in range(NLAT - 2, -1, -1):
            r_sum = r_sum + r_val
            r_flux = r_flux + r_val
            r_val = r_val + r_flux * miw_ref[field, row : row + 1, :]
            mr_ref[field, row : row + 1, :] = r_val[0:1]
        inverse = 1.0 / r_val[0:1]
        coupling = jnp.where(north[0:1] > 0.5, 0.0, inverse)
        mr_ref[field] = mr_ref[field] * inverse
        mco_ref[field, 0:1, :] = coupling
        mco_ref[field, 1:2, :] = r_sum[0:1] * inverse
        mco_ref[field, 2:3, :] = s_sum[0:1] * coupling


def prepare(obs, send_list, zonal_weight, merid_weight, north, vert_inverse):
    shape = lambda *dims: jax.ShapeDtypeStruct(dims, F32)
    return pl.pallas_call(
        prepare_kernel,
        out_shape=(
            shape(RANKS, CAP), shape(80, LANES), shape(80, LANES), shape(8, LANES),
            shape(NF, NLAT, LANES), shape(NF, NLAT, LANES), shape(NF, 8, LANES),
            jax.ShapeDtypeStruct((NF, ZP, 3 * ZP), BF16),
        ),
        in_specs=[VMEM_SPEC] * 6,
        out_specs=(VMEM_SPEC,) * 8,
        scratch_shapes=[
            pltpu.VMEM((RANKS, LANES), jnp.int32),
            pltpu.VMEM((LANES, LANES), F32),
            pltpu.VMEM((LANES, LANES), F32),
            pltpu.VMEM((LANES, LANES), F32),
            pltpu.VMEM((NF, NLAT, LANES), F32),
        ],
        compiler_params=pltpu.CompilerParams(vmem_limit_bytes=16 << 20),
        name="prepare",
    )(obs, send_list, zonal_weight.reshape(NF * NLAT, LANES), merid_weight, north, vert_inverse)


def scatter_kernel(rows_ref, lane_ref, in_ref, depth_ref, norm_ref, field_ref, scale_ref, *scratch):
    grids = scratch[:GRIDS]
    value_ref, spread_ref = scratch[GRIDS:]

    def clear(step, _):
        at = pl.ds(pl.multiple_of(step * 64, 64), 64)
        for grid in grids:
            grid[at, :] = jnp.zeros((64, LANES), F32)
        return 0

    lax.fori_loop(0, ROWS // 64, clear, 0)
    value_ref[...] = jnp.zeros((RANKS, LANES), F32)
    value_ref[:, :CAP] = in_ref[...]
    value_ref[...] = jnp.transpose(value_ref[...])
    iota = lane_iota(CAP)

    def sender(q, _):
        index = jnp.full((CAP, LANES), q, jnp.int32)
        value = lane_pick(value_ref[:CAP, :], index)
        lane = lane_pick(lane_ref[...], index)
        slot = q & 1
        spread_ref[slot] = jnp.where(iota == lane, value, 0.0)
        for k in range(CAP):
            row = rows_ref[q * CAP + k]
            grid = grids[k % GRIDS]
            at = pl.ds(row, 1)
            grid[at, :] = grid[at, :] + spread_ref[slot, k : k + 1, :]
        return 0

    lax.fori_loop(0, RANKS, sender, 0)
    level = lax.broadcasted_iota(jnp.int32, (ZP, LANES), 0)
    for field in range(NF):

        def finish(row, _, field=field):
            at = pl.ds(pl.multiple_of((field * NLAT + row) * ZP, ZP), ZP)
            total = grids[0][at, :]
            for grid in grids[1:]:
                total = total + grid[at, :]
            wet = level < depth_ref[pl.ds(row, 1), :]
            scale = jnp.where(wet, norm_ref[field, row], 0.0)
            scale_ref[field, row] = scale
            field_ref[field, row] = jnp.where(wet, scale * total, 0.0)
            return 0

        lax.fori_loop(0, NLAT, finish, 0)


def scatter(rows, lanes, incoming, depth, norm):
    full = jax.ShapeDtypeStruct((NF, NLAT, ZP, LANES), F32)
    return pl.pallas_call(
        scatter_kernel,
        out_shape=(full, full),
        in_specs=[SMEM_SPEC] + [VMEM_SPEC] * 4,
        out_specs=(VMEM_SPEC, VMEM_SPEC),
        scratch_shapes=[pltpu.VMEM((ROWS, LANES), F32)] * GRIDS
        + [pltpu.VMEM((RANKS, LANES), F32), pltpu.VMEM((2, CAP, LANES), F32)],
        compiler_params=pltpu.CompilerParams(vmem_limit_bytes=40 << 20),
        name="scatter",
    )(rows, lanes, incoming, depth, norm)


def push(source, target, send_sem, recv_sem, axis, device):
    return pltpu.make_async_remote_copy(
        src_ref=source, dst_ref=target, send_sem=send_sem, recv_sem=recv_sem,
        device_id={axis: device}, device_id_type=MESH,
    )


def solve_kernel(
    field_ref, scale_ref, zs_ref, zr_ref, zco_ref, ms_ref, mr_ref, mco_ref, vert_ref, sums_ref,
    x_ref,
    zco_all, mco_all, alpha, gamma, minv,
    zsend, zrecv, zret, zres, msend, mrecv, mret, mres,
    acc_a, acc_b, ubuf, gbuf, mtot,
    zco_s, zco_r, mco_s, mco_r, z1s, z1r, z2s, z2r, m1s, m1r, m2s, m2r,
):
    me = lax.axis_index("lon")
    my = lax.axis_index("lat")
    iota = lane_iota(ZP)
    is_solver = me < SOLVERS

    barrier = pltpu.get_barrier_semaphore()

    def greet_lon(step, _):
        pl.semaphore_signal(barrier, inc=1, device_id={"lon": (me + step) % N_LON}, device_id_type=MESH)
        return 0

    def greet_lat(step, _):
        pl.semaphore_signal(barrier, inc=1, device_id={"lat": (my + step) % N_LAT}, device_id_type=MESH)
        return 0

    lax.fori_loop(1, N_LON, greet_lon, 0)
    lax.fori_loop(1, N_LAT, greet_lat, 0)
    pl.semaphore_wait(barrier, N_LON - 1 + N_LAT - 1)

    def zco_copy(device, slot):
        return push(zco_ref, zco_all.at[slot], zco_s.at[device], zco_r.at[slot], "lon", device)

    def mco_copy(device, slot):
        return push(mco_ref, mco_all.at[slot], mco_s.at[device], mco_r.at[slot], "lat", device)

    def over_solvers(action):
        def body(step, _):
            device = (me + step) % N_LON

            @pl.when(device < SOLVERS)
            def _():
                action(device)

            return 0

        lax.fori_loop(1, N_LON, body, 0)

    def over_lon(action):
        def body(step, _):
            action((me + step) % N_LON)
            return 0

        lax.fori_loop(1, N_LON, body, 0)

    def over_lat(action):
        def body(step, _):
            action((my + step) % N_LAT)
            return 0

        lax.fori_loop(1, N_LAT, body, 0)

    over_solvers(lambda device: zco_copy(device, me).start())
    over_lat(lambda device: mco_copy(device, my).start())
    zco_all[me] = zco_ref[...]
    mco_all[my] = mco_ref[...]

    def zonal_pass(field, chunk, load, field_base):
        lines, left = [], []
        for step in range(CHUNK):
            row = chunk * CHUNK + step
            at = pl.ds(field_base + row, 1)
            s_row, r_row = zs_ref[at, :], zr_ref[at, :]
            value = load(row, step)
            for coef in (s_row, r_row):
                high, low = split(coef * value)
                left.append(jnp.concatenate([high, low], axis=1))
            lines.append((row, s_row, r_row))
        sums = jnp.dot(jnp.concatenate(left, axis=0), sums_ref[...], preferred_element_type=F32)
        tot_a, tot_b = acc_a[...], acc_b[...]
        for step, (row, s_row, r_row) in enumerate(lines):
            a_part = sums[2 * step * ZP : (2 * step + 1) * ZP]
            b_part = sums[(2 * step + 1) * ZP : (2 * step + 2) * ZP]
            x_ref[field, row] = r_row * a_part[:, :LANES] - s_row * b_part[:, :LANES]
            mine = iota == field_base + row
            tot_a = jnp.where(mine, a_part[:, LANES:], tot_a)
            tot_b = jnp.where(mine, b_part[:, LANES:], tot_b)
        acc_a[...] = tot_a
        acc_b[...] = tot_b

    def zonal_send(turn):
        acc_a[...] = acc_a[...] * zco_ref[0:1, :]
        for solver in range(SOLVERS):
            zsend[turn, solver, 0:4, :] = acc_b[4 * solver : 4 * solver + 4, :]
            zsend[turn, solver, 4:8, :] = acc_a[4 * solver : 4 * solver + 4, :]
        over_solvers(lambda device: zonal_out(turn, device, me).start())

        @pl.when(is_solver)
        def _():
            zrecv[turn, me] = zsend[turn, me]

    def zonal_out(turn, device, slot):
        return push(
            zsend.at[turn, device], zrecv.at[turn, slot], z1s.at[turn, device], z1r.at[turn, slot], "lon", device
        )

    def zonal_back(turn, device, slot):
        return push(
            zret.at[turn, device], zres.at[turn, slot], z2s.at[turn, device], z2r.at[turn, slot], "lon", device
        )

    def zonal_factor():
        over_lon(lambda device: zco_copy(0, device).wait_recv())
        coupling = zco_all[:, 0, :]
        west = jnp.concatenate([coupling[-1:], coupling[:-1]], axis=0)
        spill = zco_all[:, 2, :]
        mass = 1.0 + zco_all[:, 1, :] + jnp.concatenate([spill[-1:], spill[:-1]], axis=0)
        east = coupling
        for bit in range(5):
            stride = 1 << bit
            down = lambda v: jnp.concatenate([v[-stride:], v[:-stride]], axis=0)
            up = lambda v: jnp.concatenate([v[stride:], v[:stride]], axis=0)
            inverse = 1.0 / (mass + west + east)
            left = west * down(inverse)
            right = east * up(inverse)
            alpha[bit] = left
            gamma[bit] = right
            mass = mass + left * down(mass) + right * up(mass)
            west, east = left * down(west), right * up(east)
        minv[...] = 1.0 / mass

    def zonal_reduced(turn):
        over_lon(lambda device: zonal_out(turn, 0, device).wait_recv())
        tiles = [zrecv[turn, k] for k in range(N_LON)]
        flip = lambda v: jnp.concatenate([v[4:], v[:4]], axis=0)
        right_side = [tiles[k] + flip(tiles[k - 1]) for k in range(N_LON)]
        for bit in range(5):
            stride = 1 << bit
            right_side = [
                right_side[k]
                + alpha[bit, k : k + 1, :] * right_side[(k - stride) % N_LON]
                + gamma[bit, k : k + 1, :] * right_side[(k + stride) % N_LON]
                for k in range(N_LON)
            ]
        values = [right_side[k] * minv[k : k + 1, :] for k in range(N_LON)]
        for k in range(N_LON):
            zret[turn, k] = jnp.concatenate([values[k][:4], values[(k + 1) % N_LON][:4]], axis=0)
        over_lon(lambda device: zonal_back(turn, device, me).start())
        zres[turn, me] = zret[turn, me]

    def zonal_receive(turn):
        over_solvers(lambda device: zonal_back(turn, 0, device).wait_recv())
        ubuf[72:80, :] = jnp.zeros((8, LANES), F32)
        gbuf[72:80, :] = jnp.zeros((8, LANES), F32)
        for solver in range(SOLVERS):
            ubuf[4 * solver : 4 * solver + 4, :] = zres[turn, solver, 0:4, :]
            gbuf[4 * solver : 4 * solver + 4, :] = zres[turn, solver, 4:8, :]
        gbuf[...] = gbuf[...] * zco_ref[0:1, :] + acc_b[...]

    def zonal_values(field, chunk, field_base):
        u_all, g_all = ubuf[...], gbuf[...]
        found = []
        for step in range(CHUNK):
            row = chunk * CHUNK + step
            at = pl.ds(field_base + row, 1)
            found.append(
                x_ref[field, row]
                + zr_ref[at, :] * jnp.broadcast_to(u_all[:, step : step + 1], (ZP, LANES))
                + zs_ref[at, :] * jnp.broadcast_to(g_all[:, step : step + 1], (ZP, LANES))
            )
        ubuf[...] = pltpu.roll(u_all, LANES - CHUNK, 1)
        gbuf[...] = pltpu.roll(g_all, LANES - CHUNK, 1)
        return found

    def vertical(field, value):
        high, low = split(value)
        return jnp.dot(
            vert_ref[field], jnp.concatenate([high, high, low], axis=0), preferred_element_type=F32
        )

    def vertical_field(field):
        def body(pair, _):
            row = pair * 2
            both = jnp.concatenate([x_ref[field, row], x_ref[field, row + 1]], axis=1)
            both = vertical(field, both)
            x_ref[field, row] = both[:, :LANES]
            x_ref[field, row + 1] = both[:, LANES:]
            return 0

        lax.fori_loop(0, NLAT // 2, body, 0)

    def merid_out(turn, device, slot):
        return push(
            msend.at[turn, device], mrecv.at[turn, slot], m1s.at[turn, device], m1r.at[turn, slot], "lat", device
        )

    def merid_back(turn, device, slot):
        return push(
            mret.at[turn, device], mres.at[turn, slot], m2s.at[turn, device], m2r.at[turn, slot], "lat", device
        )

    def merid_step(field, row, value, tot_a, tot_b):
        s_row, r_row = ms_ref[field, pl.ds(row, 1), :], mr_ref[field, pl.ds(row, 1), :]
        tot_a = tot_a + s_row * value
        tot_b = tot_b + r_row * value
        x_ref[field, row] = r_row * tot_a - s_row * tot_b
        return tot_a, tot_b

    def merid_send(turn, field, tot_a, tot_b):
        mtot[field] = tot_b
        tot_a = tot_a * mco_ref[field, 0:1, :]
        for half in range(2):
            msend[turn, 2 * field + half, 0] = tot_b[40 * half : 40 * half + 40]
            msend[turn, 2 * field + half, 1] = tot_a[40 * half : 40 * half + 40]
        for half in range(2):
            solver = 2 * field + half

            @pl.when(my != solver)
            def _(solver=solver):
                merid_out(turn, solver, my).start()

            @pl.when(my == solver)
            def _(solver=solver):
                mrecv[turn, solver] = msend[turn, solver]

    def merid_reduced(turn):
        if turn == 0:
            over_lat(lambda device: mco_copy(0, device).wait_recv())
        field = my // 2
        over_lat(lambda device: merid_out(turn, 0, device).wait_recv())
        rows = [mco_all[k, field] for k in range(N_LAT)]
        mass = 1.0 + rows[0][1:2]
        reduced = mrecv[turn, 0, 0]
        kept, inverses = [], []
        for k in range(N_LAT):
            coupling = rows[k][0:1]
            inverse = 1.0 / (mass + coupling)
            kept.append(reduced)
            inverses.append(inverse)
            if k + 1 < N_LAT:
                factor = coupling * inverse
                mass = 1.0 + rows[k + 1][1:2] + rows[k][2:3] + factor * mass
                reduced = mrecv[turn, k + 1, 0] + mrecv[turn, k, 1] + factor * reduced
        value = kept[N_LAT - 1] * inverses[N_LAT - 1]
        mret[turn, N_LAT - 1, 0] = value
        mret[turn, N_LAT - 1, 1] = jnp.zeros_like(value)
        for k in range(N_LAT - 2, -1, -1):
            mret[turn, k, 1] = value
            value = (kept[k] + rows[k][0:1] * value) * inverses[k]
            mret[turn, k, 0] = value
        over_lat(lambda device: merid_back(turn, device, my).start())
        mres[turn, my] = mret[turn, my]

    def merid_edges(turn, field):
        for half in range(2):
            solver = 2 * field + half

            @pl.when(my != solver)
            def _(solver=solver):
                merid_back(turn, 0, solver).wait_recv()

        own = jnp.concatenate([mres[turn, 2 * field, 0], mres[turn, 2 * field + 1, 0]], axis=0)
        after = jnp.concatenate([mres[turn, 2 * field, 1], mres[turn, 2 * field + 1, 1]], axis=0)
        ubuf[...] = own
        gbuf[...] = after * mco_ref[field, 0:1, :] + mtot[field]

    def merid_value(field, row):
        return (
            x_ref[field, row]
            + mr_ref[field, pl.ds(row, 1), :] * ubuf[...]
            + ms_ref[field, pl.ds(row, 1), :] * gbuf[...]
        )

    nothing = jnp.zeros((ZP, LANES), F32)

    acc_a[...] = nothing
    acc_b[...] = nothing
    for field in range(NF):

        def first_pass(chunk, _, field=field):
            zonal_pass(field, chunk, lambda row, step: field_ref[field, row], field * NLAT)
            return 0

        lax.fori_loop(0, NLAT // CHUNK, first_pass, 0)
    zonal_send(0)

    @pl.when(is_solver)
    def _():
        zonal_factor()

    vertical_field(0)

    @pl.when(is_solver)
    def _():
        zonal_reduced(0)

    vertical_field(1)
    zonal_receive(0)
    both = jnp.concatenate([ubuf[...], gbuf[...]], axis=1)
    upper = vertical(0, both)
    lower = vertical(1, both)
    first_field = iota < NLAT
    ubuf[...] = jnp.where(first_field, upper[:, :LANES], lower[:, :LANES])
    gbuf[...] = jnp.where(first_field, upper[:, LANES:], lower[:, LANES:])

    for field in range(NF):

        def second_pass(chunk, carry, field=field):
            tot_a, tot_b = carry
            found = zonal_values(field, chunk, field * NLAT)
            for step in range(CHUNK):
                tot_a, tot_b = merid_step(field, chunk * CHUNK + step, found[step], tot_a, tot_b)
            return tot_a, tot_b

        tot_a, tot_b = lax.fori_loop(0, NLAT // CHUNK, second_pass, (nothing, nothing))
        merid_send(0, field, tot_a, tot_b)
    merid_reduced(0)

    for field in range(NF):
        merid_edges(0, field)

        def third_pass(row, carry, field=field):
            return merid_step(field, row, merid_value(field, row), *carry)

        tot_a, tot_b = lax.fori_loop(0, NLAT, third_pass, (nothing, nothing), unroll=2)
        merid_send(1, field, tot_a, tot_b)
    merid_reduced(1)

    acc_a[...] = nothing
    acc_b[...] = nothing
    for field in range(NF):
        merid_edges(1, field)

        def fourth_pass(chunk, _, field=field):
            zonal_pass(field, chunk, lambda row, step: merid_value(field, row), field * NLAT)
            return 0

        lax.fori_loop(0, NLAT // CHUNK, fourth_pass, 0)
    zonal_send(1)

    @pl.when(is_solver)
    def _():
        zonal_reduced(1)

    zonal_receive(1)
    for field in range(NF):

        def last_pass(chunk, _, field=field):
            found = zonal_values(field, chunk, field * NLAT)
            for step in range(CHUNK):
                row = chunk * CHUNK + step
                x_ref[field, row] = found[step] * scale_ref[field, row]
            return 0

        lax.fori_loop(0, NLAT // CHUNK, last_pass, 0)

    over_solvers(lambda device: zco_copy(device, me).wait_send())
    over_lat(lambda device: mco_copy(device, my).wait_send())
    for turn in range(2):
        over_solvers(lambda device: zonal_out(turn, device, me).wait_send())
        over_lat(lambda device: merid_out(turn, device, my).wait_send())
        over_lat(lambda device: merid_back(turn, device, my).wait_send())

        @pl.when(is_solver)
        def _(turn=turn):
            over_lon(lambda device: zonal_back(turn, device, me).wait_send())


def solve(field, scale, coefs, vert, sums):
    dma = pltpu.SemaphoreType.DMA
    vmem = lambda *dims: pltpu.VMEM(dims, F32)
    return pl.pallas_call(
        solve_kernel,
        out_shape=jax.ShapeDtypeStruct((NF, NLAT, ZP, LANES), F32),
        in_specs=[VMEM_SPEC] * 10,
        out_specs=VMEM_SPEC,
        scratch_shapes=[
            vmem(N_LON, 8, LANES), vmem(N_LAT, NF, 8, LANES),
            vmem(5, N_LON, LANES), vmem(5, N_LON, LANES), vmem(N_LON, LANES),
            vmem(2, SOLVERS, 8, LANES), vmem(2, N_LON, 8, LANES),
            vmem(2, N_LON, 8, LANES), vmem(2, SOLVERS, 8, LANES),
            vmem(2, N_LAT, 2, 40, LANES), vmem(2, N_LAT, 2, 40, LANES),
            vmem(2, N_LAT, 2, 40, LANES), vmem(2, N_LAT, 2, 40, LANES),
            vmem(ZP, LANES), vmem(ZP, LANES), vmem(ZP, LANES), vmem(ZP, LANES),
            vmem(NF, ZP, LANES),
            dma((N_LON,)), dma((N_LON,)), dma((N_LAT,)), dma((N_LAT,)),
            dma((2, N_LON)), dma((2, N_LON)), dma((2, N_LON)), dma((2, N_LON)),
            dma((2, N_LAT)), dma((2, N_LAT)), dma((2, N_LAT)), dma((2, N_LAT)),
        ],
        compiler_params=pltpu.CompilerParams(
            collective_id=1, has_side_effects=True, vmem_limit_bytes=40 << 20
        ),
        name="solve",
    )(field, scale, *coefs, vert, sums)


def pick_kernel(rows_ref, lane_ref, x_ref, out_ref, copy_ref):
    iota = lane_iota(8)

    def sender(q, acc):
        slot = q & 1
        for k in range(CAP):
            row = rows_ref[q * CAP + k]
            copy_ref[slot, k : k + 1, :] = x_ref[pl.ds(row, 1), :]
        result = []
        for part in range(CAP // 8):
            at = slice(8 * part, 8 * part + 8)
            found = lane_pick(copy_ref[slot, at, :], lane_ref[at, :])
            result.append(jnp.where(iota == q, found, acc[part]))
        return tuple(result)

    acc = lax.fori_loop(0, RANKS, sender, (jnp.zeros((8, LANES), F32),) * (CAP // 8))
    whole = jnp.concatenate(list(acc) + [jnp.zeros((LANES - CAP, LANES), F32)], axis=0)
    out_ref[...] = jnp.transpose(whole)[:, :CAP]


def pick(rows, lanes, increment):
    return pl.pallas_call(
        pick_kernel,
        out_shape=jax.ShapeDtypeStruct((RANKS, CAP), F32),
        in_specs=[SMEM_SPEC, VMEM_SPEC, VMEM_SPEC],
        out_specs=VMEM_SPEC,
        scratch_shapes=[pltpu.VMEM((2, CAP, LANES), F32)],
        compiler_params=pltpu.CompilerParams(vmem_limit_bytes=40 << 20),
        name="pick",
    )(rows, lanes, increment.reshape(ROWS, LANES))


def place_kernel(back_ref, send_ref, out_ref, idx_ref, val_ref):
    idx_ref[...] = jnp.full((RANKS, LANES), -1, jnp.int32)
    idx_ref[:, :CAP] = send_ref[...]
    val_ref[...] = jnp.zeros((RANKS, LANES), F32)
    val_ref[:, :CAP] = back_ref[...]
    row_iota = lax.broadcasted_iota(jnp.int32, (CAP, 2 * LANES), 0)
    col_iota = lax.broadcasted_iota(jnp.int32, (LANES, 2 * LANES), 0)

    def pair(step, acc):
        first, second = pl.ds(2 * step, 1), pl.ds(2 * step + 1, 1)
        index = jnp.concatenate([idx_ref[first, :], idx_ref[second, :]], axis=1)
        value = jnp.concatenate([val_ref[first, :], val_ref[second, :]], axis=1)
        high = value.astype(BF16).astype(F32)
        low = value - high
        rows = jnp.where(row_iota == (index >> 7), 1.0, 0.0).astype(BF16)
        here = col_iota == (index & 127)
        columns = jnp.concatenate(
            [jnp.where(here, high, 0.0).astype(BF16), jnp.where(here, low, 0.0).astype(BF16)], axis=0
        )
        return acc + lax.dot_general(
            rows, columns, (((1,), (1,)), ((), ())), preferred_element_type=F32
        )

    acc = lax.fori_loop(0, RANKS // 2, pair, jnp.zeros((CAP, 2 * LANES), F32), unroll=2)
    out_ref[...] = acc[:, :LANES] + acc[:, LANES:]


def place(back, send_list):
    return pl.pallas_call(
        place_kernel,
        out_shape=jax.ShapeDtypeStruct((CAP, LANES), F32),
        in_specs=[VMEM_SPEC] * 2,
        out_specs=VMEM_SPEC,
        scratch_shapes=[pltpu.VMEM((RANKS, LANES), jnp.int32), pltpu.VMEM((RANKS, LANES), F32)],
        compiler_params=pltpu.CompilerParams(vmem_limit_bytes=16 << 20),
        name="place",
    )(back, send_list)


def exchange(values):
    return lax.all_to_all(values, ("lon", "lat"), split_axis=0, concat_axis=0, tiled=True)


def local(
    obs_value, send_list, recv_cell, column_depth, zonal_weight, merid_weight, vert_inverse, norm_scale
):
    is_north = lax.axis_index("lat") == N_LAT - 1
    north = jnp.full((8, LANES), jnp.where(is_north, 1.0, 0.0), F32)
    padded = jnp.pad(vert_inverse, ((0, 0), (0, ZP - NZ), (0, ZP - NZ)))
    outgoing, *coefs, vert = prepare(
        obs_value.reshape(CAP, LANES), send_list, zonal_weight, merid_weight, north, padded
    )
    incoming = exchange(outgoing)

    cell = jnp.maximum(recv_cell, 0)
    line = cell >> 7
    lat_row = line % NLAT
    plane = line // NLAT
    field = plane // NZ
    level = plane - field * NZ
    rows = ((field * NLAT + lat_row) * ZP + level).reshape(-1)
    lanes = jnp.transpose(cell & 127)

    sums = jnp.where(
        (jnp.arange(2 * LANES)[:, None] % LANES <= jnp.arange(2 * LANES)[None, :]), 1.0, 0.0
    ).astype(BF16)

    norm = jnp.pad(jnp.transpose(norm_scale, (0, 2, 1, 3)), ((0, 0), (0, 0), (0, ZP - NZ), (0, 0)))
    gridded, scale = scatter(rows, lanes, incoming, column_depth, norm)
    whole = solve(gridded, scale, coefs, vert, sums)
    picked = pick(rows, lanes, whole)
    returned = exchange(picked)
    result = place(returned, send_list)
    increment = jnp.transpose(whole[:, :, :NZ], (0, 2, 1, 3))
    return increment, result.reshape(-1)


def solution(mesh):
    in_specs = (
        P(("lon", "lat")),
        P(("lon", "lat"), None),
        P(("lon", "lat"), None),
        P("lat", "lon"),
        P(None, "lat", "lon"),
        P(None, "lat", "lon"),
        P(),
        P(None, None, "lat", "lon"),
    )
    out_specs = (P(None, None, "lat", "lon"), P(("lon", "lat")))
    return jax.shard_map(local, mesh=mesh, in_specs=in_specs, out_specs=out_specs, check_vma=False)
```

```python
import jax
import jax.numpy as jnp
from jax import lax
from jax.experimental import pallas as pl
from jax.experimental.pallas import tpu as pltpu
from jax.sharding import PartitionSpec as P

F32 = jnp.float32
BF16 = jnp.bfloat16
MESH = pl.DeviceIdType.MESH
NF, NZ, NLAT, NLON = 2, 75, 40, 128
ZP = 80
RANKS, CAP = 128, 80
N_LON, N_LAT = 32, 4
SOLVERS = 19
LANES = 128
CHUNK = 8
GRIDS = 8
ROWS = NF * NLAT * ZP
VMEM_SPEC = pl.BlockSpec(memory_space=pltpu.VMEM)
SMEM_SPEC = pl.BlockSpec(memory_space=pltpu.SMEM)
ANY_SPEC = pl.BlockSpec(memory_space=pl.ANY)


def lane_iota(rows):
    return lax.broadcasted_iota(jnp.int32, (rows, LANES), 1)


def split(value):
    high = value.astype(BF16)
    return high, (value - high.astype(F32)).astype(BF16)


def lane_pick(table, index):
    return jnp.take_along_axis(table, index, axis=1, mode="promise_in_bounds")


def push(source, target, send_sem, recv_sem, axis, device):
    return pltpu.make_async_remote_copy(
        src_ref=source, dst_ref=target, send_sem=send_sem, recv_sem=recv_sem,
        device_id={axis: device}, device_id_type=MESH,
    )


def over(axis, count, action, limit=None):
    mine = lax.axis_index(axis)

    def body(step, _):
        device = (mine + step) % count
        if limit is None:
            action(device)
        else:
            pl.when(device < limit)(lambda: action(device))
        return 0

    lax.fori_loop(1, count, body, 0)


def over_lon(action, limit=None):
    over("lon", N_LON, action, limit)


def over_lat(action):
    over("lat", N_LAT, action)


def greet():
    barrier = pltpu.get_barrier_semaphore()
    over_lon(
        lambda device: pl.semaphore_signal(
            barrier, inc=1, device_id={"lon": device}, device_id_type=MESH
        )
    )
    over_lat(
        lambda device: pl.semaphore_signal(
            barrier, inc=1, device_id={"lat": device}, device_id_type=MESH
        )
    )


def greeted():
    pl.semaphore_wait(pltpu.get_barrier_semaphore(), N_LON - 1 + N_LAT - 1)


def zonal_coefs(zw_ref, zs_ref, zr_ref, zco_ref, iw_ref, st_ref, rt_ref, zero):
    one = zero + 1.0
    iw_ref[...] = jnp.full((LANES, LANES), 1e-3, F32)
    iw_ref[: NF * NLAT, :] = 1.0 / zw_ref[...]
    iw_ref[...] = jnp.transpose(iw_ref[...])

    def zonal_step(step, carry):
        s_val, s_flux, s_sum, r_val, r_flux, r_sum = carry
        back = LANES - 1 - step
        st_ref[pl.ds(step, 1), :] = s_val[0:1]
        s_sum = s_sum + s_val
        s_val = s_val + s_flux * iw_ref[pl.ds(step, 1), :]
        s_flux = s_flux + s_val
        r_sum = r_sum + r_val
        r_val = r_val + r_flux * iw_ref[pl.ds(back, 1), :]
        rt_ref[pl.ds(back, 1), :] = r_val[0:1]
        r_flux = r_flux + r_val
        return s_val, s_flux, s_sum, r_val, r_flux, r_sum

    _, _, s_sum, r_first, _, r_sum = lax.fori_loop(
        0, LANES, zonal_step, (zero, one, zero, zero, one, zero), unroll=8
    )
    coupling = 1.0 / r_first[0:1]
    zco_ref[...] = jnp.zeros((8, LANES), F32)
    zco_ref[0:1, :] = coupling
    zco_ref[1:2, :] = r_sum[0:1] * coupling
    zco_ref[2:3, :] = s_sum[0:1] * coupling
    zs_ref[...] = jnp.transpose(st_ref[...])[: NF * NLAT, :]
    zr_ref[...] = jnp.transpose(rt_ref[...] * coupling)[: NF * NLAT, :]


def merid_coefs(mw_ref, ms_ref, mr_ref, mco_ref, miw_ref, north, zero):
    one = zero + 1.0
    miw_ref[...] = 1.0 / mw_ref[...]
    mco_ref[...] = jnp.zeros((NF, 8, LANES), F32)
    for field in range(NF):
        s_val, s_flux, s_sum = zero, one, zero
        for row in range(NLAT):
            ms_ref[field, row : row + 1, :] = s_val[0:1]
            s_sum = s_sum + s_val
            s_val = s_val + s_flux * miw_ref[field, row : row + 1, :]
            s_flux = s_flux + s_val
        r_val = jnp.where(north > 0.5, 1.0, miw_ref[field, NLAT - 1 : NLAT, :] + zero)
        r_flux = jnp.where(north > 0.5, 0.0, one)
        r_sum = zero
        mr_ref[field, NLAT - 1 : NLAT, :] = r_val[0:1]
        for row in range(NLAT - 2, -1, -1):
            r_sum = r_sum + r_val
            r_flux = r_flux + r_val
            r_val = r_val + r_flux * miw_ref[field, row : row + 1, :]
            mr_ref[field, row : row + 1, :] = r_val[0:1]
        inverse = 1.0 / r_val[0:1]
        coupling = jnp.where(north[0:1] > 0.5, 0.0, inverse)
        mr_ref[field] = mr_ref[field] * inverse
        mco_ref[field, 0:1, :] = coupling
        mco_ref[field, 1:2, :] = r_sum[0:1] * inverse
        mco_ref[field, 2:3, :] = s_sum[0:1] * coupling


def zonal_factor(zco_all, alpha, gamma, minv):
    coupling = zco_all[:, 0, :]
    west = jnp.concatenate([coupling[-1:], coupling[:-1]], axis=0)
    spill = zco_all[:, 2, :]
    mass = 1.0 + zco_all[:, 1, :] + jnp.concatenate([spill[-1:], spill[:-1]], axis=0)
    east = coupling
    for bit in range(5):
        stride = 1 << bit
        down = lambda v: jnp.concatenate([v[-stride:], v[:-stride]], axis=0)
        up = lambda v: jnp.concatenate([v[stride:], v[:stride]], axis=0)
        inverse = 1.0 / (mass + west + east)
        left = west * down(inverse)
        right = east * up(inverse)
        alpha[bit] = left
        gamma[bit] = right
        mass = mass + left * down(mass) + right * up(mass)
        west, east = left * down(west), right * up(east)
    minv[...] = 1.0 / mass


def prepare_kernel(
    obs_ref, send_ref, zw_ref, mw_ref, north_ref, vert_in,
    out_ref, zs_ref, zr_ref, zco_ref, ms_ref, mr_ref, mco_out, vert_ref, alpha, gamma, minv,
    idx_ref, iw_ref, st_ref, rt_ref, miw_ref,
    tile_out, tile_in, rows_out, rows_in, zco_all, mco_ref, mco_all,
    o1s, o1r, o2s, o2r, zco_s, zco_r, mco_s, mco_r,
):
    me = lax.axis_index("lon")
    my = lax.axis_index("lat")
    greet()
    idx_ref[...] = jnp.full((RANKS, LANES), -1, jnp.int32)
    idx_ref[:, :CAP] = send_ref[...]
    part = 64
    for start in range(0, RANKS, part):
        index = idx_ref[start : start + part, :]
        low = index & 127
        high = index >> 7

        def gather_row(row, acc, low=low, high=high):
            line = jnp.broadcast_to(obs_ref[pl.ds(row, 1), :], (part, LANES))
            return jnp.where(high == row, lane_pick(line, low), acc)

        picked = lax.fori_loop(0, CAP, gather_row, jnp.zeros((part, LANES), F32), unroll=8)
        for step in range(part // N_LAT):
            device = start // N_LAT + step
            tile_out[device, 0:4, :] = picked[4 * step : 4 * step + 4]
            tile_out[device, 4:8, :] = jnp.zeros((4, LANES), F32)

    first = lambda device, slot: push(
        tile_out.at[device], tile_in.at[slot], o1s.at[device], o1r.at[slot], "lon", device
    )
    second = lambda device, slot: push(
        rows_out.at[device], rows_in.at[slot], o2s.at[device], o2r.at[slot], "lat", device
    )
    zco_copy = lambda device, slot: push(
        zco_ref, zco_all.at[slot], zco_s.at[device], zco_r.at[slot], "lon", device
    )
    mco_copy = lambda device, slot: push(
        mco_ref, mco_all.at[slot], mco_s.at[device], mco_r.at[slot], "lat", device
    )
    greeted()
    over_lon(lambda device: first(device, me).start())
    tile_in[me] = tile_out[me]

    zero = north_ref[...] * 0.0
    zonal_coefs(zw_ref, zs_ref, zr_ref, zco_ref, iw_ref, st_ref, rt_ref, zero)
    over_lon(lambda device: first(0, device).wait_recv())
    for lat in range(N_LAT):
        rows_out[lat] = tile_in[:, lat, :]
    over_lat(lambda device: second(device, my).start())
    rows_in[my] = rows_out[my]
    over_lon(lambda device: zco_copy(device, me).start())
    zco_all[me] = zco_ref[...]
    merid_coefs(mw_ref, ms_ref, mr_ref, mco_ref, miw_ref, north_ref[...], zero)
    over_lat(lambda device: mco_copy(device, my).start())
    mco_all[my] = mco_ref[...]
    for field in range(NF):
        product = lax.dot_general(
            vert_in[field], vert_in[field], (((1,), (1,)), ((), ())),
            precision=lax.Precision.HIGHEST, preferred_element_type=F32,
        )
        high, low = split(product)
        vert_ref[field] = jnp.concatenate([high, low, high], axis=1)
    over_lon(lambda device: zco_copy(0, device).wait_recv())
    zonal_factor(zco_all, alpha, gamma, minv)
    over_lat(lambda device: second(0, device).wait_recv())
    for lat in range(N_LAT):
        out_ref[N_LON * lat : N_LON * lat + N_LON, :] = rows_in[lat]
    over_lat(lambda device: mco_copy(0, device).wait_recv())
    mco_out[...] = mco_all[...]
    over_lon(lambda device: first(device, me).wait_send())
    over_lat(lambda device: second(device, my).wait_send())
    over_lon(lambda device: zco_copy(device, me).wait_send())
    over_lat(lambda device: mco_copy(device, my).wait_send())


def prepare(obs, send_list, zonal_weight, merid_weight, north, vert_inverse):
    shape = lambda *dims: jax.ShapeDtypeStruct(dims, F32)
    vmem = lambda *dims: pltpu.VMEM(dims, F32)
    dma = pltpu.SemaphoreType.DMA
    return pl.pallas_call(
        prepare_kernel,
        out_shape=(
            shape(RANKS, LANES), shape(80, LANES), shape(80, LANES), shape(8, LANES),
            shape(NF, NLAT, LANES), shape(NF, NLAT, LANES), shape(N_LAT, NF, 8, LANES),
            jax.ShapeDtypeStruct((NF, ZP, 3 * ZP), BF16),
            shape(5, N_LON, LANES), shape(5, N_LON, LANES), shape(N_LON, LANES),
        ),
        in_specs=[VMEM_SPEC] * 6,
        out_specs=(VMEM_SPEC,) * 11,
        scratch_shapes=[
            pltpu.VMEM((RANKS, LANES), jnp.int32),
            vmem(LANES, LANES), vmem(LANES, LANES), vmem(LANES, LANES), vmem(NF, NLAT, LANES),
            vmem(N_LON, 8, LANES), vmem(N_LON, 8, LANES),
            vmem(N_LAT, N_LON, LANES), vmem(N_LAT, N_LON, LANES),
            vmem(N_LON, 8, LANES), vmem(NF, 8, LANES), vmem(N_LAT, NF, 8, LANES),
            dma((N_LON,)), dma((N_LON,)), dma((N_LAT,)), dma((N_LAT,)),
            dma((N_LON,)), dma((N_LON,)), dma((N_LAT,)), dma((N_LAT,)),
        ],
        compiler_params=pltpu.CompilerParams(
            collective_id=0, has_side_effects=True, vmem_limit_bytes=4 << 20
        ),
        name="prepare",
    )(obs, send_list, zonal_weight.reshape(NF * NLAT, LANES), merid_weight, north, vert_inverse)


def scatter_kernel(
    rows_ref, lane_ref, in_ref, depth_ref, norm_ref, field_ref, scale_ref, norm_buf, norm_sem,
    value_ref, even_ref, odd_ref, *grids
):
    def norm_copy(field, row):
        return pltpu.make_async_copy(
            norm_ref.at[field, :, row, :],
            norm_buf.at[field, row, pl.ds(0, NZ), :],
            norm_sem.at[field, row],
        )

    for field in range(NF):

        def begin(row, _, field=field):
            norm_copy(field, row).start()
            return 0

        lax.fori_loop(0, NLAT, begin, 0)

    def clear(step, _):
        at = pl.ds(pl.multiple_of(step * 64, 64), 64)
        for grid in grids:
            grid[at, :] = jnp.zeros((64, LANES), F32)
        return 0

    lax.fori_loop(0, ROWS // 64, clear, 0)
    value_ref[...] = jnp.transpose(in_ref[...])
    iota = lane_iota(CAP)

    def spread(q):
        index = jnp.full((CAP, LANES), q, jnp.int32)
        lane = lane_pick(lane_ref[...], index)
        return jnp.where(iota == lane, lane_pick(value_ref[:CAP, :], index), 0.0)

    def add(q, source):
        for k in range(CAP):
            at = pl.ds(rows_ref[q * CAP + k], 1)
            grid = grids[k % GRIDS]
            grid[at, :] = grid[at, :] + source[k : k + 1, :]

    even_ref[...] = spread(0)

    def senders(pair, _):
        q = 2 * pair
        odd_ref[...] = spread(q + 1)
        add(q, even_ref)
        even_ref[...] = spread(jnp.minimum(q + 2, RANKS - 1))
        add(q + 1, odd_ref)
        return 0

    lax.fori_loop(0, RANKS // 2, senders, 0)
    level = lax.broadcasted_iota(jnp.int32, (ZP, LANES), 0)
    for field in range(NF):

        def finish(row, _, field=field):
            norm_copy(field, row).wait()
            at = pl.ds(pl.multiple_of((field * NLAT + row) * ZP, ZP), ZP)
            total = [grid[at, :] for grid in grids]
            while len(total) > 1:
                total = [one + two for one, two in zip(total[::2], total[1::2])]
            wet = level < depth_ref[pl.ds(row, 1), :]
            scale = jnp.where(wet, norm_buf[field, row], 0.0)
            scale_ref[field, row] = scale
            field_ref[field, row] = jnp.where(wet, scale * total[0], 0.0)
            return 0

        lax.fori_loop(0, NLAT, finish, 0)


def scatter(rows, lanes, incoming, depth, norm):
    full = jax.ShapeDtypeStruct((NF, NLAT, ZP, LANES), F32)
    return pl.pallas_call(
        scatter_kernel,
        out_shape=(full, full),
        in_specs=[SMEM_SPEC] + [VMEM_SPEC] * 3 + [ANY_SPEC],
        out_specs=(VMEM_SPEC, VMEM_SPEC),
        scratch_shapes=[
            pltpu.VMEM((NF, NLAT, ZP, LANES), F32), pltpu.SemaphoreType.DMA((NF, NLAT)),
            pltpu.VMEM((LANES, LANES), F32), pltpu.VMEM((CAP, LANES), F32), pltpu.VMEM((CAP, LANES), F32),
        ]
        + [pltpu.VMEM((ROWS, LANES), F32)] * GRIDS,
        compiler_params=pltpu.CompilerParams(vmem_limit_bytes=40 << 20),
        name="scatter",
    )(rows, lanes, incoming, depth, norm)


def solve_kernel(
    field_ref, scale_ref, zs_ref, zr_ref, zco_ref, ms_ref, mr_ref, mco_all, vert_ref,
    alpha, gamma, minv, sums_ref,
    x_ref,
    zsend, zrecv, zret, zres, msend, mrecv, mret, mres,
    acc_a, acc_b, ubuf, gbuf, mtot,
    z1s, z1r, z2s, z2r, m1s, m1r, m2s, m2r,
):
    me = lax.axis_index("lon")
    my = lax.axis_index("lat")
    iota = lane_iota(ZP)
    is_solver = me < SOLVERS

    greet()
    over_solvers = lambda action: over_lon(action, SOLVERS)

    def zonal_pass(field, chunk, load, field_base):
        lines, left = [], []
        for step in range(CHUNK):
            row = chunk * CHUNK + step
            at = pl.ds(field_base + row, 1)
            s_row, r_row = zs_ref[at, :], zr_ref[at, :]
            value = load(row, step)
            for coef in (s_row, r_row):
                high, low = split(coef * value)
                left.append(jnp.concatenate([high, low], axis=1))
            lines.append((row, s_row, r_row))
        sums = jnp.dot(jnp.concatenate(left, axis=0), sums_ref[...], preferred_element_type=F32)
        tot_a, tot_b = acc_a[...], acc_b[...]
        for step, (row, s_row, r_row) in enumerate(lines):
            a_part = sums[2 * step * ZP : (2 * step + 1) * ZP]
            b_part = sums[(2 * step + 1) * ZP : (2 * step + 2) * ZP]
            x_ref[field, row] = r_row * a_part[:, :LANES] - s_row * b_part[:, :LANES]
            mine = iota == field_base + row
            tot_a = jnp.where(mine, a_part[:, LANES:], tot_a)
            tot_b = jnp.where(mine, b_part[:, LANES:], tot_b)
        acc_a[...] = tot_a
        acc_b[...] = tot_b

    def zonal_send(turn):
        acc_a[...] = acc_a[...] * zco_ref[0:1, :]
        for solver in range(SOLVERS):
            zsend[turn, solver, 0:4, :] = acc_b[4 * solver : 4 * solver + 4, :]
            zsend[turn, solver, 4:8, :] = acc_a[4 * solver : 4 * solver + 4, :]
        over_solvers(lambda device: zonal_out(turn, device, me).start())

        @pl.when(is_solver)
        def _():
            zrecv[turn, me] = zsend[turn, me]

    def zonal_out(turn, device, slot):
        return push(
            zsend.at[turn, device], zrecv.at[turn, slot], z1s.at[turn, device], z1r.at[turn, slot], "lon", device
        )

    def zonal_back(turn, device, slot):
        return push(
            zret.at[turn, device], zres.at[turn, slot], z2s.at[turn, device], z2r.at[turn, slot], "lon", device
        )

    def zonal_reduced(turn):
        over_lon(lambda device: zonal_out(turn, 0, device).wait_recv())
        tiles = [zrecv[turn, k] for k in range(N_LON)]
        flip = lambda v: jnp.concatenate([v[4:], v[:4]], axis=0)
        right_side = [tiles[k] + flip(tiles[k - 1]) for k in range(N_LON)]
        for bit in range(5):
            stride = 1 << bit
            right_side = [
                right_side[k]
                + alpha[bit, k : k + 1, :] * right_side[(k - stride) % N_LON]
                + gamma[bit, k : k + 1, :] * right_side[(k + stride) % N_LON]
                for k in range(N_LON)
            ]
        values = [right_side[k] * minv[k : k + 1, :] for k in range(N_LON)]
        for k in range(N_LON):
            zret[turn, k] = jnp.concatenate([values[k][:4], values[(k + 1) % N_LON][:4]], axis=0)
        over_lon(lambda device: zonal_back(turn, device, me).start())
        zres[turn, me] = zret[turn, me]

    def zonal_receive(turn):
        over_solvers(lambda device: zonal_back(turn, 0, device).wait_recv())
        ubuf[72:80, :] = jnp.zeros((8, LANES), F32)
        gbuf[72:80, :] = jnp.zeros((8, LANES), F32)
        for solver in range(SOLVERS):
            ubuf[4 * solver : 4 * solver + 4, :] = zres[turn, solver, 0:4, :]
            gbuf[4 * solver : 4 * solver + 4, :] = zres[turn, solver, 4:8, :]
        gbuf[...] = gbuf[...] * zco_ref[0:1, :] + acc_b[...]

    def zonal_values(field, chunk, field_base):
        u_all, g_all = ubuf[...], gbuf[...]
        found = []
        for step in range(CHUNK):
            row = chunk * CHUNK + step
            at = pl.ds(field_base + row, 1)
            found.append(
                x_ref[field, row]
                + zr_ref[at, :] * jnp.broadcast_to(u_all[:, step : step + 1], (ZP, LANES))
                + zs_ref[at, :] * jnp.broadcast_to(g_all[:, step : step + 1], (ZP, LANES))
            )
        ubuf[...] = pltpu.roll(u_all, LANES - CHUNK, 1)
        gbuf[...] = pltpu.roll(g_all, LANES - CHUNK, 1)
        return found

    def vertical(field, value):
        high, low = split(value)
        return jnp.dot(
            vert_ref[field], jnp.concatenate([high, high, low], axis=0), preferred_element_type=F32
        )

    def vertical_field(field):
        def body(step, _):
            row = step * CHUNK
            value = jnp.concatenate([x_ref[field, row + k] for k in range(CHUNK)], axis=1)
            value = vertical(field, value)
            for k in range(CHUNK):
                x_ref[field, row + k] = value[:, k * LANES : (k + 1) * LANES]
            return 0

        lax.fori_loop(0, NLAT // CHUNK, body, 0)

    def merid_out(turn, device, slot):
        return push(
            msend.at[turn, device], mrecv.at[turn, slot], m1s.at[turn, device], m1r.at[turn, slot], "lat", device
        )

    def merid_back(turn, device, slot):
        return push(
            mret.at[turn, device], mres.at[turn, slot], m2s.at[turn, device], m2r.at[turn, slot], "lat", device
        )

    def merid_step(field, row, value, tot_a, tot_b):
        s_row, r_row = ms_ref[field, pl.ds(row, 1), :], mr_ref[field, pl.ds(row, 1), :]
        tot_a = tot_a + s_row * value
        tot_b = tot_b + r_row * value
        x_ref[field, row] = r_row * tot_a - s_row * tot_b
        return tot_a, tot_b

    def merid_send(turn, field, tot_a, tot_b):
        mtot[field] = tot_b
        tot_a = tot_a * mco_all[my, field, 0:1, :]
        for half in range(2):
            msend[turn, 2 * field + half, 0] = tot_b[40 * half : 40 * half + 40]
            msend[turn, 2 * field + half, 1] = tot_a[40 * half : 40 * half + 40]
        for half in range(2):
            solver = 2 * field + half

            @pl.when(my != solver)
            def _(solver=solver):
                merid_out(turn, solver, my).start()

            @pl.when(my == solver)
            def _(solver=solver):
                mrecv[turn, solver] = msend[turn, solver]

    def merid_reduced(turn):
        field = my // 2
        over_lat(lambda device: merid_out(turn, 0, device).wait_recv())
        rows = [mco_all[k, field] for k in range(N_LAT)]
        mass = 1.0 + rows[0][1:2]
        reduced = mrecv[turn, 0, 0]
        kept, inverses = [], []
        for k in range(N_LAT):
            coupling = rows[k][0:1]
            inverse = 1.0 / (mass + coupling)
            kept.append(reduced)
            inverses.append(inverse)
            if k + 1 < N_LAT:
                factor = coupling * inverse
                mass = 1.0 + rows[k + 1][1:2] + rows[k][2:3] + factor * mass
                reduced = mrecv[turn, k + 1, 0] + mrecv[turn, k, 1] + factor * reduced
        value = kept[N_LAT - 1] * inverses[N_LAT - 1]
        mret[turn, N_LAT - 1, 0] = value
        mret[turn, N_LAT - 1, 1] = jnp.zeros_like(value)
        for k in range(N_LAT - 2, -1, -1):
            mret[turn, k, 1] = value
            value = (kept[k] + rows[k][0:1] * value) * inverses[k]
            mret[turn, k, 0] = value
        over_lat(lambda device: merid_back(turn, device, my).start())
        mres[turn, my] = mret[turn, my]

    def merid_edges(turn, field):
        for half in range(2):
            solver = 2 * field + half

            @pl.when(my != solver)
            def _(solver=solver):
                merid_back(turn, 0, solver).wait_recv()

        own = jnp.concatenate([mres[turn, 2 * field, 0], mres[turn, 2 * field + 1, 0]], axis=0)
        after = jnp.concatenate([mres[turn, 2 * field, 1], mres[turn, 2 * field + 1, 1]], axis=0)
        ubuf[...] = own
        gbuf[...] = after * mco_all[my, field, 0:1, :] + mtot[field]

    def merid_value(field, row):
        return (
            x_ref[field, row]
            + mr_ref[field, pl.ds(row, 1), :] * ubuf[...]
            + ms_ref[field, pl.ds(row, 1), :] * gbuf[...]
        )

    nothing = jnp.zeros((ZP, LANES), F32)

    acc_a[...] = nothing
    acc_b[...] = nothing
    for field in range(NF):

        def first_pass(chunk, _, field=field):
            zonal_pass(field, chunk, lambda row, step: field_ref[field, row], field * NLAT)
            return 0

        lax.fori_loop(0, NLAT // CHUNK, first_pass, 0)
    greeted()
    zonal_send(0)
    vertical_field(0)

    @pl.when(is_solver)
    def _():
        zonal_reduced(0)

    vertical_field(1)
    zonal_receive(0)
    both = jnp.concatenate([ubuf[...], gbuf[...]], axis=1)
    upper = vertical(0, both)
    lower = vertical(1, both)
    first_field = iota < NLAT
    ubuf[...] = jnp.where(first_field, upper[:, :LANES], lower[:, :LANES])
    gbuf[...] = jnp.where(first_field, upper[:, LANES:], lower[:, LANES:])

    for field in range(NF):

        def second_pass(chunk, carry, field=field):
            tot_a, tot_b = carry
            found = zonal_values(field, chunk, field * NLAT)
            for step in range(CHUNK):
                tot_a, tot_b = merid_step(field, chunk * CHUNK + step, found[step], tot_a, tot_b)
            return tot_a, tot_b

        tot_a, tot_b = lax.fori_loop(0, NLAT // CHUNK, second_pass, (nothing, nothing))
        merid_send(0, field, tot_a, tot_b)
    merid_reduced(0)

    for field in range(NF):
        merid_edges(0, field)

        def third_pass(row, carry, field=field):
            return merid_step(field, row, merid_value(field, row), *carry)

        tot_a, tot_b = lax.fori_loop(0, NLAT, third_pass, (nothing, nothing), unroll=2)
        merid_send(1, field, tot_a, tot_b)
    merid_reduced(1)

    acc_a[...] = nothing
    acc_b[...] = nothing
    for field in range(NF):
        merid_edges(1, field)

        def fourth_pass(chunk, _, field=field):
            zonal_pass(field, chunk, lambda row, step: merid_value(field, row), field * NLAT)
            return 0

        lax.fori_loop(0, NLAT // CHUNK, fourth_pass, 0)
    zonal_send(1)

    @pl.when(is_solver)
    def _():
        zonal_reduced(1)

    zonal_receive(1)
    for field in range(NF):

        def last_pass(chunk, _, field=field):
            found = zonal_values(field, chunk, field * NLAT)
            for step in range(CHUNK):
                row = chunk * CHUNK + step
                x_ref[field, row] = found[step] * scale_ref[field, row]
            return 0

        lax.fori_loop(0, NLAT // CHUNK, last_pass, 0)

    for turn in range(2):
        over_solvers(lambda device: zonal_out(turn, device, me).wait_send())
        over_lat(lambda device: merid_out(turn, device, my).wait_send())
        over_lat(lambda device: merid_back(turn, device, my).wait_send())

        @pl.when(is_solver)
        def _(turn=turn):
            over_lon(lambda device: zonal_back(turn, device, me).wait_send())


def solve(field, scale, coefs, sums):
    dma = pltpu.SemaphoreType.DMA
    vmem = lambda *dims: pltpu.VMEM(dims, F32)
    return pl.pallas_call(
        solve_kernel,
        out_shape=jax.ShapeDtypeStruct((NF, NLAT, ZP, LANES), F32),
        in_specs=[VMEM_SPEC] * 13,
        out_specs=VMEM_SPEC,
        scratch_shapes=[
            vmem(2, SOLVERS, 8, LANES), vmem(2, N_LON, 8, LANES),
            vmem(2, N_LON, 8, LANES), vmem(2, SOLVERS, 8, LANES),
            vmem(2, N_LAT, 2, 40, LANES), vmem(2, N_LAT, 2, 40, LANES),
            vmem(2, N_LAT, 2, 40, LANES), vmem(2, N_LAT, 2, 40, LANES),
            vmem(ZP, LANES), vmem(ZP, LANES), vmem(ZP, LANES), vmem(ZP, LANES),
            vmem(NF, ZP, LANES),
            dma((2, N_LON)), dma((2, N_LON)), dma((2, N_LON)), dma((2, N_LON)),
            dma((2, N_LAT)), dma((2, N_LAT)), dma((2, N_LAT)), dma((2, N_LAT)),
        ],
        compiler_params=pltpu.CompilerParams(
            collective_id=1, has_side_effects=True, vmem_limit_bytes=18 << 20
        ),
        name="solve",
    )(field, scale, *coefs, sums)


def pick_kernel(rows_ref, lane_ref, x_ref, out_ref, inc_ref, inc_sem, *copies):
    iota = lane_iota(8)

    def inc_copy(field, row):
        return pltpu.make_async_copy(
            x_ref.at[pl.ds(pl.multiple_of((field * NLAT + row) * ZP, ZP), NZ), :],
            inc_ref.at[field, :, row, :],
            inc_sem.at[field, row],
        )

    def over_rows(action):
        for field in range(NF):

            def body(row, _, field=field):
                action(inc_copy(field, row))
                return 0

            lax.fori_loop(0, NLAT, body, 0)

    over_rows(lambda copy: copy.start())
    group = len(copies)

    def senders(step, acc):
        acc = list(acc)
        for part in range(group):
            q = step * group + part
            for k in range(CAP):
                copies[part][k : k + 1, :] = x_ref[pl.ds(rows_ref[q * CAP + k], 1), :]
        for part in range(group):
            q = step * group + part
            for tile in range(CAP // 8):
                at = slice(8 * tile, 8 * tile + 8)
                found = lane_pick(copies[part][at, :], lane_ref[at, :])
                acc[tile] = jnp.where(iota == q, found, acc[tile])
        return tuple(acc)

    acc = lax.fori_loop(0, RANKS // group, senders, (jnp.zeros((8, LANES), F32),) * (CAP // 8))
    whole = jnp.concatenate(list(acc) + [jnp.zeros((LANES - CAP, LANES), F32)], axis=0)
    out_ref[...] = jnp.transpose(whole)
    over_rows(lambda copy: copy.wait())


def pick(rows, lanes, increment):
    return pl.pallas_call(
        pick_kernel,
        out_shape=(
            jax.ShapeDtypeStruct((RANKS, LANES), F32),
            jax.ShapeDtypeStruct((NF, NZ, NLAT, LANES), F32),
        ),
        in_specs=[SMEM_SPEC, VMEM_SPEC, VMEM_SPEC],
        out_specs=(VMEM_SPEC, ANY_SPEC),
        scratch_shapes=[pltpu.SemaphoreType.DMA((NF, NLAT))] + [pltpu.VMEM((CAP, LANES), F32)] * 8,
        compiler_params=pltpu.CompilerParams(vmem_limit_bytes=8 << 20),
        name="pick",
    )(rows, lanes, increment.reshape(ROWS, LANES))


def place_kernel(
    picked_ref, send_ref, out_ref, idx_ref, val_ref, rows_in, tile_out, tile_in, b1s, b1r, b2s, b2r
):
    me = lax.axis_index("lon")
    my = lax.axis_index("lat")
    greet()
    idx_ref[...] = jnp.full((RANKS, LANES), -1, jnp.int32)
    idx_ref[:, :CAP] = send_ref[...]
    first = lambda device, slot: push(
        picked_ref.at[device], rows_in.at[slot], b1s.at[device], b1r.at[slot], "lat", device
    )
    second = lambda device, slot: push(
        tile_out.at[device], tile_in.at[slot], b2s.at[device], b2r.at[slot], "lon", device
    )
    greeted()
    over_lat(lambda device: first(device, my).start())
    rows_in[my] = picked_ref[my]
    tile_out[...] = jnp.zeros((N_LON, 8, LANES), F32)
    over_lat(lambda device: first(0, device).wait_recv())
    for device in range(N_LON):
        for lat in range(N_LAT):
            tile_out[device, lat : lat + 1, :] = rows_in[lat, device : device + 1, :]
    over_lon(lambda device: second(device, me).start())
    tile_in[me] = tile_out[me]
    over_lon(lambda device: second(0, device).wait_recv())
    for device in range(N_LON):
        val_ref[4 * device : 4 * device + 4, :] = tile_in[device, 0:4, :]
    row_iota = lax.broadcasted_iota(jnp.int32, (CAP, 2 * LANES), 0)
    col_iota = lax.broadcasted_iota(jnp.int32, (LANES, 2 * LANES), 0)

    def pair(step, acc):
        left, right = pl.ds(2 * step, 1), pl.ds(2 * step + 1, 1)
        index = jnp.concatenate([idx_ref[left, :], idx_ref[right, :]], axis=1)
        value = jnp.concatenate([val_ref[left, :], val_ref[right, :]], axis=1)
        high = value.astype(BF16).astype(F32)
        low = value - high
        rows = jnp.where(row_iota == (index >> 7), 1.0, 0.0).astype(BF16)
        here = col_iota == (index & 127)
        columns = jnp.concatenate(
            [jnp.where(here, high, 0.0).astype(BF16), jnp.where(here, low, 0.0).astype(BF16)], axis=0
        )
        return acc + lax.dot_general(
            rows, columns, (((1,), (1,)), ((), ())), preferred_element_type=F32
        )

    acc = lax.fori_loop(0, RANKS // 2, pair, jnp.zeros((CAP, 2 * LANES), F32), unroll=4)
    out_ref[...] = acc[:, :LANES] + acc[:, LANES:]
    over_lat(lambda device: first(device, my).wait_send())
    over_lon(lambda device: second(device, me).wait_send())


def place(picked, send_list):
    vmem = lambda *dims: pltpu.VMEM(dims, F32)
    dma = pltpu.SemaphoreType.DMA
    return pl.pallas_call(
        place_kernel,
        out_shape=jax.ShapeDtypeStruct((CAP, LANES), F32),
        in_specs=[VMEM_SPEC] * 2,
        out_specs=VMEM_SPEC,
        scratch_shapes=[
            pltpu.VMEM((RANKS, LANES), jnp.int32), vmem(RANKS, LANES), vmem(N_LAT, N_LON, LANES),
            vmem(N_LON, 8, LANES), vmem(N_LON, 8, LANES),
            dma((N_LAT,)), dma((N_LAT,)), dma((N_LON,)), dma((N_LON,)),
        ],
        compiler_params=pltpu.CompilerParams(
            collective_id=2, has_side_effects=True, vmem_limit_bytes=4 << 20
        ),
        name="place",
    )(picked.reshape(N_LAT, N_LON, LANES), send_list)


def local(
    obs_value, send_list, recv_cell, column_depth, zonal_weight, merid_weight, vert_inverse, norm_scale
):
    is_north = lax.axis_index("lat") == N_LAT - 1
    north = jnp.full((8, LANES), jnp.where(is_north, 1.0, 0.0), F32)
    padded = jnp.pad(vert_inverse, ((0, 0), (0, ZP - NZ), (0, ZP - NZ)))
    incoming, *coefs = prepare(
        obs_value.reshape(CAP, LANES), send_list, zonal_weight, merid_weight, north, padded
    )

    cell = jnp.swapaxes(jnp.maximum(recv_cell, 0).reshape(N_LON, N_LAT, CAP), 0, 1)
    cell = cell.reshape(RANKS, CAP)
    line = cell >> 7
    lat_row = line % NLAT
    plane = line // NLAT
    field = plane // NZ
    level = plane - field * NZ
    rows = ((field * NLAT + lat_row) * ZP + level).reshape(-1)
    lanes = jnp.transpose(cell & 127)
    sums = jnp.where(
        (jnp.arange(2 * LANES)[:, None] % LANES <= jnp.arange(2 * LANES)[None, :]), 1.0, 0.0
    ).astype(BF16)

    gridded, scale = scatter(rows, lanes, incoming, column_depth, norm_scale)
    whole = solve(gridded, scale, coefs, sums)
    picked, increment = pick(rows, lanes, whole)
    return increment, place(picked, send_list).reshape(-1)


def solution(mesh):
    in_specs = (
        P(("lon", "lat")),
        P(("lon", "lat"), None),
        P(("lon", "lat"), None),
        P("lat", "lon"),
        P(None, "lat", "lon"),
        P(None, "lat", "lon"),
        P(),
        P(None, None, "lat", "lon"),
    )
    out_specs = (P(None, None, "lat", "lon"), P(("lon", "lat")))
    return jax.shard_map(local, mesh=mesh, in_specs=in_specs, out_specs=out_specs, check_vma=False)
```

```python
import jax
import jax.numpy as jnp
from jax import lax
from jax.experimental import pallas as pl
from jax.experimental.pallas import tpu as pltpu
from jax.sharding import PartitionSpec as P

F32 = jnp.float32
BF16 = jnp.bfloat16
MESH = pl.DeviceIdType.MESH
NF, NZ, NLAT, NLON = 2, 75, 40, 128
ZP = 80
RANKS, CAP = 128, 80
N_LON, N_LAT = 32, 4
GROUPS = 15
GROUP = 5
SPLIT = 24
LANES = 128
CHUNK = 8
GRIDS = 8
ROWS = NF * NLAT * ZP
VMEM_SPEC = pl.BlockSpec(memory_space=pltpu.VMEM)
SMEM_SPEC = pl.BlockSpec(memory_space=pltpu.SMEM)
ANY_SPEC = pl.BlockSpec(memory_space=pl.ANY)


def lane_iota(rows):
    return lax.broadcasted_iota(jnp.int32, (rows, LANES), 1)


def split(value):
    high = value.astype(BF16)
    return high, (value - high.astype(F32)).astype(BF16)


def lane_pick(table, index):
    return jnp.take_along_axis(table, index, axis=1, mode="promise_in_bounds")


def push(source, target, send_sem, recv_sem, axis, device):
    return pltpu.make_async_remote_copy(
        src_ref=source, dst_ref=target, send_sem=send_sem, recv_sem=recv_sem,
        device_id={axis: device}, device_id_type=MESH,
    )


def over(axis, count, action):
    mine = lax.axis_index(axis)

    def body(step, _):
        action((mine + step) % count)
        return 0

    lax.fori_loop(1, count, body, 0)


def over_lon(action):
    over("lon", N_LON, action)


def over_lat(action):
    over("lat", N_LAT, action)


def greet():
    barrier = pltpu.get_barrier_semaphore()
    over_lon(
        lambda device: pl.semaphore_signal(
            barrier, inc=1, device_id={"lon": device}, device_id_type=MESH
        )
    )
    over_lat(
        lambda device: pl.semaphore_signal(
            barrier, inc=1, device_id={"lat": device}, device_id_type=MESH
        )
    )


def greeted():
    pl.semaphore_wait(pltpu.get_barrier_semaphore(), N_LON - 1 + N_LAT - 1)


def zonal_coefs(zw_ref, zs_ref, zr_ref, zco_ref, iw_ref, st_ref, rt_ref, zero):
    one = zero + 1.0
    iw_ref[...] = jnp.full((LANES, LANES), 1e-3, F32)
    iw_ref[: NF * NLAT, :] = 1.0 / zw_ref[...]
    iw_ref[...] = jnp.transpose(iw_ref[...])

    def zonal_step(step, carry):
        s_val, s_flux, s_sum, r_val, r_flux, r_sum = carry
        back = LANES - 1 - step
        st_ref[pl.ds(step, 1), :] = s_val[0:1]
        s_sum = s_sum + s_val
        s_val = s_val + s_flux * iw_ref[pl.ds(step, 1), :]
        s_flux = s_flux + s_val
        r_sum = r_sum + r_val
        r_val = r_val + r_flux * iw_ref[pl.ds(back, 1), :]
        rt_ref[pl.ds(back, 1), :] = r_val[0:1]
        r_flux = r_flux + r_val
        return s_val, s_flux, s_sum, r_val, r_flux, r_sum

    _, _, s_sum, r_first, _, r_sum = lax.fori_loop(
        0, LANES, zonal_step, (zero, one, zero, zero, one, zero), unroll=8
    )
    coupling = 1.0 / r_first[0:1]
    zco_ref[...] = jnp.zeros((8, LANES), F32)
    zco_ref[0:1, :] = coupling
    zco_ref[1:2, :] = r_sum[0:1] * coupling
    zco_ref[2:3, :] = s_sum[0:1] * coupling
    zs_ref[...] = jnp.transpose(st_ref[...])[: NF * NLAT, :]
    zr_ref[...] = jnp.transpose(rt_ref[...] * coupling)[: NF * NLAT, :]


def merid_coefs(mw_ref, ms_ref, mr_ref, mss_ref, mrr_ref, mco_ref, miw_ref, north, zero):
    one = zero + 1.0
    miw_ref[...] = 1.0 / mw_ref[...]
    mco_ref[...] = jnp.zeros((NF, 8, LANES), F32)
    for field in range(NF):
        s_val, s_flux, s_sum = zero, one, zero
        for row in range(NLAT):
            ms_ref[field, row : row + 1, :] = s_val[0:1]
            s_sum = s_sum + s_val
            s_val = s_val + s_flux * miw_ref[field, row : row + 1, :]
            s_flux = s_flux + s_val
        r_val = jnp.where(north > 0.5, 1.0, miw_ref[field, NLAT - 1 : NLAT, :] + zero)
        r_flux = jnp.where(north > 0.5, 0.0, one)
        r_sum = zero
        mr_ref[field, NLAT - 1 : NLAT, :] = r_val[0:1]
        for row in range(NLAT - 2, -1, -1):
            r_sum = r_sum + r_val
            r_flux = r_flux + r_val
            r_val = r_val + r_flux * miw_ref[field, row : row + 1, :]
            mr_ref[field, row : row + 1, :] = r_val[0:1]
        inverse = 1.0 / r_val[0:1]
        coupling = jnp.where(north[0:1] > 0.5, 0.0, inverse)
        mr_ref[field] = mr_ref[field] * inverse
        sum_rr, sum_rs = zero, zero
        for row in range(NLAT - 1, -1, -1):
            at = slice(row, row + 1)
            s_row, r_row = ms_ref[field, at, :], mr_ref[field, at, :]
            mrr_ref[field, at, :] = s_row * sum_rr[0:1]
            mss_ref[field, at, :] = s_row * sum_rs[0:1]
            sum_rr = sum_rr + r_row * r_row
            sum_rs = sum_rs + r_row * s_row
        sum_sr, sum_ss = zero, zero
        for row in range(NLAT):
            at = slice(row, row + 1)
            s_row, r_row = ms_ref[field, at, :], mr_ref[field, at, :]
            sum_sr = sum_sr + s_row * r_row
            sum_ss = sum_ss + s_row * s_row
            mrr_ref[field, at, :] = mrr_ref[field, at, :] + r_row * sum_sr[0:1]
            mss_ref[field, at, :] = mss_ref[field, at, :] + r_row * sum_ss[0:1]
        mco_ref[field, 0:1, :] = coupling
        mco_ref[field, 1:2, :] = r_sum[0:1] * inverse
        mco_ref[field, 2:3, :] = s_sum[0:1] * coupling
        mco_ref[field, 3:4, :] = sum_rr[0:1]
        mco_ref[field, 4:5, :] = sum_rs[0:1] * coupling
        mco_ref[field, 5:6, :] = sum_ss[0:1] * coupling * coupling


def zonal_factor(zco_all, alpha, gamma, minv):
    coupling = zco_all[:, 0, :]
    west = jnp.concatenate([coupling[-1:], coupling[:-1]], axis=0)
    spill = zco_all[:, 2, :]
    mass = 1.0 + zco_all[:, 1, :] + jnp.concatenate([spill[-1:], spill[:-1]], axis=0)
    east = coupling
    for bit in range(5):
        stride = 1 << bit
        down = lambda v: jnp.concatenate([v[-stride:], v[:-stride]], axis=0)
        up = lambda v: jnp.concatenate([v[stride:], v[:stride]], axis=0)
        inverse = 1.0 / (mass + west + east)
        left = west * down(inverse)
        right = east * up(inverse)
        for field in range(NF):
            alpha[field, bit] = to_field(left, field)
            gamma[field, bit] = to_field(right, field)
        mass = mass + left * down(mass) + right * up(mass)
        west, east = left * down(west), right * up(east)
    for field in range(NF):
        minv[field] = to_field(1.0 / mass, field)


def to_field(rows, field):
    return rows if field == 0 else pltpu.roll(rows, LANES - field * NLAT, 1)


def gather_lines(table_ref, count, high, low, base):
    def step(row, acc):
        line = jnp.broadcast_to(table_ref[pl.ds(row, 1), :], (ZP, LANES))
        return jnp.where(high == row + base, lane_pick(line, low), acc)

    return lax.fori_loop(0, count, step, jnp.zeros((ZP, LANES), F32), unroll=8)


def two_phase(tile_out, tile_in, rows_out, rows_in, sems):
    me = lax.axis_index("lon")
    my = lax.axis_index("lat")
    s1, r1, s2, r2 = sems
    first = lambda device, slot: push(
        tile_out.at[device], tile_in.at[slot], s1.at[device], r1.at[slot], "lon", device
    )
    second = lambda device, slot: push(
        rows_out.at[device], rows_in.at[slot], s2.at[device], r2.at[slot], "lat", device
    )

    def begin():
        over_lon(lambda device: first(device, me).start())
        tile_in[me] = tile_out[me]

    def middle():
        over_lon(lambda device: first(0, device).wait_recv())
        for lat in range(N_LAT):
            rows_out[lat] = tile_in[:, lat, :]
        over_lat(lambda device: second(device, my).start())
        rows_in[my] = rows_out[my]

    def end():
        over_lat(lambda device: second(0, device).wait_recv())

    def sent():
        over_lon(lambda device: first(device, me).wait_send())
        over_lat(lambda device: second(device, my).wait_send())

    return begin, middle, end, sent


def prepare_kernel(
    obs_ref, send_ref, zw_ref, mw_ref, north_ref, vert_in,
    out_ref, zs_ref, zr_ref, zco_out, ms_ref, mr_ref, mss_ref, mrr_ref, mco_out, vert_ref,
    alpha, gamma, minv, sums_ref,
    iw_ref, st_ref, rt_ref, miw_ref, prod_ref,
    tile_out, tile_in, rows_out, rows_in, zco_ref, zco_all, mco_ref, mco_all,
    o1s, o1r, o2s, o2r, zco_s, zco_r, mco_s, mco_r,
):
    me = lax.axis_index("lon")
    my = lax.axis_index("lat")
    greet()
    index = send_ref[...]
    picked = gather_lines(obs_ref, CAP, index >> 7, index & 127, 0)
    picked = jnp.transpose(
        jnp.concatenate([picked, jnp.zeros((LANES - CAP, LANES), F32)], axis=0)
    )
    for device in range(N_LON):
        tile_out[device, 0:4, :] = picked[4 * device : 4 * device + 4]
        tile_out[device, 4:8, :] = jnp.zeros((4, LANES), F32)

    begin, middle, end, sent = two_phase(tile_out, tile_in, rows_out, rows_in, (o1s, o1r, o2s, o2r))
    zco_copy = lambda device, slot: push(
        zco_ref, zco_all.at[slot], zco_s.at[device], zco_r.at[slot], "lon", device
    )
    mco_copy = lambda device, slot: push(
        mco_ref, mco_all.at[slot], mco_s.at[device], mco_r.at[slot], "lat", device
    )
    greeted()
    begin()
    zero = north_ref[...] * 0.0
    zonal_coefs(zw_ref, zs_ref, zr_ref, zco_ref, iw_ref, st_ref, rt_ref, zero)
    middle()
    over_lon(lambda device: zco_copy(device, me).start())
    zco_all[me] = zco_ref[...]
    for field in range(NF):
        zco_out[field] = to_field(zco_ref[...], field)
    merid_coefs(mw_ref, ms_ref, mr_ref, mss_ref, mrr_ref, mco_ref, miw_ref, north_ref[...], zero)
    over_lat(lambda device: mco_copy(device, my).start())
    mco_all[my] = mco_ref[...]
    prod_ref[...] = jnp.zeros((ZP, LANES), F32)
    for field in range(NF):
        matrix = vert_in[:, field, :]
        prod_ref[:NZ, :NZ] = lax.dot_general(
            matrix, matrix, (((1,), (1,)), ((), ())),
            precision=lax.Precision.HIGHEST, preferred_element_type=F32,
        )
        high, low = split(prod_ref[:, :ZP])
        vert_ref[field] = jnp.concatenate([high, low, high], axis=1)
    source = lax.broadcasted_iota(jnp.int32, (2 * LANES, 2 * LANES), 0) & 127
    target = lax.broadcasted_iota(jnp.int32, (2 * LANES, 2 * LANES), 1)
    sums_ref[...] = jnp.where(source <= target, 1.0, 0.0).astype(BF16)
    end()
    for lat in range(N_LAT):
        out_ref[N_LON * lat : N_LON * lat + N_LON, :] = rows_in[lat]
    over_lon(lambda device: zco_copy(0, device).wait_recv())
    zonal_factor(zco_all, alpha, gamma, minv)
    over_lat(lambda device: mco_copy(0, device).wait_recv())
    mco_out[...] = mco_all[...]
    sent()
    over_lon(lambda device: zco_copy(device, me).wait_send())
    over_lat(lambda device: mco_copy(device, my).wait_send())


def prepare(obs, send_list, zonal_weight, merid_weight, north, vert_inverse):
    shape = lambda *dims: jax.ShapeDtypeStruct(dims, F32)
    vmem = lambda *dims: pltpu.VMEM(dims, F32)
    dma = pltpu.SemaphoreType.DMA
    return pl.pallas_call(
        prepare_kernel,
        out_shape=(
            shape(RANKS, LANES), shape(80, LANES), shape(80, LANES), shape(NF, 8, LANES),
            shape(NF, NLAT, LANES), shape(NF, NLAT, LANES),
            shape(NF, NLAT, LANES), shape(NF, NLAT, LANES), shape(N_LAT, NF, 8, LANES),
            jax.ShapeDtypeStruct((NF, ZP, 3 * ZP), BF16),
            shape(NF, 5, N_LON, LANES), shape(NF, 5, N_LON, LANES), shape(NF, N_LON, LANES),
            jax.ShapeDtypeStruct((2 * LANES, 2 * LANES), BF16),
        ),
        in_specs=[VMEM_SPEC] * 6,
        out_specs=(VMEM_SPEC,) * 14,
        scratch_shapes=[
            vmem(LANES, LANES), vmem(LANES, LANES), vmem(LANES, LANES), vmem(NF, NLAT, LANES),
            vmem(ZP, LANES),
            vmem(N_LON, 8, LANES), vmem(N_LON, 8, LANES),
            vmem(N_LAT, N_LON, LANES), vmem(N_LAT, N_LON, LANES),
            vmem(8, LANES), vmem(N_LON, 8, LANES), vmem(NF, 8, LANES), vmem(N_LAT, NF, 8, LANES),
            dma((N_LON,)), dma((N_LON,)), dma((N_LAT,)), dma((N_LAT,)),
            dma((N_LON,)), dma((N_LON,)), dma((N_LAT,)), dma((N_LAT,)),
        ],
        compiler_params=pltpu.CompilerParams(
            collective_id=0, has_side_effects=True, vmem_limit_bytes=6 << 20
        ),
        name="prepare",
    )(obs, send_list, zonal_weight.reshape(NF * NLAT, LANES), merid_weight, north, vert_inverse)


def scatter_kernel(
    rows_ref, lane_ref, in_ref, depth_ref, norm_ref, field_ref, scale_ref, norm_buf, norm_sem,
    value_ref, even_ref, odd_ref, *grids
):
    def norm_copy(field, row):
        return pltpu.make_async_copy(
            norm_ref.at[field, :, row, :],
            norm_buf.at[field, row, pl.ds(0, NZ), :],
            norm_sem.at[field, row],
        )

    for field in range(NF):

        def begin(row, _, field=field):
            norm_copy(field, row).start()
            return 0

        lax.fori_loop(0, NLAT, begin, 0)

    def clear(step, _):
        at = pl.ds(pl.multiple_of(step * 64, 64), 64)
        for grid in grids:
            grid[at, :] = jnp.zeros((64, LANES), F32)
        return 0

    lax.fori_loop(0, ROWS // 64, clear, 0)
    value_ref[...] = jnp.transpose(in_ref[...])
    iota = lane_iota(CAP)

    def spread(q):
        index = jnp.full((CAP, LANES), q, jnp.int32)
        place = jnp.full((CAP, LANES), (q % N_LAT) * N_LON + q // N_LAT, jnp.int32)
        lane = lane_pick(lane_ref[...], index)
        return jnp.where(iota == lane, lane_pick(value_ref[:CAP, :], place), 0.0)

    def add(q, source):
        for k in range(CAP):
            at = pl.ds(rows_ref[k * RANKS + q], 1)
            grid = grids[k % GRIDS]
            grid[at, :] = grid[at, :] + source[k : k + 1, :]

    even_ref[...] = spread(0)

    def senders(pair, _):
        q = 2 * pair
        odd_ref[...] = spread(q + 1)
        add(q, even_ref)
        even_ref[...] = spread(jnp.minimum(q + 2, RANKS - 1))
        add(q + 1, odd_ref)
        return 0

    lax.fori_loop(0, RANKS // 2, senders, 0)
    level = lax.broadcasted_iota(jnp.int32, (ZP, LANES), 0)
    for field in range(NF):

        def finish(row, _, field=field):
            norm_copy(field, row).wait()
            at = pl.ds(pl.multiple_of((field * NLAT + row) * ZP, ZP), ZP)
            total = [grid[at, :] for grid in grids]
            while len(total) > 1:
                total = [one + two for one, two in zip(total[::2], total[1::2])]
            wet = level < depth_ref[pl.ds(row, 1), :]
            scale = jnp.where(wet, norm_buf[field, row], 0.0)
            scale_ref[field, row] = scale
            field_ref[field, row] = jnp.where(wet, scale * total[0], 0.0)
            return 0

        lax.fori_loop(0, NLAT, finish, 0)


def scatter(rows, lanes, incoming, depth, norm):
    full = jax.ShapeDtypeStruct((NF, NLAT, ZP, LANES), F32)
    return pl.pallas_call(
        scatter_kernel,
        out_shape=(full, full),
        in_specs=[SMEM_SPEC] + [VMEM_SPEC] * 3 + [pl.BlockSpec(memory_space=pltpu.HBM)],
        out_specs=(VMEM_SPEC, VMEM_SPEC),
        scratch_shapes=[
            pltpu.VMEM((NF, NLAT, ZP, LANES), F32), pltpu.SemaphoreType.DMA((NF, NLAT)),
            pltpu.VMEM((LANES, LANES), F32), pltpu.VMEM((CAP, LANES), F32), pltpu.VMEM((CAP, LANES), F32),
        ]
        + [pltpu.VMEM((ROWS, LANES), F32)] * GRIDS,
        compiler_params=pltpu.CompilerParams(vmem_limit_bytes=40 << 20),
        name="scatter",
    )(rows, lanes, incoming, depth, norm)


def solve_kernel(
    field_ref, scale_ref, zs_ref, zr_ref, zco_ref, ms_ref, mr_ref, mss_ref, mrr_ref, mco_all,
    vert_ref, alpha, gamma, minv, sums_ref,
    x_ref,
    zsend, zrecv, zret, zres, msend, mrecv, mret, mres,
    acc_a, acc_b, ubuf, gbuf, mtot, mbuf,
    z1s, z1r, z2s, z2r, m1s, m1r, m2s, m2r,
):
    me = lax.axis_index("lon")
    my = lax.axis_index("lat")
    iota = lane_iota(ZP)
    half = N_LON // NF
    my_field = me // half
    is_solver = me % half < GROUPS
    nothing = jnp.zeros((ZP, LANES), F32)
    greet()


    def zonal_out(turn, field, group, slot):
        return push(
            zsend.at[turn, field, group], zrecv.at[turn, slot],
            z1s.at[turn, field, group], z1r.at[turn, slot], "lon", field * half + group,
        )

    def zonal_back(turn, device, field, group):
        return push(
            zret.at[turn, device], zres.at[turn, field, group],
            z2s.at[turn, device], z2r.at[turn, field, group], "lon", device,
        )

    def others(field, action):
        for group in range(GROUPS):
            pl.when(me != field * half + group)(lambda group=group: action(group))

    def zonal_pass(turn, field, load):
        def chunk_pass(chunk, _):
            lines, left = [], []
            for step in range(CHUNK):
                row = chunk * CHUNK + step
                at = pl.ds(field * NLAT + row, 1)
                s_row, r_row = zs_ref[at, :], zr_ref[at, :]
                value = load(row)
                for coef in (s_row, r_row):
                    high, low = split(coef * value)
                    left.append(jnp.concatenate([high, low], axis=1))
                lines.append((row, s_row, r_row))
            sums = jnp.dot(
                jnp.concatenate(left, axis=0), sums_ref[...], preferred_element_type=F32
            )
            tot_a, tot_b = acc_a[...], acc_b[field]
            for step, (row, s_row, r_row) in enumerate(lines):
                a_part = sums[2 * step * ZP : (2 * step + 1) * ZP]
                b_part = sums[(2 * step + 1) * ZP : (2 * step + 2) * ZP]
                x_ref[field, row] = r_row * a_part[:, :LANES] - s_row * b_part[:, :LANES]
                mine = iota == row
                tot_a = jnp.where(mine, a_part[:, LANES:], tot_a)
                tot_b = jnp.where(mine, b_part[:, LANES:], tot_b)
            acc_a[...] = tot_a
            acc_b[field] = tot_b
            return 0

        acc_a[...] = nothing
        acc_b[field] = nothing
        lax.fori_loop(0, NLAT // CHUNK, chunk_pass, 0)
        acc_a[...] = acc_a[...] * zco_ref[field, 0:1, :]
        for group in range(GROUPS):
            at = slice(GROUP * group, GROUP * group + GROUP)
            zsend[turn, field, group, 0:GROUP, :] = acc_b[field, at, :]
            zsend[turn, field, group, 8 : 8 + GROUP, :] = acc_a[at, :]

    def zonal_send(turn, field):
        others(field, lambda group: zonal_out(turn, field, group, me).start())

        @pl.when(is_solver & (my_field == field))
        def _():
            zrecv[turn, me] = zsend[turn, field, me % half]

    def zonal_reduced(turn):
        mine = me % half
        over_lon(lambda device: zonal_out(turn, 0, 0, device).wait_recv())
        right_side = [
            zrecv[turn, k, 0:8, :] + zrecv[turn, (k - 1) % N_LON, 8:16, :] for k in range(N_LON)
        ]
        for bit in range(5):
            stride = 1 << bit
            right_side = [
                right_side[k]
                + alpha[my_field, bit, k : k + 1, :] * right_side[(k - stride) % N_LON]
                + gamma[my_field, bit, k : k + 1, :] * right_side[(k + stride) % N_LON]
                for k in range(N_LON)
            ]
        values = [right_side[k] * minv[my_field, k : k + 1, :] for k in range(N_LON)]
        for k in range(N_LON):
            zret[turn, k, 0:8, :] = values[k]
            zret[turn, k, 8:16, :] = values[(k + 1) % N_LON]
        over_lon(lambda device: zonal_back(turn, device, my_field, mine).start())
        zres[turn, my_field, mine] = zret[turn, me]

    def zonal_receive(turn, field):
        others(field, lambda group: zonal_back(turn, 0, field, group).wait_recv())
        ubuf[72:80, :] = jnp.zeros((8, LANES), F32)
        gbuf[72:80, :] = jnp.zeros((8, LANES), F32)
        for group in range(GROUPS):
            at = slice(GROUP * group, GROUP * group + GROUP)
            ubuf[at, :] = zres[turn, field, group, 0:GROUP, :]
            gbuf[at, :] = zres[turn, field, group, 8 : 8 + GROUP, :]
        gbuf[...] = gbuf[...] * zco_ref[field, 0:1, :] + acc_b[field]

    def zonal_values(field, chunk):
        u_all, g_all = ubuf[...], gbuf[...]
        found = []
        for step in range(CHUNK):
            row = chunk * CHUNK + step
            at = pl.ds(field * NLAT + row, 1)
            found.append(
                x_ref[field, row]
                + zr_ref[at, :] * jnp.broadcast_to(u_all[:, step : step + 1], (ZP, LANES))
                + zs_ref[at, :] * jnp.broadcast_to(g_all[:, step : step + 1], (ZP, LANES))
            )
        ubuf[...] = pltpu.roll(u_all, LANES - CHUNK, 1)
        gbuf[...] = pltpu.roll(g_all, LANES - CHUNK, 1)
        return found


    def vertical(field, value):
        high, low = split(value)
        return jnp.dot(
            vert_ref[field], jnp.concatenate([high, high, low], axis=0), preferred_element_type=F32
        )

    def vertical_field(field):
        def body(step, _):
            row = step * CHUNK
            value = jnp.concatenate([x_ref[field, row + k] for k in range(CHUNK)], axis=1)
            value = vertical(field, value)
            for k in range(CHUNK):
                x_ref[field, row + k] = value[:, k * LANES : (k + 1) * LANES]
            return 0

        lax.fori_loop(0, NLAT // CHUNK, body, 0)


    def merid_out(field, device, slot):
        return push(
            msend.at[field, device], mrecv.at[field, slot],
            m1s.at[field, device], m1r.at[field, slot], "lat", device,
        )

    def merid_back(field, device, slot):
        return push(
            mret.at[field, device], mres.at[field, slot],
            m2s.at[field, device], m2r.at[field, slot], "lat", device,
        )

    def merid_pass(field):
        def one(chunk, carry):
            tot_a, tot_b = carry
            found = zonal_values(field, chunk)
            for step in range(CHUNK):
                row = chunk * CHUNK + step
                s_row, r_row = ms_ref[field, pl.ds(row, 1), :], mr_ref[field, pl.ds(row, 1), :]
                tot_a = tot_a + s_row * found[step]
                tot_b = tot_b + r_row * found[step]
                x_ref[field, row] = r_row * tot_a - s_row * tot_b
            return tot_a, tot_b

        a_one, b_one = lax.fori_loop(0, NLAT // CHUNK, one, (nothing, nothing))
        ubuf[...] = b_one

        def two(row, carry):
            tot_a, tot_b = carry
            s_row, r_row = ms_ref[field, pl.ds(row, 1), :], mr_ref[field, pl.ds(row, 1), :]
            value = x_ref[field, row] + s_row * ubuf[...]
            tot_a = tot_a + s_row * value
            tot_b = tot_b + r_row * value
            x_ref[field, row] = r_row * tot_a - s_row * tot_b
            return tot_a, tot_b

        a_two, b_two = lax.fori_loop(0, NLAT, two, (nothing, nothing), unroll=4)
        mtot[field] = b_two
        coupling = mco_all[my, field, 0:1, :]
        for part, value in enumerate((b_one, a_one * coupling, b_two, a_two * coupling)):
            for solver in range(N_LAT):
                count = min(SPLIT, ZP - SPLIT * solver)
                msend[field, solver, part, 0:count, :] = value[SPLIT * solver : SPLIT * solver + count]
                if count < SPLIT:
                    msend[field, solver, part, count:SPLIT, :] = jnp.zeros(
                        (SPLIT - count, LANES), F32
                    )
        over_lat(lambda device: merid_out(field, device, my).start())
        mrecv[field, my] = msend[field, my]

    def merid_reduced(field):
        over_lat(lambda device: merid_out(field, 0, device).wait_recv())
        coef = lambda k, row: mco_all[k, field, row : row + 1, :]
        part = lambda k, index: mrecv[field, k, index]

        def solve_four(right_side):
            mass = 1.0 + coef(0, 1)
            reduced = right_side[0]
            kept, inverses, values = [], [], [None] * N_LAT
            for k in range(N_LAT):
                inverse = 1.0 / (mass + coef(k, 0))
                kept.append(reduced)
                inverses.append(inverse)
                if k + 1 < N_LAT:
                    factor = coef(k, 0) * inverse
                    mass = 1.0 + coef(k + 1, 1) + coef(k, 2) + factor * mass
                    reduced = right_side[k + 1] + factor * reduced
            values[-1] = kept[-1] * inverses[-1]
            for k in range(N_LAT - 2, -1, -1):
                values[k] = (kept[k] + coef(k, 0) * values[k + 1]) * inverses[k]
            return values

        none = jnp.zeros((SPLIT, LANES), F32)
        u = solve_four([part(k, 0) + (part(k - 1, 1) if k else none) for k in range(N_LAT)]) + [none]
        second = []
        for k in range(N_LAT):
            value = part(k, 2) + coef(k, 3) * u[k] + coef(k, 4) * u[k + 1]
            if k:
                value = value + part(k - 1, 3) + coef(k - 1, 4) * u[k - 1] + coef(k - 1, 5) * u[k]
            second.append(value)
        v = solve_four(second) + [none]
        for k in range(N_LAT):
            for index, value in enumerate((u[k], u[k + 1], v[k], v[k + 1])):
                mret[field, k, index] = value
        over_lat(lambda device: merid_back(field, device, my).start())
        mres[field, my] = mret[field, my]

    def merid_receive(field):
        over_lat(lambda device: merid_back(field, 0, device).wait_recv())
        for index in range(4):
            for solver in range(N_LAT):
                count = min(SPLIT, ZP - SPLIT * solver)
                mbuf[index, SPLIT * solver : SPLIT * solver + count, :] = mres[
                    field, solver, index, 0:count, :
                ]
        coupling = mco_all[my, field, 0:1, :]
        mbuf[1] = mbuf[1] * coupling
        mbuf[3] = mbuf[3] * coupling + mtot[field]

    def merid_value(field, row):
        at = pl.ds(row, 1)
        return (
            x_ref[field, row]
            + mrr_ref[field, at, :] * mbuf[0]
            + mss_ref[field, at, :] * mbuf[1]
            + mr_ref[field, at, :] * mbuf[2]
            + ms_ref[field, at, :] * mbuf[3]
        )

    zonal_pass(0, 0, lambda row: field_ref[0, row])
    greeted()
    zonal_send(0, 0)
    zonal_pass(0, 1, lambda row: field_ref[1, row])
    zonal_send(0, 1)
    vertical_field(0)
    pl.when(is_solver & (my_field == 0))(lambda: zonal_reduced(0))
    vertical_field(1)
    pl.when(is_solver & (my_field == 1))(lambda: zonal_reduced(0))

    for field in range(NF):
        zonal_receive(0, field)
        both = vertical(field, jnp.concatenate([ubuf[...], gbuf[...]], axis=1))
        ubuf[...] = both[:, :LANES]
        gbuf[...] = both[:, LANES:]
        merid_pass(field)
    for field in range(NF):
        merid_reduced(field)

    for field in range(NF):
        merid_receive(field)
        zonal_pass(1, field, lambda row, field=field: merid_value(field, row))
        zonal_send(1, field)
    pl.when(is_solver)(lambda: zonal_reduced(1))
    for field in range(NF):
        zonal_receive(1, field)

        def last_pass(chunk, _, field=field):
            found = zonal_values(field, chunk)
            for step in range(CHUNK):
                row = chunk * CHUNK + step
                x_ref[field, row] = found[step] * scale_ref[field, row]
            return 0

        lax.fori_loop(0, NLAT // CHUNK, last_pass, 0)

    for field in range(NF):
        over_lat(lambda device, field=field: merid_out(field, device, my).wait_send())
        over_lat(lambda device, field=field: merid_back(field, device, my).wait_send())
        for turn in range(2):
            others(
                field,
                lambda group, turn=turn, field=field: zonal_out(turn, field, group, me).wait_send(),
            )

    @pl.when(is_solver)
    def _():
        for turn in range(2):
            over_lon(lambda device, turn=turn: zonal_back(turn, device, 0, 0).wait_send())


def solve(field, scale, coefs):
    dma = pltpu.SemaphoreType.DMA
    vmem = lambda *dims: pltpu.VMEM(dims, F32)
    return pl.pallas_call(
        solve_kernel,
        out_shape=jax.ShapeDtypeStruct((NF, NLAT, ZP, LANES), F32),
        in_specs=[VMEM_SPEC] * 15,
        out_specs=VMEM_SPEC,
        scratch_shapes=[
            vmem(2, NF, GROUPS, 16, LANES), vmem(2, N_LON, 16, LANES),
            vmem(2, N_LON, 16, LANES), vmem(2, NF, GROUPS, 16, LANES),
            vmem(NF, N_LAT, 4, SPLIT, LANES), vmem(NF, N_LAT, 4, SPLIT, LANES),
            vmem(NF, N_LAT, 4, SPLIT, LANES), vmem(NF, N_LAT, 4, SPLIT, LANES),
            vmem(ZP, LANES), vmem(NF, ZP, LANES), vmem(ZP, LANES), vmem(ZP, LANES),
            vmem(NF, ZP, LANES), vmem(4, ZP, LANES),
            dma((2, NF, GROUPS)), dma((2, N_LON)), dma((2, N_LON)), dma((2, NF, GROUPS)),
            dma((NF, N_LAT)), dma((NF, N_LAT)), dma((NF, N_LAT)), dma((NF, N_LAT)),
        ],
        compiler_params=pltpu.CompilerParams(
            collective_id=1, has_side_effects=True, vmem_limit_bytes=20 << 20
        ),
        name="solve",
    )(field, scale, *coefs)


def pick_kernel(rows_ref, lane_ref, x_ref, out_ref, inc_ref, inc_sem, *copies):
    iota = lane_iota(8)

    def inc_copy(field, row):
        return pltpu.make_async_copy(
            x_ref.at[pl.ds(pl.multiple_of((field * NLAT + row) * ZP, ZP), NZ), :],
            inc_ref.at[field, :, row, :],
            inc_sem.at[field, row],
        )

    def over_rows(action):
        for field in range(NF):

            def body(row, _, field=field):
                action(inc_copy(field, row))
                return 0

            lax.fori_loop(0, NLAT, body, 0)

    over_rows(lambda copy: copy.start())
    group = len(copies)

    def senders(step, acc):
        acc = list(acc)
        for part in range(group):
            q = step * group + part
            for k in range(CAP):
                copies[part][k : k + 1, :] = x_ref[pl.ds(rows_ref[k * RANKS + q], 1), :]
        for part in range(group):
            q = step * group + part
            for tile in range(CAP // 8):
                at = slice(8 * tile, 8 * tile + 8)
                found = lane_pick(copies[part][at, :], lane_ref[at, :])
                acc[tile] = jnp.where(iota == q, found, acc[tile])
        return tuple(acc)

    acc = lax.fori_loop(0, RANKS // group, senders, (jnp.zeros((8, LANES), F32),) * (CAP // 8))
    whole = jnp.concatenate(list(acc) + [jnp.zeros((LANES - CAP, LANES), F32)], axis=0)
    whole = jnp.transpose(whole)
    for device in range(N_LON):
        out_ref[device, 0:4, :] = whole[4 * device : 4 * device + 4]
        out_ref[device, 4:8, :] = jnp.zeros((4, LANES), F32)
    over_rows(lambda copy: copy.wait())


def pick(rows, lanes, increment):
    return pl.pallas_call(
        pick_kernel,
        out_shape=(
            jax.ShapeDtypeStruct((N_LON, 8, LANES), F32),
            jax.ShapeDtypeStruct((NF, NZ, NLAT, LANES), F32),
        ),
        in_specs=[SMEM_SPEC, VMEM_SPEC, VMEM_SPEC],
        out_specs=(VMEM_SPEC, ANY_SPEC),
        scratch_shapes=[pltpu.SemaphoreType.DMA((NF, NLAT))] + [pltpu.VMEM((CAP, LANES), F32)] * 8,
        compiler_params=pltpu.CompilerParams(vmem_limit_bytes=8 << 20),
        name="pick",
    )(rows, lanes, increment.reshape(ROWS, LANES))


def place_kernel(
    tile_out, send_ref, out_ref, idx_ref, val_ref, tile_in, rows_out, rows_in, b1s, b1r, b2s, b2r
):
    greet()
    none = jnp.full((LANES - CAP, LANES), -1, jnp.int32)
    idx_ref[...] = jnp.transpose(jnp.concatenate([send_ref[...], none], axis=0))
    begin, middle, end, sent = two_phase(tile_out, tile_in, rows_out, rows_in, (b1s, b1r, b2s, b2r))
    row_iota = lax.broadcasted_iota(jnp.int32, (CAP, 2 * LANES), 0)
    col_iota = lax.broadcasted_iota(jnp.int32, (LANES, 2 * LANES), 0)
    lane = lax.broadcasted_iota(jnp.int32, (LANES, 2 * LANES), 1)
    slot = (lane & 127).astype(F32)
    second_half = lane >> 7

    def pair(step, acc):
        left, right = pl.ds(2 * step, 1), pl.ds(2 * step + 1, 1)
        index = jnp.concatenate([idx_ref[left, :], idx_ref[right, :]], axis=1)
        rows = jnp.where(row_iota == (index >> 7), 1.0, 0.0).astype(BF16)
        here = col_iota == (index & 127)
        number = 2 * step + second_half
        number = ((number % N_LAT) * N_LON + number // N_LAT + 1).astype(F32)
        columns = jnp.concatenate(
            [jnp.where(here, number, 0.0).astype(BF16), jnp.where(here, slot, 0.0).astype(BF16)],
            axis=0,
        )
        return acc + lax.dot_general(
            rows, columns, (((1,), (1,)), ((), ())), preferred_element_type=F32
        )

    def pairs(start, stop, acc):
        return lax.fori_loop(start, stop, pair, acc, unroll=4)

    acc = jnp.zeros((CAP, 2 * LANES), F32)
    greeted()
    begin()
    acc = pairs(0, RANKS // 4, acc)
    middle()
    acc = pairs(RANKS // 4, RANKS // 2, acc)
    high = acc[:, :LANES].astype(jnp.int32)
    low = acc[:, LANES:].astype(jnp.int32)
    end()
    for lat in range(N_LAT):
        val_ref[N_LON * lat : N_LON * lat + N_LON, :] = rows_in[lat]
    out_ref[...] = gather_lines(val_ref, RANKS, high, low, 1)
    sent()


def place(tiles, send_list):
    vmem = lambda *dims: pltpu.VMEM(dims, F32)
    dma = pltpu.SemaphoreType.DMA
    return pl.pallas_call(
        place_kernel,
        out_shape=jax.ShapeDtypeStruct((CAP, LANES), F32),
        in_specs=[VMEM_SPEC] * 2,
        out_specs=VMEM_SPEC,
        scratch_shapes=[
            pltpu.VMEM((RANKS, LANES), jnp.int32), vmem(RANKS, LANES),
            vmem(N_LON, 8, LANES), vmem(N_LAT, N_LON, LANES), vmem(N_LAT, N_LON, LANES),
            dma((N_LON,)), dma((N_LON,)), dma((N_LAT,)), dma((N_LAT,)),
        ],
        compiler_params=pltpu.CompilerParams(
            collective_id=2, has_side_effects=True, vmem_limit_bytes=6 << 20
        ),
        name="place",
    )(tiles, send_list)


def local(
    obs_value, send_list, recv_cell, column_depth, zonal_weight, merid_weight, vert_inverse, norm_scale
):
    is_north = lax.axis_index("lat") == N_LAT - 1
    north = jnp.full((8, LANES), jnp.where(is_north, 1.0, 0.0), F32)
    sends = jnp.transpose(send_list)
    incoming, *coefs = prepare(
        obs_value.reshape(CAP, LANES), sends, zonal_weight, merid_weight, north,
        jnp.transpose(vert_inverse, (1, 0, 2)),
    )
    cell = jnp.maximum(jnp.transpose(recv_cell), 0)
    line = cell >> 7
    plane = line // NLAT
    lat_row = line - plane * NLAT
    field = (plane >= NZ).astype(jnp.int32)
    level = plane - field * NZ
    rows = ((field * NLAT + lat_row) * ZP + level).reshape(-1)

    gridded, scale = scatter(rows, cell & 127, incoming, column_depth, norm_scale)
    whole = solve(gridded, scale, coefs)
    tiles, increment = pick(rows, cell & 127, whole)
    return increment, place(tiles, sends).reshape(-1)


def solution(mesh):
    in_specs = (
        P(("lon", "lat")),
        P(("lon", "lat"), None),
        P(("lon", "lat"), None),
        P("lat", "lon"),
        P(None, "lat", "lon"),
        P(None, "lat", "lon"),
        P(),
        P(None, None, "lat", "lon"),
    )
    out_specs = (P(None, None, "lat", "lon"), P(("lon", "lat")))
    return jax.shard_map(local, mesh=mesh, in_specs=in_specs, out_specs=out_specs, check_vma=False)
```

```python
import jax
import jax.numpy as jnp
from jax import lax
from jax.experimental import pallas as pl
from jax.experimental.pallas import tpu as pltpu
from jax.sharding import PartitionSpec as P

F32 = jnp.float32
BF16 = jnp.bfloat16
MESH = pl.DeviceIdType.MESH
NF, NZ, NLAT, NLON = 2, 75, 40, 128
ZP = 80
RANKS, CAP = 128, 80
N_LON, N_LAT = 32, 4
GROUPS = 15
GROUP = 5
LANES = 128
CHUNK = 8
HALF = 64
GRIDS = 8
ROWS = NF * NLAT * ZP
ZW_AT, MW_AT, VERT_AT = 80, 160, 240
DEPTH_AT = 160
VMEM_SPEC = pl.BlockSpec(memory_space=pltpu.VMEM)
SMEM_SPEC = pl.BlockSpec(memory_space=pltpu.SMEM)
ANY_SPEC = pl.BlockSpec(memory_space=pl.ANY)


def cost(micros):
    return pl.CostEstimate(flops=0, bytes_accessed=int(micros * 3.6e6), transcendentals=0)


def lane_iota(rows):
    return lax.broadcasted_iota(jnp.int32, (rows, LANES), 1)


def split(value):
    high = value.astype(BF16)
    return high, (value - high.astype(F32)).astype(BF16)


def lane_pick(table, index):
    return jnp.take_along_axis(table, index, axis=1, mode="promise_in_bounds")


def push(source, target, send_sem, recv_sem, axis, device):
    return pltpu.make_async_remote_copy(
        src_ref=source, dst_ref=target, send_sem=send_sem, recv_sem=recv_sem,
        device_id={axis: device}, device_id_type=MESH,
    )


def over(axis, count, action):
    mine = lax.axis_index(axis)

    def body(step, _):
        action((mine + step) % count)
        return 0

    lax.fori_loop(1, count, body, 0)


def over_lon(action):
    over("lon", N_LON, action)


def over_lat(action):
    over("lat", N_LAT, action)


def greet():
    barrier = pltpu.get_barrier_semaphore()
    over_lon(
        lambda device: pl.semaphore_signal(
            barrier, inc=1, device_id={"lon": device}, device_id_type=MESH
        )
    )
    over_lat(
        lambda device: pl.semaphore_signal(
            barrier, inc=1, device_id={"lat": device}, device_id_type=MESH
        )
    )


def greeted():
    pl.semaphore_wait(pltpu.get_barrier_semaphore(), N_LON - 1 + N_LAT - 1)


def zonal_coefs(floats_ref, zs_ref, zr_ref, zco_ref, iw_ref, st_ref, rt_ref, zero):
    one = zero + 1.0
    iw_ref[...] = jnp.full((LANES, LANES), 1e-3, F32)
    iw_ref[: NF * NLAT, :] = 1.0 / floats_ref[ZW_AT : ZW_AT + NF * NLAT, :]
    iw_ref[...] = jnp.transpose(iw_ref[...])

    def zonal_step(step, carry):
        s_val, s_flux, s_sum, r_val, r_flux, r_sum = carry
        back = LANES - 1 - step
        st_ref[pl.ds(step, 1), :] = s_val[0:1]
        s_sum = s_sum + s_val
        s_val = s_val + s_flux * iw_ref[pl.ds(step, 1), :]
        s_flux = s_flux + s_val
        r_sum = r_sum + r_val
        r_val = r_val + r_flux * iw_ref[pl.ds(back, 1), :]
        rt_ref[pl.ds(back, 1), :] = r_val[0:1]
        r_flux = r_flux + r_val
        return s_val, s_flux, s_sum, r_val, r_flux, r_sum

    _, _, s_sum, r_first, _, r_sum = lax.fori_loop(
        0, LANES, zonal_step, (zero, one, zero, zero, one, zero), unroll=8
    )
    coupling = 1.0 / r_first[0:1]
    zco_ref[...] = jnp.zeros((8, LANES), F32)
    zco_ref[0:1, :] = coupling
    zco_ref[1:2, :] = r_sum[0:1] * coupling
    zco_ref[2:3, :] = s_sum[0:1] * coupling
    zs_ref[...] = jnp.transpose(st_ref[...])[: NF * NLAT, :]
    zr_ref[...] = jnp.transpose(rt_ref[...] * coupling)[: NF * NLAT, :]


def merid_coefs(floats_ref, ms_ref, mr_ref, mss_ref, mrr_ref, mco_ref, miw_ref, north, zero):
    one = zero + 1.0
    for field in range(NF):
        at = MW_AT + field * NLAT
        miw_ref[field] = 1.0 / floats_ref[at : at + NLAT, :]
    mco_ref[...] = jnp.zeros((NF, 8, LANES), F32)
    for field in range(NF):
        s_val, s_flux, s_sum = zero, one, zero
        for row in range(NLAT):
            ms_ref[field, row : row + 1, :] = s_val[0:1]
            s_sum = s_sum + s_val
            s_val = s_val + s_flux * miw_ref[field, row : row + 1, :]
            s_flux = s_flux + s_val
        r_val = jnp.where(north > 0.5, 1.0, miw_ref[field, NLAT - 1 : NLAT, :] + zero)
        r_flux = jnp.where(north > 0.5, 0.0, one)
        r_sum = zero
        mr_ref[field, NLAT - 1 : NLAT, :] = r_val[0:1]
        for row in range(NLAT - 2, -1, -1):
            r_sum = r_sum + r_val
            r_flux = r_flux + r_val
            r_val = r_val + r_flux * miw_ref[field, row : row + 1, :]
            mr_ref[field, row : row + 1, :] = r_val[0:1]
        inverse = 1.0 / r_val[0:1]
        coupling = jnp.where(north[0:1] > 0.5, 0.0, inverse)
        mr_ref[field] = mr_ref[field] * inverse
        sum_rr, sum_rs = zero, zero
        for row in range(NLAT - 1, -1, -1):
            at = slice(row, row + 1)
            s_row, r_row = ms_ref[field, at, :], mr_ref[field, at, :]
            mrr_ref[field, at, :] = s_row * sum_rr[0:1]
            mss_ref[field, at, :] = s_row * sum_rs[0:1]
            sum_rr = sum_rr + r_row * r_row
            sum_rs = sum_rs + r_row * s_row
        sum_sr, sum_ss = zero, zero
        for row in range(NLAT):
            at = slice(row, row + 1)
            s_row, r_row = ms_ref[field, at, :], mr_ref[field, at, :]
            sum_sr = sum_sr + s_row * r_row
            sum_ss = sum_ss + s_row * s_row
            mrr_ref[field, at, :] = mrr_ref[field, at, :] + r_row * sum_sr[0:1]
            mss_ref[field, at, :] = mss_ref[field, at, :] + r_row * sum_ss[0:1]
        mco_ref[field, 0:1, :] = coupling
        mco_ref[field, 1:2, :] = r_sum[0:1] * inverse
        mco_ref[field, 2:3, :] = s_sum[0:1] * coupling
        mco_ref[field, 3:4, :] = sum_rr[0:1]
        mco_ref[field, 4:5, :] = sum_rs[0:1] * coupling
        mco_ref[field, 5:6, :] = sum_ss[0:1] * coupling * coupling


def zonal_factor(zco_all, alpha, gamma, minv):
    coupling = zco_all[:, 0, :]
    west = jnp.concatenate([coupling[-1:], coupling[:-1]], axis=0)
    spill = zco_all[:, 2, :]
    mass = 1.0 + zco_all[:, 1, :] + jnp.concatenate([spill[-1:], spill[:-1]], axis=0)
    east = coupling
    for bit in range(5):
        stride = 1 << bit
        down = lambda v: jnp.concatenate([v[-stride:], v[:-stride]], axis=0)
        up = lambda v: jnp.concatenate([v[stride:], v[:stride]], axis=0)
        inverse = 1.0 / (mass + west + east)
        left = west * down(inverse)
        right = east * up(inverse)
        for field in range(NF):
            alpha[field, bit] = to_field(left, field)
            gamma[field, bit] = to_field(right, field)
        mass = mass + left * down(mass) + right * up(mass)
        west, east = left * down(west), right * up(east)
    for field in range(NF):
        minv[field] = to_field(1.0 / mass, field)


def to_field(rows, field):
    return rows if field == 0 else pltpu.roll(rows, LANES - field * NLAT, 1)


def gather_lines(table_ref, count, high, low, base):
    def step(row, acc):
        line = jnp.broadcast_to(table_ref[pl.ds(row, 1), :], (ZP, LANES))
        return jnp.where(high == row + base, lane_pick(line, low), acc)

    return lax.fori_loop(0, count, step, jnp.zeros((ZP, LANES), F32), unroll=8)


def two_phase(tile_out, tile_in, rows_out, rows_in, sems):
    me = lax.axis_index("lon")
    my = lax.axis_index("lat")
    s1, r1, s2, r2 = sems
    first = lambda device, slot: push(
        tile_out.at[device], tile_in.at[slot], s1.at[device], r1.at[slot], "lon", device
    )
    second = lambda device, slot: push(
        rows_out.at[device], rows_in.at[slot], s2.at[device], r2.at[slot], "lat", device
    )

    def begin():
        over_lon(lambda device: first(device, me).start())
        tile_in[me] = tile_out[me]

    def middle():
        over_lon(lambda device: first(0, device).wait_recv())
        for lat in range(N_LAT):
            rows_out[lat] = tile_in[:, lat, :]
        over_lat(lambda device: second(device, my).start())
        rows_in[my] = rows_out[my]

    def end():
        over_lat(lambda device: second(0, device).wait_recv())

    def sent():
        over_lon(lambda device: first(device, me).wait_send())
        over_lat(lambda device: second(device, my).wait_send())

    return begin, middle, end, sent


def prepare_kernel(
    ints_ref, floats_ref, north_ref,
    out_ref, zs_ref, zr_ref, zco_out, ms_ref, mr_ref, mss_ref, mrr_ref, mco_out, vert_ref,
    alpha, gamma, minv, sums_ref, *rest
):
    grids, rest = rest[:GRIDS], rest[GRIDS:]
    prepare_body(
        ints_ref, floats_ref, north_ref, out_ref, zs_ref, zr_ref, zco_out, ms_ref, mr_ref, mss_ref,
        mrr_ref, mco_out, vert_ref, alpha, gamma, minv, sums_ref, grids, *rest,
    )


def prepare_body(
    ints_ref, floats_ref, north_ref,
    out_ref, zs_ref, zr_ref, zco_out, ms_ref, mr_ref, mss_ref, mrr_ref, mco_out, vert_ref,
    alpha, gamma, minv, sums_ref, grids,
    iw_ref, st_ref, rt_ref, miw_ref, prod_ref,
    tile_out, tile_in, rows_out, rows_in, zco_ref, zco_all, mco_ref, mco_all,
    o1s, o1r, o2s, o2r, zco_s, zco_r, mco_s, mco_r,
):
    me = lax.axis_index("lon")
    my = lax.axis_index("lat")
    greet()
    index = ints_ref[0:CAP, :]
    picked = gather_lines(floats_ref, CAP, index >> 7, index & 127, 0)
    picked = jnp.transpose(
        jnp.concatenate([picked, jnp.zeros((LANES - CAP, LANES), F32)], axis=0)
    )
    for device in range(N_LON):
        tile_out[device, 0:4, :] = picked[4 * device : 4 * device + 4]
        tile_out[device, 4:8, :] = jnp.zeros((4, LANES), F32)

    begin, middle, end, sent = two_phase(tile_out, tile_in, rows_out, rows_in, (o1s, o1r, o2s, o2r))
    zco_copy = lambda device, slot: push(
        zco_ref, zco_all.at[slot], zco_s.at[device], zco_r.at[slot], "lon", device
    )
    mco_copy = lambda device, slot: push(
        mco_ref, mco_all.at[slot], mco_s.at[device], mco_r.at[slot], "lat", device
    )
    greeted()
    begin()
    zero = north_ref[...] * 0.0
    zonal_coefs(floats_ref, zs_ref, zr_ref, zco_ref, iw_ref, st_ref, rt_ref, zero)
    middle()
    over_lon(lambda device: zco_copy(device, me).start())
    zco_all[me] = zco_ref[...]
    for field in range(NF):
        zco_out[field] = to_field(zco_ref[...], field)
    merid_coefs(floats_ref, ms_ref, mr_ref, mss_ref, mrr_ref, mco_ref, miw_ref, north_ref[...], zero)
    over_lat(lambda device: mco_copy(device, my).start())
    mco_all[my] = mco_ref[...]
    prod_ref[...] = jnp.zeros((ZP, LANES), F32)
    for field in range(NF):
        matrix = floats_ref[pl.ds(VERT_AT + field, NZ, stride=NF), :]
        prod_ref[:NZ, :NZ] = lax.dot_general(
            matrix, matrix, (((1,), (1,)), ((), ())),
            precision=lax.Precision.HIGHEST, preferred_element_type=F32,
        )
        high, low = split(prod_ref[:, :ZP])
        vert_ref[field] = jnp.concatenate([high, low, high], axis=1)
    source = lax.broadcasted_iota(jnp.int32, (2 * LANES, 2 * LANES), 0) & 127
    target = lax.broadcasted_iota(jnp.int32, (2 * LANES, 2 * LANES), 1)
    sums_ref[...] = jnp.where(source <= target, 1.0, 0.0).astype(BF16)
    def clear(step, _):
        at = pl.ds(pl.multiple_of(step * 64, 64), 64)
        for grid in grids:
            grid[at, :] = jnp.zeros((64, LANES), F32)
        return 0

    lax.fori_loop(0, ROWS // 64, clear, 0)
    end()
    for lat in range(N_LAT):
        out_ref[N_LON * lat : N_LON * lat + N_LON, :] = rows_in[lat]
    over_lon(lambda device: zco_copy(0, device).wait_recv())
    zonal_factor(zco_all, alpha, gamma, minv)
    over_lat(lambda device: mco_copy(0, device).wait_recv())
    mco_out[...] = mco_all[...]
    sent()
    over_lon(lambda device: zco_copy(device, me).wait_send())
    over_lat(lambda device: mco_copy(device, my).wait_send())


def prepare(ints, floats, north):
    shape = lambda *dims: jax.ShapeDtypeStruct(dims, F32)
    vmem = lambda *dims: pltpu.VMEM(dims, F32)
    dma = pltpu.SemaphoreType.DMA
    return pl.pallas_call(
        prepare_kernel,
        out_shape=(
            shape(RANKS, LANES), shape(80, LANES), shape(80, LANES), shape(NF, 8, LANES),
            shape(NF, NLAT, LANES), shape(NF, NLAT, LANES),
            shape(NF, NLAT, LANES), shape(NF, NLAT, LANES), shape(N_LAT, NF, 8, LANES),
            jax.ShapeDtypeStruct((NF, ZP, 3 * ZP), BF16),
            shape(NF, 5, N_LON, LANES), shape(NF, 5, N_LON, LANES), shape(NF, N_LON, LANES),
            jax.ShapeDtypeStruct((2 * LANES, 2 * LANES), BF16),
        )
        + (shape(ROWS, LANES),) * GRIDS,
        in_specs=[VMEM_SPEC] * 3,
        out_specs=(VMEM_SPEC,) * (14 + GRIDS),
        scratch_shapes=[
            vmem(LANES, LANES), vmem(LANES, LANES), vmem(LANES, LANES), vmem(NF, NLAT, LANES),
            vmem(ZP, LANES),
            vmem(N_LON, 8, LANES), vmem(N_LON, 8, LANES),
            vmem(N_LAT, N_LON, LANES), vmem(N_LAT, N_LON, LANES),
            vmem(8, LANES), vmem(N_LON, 8, LANES), vmem(NF, 8, LANES), vmem(N_LAT, NF, 8, LANES),
            dma((N_LON,)), dma((N_LON,)), dma((N_LAT,)), dma((N_LAT,)),
            dma((N_LON,)), dma((N_LON,)), dma((N_LAT,)), dma((N_LAT,)),
        ],
        compiler_params=pltpu.CompilerParams(
            collective_id=0, has_side_effects=True, vmem_limit_bytes=6 << 20
        ),
        cost_estimate=cost(15),
        name="prepare",
    )(ints, floats, north)


def scatter_kernel(rows_ref, ints_ref, in_ref, norm_ref, *refs):
    grids = refs[GRIDS : 2 * GRIDS]
    norm_buf, norm_sem, value_ref, even_ref, odd_ref = refs[2 * GRIDS :]

    def norm_copy(field, row):
        return pltpu.make_async_copy(
            norm_ref.at[field, :, row, :],
            norm_buf.at[field, row, pl.ds(0, NZ), :],
            norm_sem.at[field, row],
        )

    def over_rows(action):
        for field in range(NF):

            def body(row, _, field=field):
                action(norm_copy(field, row))
                return 0

            lax.fori_loop(0, NLAT, body, 0)

    over_rows(lambda copy: copy.start())
    value_ref[...] = jnp.transpose(in_ref[...])
    iota = lane_iota(CAP)

    def spread(q):
        index = jnp.full((CAP, LANES), q, jnp.int32)
        place = jnp.full((CAP, LANES), (q % N_LAT) * N_LON + q // N_LAT, jnp.int32)
        lane = lane_pick(ints_ref[CAP : 2 * CAP, :], index)
        return jnp.where(iota == lane, lane_pick(value_ref[:CAP, :], place), 0.0)

    def add(q, source):
        for k in range(CAP):
            at = pl.ds(rows_ref[k, q], 1)
            grid = grids[k % GRIDS]
            grid[at, :] = grid[at, :] + source[k : k + 1, :]

    even_ref[...] = spread(0)

    def senders(pair, _):
        q = 2 * pair
        odd_ref[...] = spread(q + 1)
        add(q, even_ref)
        even_ref[...] = spread(jnp.minimum(q + 2, RANKS - 1))
        add(q + 1, odd_ref)
        return 0

    lax.fori_loop(0, RANKS // 2, senders, 0)
    over_rows(lambda copy: copy.wait())


def scatter(rows, ints, incoming, norm, grids):
    grid = jax.ShapeDtypeStruct((ROWS, LANES), F32)
    return pl.pallas_call(
        scatter_kernel,
        out_shape=(grid,) * GRIDS + (jax.ShapeDtypeStruct((NF, NLAT, ZP, LANES), F32),),
        in_specs=[SMEM_SPEC] + [VMEM_SPEC] * 2 + [ANY_SPEC] + [VMEM_SPEC] * GRIDS,
        out_specs=(VMEM_SPEC,) * (GRIDS + 1),
        input_output_aliases={4 + index: index for index in range(GRIDS)},
        scratch_shapes=[
            pltpu.SemaphoreType.DMA((NF, NLAT)),
            pltpu.VMEM((LANES, LANES), F32), pltpu.VMEM((CAP, LANES), F32), pltpu.VMEM((CAP, LANES), F32),
        ],
        compiler_params=pltpu.CompilerParams(vmem_limit_bytes=6 << 20),
        cost_estimate=cost(12),
        name="scatter",
    )(rows, ints, incoming, norm, *grids)


def solve_kernel(*refs):
    solve_body(refs[:GRIDS], *refs[GRIDS:])


def solve_body(
    grids, norm_ref, ints_ref, zs_ref, zr_ref, zco_ref, ms_ref, mr_ref, mss_ref, mrr_ref, mco_all,
    vert_ref, alpha, gamma, minv, sums_ref,
    x_ref,
    zsend, zrecv, zret, zres, msend, mrecv, mval,
    acc_a, acc_b, ubuf, gbuf, mtot, mbuf,
    z1s, z1r, z2s, z2r, m1s, m1r,
):
    me = lax.axis_index("lon")
    my = lax.axis_index("lat")
    iota = lane_iota(ZP)
    half = N_LON // NF
    my_field = me // half
    is_solver = me % half < GROUPS
    nothing = jnp.zeros((ZP, LANES), F32)
    greet()


    def zonal_out(turn, field, group, slot):
        return push(
            zsend.at[turn, field, group], zrecv.at[turn, slot],
            z1s.at[turn, field, group], z1r.at[turn, slot], "lon", field * half + group,
        )

    def zonal_back(turn, device, field, group):
        return push(
            zret.at[turn, device], zres.at[turn, field, group],
            z2s.at[turn, device], z2r.at[turn, field, group], "lon", device,
        )

    def others(field, action):
        for group in range(GROUPS):
            pl.when(me != field * half + group)(lambda group=group: action(group))

    def zonal_pass(turn, field, load):
        def chunk_pass(chunk, _):
            lines, left = [], []
            for step in range(CHUNK):
                row = chunk * CHUNK + step
                at = pl.ds(field * NLAT + row, 1)
                s_row, r_row = zs_ref[at, :], zr_ref[at, :]
                value = load(row)
                for coef in (s_row, r_row):
                    high, low = split(coef * value)
                    left.append(jnp.concatenate([high, low], axis=1))
                lines.append((row, s_row, r_row))
            sums = jnp.dot(
                jnp.concatenate(left, axis=0), sums_ref[...], preferred_element_type=F32
            )
            tot_a, tot_b = acc_a[...], acc_b[field]
            for step, (row, s_row, r_row) in enumerate(lines):
                a_part = sums[2 * step * ZP : (2 * step + 1) * ZP]
                b_part = sums[(2 * step + 1) * ZP : (2 * step + 2) * ZP]
                x_ref[field, row] = r_row * a_part[:, :LANES] - s_row * b_part[:, :LANES]
                mine = iota == row
                tot_a = jnp.where(mine, a_part[:, LANES:], tot_a)
                tot_b = jnp.where(mine, b_part[:, LANES:], tot_b)
            acc_a[...] = tot_a
            acc_b[field] = tot_b
            return 0

        acc_a[...] = nothing
        acc_b[field] = nothing
        lax.fori_loop(0, NLAT // CHUNK, chunk_pass, 0)
        acc_a[...] = acc_b[field] + pltpu.roll(acc_a[...] * zco_ref[field, 0:1, :], HALF, 1)
        for group in range(GROUPS):
            at = slice(GROUP * group, GROUP * group + GROUP)
            zsend[turn, field, group, 0:GROUP, :] = acc_a[at, :]

    def zonal_send(turn, field):
        others(field, lambda group: zonal_out(turn, field, group, me).start())

        @pl.when(is_solver & (my_field == field))
        def _():
            zrecv[turn, me] = zsend[turn, field, me % half]

    def zonal_reduced(turn):
        mine = me % half
        over_lon(lambda device: zonal_out(turn, 0, 0, device).wait_recv())
        right_side = [
            zrecv[turn, k] + pltpu.roll(zrecv[turn, (k - 1) % N_LON], HALF, 1) for k in range(N_LON)
        ]
        for bit in range(5):
            stride = 1 << bit
            right_side = [
                right_side[k]
                + alpha[my_field, bit, k : k + 1, :] * right_side[(k - stride) % N_LON]
                + gamma[my_field, bit, k : k + 1, :] * right_side[(k + stride) % N_LON]
                for k in range(N_LON)
            ]
        values = [right_side[k] * minv[my_field, k : k + 1, :] for k in range(N_LON)]
        for k in range(N_LON):
            zret[turn, k] = jnp.where(
                iota[0:8] < HALF, values[k], pltpu.roll(values[(k + 1) % N_LON], HALF, 1)
            )
        over_lon(lambda device: zonal_back(turn, device, my_field, mine).start())
        zres[turn, my_field, mine] = zret[turn, me]

    def zonal_receive(turn, field):
        others(field, lambda group: zonal_back(turn, 0, field, group).wait_recv())
        ubuf[72:80, :] = jnp.zeros((8, LANES), F32)
        for group in range(GROUPS):
            at = slice(GROUP * group, GROUP * group + GROUP)
            ubuf[at, :] = zres[turn, field, group, 0:GROUP, :]
        gbuf[...] = pltpu.roll(ubuf[...], HALF, 1) * zco_ref[field, 0:1, :] + acc_b[field]

    def zonal_values(field, chunk):
        u_all, g_all = ubuf[...], gbuf[...]
        found = []
        for step in range(CHUNK):
            row = chunk * CHUNK + step
            at = pl.ds(field * NLAT + row, 1)
            found.append(
                x_ref[field, row]
                + zr_ref[at, :] * jnp.broadcast_to(u_all[:, step : step + 1], (ZP, LANES))
                + zs_ref[at, :] * jnp.broadcast_to(g_all[:, step : step + 1], (ZP, LANES))
            )
        ubuf[...] = pltpu.roll(u_all, LANES - CHUNK, 1)
        gbuf[...] = pltpu.roll(g_all, LANES - CHUNK, 1)
        return found


    def vertical(field, value):
        high, low = split(value)
        return jnp.dot(
            vert_ref[field], jnp.concatenate([high, high, low], axis=0), preferred_element_type=F32
        )

    def vertical_field(field):
        def body(step, _):
            row = step * CHUNK
            value = jnp.concatenate([x_ref[field, row + k] for k in range(CHUNK)], axis=1)
            value = vertical(field, value)
            for k in range(CHUNK):
                x_ref[field, row + k] = value[:, k * LANES : (k + 1) * LANES]
            return 0

        lax.fori_loop(0, NLAT // CHUNK, body, 0)


    def merid_out(field, device, slot):
        return push(
            msend.at[field], mrecv.at[field, slot],
            m1s.at[field, device], m1r.at[field, slot], "lat", device,
        )

    def merid_pass(field):
        def one(chunk, carry):
            tot_a, tot_b = carry
            found = zonal_values(field, chunk)
            for step in range(CHUNK):
                row = chunk * CHUNK + step
                s_row, r_row = ms_ref[field, pl.ds(row, 1), :], mr_ref[field, pl.ds(row, 1), :]
                tot_a = tot_a + s_row * found[step]
                tot_b = tot_b + r_row * found[step]
                x_ref[field, row] = r_row * tot_a - s_row * tot_b
            return tot_a, tot_b

        a_one, b_one = lax.fori_loop(0, NLAT // CHUNK, one, (nothing, nothing))
        ubuf[...] = b_one

        def two(row, carry):
            tot_a, tot_b = carry
            s_row, r_row = ms_ref[field, pl.ds(row, 1), :], mr_ref[field, pl.ds(row, 1), :]
            value = x_ref[field, row] + s_row * ubuf[...]
            tot_a = tot_a + s_row * value
            tot_b = tot_b + r_row * value
            x_ref[field, row] = r_row * tot_a - s_row * tot_b
            return tot_a, tot_b

        a_two, b_two = lax.fori_loop(0, NLAT, two, (nothing, nothing), unroll=4)
        mtot[field] = b_two
        coupling = mco_all[my, field, 0:1, :]
        for part, value in enumerate((b_one, a_one * coupling, b_two, a_two * coupling)):
            msend[field, part] = value
        over_lat(lambda device: merid_out(field, device, my).start())
        mrecv[field, my] = msend[field]

    def merid_reduced(field):
        over_lat(lambda device: merid_out(field, 0, device).wait_recv())
        coef = lambda k, row: mco_all[k, field, row : row + 1, :]

        def tile(step, _):
            at = pl.ds(pl.multiple_of(step * 8, 8), 8)
            part = lambda k, index: mrecv[field, k, index, at, :]

            def solve_four(right_side):
                mass = 1.0 + coef(0, 1)
                reduced = right_side[0]
                kept, inverses, values = [], [], [None] * N_LAT
                for k in range(N_LAT):
                    inverse = 1.0 / (mass + coef(k, 0))
                    kept.append(reduced)
                    inverses.append(inverse)
                    if k + 1 < N_LAT:
                        factor = coef(k, 0) * inverse
                        mass = 1.0 + coef(k + 1, 1) + coef(k, 2) + factor * mass
                        reduced = right_side[k + 1] + factor * reduced
                values[-1] = kept[-1] * inverses[-1]
                for k in range(N_LAT - 2, -1, -1):
                    values[k] = (kept[k] + coef(k, 0) * values[k + 1]) * inverses[k]
                return values

            none = jnp.zeros((8, LANES), F32)
            u = solve_four([part(k, 0) + (part(k - 1, 1) if k else none) for k in range(N_LAT)])
            u = u + [none]
            second = []
            for k in range(N_LAT):
                value = part(k, 2) + coef(k, 3) * u[k] + coef(k, 4) * u[k + 1]
                if k:
                    value = value + part(k - 1, 3) + coef(k - 1, 4) * u[k - 1] + coef(k - 1, 5) * u[k]
                second.append(value)
            v = solve_four(second) + [none]
            for k in range(N_LAT + 1):
                mval[0, k, at, :] = u[k]
                mval[1, k, at, :] = v[k]
            return 0

        lax.fori_loop(0, ZP // 8, tile, 0)
        coupling = mco_all[my, field, 0:1, :]
        mbuf[0] = mval[0, my]
        mbuf[1] = mval[0, my + 1] * coupling
        mbuf[2] = mval[1, my]
        mbuf[3] = mval[1, my + 1] * coupling + mtot[field]

    def merid_value(field, row):
        at = pl.ds(row, 1)
        return (
            x_ref[field, row]
            + mrr_ref[field, at, :] * mbuf[0]
            + mss_ref[field, at, :] * mbuf[1]
            + mr_ref[field, at, :] * mbuf[2]
            + ms_ref[field, at, :] * mbuf[3]
        )

    level = lax.broadcasted_iota(jnp.int32, (ZP, LANES), 0)

    def scale(field, row):
        wet = level < ints_ref[pl.ds(DEPTH_AT + row, 1), :]
        return jnp.where(wet, norm_ref[field, row], 0.0)

    def scaled_grid(field):
        def load(row):
            at = pl.ds(pl.multiple_of((field * NLAT + row) * ZP, ZP), ZP)
            total = [grid[at, :] for grid in grids]
            while len(total) > 1:
                total = [one + two for one, two in zip(total[::2], total[1::2])]
            return scale(field, row) * total[0]

        return load

    zonal_pass(0, 0, scaled_grid(0))
    greeted()
    zonal_send(0, 0)
    zonal_pass(0, 1, scaled_grid(1))
    zonal_send(0, 1)
    vertical_field(0)
    pl.when(is_solver & (my_field == 0))(lambda: zonal_reduced(0))
    vertical_field(1)
    pl.when(is_solver & (my_field == 1))(lambda: zonal_reduced(0))

    for field in range(NF):
        zonal_receive(0, field)
        both = vertical(field, jnp.concatenate([ubuf[...], gbuf[...]], axis=1))
        ubuf[...] = both[:, :LANES]
        gbuf[...] = both[:, LANES:]
        merid_pass(field)

    for field in range(NF):
        merid_reduced(field)
        zonal_pass(1, field, lambda row, field=field: merid_value(field, row))
        zonal_send(1, field)
    pl.when(is_solver)(lambda: zonal_reduced(1))
    for field in range(NF):
        zonal_receive(1, field)

        def last_pass(chunk, _, field=field):
            found = zonal_values(field, chunk)
            for step in range(CHUNK):
                row = chunk * CHUNK + step
                x_ref[field, row] = found[step] * scale(field, row)
            return 0

        lax.fori_loop(0, NLAT // CHUNK, last_pass, 0)

    for field in range(NF):
        over_lat(lambda device, field=field: merid_out(field, device, my).wait_send())
        for turn in range(2):
            others(
                field,
                lambda group, turn=turn, field=field: zonal_out(turn, field, group, me).wait_send(),
            )

    @pl.when(is_solver)
    def _():
        for turn in range(2):
            over_lon(lambda device, turn=turn: zonal_back(turn, device, 0, 0).wait_send())


def solve(grids, norm, ints, coefs):
    dma = pltpu.SemaphoreType.DMA
    vmem = lambda *dims: pltpu.VMEM(dims, F32)
    return pl.pallas_call(
        solve_kernel,
        out_shape=jax.ShapeDtypeStruct((NF, NLAT, ZP, LANES), F32),
        in_specs=[VMEM_SPEC] * (15 + GRIDS),
        out_specs=VMEM_SPEC,
        scratch_shapes=[
            vmem(2, NF, GROUPS, 8, LANES), vmem(2, N_LON, 8, LANES),
            vmem(2, N_LON, 8, LANES), vmem(2, NF, GROUPS, 8, LANES),
            vmem(NF, 4, ZP, LANES), vmem(NF, N_LAT, 4, ZP, LANES), vmem(2, N_LAT + 1, ZP, LANES),
            vmem(ZP, LANES), vmem(NF, ZP, LANES), vmem(ZP, LANES), vmem(ZP, LANES),
            vmem(NF, ZP, LANES), vmem(4, ZP, LANES),
            dma((2, NF, GROUPS)), dma((2, N_LON)), dma((2, N_LON)), dma((2, NF, GROUPS)),
            dma((NF, N_LAT)), dma((NF, N_LAT)),
        ],
        compiler_params=pltpu.CompilerParams(
            collective_id=1, has_side_effects=True, vmem_limit_bytes=10 << 20
        ),
        cost_estimate=cost(40),
        name="solve",
    )(*grids, norm, ints, *coefs)


def pick_kernel(rows_ref, ints_ref, x_ref, out_ref, inc_ref, inc_sem, *copies):
    iota = lane_iota(8)

    def inc_copy(field, row):
        return pltpu.make_async_copy(
            x_ref.at[pl.ds(pl.multiple_of((field * NLAT + row) * ZP, ZP), NZ), :],
            inc_ref.at[field, :, row, :],
            inc_sem.at[field, row],
        )

    def over_rows(action):
        for field in range(NF):

            def body(row, _, field=field):
                action(inc_copy(field, row))
                return 0

            lax.fori_loop(0, NLAT, body, 0)

    over_rows(lambda copy: copy.start())
    group = len(copies)

    def senders(step, acc):
        acc = list(acc)
        for part in range(group):
            q = step * group + part
            for k in range(CAP):
                copies[part][k : k + 1, :] = x_ref[pl.ds(rows_ref[k, q], 1), :]
        for part in range(group):
            q = step * group + part
            for tile in range(CAP // 8):
                at = slice(8 * tile, 8 * tile + 8)
                found = lane_pick(
                    copies[part][at, :], ints_ref[CAP + 8 * tile : CAP + 8 * tile + 8, :]
                )
                acc[tile] = jnp.where(iota == q, found, acc[tile])
        return tuple(acc)

    acc = lax.fori_loop(0, RANKS // group, senders, (jnp.zeros((8, LANES), F32),) * (CAP // 8))
    whole = jnp.concatenate(list(acc) + [jnp.zeros((LANES - CAP, LANES), F32)], axis=0)
    whole = jnp.transpose(whole)
    for device in range(N_LON):
        out_ref[device, 0:4, :] = whole[4 * device : 4 * device + 4]
        out_ref[device, 4:8, :] = jnp.zeros((4, LANES), F32)
    over_rows(lambda copy: copy.wait())


def pick(rows, ints, increment):
    return pl.pallas_call(
        pick_kernel,
        out_shape=(
            jax.ShapeDtypeStruct((N_LON, 8, LANES), F32),
            jax.ShapeDtypeStruct((NF, NZ, NLAT, LANES), F32),
        ),
        in_specs=[SMEM_SPEC, VMEM_SPEC, VMEM_SPEC],
        out_specs=(VMEM_SPEC, ANY_SPEC),
        scratch_shapes=[pltpu.SemaphoreType.DMA((NF, NLAT))] + [pltpu.VMEM((CAP, LANES), F32)] * 8,
        compiler_params=pltpu.CompilerParams(vmem_limit_bytes=8 << 20),
        cost_estimate=cost(14),
        name="pick",
    )(rows, ints, increment.reshape(ROWS, LANES))


def place_kernel(
    tile_out, ints_ref, out_ref,
    idx_ref, val_ref, rows_oh, cols_oh, tile_in, rows_out, rows_in, b1s, b1r, b2s, b2r,
):
    greet()
    none = jnp.full((LANES - CAP, LANES), -1, jnp.int32)
    idx_ref[...] = jnp.transpose(jnp.concatenate([ints_ref[0:CAP, :], none], axis=0))
    begin, middle, end, sent = two_phase(tile_out, tile_in, rows_out, rows_in, (b1s, b1r, b2s, b2r))
    row_iota = lax.broadcasted_iota(jnp.int32, (CAP, 2 * LANES), 0)
    col_iota = lax.broadcasted_iota(jnp.int32, (LANES, 2 * LANES), 0)

    def build(step, _):
        lat = step // (N_LON // 2)
        left = (step % (N_LON // 2)) * 2 * N_LAT + lat
        index = jnp.concatenate(
            [idx_ref[pl.ds(left, 1), :], idx_ref[pl.ds(left + N_LAT, 1), :]], axis=1
        )
        rows_oh[step] = jnp.where(row_iota == (index >> 7), 1.0, 0.0).astype(BF16)
        cols_oh[step] = jnp.where(col_iota == (index & 127), 1.0, 0.0).astype(BF16)
        return 0

    def add(step, acc):
        value = jnp.concatenate(
            [val_ref[pl.ds(2 * step, 1), :], val_ref[pl.ds(2 * step + 1, 1), :]], axis=1
        )
        high, low = split(value)
        rows = rows_oh[step]
        return acc + lax.dot_general(
            jnp.concatenate([rows * high, rows * low], axis=0), cols_oh[step],
            (((1,), (1,)), ((), ())), preferred_element_type=F32,
        )

    greeted()
    begin()
    lax.fori_loop(0, RANKS // 4, build, 0, unroll=2)
    middle()
    lax.fori_loop(RANKS // 4, RANKS // 2, build, 0, unroll=2)
    end()
    for lat in range(N_LAT):
        val_ref[N_LON * lat : N_LON * lat + N_LON, :] = rows_in[lat]
    acc = lax.fori_loop(0, RANKS // 2, add, jnp.zeros((2 * CAP, LANES), F32), unroll=8)
    out_ref[...] = acc[:CAP] + acc[CAP:]
    sent()


def place(tiles, ints):
    vmem = lambda *dims: pltpu.VMEM(dims, F32)
    dma = pltpu.SemaphoreType.DMA
    return pl.pallas_call(
        place_kernel,
        out_shape=jax.ShapeDtypeStruct((CAP, LANES), F32),
        in_specs=[VMEM_SPEC] * 2,
        out_specs=VMEM_SPEC,
        scratch_shapes=[
            pltpu.VMEM((RANKS, LANES), jnp.int32), vmem(RANKS, LANES),
            pltpu.VMEM((RANKS // 2, CAP, 2 * LANES), BF16),
            pltpu.VMEM((RANKS // 2, LANES, 2 * LANES), BF16),
            vmem(N_LON, 8, LANES), vmem(N_LAT, N_LON, LANES), vmem(N_LAT, N_LON, LANES),
            dma((N_LON,)), dma((N_LON,)), dma((N_LAT,)), dma((N_LAT,)),
        ],
        compiler_params=pltpu.CompilerParams(
            collective_id=2, has_side_effects=True, vmem_limit_bytes=10 << 20
        ),
        cost_estimate=cost(15),
        name="place",
    )(tiles, ints)


def local(
    obs_value, send_list, recv_cell, column_depth, zonal_weight, merid_weight, vert_inverse, norm_scale
):
    is_north = lax.axis_index("lat") == N_LAT - 1
    north = jnp.full((8, LANES), jnp.where(is_north, 1.0, 0.0), F32)
    cell = jnp.maximum(jnp.transpose(recv_cell), 0)
    line = cell >> 7
    plane = line // NLAT
    lat_row = line - plane * NLAT
    field = (plane >= NZ).astype(jnp.int32)
    level = plane - field * NZ
    rows = (field * NLAT + lat_row) * ZP + level
    ints = jnp.concatenate([jnp.transpose(send_list), cell & 127, column_depth], axis=0)
    vert = jnp.transpose(vert_inverse, (1, 0, 2)).reshape(NF * NZ, NZ)
    floats = jnp.concatenate(
        [
            obs_value.reshape(CAP, LANES),
            zonal_weight.reshape(NF * NLAT, LANES),
            merid_weight.reshape(NF * NLAT, LANES),
            jnp.pad(vert, ((0, 0), (0, LANES - NZ))),
        ],
        axis=0,
    )
    made = prepare(ints, floats, north)
    incoming, coefs, grids = made[0], made[1:14], made[14:]
    *grids, norm = scatter(rows, ints, incoming, norm_scale, grids)
    whole = solve(grids, norm, ints, coefs)
    tiles, increment = pick(rows, ints, whole)
    return increment, place(tiles, ints).reshape(-1)


def solution(mesh):
    in_specs = (
        P(("lon", "lat")),
        P(("lon", "lat"), None),
        P(("lon", "lat"), None),
        P("lat", "lon"),
        P(None, "lat", "lon"),
        P(None, "lat", "lon"),
        P(),
        P(None, None, "lat", "lon"),
    )
    out_specs = (P(None, None, "lat", "lon"), P(("lon", "lat")))
    return jax.shard_map(local, mesh=mesh, in_specs=in_specs, out_specs=out_specs, check_vma=False)
```

```python
import jax
import jax.numpy as jnp
from jax import lax
from jax.experimental import pallas as pl
from jax.experimental.pallas import tpu as pltpu
from jax.sharding import PartitionSpec as P

F32 = jnp.float32
BF16 = jnp.bfloat16
MESH = pl.DeviceIdType.MESH
NF, NZ, NLAT, NLON = 2, 75, 40, 128
ZP = 80
RANKS, CAP = 128, 80
N_LON, N_LAT = 32, 4
GROUPS = 15
GROUP = 5
LANES = 128
CHUNK = 20
HALF = 64
VERT_CHUNK = 10
GRIDS = 8
ROWS = NF * NLAT * ZP
ZW_AT, MW_AT, VERT_AT = 80, 160, 240
DEPTH_AT = 160
VMEM_SPEC = pl.BlockSpec(memory_space=pltpu.VMEM)
SMEM_SPEC = pl.BlockSpec(memory_space=pltpu.SMEM)
ANY_SPEC = pl.BlockSpec(memory_space=pl.ANY)


def cost(micros):
    return pl.CostEstimate(flops=0, bytes_accessed=int(micros * 3.6e6), transcendentals=0)


def lane_iota(rows):
    return lax.broadcasted_iota(jnp.int32, (rows, LANES), 1)


def split(value):
    high = value.astype(BF16)
    return high, (value - high.astype(F32)).astype(BF16)


def lane_pick(table, index):
    return jnp.take_along_axis(table, index, axis=1, mode="promise_in_bounds")


def push(source, target, send_sem, recv_sem, axis, device):
    return pltpu.make_async_remote_copy(
        src_ref=source, dst_ref=target, send_sem=send_sem, recv_sem=recv_sem,
        device_id={axis: device}, device_id_type=MESH,
    )


def over(axis, count, action):
    mine = lax.axis_index(axis)

    def body(step, _):
        action((mine + step) % count)
        return 0

    lax.fori_loop(1, count, body, 0)


def over_lon(action):
    over("lon", N_LON, action)


def over_lat(action):
    over("lat", N_LAT, action)


def greet():
    barrier = pltpu.get_barrier_semaphore()
    over_lon(
        lambda device: pl.semaphore_signal(
            barrier, inc=1, device_id={"lon": device}, device_id_type=MESH
        )
    )
    over_lat(
        lambda device: pl.semaphore_signal(
            barrier, inc=1, device_id={"lat": device}, device_id_type=MESH
        )
    )


def greeted():
    pl.semaphore_wait(pltpu.get_barrier_semaphore(), N_LON - 1 + N_LAT - 1)


def zonal_coefs(floats_ref, zs_ref, zr_ref, zco_ref, iw_ref, st_ref, rt_ref, zero):
    one = zero + 1.0
    iw_ref[...] = jnp.full((LANES, LANES), 1e-3, F32)
    iw_ref[: NF * NLAT, :] = 1.0 / floats_ref[ZW_AT : ZW_AT + NF * NLAT, :]
    iw_ref[...] = jnp.transpose(iw_ref[...])

    def zonal_step(step, carry):
        s_val, s_flux, s_sum, r_val, r_flux, r_sum = carry
        back = LANES - 1 - step
        st_ref[pl.ds(step, 1), :] = s_val[0:1]
        s_sum = s_sum + s_val
        s_val = s_val + s_flux * iw_ref[pl.ds(step, 1), :]
        s_flux = s_flux + s_val
        r_sum = r_sum + r_val
        r_val = r_val + r_flux * iw_ref[pl.ds(back, 1), :]
        rt_ref[pl.ds(back, 1), :] = r_val[0:1]
        r_flux = r_flux + r_val
        return s_val, s_flux, s_sum, r_val, r_flux, r_sum

    _, _, s_sum, r_first, _, r_sum = lax.fori_loop(
        0, LANES, zonal_step, (zero, one, zero, zero, one, zero), unroll=8
    )
    coupling = 1.0 / r_first[0:1]
    zco_ref[...] = jnp.zeros((8, LANES), F32)
    zco_ref[0:1, :] = coupling
    zco_ref[1:2, :] = r_sum[0:1] * coupling
    zco_ref[2:3, :] = s_sum[0:1] * coupling
    zs_ref[...] = jnp.transpose(st_ref[...])[: NF * NLAT, :]
    zr_ref[...] = jnp.transpose(rt_ref[...] * coupling)[: NF * NLAT, :]


def merid_coefs(floats_ref, ms_ref, mr_ref, mss_ref, mrr_ref, mco_ref, miw_ref, north, zero):
    one = zero + 1.0
    for field in range(NF):
        at = MW_AT + field * NLAT
        miw_ref[field] = 1.0 / floats_ref[at : at + NLAT, :]
    mco_ref[...] = jnp.zeros((NF, 8, LANES), F32)
    for field in range(NF):
        s_val, s_flux, s_sum = zero, one, zero
        for row in range(NLAT):
            ms_ref[field, row : row + 1, :] = s_val[0:1]
            s_sum = s_sum + s_val
            s_val = s_val + s_flux * miw_ref[field, row : row + 1, :]
            s_flux = s_flux + s_val
        r_val = jnp.where(north > 0.5, 1.0, miw_ref[field, NLAT - 1 : NLAT, :] + zero)
        r_flux = jnp.where(north > 0.5, 0.0, one)
        r_sum = zero
        mr_ref[field, NLAT - 1 : NLAT, :] = r_val[0:1]
        for row in range(NLAT - 2, -1, -1):
            r_sum = r_sum + r_val
            r_flux = r_flux + r_val
            r_val = r_val + r_flux * miw_ref[field, row : row + 1, :]
            mr_ref[field, row : row + 1, :] = r_val[0:1]
        inverse = 1.0 / r_val[0:1]
        coupling = jnp.where(north[0:1] > 0.5, 0.0, inverse)
        mr_ref[field] = mr_ref[field] * inverse
        sum_rr, sum_rs = zero, zero
        for row in range(NLAT - 1, -1, -1):
            at = slice(row, row + 1)
            s_row, r_row = ms_ref[field, at, :], mr_ref[field, at, :]
            mrr_ref[field, at, :] = s_row * sum_rr[0:1]
            mss_ref[field, at, :] = s_row * sum_rs[0:1]
            sum_rr = sum_rr + r_row * r_row
            sum_rs = sum_rs + r_row * s_row
        sum_sr, sum_ss = zero, zero
        for row in range(NLAT):
            at = slice(row, row + 1)
            s_row, r_row = ms_ref[field, at, :], mr_ref[field, at, :]
            sum_sr = sum_sr + s_row * r_row
            sum_ss = sum_ss + s_row * s_row
            mrr_ref[field, at, :] = mrr_ref[field, at, :] + r_row * sum_sr[0:1]
            mss_ref[field, at, :] = mss_ref[field, at, :] + r_row * sum_ss[0:1]
        mco_ref[field, 0:1, :] = coupling
        mco_ref[field, 1:2, :] = r_sum[0:1] * inverse
        mco_ref[field, 2:3, :] = s_sum[0:1] * coupling
        mco_ref[field, 3:4, :] = sum_rr[0:1]
        mco_ref[field, 4:5, :] = sum_rs[0:1] * coupling
        mco_ref[field, 5:6, :] = sum_ss[0:1] * coupling * coupling


def zonal_factor(zco_all, alpha, gamma, minv):
    coupling = zco_all[:, 0, :]
    west = jnp.concatenate([coupling[-1:], coupling[:-1]], axis=0)
    spill = zco_all[:, 2, :]
    mass = 1.0 + zco_all[:, 1, :] + jnp.concatenate([spill[-1:], spill[:-1]], axis=0)
    east = coupling
    for bit in range(5):
        stride = 1 << bit
        down = lambda v: jnp.concatenate([v[-stride:], v[:-stride]], axis=0)
        up = lambda v: jnp.concatenate([v[stride:], v[:stride]], axis=0)
        inverse = 1.0 / (mass + west + east)
        left = west * down(inverse)
        right = east * up(inverse)
        for field in range(NF):
            alpha[field, bit] = to_field(left, field)
            gamma[field, bit] = to_field(right, field)
        mass = mass + left * down(mass) + right * up(mass)
        west, east = left * down(west), right * up(east)
    for field in range(NF):
        minv[field] = to_field(1.0 / mass, field)


def to_field(rows, field):
    return rows if field == 0 else pltpu.roll(rows, LANES - field * NLAT, 1)


def gather_lines(table_ref, count, high, low, base):
    def step(row, acc):
        line = jnp.broadcast_to(table_ref[pl.ds(row, 1), :], (ZP, LANES))
        return jnp.where(high == row + base, lane_pick(line, low), acc)

    return lax.fori_loop(0, count, step, jnp.zeros((ZP, LANES), F32), unroll=8)


def two_phase(tile_out, tile_in, rows_out, rows_in, sems):
    me = lax.axis_index("lon")
    my = lax.axis_index("lat")
    s1, r1, s2, r2 = sems
    first = lambda device, slot: push(
        tile_out.at[device], tile_in.at[slot], s1.at[device], r1.at[slot], "lon", device
    )
    second = lambda device, slot: push(
        rows_out.at[device], rows_in.at[slot], s2.at[device], r2.at[slot], "lat", device
    )

    def begin():
        over_lon(lambda device: first(device, me).start())
        tile_in[me] = tile_out[me]

    def middle():
        over_lon(lambda device: first(0, device).wait_recv())
        for lat in range(N_LAT):
            rows_out[lat] = tile_in[:, lat, :]
        over_lat(lambda device: second(device, my).start())
        rows_in[my] = rows_out[my]

    def end():
        over_lat(lambda device: second(0, device).wait_recv())

    def sent():
        over_lon(lambda device: first(device, me).wait_send())
        over_lat(lambda device: second(device, my).wait_send())

    return begin, middle, end, sent


def prepare_kernel(
    ints_ref, floats_ref, north_ref,
    out_ref, zs_ref, zr_ref, zco_out, ms_ref, mr_ref, mss_ref, mrr_ref, mco_out, vert_ref,
    alpha, gamma, minv, sums_ref, row_ref, *rest
):
    grids, rest = rest[:GRIDS], rest[GRIDS:]
    prepare_body(
        ints_ref, floats_ref, north_ref, out_ref, zs_ref, zr_ref, zco_out, ms_ref, mr_ref, mss_ref,
        mrr_ref, mco_out, vert_ref, alpha, gamma, minv, sums_ref, row_ref, grids, *rest,
    )


def prepare_body(
    ints_ref, floats_ref, north_ref,
    out_ref, zs_ref, zr_ref, zco_out, ms_ref, mr_ref, mss_ref, mrr_ref, mco_out, vert_ref,
    alpha, gamma, minv, sums_ref, row_ref, grids,
    iw_ref, st_ref, rt_ref, miw_ref, prod_ref,
    tile_out, tile_in, rows_out, rows_in, zco_ref, zco_all, mco_ref, mco_all,
    o1s, o1r, o2s, o2r, zco_s, zco_r, mco_s, mco_r,
):
    me = lax.axis_index("lon")
    my = lax.axis_index("lat")
    greet()
    index = ints_ref[0:CAP, :]
    picked = gather_lines(floats_ref, CAP, index >> 7, index & 127, 0)
    picked = jnp.transpose(
        jnp.concatenate([picked, jnp.zeros((LANES - CAP, LANES), F32)], axis=0)
    )
    for device in range(N_LON):
        tile_out[device, 0:4, :] = picked[4 * device : 4 * device + 4]
        tile_out[device, 4:8, :] = jnp.zeros((4, LANES), F32)

    begin, middle, end, sent = two_phase(tile_out, tile_in, rows_out, rows_in, (o1s, o1r, o2s, o2r))
    zco_copy = lambda device, slot: push(
        zco_ref, zco_all.at[slot], zco_s.at[device], zco_r.at[slot], "lon", device
    )
    mco_copy = lambda device, slot: push(
        mco_ref, mco_all.at[slot], mco_s.at[device], mco_r.at[slot], "lat", device
    )
    greeted()
    begin()
    zero = north_ref[...] * 0.0
    zonal_coefs(floats_ref, zs_ref, zr_ref, zco_ref, iw_ref, st_ref, rt_ref, zero)
    over_lon(lambda device: zco_copy(device, me).start())
    zco_all[me] = zco_ref[...]
    merid_coefs(floats_ref, ms_ref, mr_ref, mss_ref, mrr_ref, mco_ref, miw_ref, north_ref[...], zero)
    over_lat(lambda device: mco_copy(device, my).start())
    mco_all[my] = mco_ref[...]
    middle()
    for field in range(NF):
        zco_out[field] = to_field(zco_ref[...], field)
    cell = jnp.maximum(ints_ref[CAP : 2 * CAP, :], 0)
    line = cell >> 7
    plane = line // NLAT
    second_field = (plane >= NZ).astype(jnp.int32)
    row_ref[...] = (second_field * NLAT + line - plane * NLAT) * ZP + plane - second_field * NZ
    prod_ref[...] = jnp.zeros((ZP, LANES), F32)
    for field in range(NF):
        matrix = floats_ref[pl.ds(VERT_AT + field, NZ, stride=NF), :]
        prod_ref[:NZ, :NZ] = lax.dot_general(
            matrix, matrix, (((1,), (1,)), ((), ())),
            precision=lax.Precision.HIGHEST, preferred_element_type=F32,
        )
        high, low = split(prod_ref[:, :ZP])
        vert_ref[field] = jnp.concatenate([high, low, high], axis=1)
    source = lax.broadcasted_iota(jnp.int32, (2 * LANES, 2 * LANES), 0) & 127
    target = lax.broadcasted_iota(jnp.int32, (2 * LANES, 2 * LANES), 1)
    sums_ref[...] = jnp.where(source <= target, 1.0, 0.0).astype(BF16)
    def clear(step, _):
        at = pl.ds(pl.multiple_of(step * 64, 64), 64)
        for grid in grids:
            grid[at, :] = jnp.zeros((64, LANES), F32)
        return 0

    lax.fori_loop(0, ROWS // 64, clear, 0)
    end()
    for lat in range(N_LAT):
        out_ref[N_LON * lat : N_LON * lat + N_LON, :] = rows_in[lat]
    over_lon(lambda device: zco_copy(0, device).wait_recv())
    zonal_factor(zco_all, alpha, gamma, minv)
    over_lat(lambda device: mco_copy(0, device).wait_recv())
    mco_out[...] = mco_all[...]
    sent()
    over_lon(lambda device: zco_copy(device, me).wait_send())
    over_lat(lambda device: mco_copy(device, my).wait_send())


def prepare(ints, floats, north):
    shape = lambda *dims: jax.ShapeDtypeStruct(dims, F32)
    vmem = lambda *dims: pltpu.VMEM(dims, F32)
    dma = pltpu.SemaphoreType.DMA
    return pl.pallas_call(
        prepare_kernel,
        out_shape=(
            shape(RANKS, LANES), shape(80, LANES), shape(80, LANES), shape(NF, 8, LANES),
            shape(NF, NLAT, LANES), shape(NF, NLAT, LANES),
            shape(NF, NLAT, LANES), shape(NF, NLAT, LANES), shape(N_LAT, NF, 8, LANES),
            jax.ShapeDtypeStruct((NF, ZP, 3 * ZP), BF16),
            shape(NF, 5, N_LON, LANES), shape(NF, 5, N_LON, LANES), shape(NF, N_LON, LANES),
            jax.ShapeDtypeStruct((2 * LANES, 2 * LANES), BF16),
            jax.ShapeDtypeStruct((CAP, LANES), jnp.int32),
        )
        + (shape(ROWS, LANES),) * GRIDS,
        in_specs=[VMEM_SPEC] * 3,
        out_specs=(VMEM_SPEC,) * (15 + GRIDS),
        scratch_shapes=[
            vmem(LANES, LANES), vmem(LANES, LANES), vmem(LANES, LANES), vmem(NF, NLAT, LANES),
            vmem(ZP, LANES),
            vmem(N_LON, 8, LANES), vmem(N_LON, 8, LANES),
            vmem(N_LAT, N_LON, LANES), vmem(N_LAT, N_LON, LANES),
            vmem(8, LANES), vmem(N_LON, 8, LANES), vmem(NF, 8, LANES), vmem(N_LAT, NF, 8, LANES),
            dma((N_LON,)), dma((N_LON,)), dma((N_LAT,)), dma((N_LAT,)),
            dma((N_LON,)), dma((N_LON,)), dma((N_LAT,)), dma((N_LAT,)),
        ],
        compiler_params=pltpu.CompilerParams(
            collective_id=0, has_side_effects=True, vmem_limit_bytes=6 << 20
        ),
        cost_estimate=cost(15),
        name="prepare",
    )(ints, floats, north)


def scatter_kernel(rows_ref, ints_ref, in_ref, norm_ref, *refs):
    grids = refs[GRIDS : 2 * GRIDS]
    norm_buf, norm_sem, value_ref, even_ref, odd_ref = refs[2 * GRIDS :]

    def norm_copy(field, row):
        return pltpu.make_async_copy(
            norm_ref.at[field, :, row, :],
            norm_buf.at[field, row, pl.ds(0, NZ), :],
            norm_sem.at[field, row],
        )

    def over_rows(action):
        for field in range(NF):

            def body(row, _, field=field):
                action(norm_copy(field, row))
                return 0

            lax.fori_loop(0, NLAT, body, 0)

    over_rows(lambda copy: copy.start())
    value_ref[...] = jnp.transpose(in_ref[...])
    iota = lane_iota(CAP)

    def spread(q):
        index = jnp.full((CAP, LANES), q, jnp.int32)
        place = jnp.full((CAP, LANES), (q % N_LAT) * N_LON + q // N_LAT, jnp.int32)
        lane = lane_pick(ints_ref[CAP : 2 * CAP, :] & 127, index)
        return jnp.where(iota == lane, lane_pick(value_ref[:CAP, :], place), 0.0)

    def add(q, source):
        for k in range(CAP):
            at = pl.ds(rows_ref[k * RANKS + q], 1)
            grid = grids[k % GRIDS]
            grid[at, :] = grid[at, :] + source[k : k + 1, :]

    even_ref[...] = spread(0)

    def senders(pair, _):
        q = 2 * pair
        odd_ref[...] = spread(q + 1)
        add(q, even_ref)
        even_ref[...] = spread(jnp.minimum(q + 2, RANKS - 1))
        add(q + 1, odd_ref)
        return 0

    lax.fori_loop(0, RANKS // 2, senders, 0)
    over_rows(lambda copy: copy.wait())


def scatter(rows, ints, incoming, norm, grids):
    grid = jax.ShapeDtypeStruct((ROWS, LANES), F32)
    return pl.pallas_call(
        scatter_kernel,
        out_shape=(grid,) * GRIDS + (jax.ShapeDtypeStruct((NF, NLAT, ZP, LANES), F32),),
        in_specs=[SMEM_SPEC] + [VMEM_SPEC] * 2 + [ANY_SPEC] + [VMEM_SPEC] * GRIDS,
        out_specs=(VMEM_SPEC,) * (GRIDS + 1),
        input_output_aliases={4 + index: index for index in range(GRIDS)},
        scratch_shapes=[
            pltpu.SemaphoreType.DMA((NF, NLAT)),
            pltpu.VMEM((LANES, LANES), F32), pltpu.VMEM((CAP, LANES), F32), pltpu.VMEM((CAP, LANES), F32),
        ],
        compiler_params=pltpu.CompilerParams(vmem_limit_bytes=6 << 20),
        cost_estimate=cost(12),
        name="scatter",
    )(rows, ints, incoming, norm, *grids)


def solve_kernel(*refs):
    solve_body(refs[:GRIDS], *refs[GRIDS:])


def solve_body(
    grids, norm_ref, ints_ref, zs_ref, zr_ref, zco_ref, ms_ref, mr_ref, mss_ref, mrr_ref, mco_all,
    vert_ref, alpha, gamma, minv, sums_ref,
    x_ref,
    zsend, zrecv, zret, zres, msend, mrecv, mval,
    acc_a, acc_b, ubuf, gbuf, mtot, mbuf,
    z1s, z1r, z2s, z2r, m1s, m1r,
):
    me = lax.axis_index("lon")
    my = lax.axis_index("lat")
    iota = lane_iota(ZP)
    half = N_LON // NF
    my_field = me // half
    is_solver = me % half < GROUPS
    nothing = jnp.zeros((ZP, LANES), F32)
    greet()


    def zonal_out(turn, field, group, slot):
        return push(
            zsend.at[turn, field, group], zrecv.at[turn, slot],
            z1s.at[turn, field, group], z1r.at[turn, slot], "lon", field * half + group,
        )

    def zonal_back(turn, device, field, group):
        return push(
            zret.at[turn, device], zres.at[turn, field, group],
            z2s.at[turn, device], z2r.at[turn, field, group], "lon", device,
        )

    def others(field, action):
        for group in range(GROUPS):
            pl.when(me != field * half + group)(lambda group=group: action(group))

    def zonal_pass(turn, field, load):
        def chunk_pass(chunk, _):
            lines, left = [], []
            for step in range(CHUNK):
                row = chunk * CHUNK + step
                at = pl.ds(field * NLAT + row, 1)
                s_row, r_row = zs_ref[at, :], zr_ref[at, :]
                value = load(row)
                for coef in (s_row, r_row):
                    high, low = split(coef * value)
                    left.append(jnp.concatenate([high, low], axis=1))
                lines.append((row, s_row, r_row))
            sums = jnp.dot(
                jnp.concatenate(left, axis=0), sums_ref[...], preferred_element_type=F32
            )
            tot_a, tot_b = acc_a[...], acc_b[field]
            for step, (row, s_row, r_row) in enumerate(lines):
                a_part = sums[2 * step * ZP : (2 * step + 1) * ZP]
                b_part = sums[(2 * step + 1) * ZP : (2 * step + 2) * ZP]
                x_ref[field, row] = r_row * a_part[:, :LANES] - s_row * b_part[:, :LANES]
                mine = iota == row
                tot_a = jnp.where(mine, a_part[:, LANES:], tot_a)
                tot_b = jnp.where(mine, b_part[:, LANES:], tot_b)
            acc_a[...] = tot_a
            acc_b[field] = tot_b
            return 0

        acc_a[...] = nothing
        acc_b[field] = nothing
        lax.fori_loop(0, NLAT // CHUNK, chunk_pass, 0)
        acc_a[...] = acc_b[field] + pltpu.roll(acc_a[...] * zco_ref[field, 0:1, :], HALF, 1)
        for group in range(GROUPS):
            at = slice(GROUP * group, GROUP * group + GROUP)
            zsend[turn, field, group, 0:GROUP, :] = acc_a[at, :]

    def zonal_send(turn, field):
        others(field, lambda group: zonal_out(turn, field, group, me).start())

        @pl.when(is_solver & (my_field == field))
        def _():
            zrecv[turn, me] = zsend[turn, field, me % half]

    def zonal_reduced(turn):
        mine = me % half
        over_lon(lambda device: zonal_out(turn, 0, 0, device).wait_recv())
        right_side = [
            zrecv[turn, k] + pltpu.roll(zrecv[turn, (k - 1) % N_LON], HALF, 1) for k in range(N_LON)
        ]
        for bit in range(5):
            stride = 1 << bit
            right_side = [
                right_side[k]
                + alpha[my_field, bit, k : k + 1, :] * right_side[(k - stride) % N_LON]
                + gamma[my_field, bit, k : k + 1, :] * right_side[(k + stride) % N_LON]
                for k in range(N_LON)
            ]
        values = [right_side[k] * minv[my_field, k : k + 1, :] for k in range(N_LON)]
        for k in range(N_LON):
            zret[turn, k] = jnp.where(
                iota[0:8] < HALF, values[k], pltpu.roll(values[(k + 1) % N_LON], HALF, 1)
            )
        over_lon(lambda device: zonal_back(turn, device, my_field, mine).start())
        zres[turn, my_field, mine] = zret[turn, me]

    def zonal_receive(turn, field):
        others(field, lambda group: zonal_back(turn, 0, field, group).wait_recv())
        ubuf[72:80, :] = jnp.zeros((8, LANES), F32)
        for group in range(GROUPS):
            at = slice(GROUP * group, GROUP * group + GROUP)
            ubuf[at, :] = zres[turn, field, group, 0:GROUP, :]
        gbuf[...] = pltpu.roll(ubuf[...], HALF, 1) * zco_ref[field, 0:1, :] + acc_b[field]

    def zonal_values(field, chunk):
        u_all, g_all = ubuf[...], gbuf[...]
        found = []
        for step in range(CHUNK):
            row = chunk * CHUNK + step
            at = pl.ds(field * NLAT + row, 1)
            found.append(
                x_ref[field, row]
                + zr_ref[at, :] * jnp.broadcast_to(u_all[:, step : step + 1], (ZP, LANES))
                + zs_ref[at, :] * jnp.broadcast_to(g_all[:, step : step + 1], (ZP, LANES))
            )
        ubuf[...] = pltpu.roll(u_all, LANES - CHUNK, 1)
        gbuf[...] = pltpu.roll(g_all, LANES - CHUNK, 1)
        return found


    def vertical(field, value):
        high, low = split(value)
        return jnp.dot(
            vert_ref[field], jnp.concatenate([high, high, low], axis=0), preferred_element_type=F32
        )

    def vertical_field(field):
        def body(step, _):
            row = step * VERT_CHUNK
            value = jnp.concatenate([x_ref[field, row + k] for k in range(VERT_CHUNK)], axis=1)
            value = vertical(field, value)
            for k in range(VERT_CHUNK):
                x_ref[field, row + k] = value[:, k * LANES : (k + 1) * LANES]
            return 0

        lax.fori_loop(0, NLAT // VERT_CHUNK, body, 0)


    def merid_out(field, device, slot):
        return push(
            msend.at[field], mrecv.at[field, slot],
            m1s.at[field, device], m1r.at[field, slot], "lat", device,
        )

    def merid_pass(field):
        def one(chunk, carry):
            tot_a, tot_b = carry
            found = zonal_values(field, chunk)
            for step in range(CHUNK):
                row = chunk * CHUNK + step
                s_row, r_row = ms_ref[field, pl.ds(row, 1), :], mr_ref[field, pl.ds(row, 1), :]
                tot_a = tot_a + s_row * found[step]
                tot_b = tot_b + r_row * found[step]
                x_ref[field, row] = r_row * tot_a - s_row * tot_b
            return tot_a, tot_b

        a_one, b_one = lax.fori_loop(0, NLAT // CHUNK, one, (nothing, nothing))
        ubuf[...] = b_one

        def two(row, carry):
            tot_a, tot_b = carry
            s_row, r_row = ms_ref[field, pl.ds(row, 1), :], mr_ref[field, pl.ds(row, 1), :]
            value = x_ref[field, row] + s_row * ubuf[...]
            tot_a = tot_a + s_row * value
            tot_b = tot_b + r_row * value
            x_ref[field, row] = r_row * tot_a - s_row * tot_b
            return tot_a, tot_b

        a_two, b_two = lax.fori_loop(0, NLAT, two, (nothing, nothing), unroll=4)
        mtot[field] = b_two
        coupling = mco_all[my, field, 0:1, :]
        for part, value in enumerate((b_one, a_one * coupling, b_two, a_two * coupling)):
            msend[field, part] = value
        over_lat(lambda device: merid_out(field, device, my).start())
        mrecv[field, my] = msend[field]

    def merid_reduced(field):
        over_lat(lambda device: merid_out(field, 0, device).wait_recv())
        coef = lambda k, row: mco_all[k, field, row : row + 1, :]

        def tile(step, _):
            at = pl.ds(pl.multiple_of(step * 8, 8), 8)
            part = lambda k, index: mrecv[field, k, index, at, :]

            def solve_four(right_side):
                mass = 1.0 + coef(0, 1)
                reduced = right_side[0]
                kept, inverses, values = [], [], [None] * N_LAT
                for k in range(N_LAT):
                    inverse = 1.0 / (mass + coef(k, 0))
                    kept.append(reduced)
                    inverses.append(inverse)
                    if k + 1 < N_LAT:
                        factor = coef(k, 0) * inverse
                        mass = 1.0 + coef(k + 1, 1) + coef(k, 2) + factor * mass
                        reduced = right_side[k + 1] + factor * reduced
                values[-1] = kept[-1] * inverses[-1]
                for k in range(N_LAT - 2, -1, -1):
                    values[k] = (kept[k] + coef(k, 0) * values[k + 1]) * inverses[k]
                return values

            none = jnp.zeros((8, LANES), F32)
            u = solve_four([part(k, 0) + (part(k - 1, 1) if k else none) for k in range(N_LAT)])
            u = u + [none]
            second = []
            for k in range(N_LAT):
                value = part(k, 2) + coef(k, 3) * u[k] + coef(k, 4) * u[k + 1]
                if k:
                    value = value + part(k - 1, 3) + coef(k - 1, 4) * u[k - 1] + coef(k - 1, 5) * u[k]
                second.append(value)
            v = solve_four(second) + [none]
            for k in range(N_LAT + 1):
                mval[0, k, at, :] = u[k]
                mval[1, k, at, :] = v[k]
            return 0

        lax.fori_loop(0, ZP // 8, tile, 0)
        coupling = mco_all[my, field, 0:1, :]
        mbuf[0] = mval[0, my]
        mbuf[1] = mval[0, my + 1] * coupling
        mbuf[2] = mval[1, my]
        mbuf[3] = mval[1, my + 1] * coupling + mtot[field]

    def merid_value(field, row):
        at = pl.ds(row, 1)
        return (
            x_ref[field, row]
            + mrr_ref[field, at, :] * mbuf[0]
            + mss_ref[field, at, :] * mbuf[1]
            + mr_ref[field, at, :] * mbuf[2]
            + ms_ref[field, at, :] * mbuf[3]
        )

    level = lax.broadcasted_iota(jnp.int32, (ZP, LANES), 0)

    def scale(field, row):
        wet = level < ints_ref[pl.ds(DEPTH_AT + row, 1), :]
        return jnp.where(wet, norm_ref[field, row], 0.0)

    def scaled_grid(field):
        def load(row):
            at = pl.ds(pl.multiple_of((field * NLAT + row) * ZP, ZP), ZP)
            total = [grid[at, :] for grid in grids]
            while len(total) > 1:
                total = [one + two for one, two in zip(total[::2], total[1::2])]
            return scale(field, row) * total[0]

        return load

    zonal_pass(0, 0, scaled_grid(0))
    greeted()
    zonal_send(0, 0)
    zonal_pass(0, 1, scaled_grid(1))
    zonal_send(0, 1)
    vertical_field(0)
    pl.when(is_solver & (my_field == 0))(lambda: zonal_reduced(0))
    vertical_field(1)
    pl.when(is_solver & (my_field == 1))(lambda: zonal_reduced(0))

    for field in range(NF):
        zonal_receive(0, field)
        both = vertical(field, jnp.concatenate([ubuf[...], gbuf[...]], axis=1))
        ubuf[...] = both[:, :LANES]
        gbuf[...] = both[:, LANES:]
        merid_pass(field)

    for field in range(NF):
        merid_reduced(field)
        zonal_pass(1, field, lambda row, field=field: merid_value(field, row))
        zonal_send(1, field)
    pl.when(is_solver)(lambda: zonal_reduced(1))
    for field in range(NF):
        zonal_receive(1, field)

        def last_pass(chunk, _, field=field):
            found = zonal_values(field, chunk)
            for step in range(CHUNK):
                row = chunk * CHUNK + step
                x_ref[field, row] = found[step] * scale(field, row)
            return 0

        lax.fori_loop(0, NLAT // CHUNK, last_pass, 0)

    for field in range(NF):
        over_lat(lambda device, field=field: merid_out(field, device, my).wait_send())
        for turn in range(2):
            others(
                field,
                lambda group, turn=turn, field=field: zonal_out(turn, field, group, me).wait_send(),
            )

    @pl.when(is_solver)
    def _():
        for turn in range(2):
            over_lon(lambda device, turn=turn: zonal_back(turn, device, 0, 0).wait_send())


def solve(grids, norm, ints, coefs):
    dma = pltpu.SemaphoreType.DMA
    vmem = lambda *dims: pltpu.VMEM(dims, F32)
    return pl.pallas_call(
        solve_kernel,
        out_shape=jax.ShapeDtypeStruct((NF, NLAT, ZP, LANES), F32),
        in_specs=[VMEM_SPEC] * (15 + GRIDS),
        out_specs=VMEM_SPEC,
        scratch_shapes=[
            vmem(2, NF, GROUPS, 8, LANES), vmem(2, N_LON, 8, LANES),
            vmem(2, N_LON, 8, LANES), vmem(2, NF, GROUPS, 8, LANES),
            vmem(NF, 4, ZP, LANES), vmem(NF, N_LAT, 4, ZP, LANES), vmem(2, N_LAT + 1, ZP, LANES),
            vmem(ZP, LANES), vmem(NF, ZP, LANES), vmem(ZP, LANES), vmem(ZP, LANES),
            vmem(NF, ZP, LANES), vmem(4, ZP, LANES),
            dma((2, NF, GROUPS)), dma((2, N_LON)), dma((2, N_LON)), dma((2, NF, GROUPS)),
            dma((NF, N_LAT)), dma((NF, N_LAT)),
        ],
        compiler_params=pltpu.CompilerParams(
            collective_id=1, has_side_effects=True, vmem_limit_bytes=10 << 20
        ),
        cost_estimate=cost(40),
        name="solve",
    )(*grids, norm, ints, *coefs)


def pick_kernel(rows_ref, ints_ref, x_ref, out_ref, inc_ref, inc_sem, *copies):
    iota = lane_iota(8)

    def inc_copy(field, row):
        return pltpu.make_async_copy(
            x_ref.at[pl.ds(pl.multiple_of((field * NLAT + row) * ZP, ZP), NZ), :],
            inc_ref.at[field, :, row, :],
            inc_sem.at[field, row],
        )

    def over_rows(action):
        for field in range(NF):

            def body(row, _, field=field):
                action(inc_copy(field, row))
                return 0

            lax.fori_loop(0, NLAT, body, 0)

    over_rows(lambda copy: copy.start())
    group = len(copies)

    def senders(step, acc):
        acc = list(acc)
        for part in range(group):
            q = step * group + part
            for k in range(CAP):
                copies[part][k : k + 1, :] = x_ref[pl.ds(rows_ref[k * RANKS + q], 1), :]
        for part in range(group):
            q = step * group + part
            for tile in range(CAP // 8):
                at = slice(8 * tile, 8 * tile + 8)
                found = lane_pick(
                    copies[part][at, :], ints_ref[CAP + 8 * tile : CAP + 8 * tile + 8, :] & 127
                )
                acc[tile] = jnp.where(iota == q, found, acc[tile])
        return tuple(acc)

    acc = lax.fori_loop(0, RANKS // group, senders, (jnp.zeros((8, LANES), F32),) * (CAP // 8))
    whole = jnp.concatenate(list(acc) + [jnp.zeros((LANES - CAP, LANES), F32)], axis=0)
    whole = jnp.transpose(whole)
    for device in range(N_LON):
        out_ref[device, 0:4, :] = whole[4 * device : 4 * device + 4]
        out_ref[device, 4:8, :] = jnp.zeros((4, LANES), F32)
    over_rows(lambda copy: copy.wait())


def pick(rows, ints, increment):
    return pl.pallas_call(
        pick_kernel,
        out_shape=(
            jax.ShapeDtypeStruct((N_LON, 8, LANES), F32),
            jax.ShapeDtypeStruct((NF, NZ, NLAT, LANES), F32),
        ),
        in_specs=[SMEM_SPEC, VMEM_SPEC, VMEM_SPEC],
        out_specs=(VMEM_SPEC, ANY_SPEC),
        scratch_shapes=[pltpu.SemaphoreType.DMA((NF, NLAT))] + [pltpu.VMEM((CAP, LANES), F32)] * 16,
        compiler_params=pltpu.CompilerParams(vmem_limit_bytes=8 << 20),
        cost_estimate=cost(14),
        name="pick",
    )(rows, ints, increment.reshape(ROWS, LANES))


def place_kernel(
    tile_out, ints_ref, out_ref,
    idx_ref, val_ref, rows_oh, cols_oh, tile_in, rows_out, rows_in, b1s, b1r, b2s, b2r,
):
    greet()
    none = jnp.full((LANES - CAP, LANES), -1, jnp.int32)
    idx_ref[...] = jnp.transpose(jnp.concatenate([ints_ref[0:CAP, :], none], axis=0))
    begin, middle, end, sent = two_phase(tile_out, tile_in, rows_out, rows_in, (b1s, b1r, b2s, b2r))
    row_iota = lax.broadcasted_iota(jnp.int32, (CAP, 2 * LANES), 0)
    col_iota = lax.broadcasted_iota(jnp.int32, (LANES, 2 * LANES), 0)

    def build(step, _):
        lat = step // (N_LON // 2)
        left = (step % (N_LON // 2)) * 2 * N_LAT + lat
        index = jnp.concatenate(
            [idx_ref[pl.ds(left, 1), :], idx_ref[pl.ds(left + N_LAT, 1), :]], axis=1
        )
        rows_oh[step] = jnp.where(row_iota == (index >> 7), 1.0, 0.0).astype(BF16)
        cols_oh[step] = jnp.where(col_iota == (index & 127), 1.0, 0.0).astype(BF16)
        return 0

    def add(step, acc):
        value = jnp.concatenate(
            [val_ref[pl.ds(2 * step, 1), :], val_ref[pl.ds(2 * step + 1, 1), :]], axis=1
        )
        high, low = split(value)
        rows = rows_oh[step]
        return acc + lax.dot_general(
            jnp.concatenate([rows * high, rows * low], axis=0), cols_oh[step],
            (((1,), (1,)), ((), ())), preferred_element_type=F32,
        )

    greeted()
    begin()
    lax.fori_loop(0, RANKS // 4, build, 0, unroll=2)
    middle()
    lax.fori_loop(RANKS // 4, RANKS // 2, build, 0, unroll=2)
    end()
    for lat in range(N_LAT):
        val_ref[N_LON * lat : N_LON * lat + N_LON, :] = rows_in[lat]
    acc = lax.fori_loop(0, RANKS // 2, add, jnp.zeros((2 * CAP, LANES), F32), unroll=8)
    out_ref[...] = acc[:CAP] + acc[CAP:]
    sent()


def place(tiles, ints):
    vmem = lambda *dims: pltpu.VMEM(dims, F32)
    dma = pltpu.SemaphoreType.DMA
    return pl.pallas_call(
        place_kernel,
        out_shape=jax.ShapeDtypeStruct((CAP, LANES), F32),
        in_specs=[VMEM_SPEC] * 2,
        out_specs=VMEM_SPEC,
        scratch_shapes=[
            pltpu.VMEM((RANKS, LANES), jnp.int32), vmem(RANKS, LANES),
            pltpu.VMEM((RANKS // 2, CAP, 2 * LANES), BF16),
            pltpu.VMEM((RANKS // 2, LANES, 2 * LANES), BF16),
            vmem(N_LON, 8, LANES), vmem(N_LAT, N_LON, LANES), vmem(N_LAT, N_LON, LANES),
            dma((N_LON,)), dma((N_LON,)), dma((N_LAT,)), dma((N_LAT,)),
        ],
        compiler_params=pltpu.CompilerParams(
            collective_id=2, has_side_effects=True, vmem_limit_bytes=10 << 20
        ),
        cost_estimate=cost(15),
        name="place",
    )(tiles, ints)


def local(
    obs_value, send_list, recv_cell, column_depth, zonal_weight, merid_weight, vert_inverse, norm_scale
):
    is_north = lax.axis_index("lat") == N_LAT - 1
    north = jnp.full((8, LANES), jnp.where(is_north, 1.0, 0.0), F32)
    ints = jnp.concatenate(
        [jnp.transpose(send_list), jnp.transpose(recv_cell), column_depth], axis=0
    )
    vert = jnp.transpose(vert_inverse, (1, 0, 2)).reshape(NF * NZ, NZ)
    floats = jnp.concatenate(
        [
            obs_value.reshape(CAP, LANES),
            zonal_weight.reshape(NF * NLAT, LANES),
            merid_weight.reshape(NF * NLAT, LANES),
            jnp.pad(vert, ((0, 0), (0, LANES - NZ))),
        ],
        axis=0,
    )
    made = prepare(ints, floats, north)
    incoming, coefs, rows, grids = made[0], made[1:14], made[14].reshape(-1), made[15:]
    *grids, norm = scatter(rows, ints, incoming, norm_scale, grids)
    whole = solve(grids, norm, ints, coefs)
    tiles, increment = pick(rows, ints, whole)
    return increment, place(tiles, ints).reshape(-1)


def solution(mesh):
    in_specs = (
        P(("lon", "lat")),
        P(("lon", "lat"), None),
        P(("lon", "lat"), None),
        P("lat", "lon"),
        P(None, "lat", "lon"),
        P(None, "lat", "lon"),
        P(),
        P(None, None, "lat", "lon"),
    )
    out_specs = (P(None, None, "lat", "lon"), P(("lon", "lat")))
    return jax.shard_map(local, mesh=mesh, in_specs=in_specs, out_specs=out_specs, check_vma=False)
```

```python
import jax
import jax.numpy as jnp
from jax import lax
from jax.experimental import pallas as pl
from jax.experimental.pallas import tpu as pltpu
from jax.sharding import PartitionSpec as P

F32 = jnp.float32
BF16 = jnp.bfloat16
MESH = pl.DeviceIdType.MESH
NF, NZ, NLAT, NLON = 2, 75, 40, 128
ZP = 80
RANKS, CAP = 128, 80
N_LON, N_LAT = 32, 4
GROUPS = 15
GROUP = 5
LANES = 128
CHUNK = 20
HALF = 64
SPLIT = 24
VERT_CHUNK = 10
GRIDS = 8
ROWS = NF * NLAT * ZP
ZW_AT, MW_AT, VERT_AT = 80, 160, 240
DEPTH_AT = 160
VMEM_SPEC = pl.BlockSpec(memory_space=pltpu.VMEM)
SMEM_SPEC = pl.BlockSpec(memory_space=pltpu.SMEM)
ANY_SPEC = pl.BlockSpec(memory_space=pl.ANY)


def cost(micros):
    return pl.CostEstimate(flops=0, bytes_accessed=int(micros * 3.6e6), transcendentals=0)


def lane_iota(rows):
    return lax.broadcasted_iota(jnp.int32, (rows, LANES), 1)


def split(value):
    high = value.astype(BF16)
    return high, (value - high.astype(F32)).astype(BF16)


def lane_pick(table, index):
    return jnp.take_along_axis(table, index, axis=1, mode="promise_in_bounds")


def push(source, target, send_sem, recv_sem, axis, device):
    return pltpu.make_async_remote_copy(
        src_ref=source, dst_ref=target, send_sem=send_sem, recv_sem=recv_sem,
        device_id={axis: device}, device_id_type=MESH,
    )


def over(axis, count, action):
    mine = lax.axis_index(axis)

    def body(step, _):
        action((mine + step) % count)
        return 0

    lax.fori_loop(1, count, body, 0)


def over_lon(action):
    over("lon", N_LON, action)


def over_lat(action):
    over("lat", N_LAT, action)


def greet():
    barrier = pltpu.get_barrier_semaphore()
    over_lon(
        lambda device: pl.semaphore_signal(
            barrier, inc=1, device_id={"lon": device}, device_id_type=MESH
        )
    )
    over_lat(
        lambda device: pl.semaphore_signal(
            barrier, inc=1, device_id={"lat": device}, device_id_type=MESH
        )
    )


def greeted():
    pl.semaphore_wait(pltpu.get_barrier_semaphore(), N_LON - 1 + N_LAT - 1)


def zonal_coefs(floats_ref, zs_ref, zr_ref, zco_ref, iw_ref, st_ref, rt_ref, zero):
    one = zero + 1.0
    iw_ref[...] = jnp.full((LANES, LANES), 1e-3, F32)
    iw_ref[: NF * NLAT, :] = 1.0 / floats_ref[ZW_AT : ZW_AT + NF * NLAT, :]
    iw_ref[...] = jnp.transpose(iw_ref[...])

    def zonal_step(step, carry):
        s_val, s_flux, s_sum, r_val, r_flux, r_sum = carry
        back = LANES - 1 - step
        st_ref[pl.ds(step, 1), :] = s_val[0:1]
        s_sum = s_sum + s_val
        s_val = s_val + s_flux * iw_ref[pl.ds(step, 1), :]
        s_flux = s_flux + s_val
        r_sum = r_sum + r_val
        r_val = r_val + r_flux * iw_ref[pl.ds(back, 1), :]
        rt_ref[pl.ds(back, 1), :] = r_val[0:1]
        r_flux = r_flux + r_val
        return s_val, s_flux, s_sum, r_val, r_flux, r_sum

    _, _, s_sum, r_first, _, r_sum = lax.fori_loop(
        0, LANES, zonal_step, (zero, one, zero, zero, one, zero), unroll=8
    )
    coupling = 1.0 / r_first[0:1]
    zco_ref[...] = jnp.zeros((8, LANES), F32)
    zco_ref[0:1, :] = coupling
    zco_ref[1:2, :] = r_sum[0:1] * coupling
    zco_ref[2:3, :] = s_sum[0:1] * coupling
    zs_ref[...] = jnp.transpose(st_ref[...])[: NF * NLAT, :]
    zr_ref[...] = jnp.transpose(rt_ref[...] * coupling)[: NF * NLAT, :]


def merid_coefs(floats_ref, ms_ref, mr_ref, mss_ref, mrr_ref, mco_ref, miw_ref, north, zero):
    one = zero + 1.0
    for field in range(NF):
        at = MW_AT + field * NLAT
        miw_ref[field] = 1.0 / floats_ref[at : at + NLAT, :]
    mco_ref[...] = jnp.zeros((NF, 8, LANES), F32)
    for field in range(NF):
        s_val, s_flux, s_sum = zero, one, zero
        for row in range(NLAT):
            ms_ref[field, row : row + 1, :] = s_val[0:1]
            s_sum = s_sum + s_val
            s_val = s_val + s_flux * miw_ref[field, row : row + 1, :]
            s_flux = s_flux + s_val
        r_val = jnp.where(north > 0.5, 1.0, miw_ref[field, NLAT - 1 : NLAT, :] + zero)
        r_flux = jnp.where(north > 0.5, 0.0, one)
        r_sum = zero
        mr_ref[field, NLAT - 1 : NLAT, :] = r_val[0:1]
        for row in range(NLAT - 2, -1, -1):
            r_sum = r_sum + r_val
            r_flux = r_flux + r_val
            r_val = r_val + r_flux * miw_ref[field, row : row + 1, :]
            mr_ref[field, row : row + 1, :] = r_val[0:1]
        inverse = 1.0 / r_val[0:1]
        coupling = jnp.where(north[0:1] > 0.5, 0.0, inverse)
        mr_ref[field] = mr_ref[field] * inverse
        sum_rr, sum_rs = zero, zero
        for row in range(NLAT - 1, -1, -1):
            at = slice(row, row + 1)
            s_row, r_row = ms_ref[field, at, :], mr_ref[field, at, :]
            mrr_ref[field, at, :] = s_row * sum_rr[0:1]
            mss_ref[field, at, :] = s_row * sum_rs[0:1]
            sum_rr = sum_rr + r_row * r_row
            sum_rs = sum_rs + r_row * s_row
        sum_sr, sum_ss = zero, zero
        for row in range(NLAT):
            at = slice(row, row + 1)
            s_row, r_row = ms_ref[field, at, :], mr_ref[field, at, :]
            sum_sr = sum_sr + s_row * r_row
            sum_ss = sum_ss + s_row * s_row
            mrr_ref[field, at, :] = mrr_ref[field, at, :] + r_row * sum_sr[0:1]
            mss_ref[field, at, :] = mss_ref[field, at, :] + r_row * sum_ss[0:1]
        mco_ref[field, 0:1, :] = coupling
        mco_ref[field, 1:2, :] = r_sum[0:1] * inverse
        mco_ref[field, 2:3, :] = s_sum[0:1] * coupling
        mco_ref[field, 3:4, :] = sum_rr[0:1]
        mco_ref[field, 4:5, :] = sum_rs[0:1] * coupling
        mco_ref[field, 5:6, :] = sum_ss[0:1] * coupling * coupling


def zonal_factor(zco_all, alpha, gamma, minv):
    coupling = zco_all[:, 0, :]
    west = jnp.concatenate([coupling[-1:], coupling[:-1]], axis=0)
    spill = zco_all[:, 2, :]
    mass = 1.0 + zco_all[:, 1, :] + jnp.concatenate([spill[-1:], spill[:-1]], axis=0)
    east = coupling
    for bit in range(5):
        stride = 1 << bit
        down = lambda v: jnp.concatenate([v[-stride:], v[:-stride]], axis=0)
        up = lambda v: jnp.concatenate([v[stride:], v[:stride]], axis=0)
        inverse = 1.0 / (mass + west + east)
        left = west * down(inverse)
        right = east * up(inverse)
        for field in range(NF):
            alpha[field, bit] = to_field(left, field)
            gamma[field, bit] = to_field(right, field)
        mass = mass + left * down(mass) + right * up(mass)
        west, east = left * down(west), right * up(east)
    for field in range(NF):
        minv[field] = to_field(1.0 / mass, field)


def to_field(rows, field):
    return rows if field == 0 else pltpu.roll(rows, LANES - field * NLAT, 1)


def gather_lines(table_ref, count, high, low, base):
    def step(row, acc):
        line = jnp.broadcast_to(table_ref[pl.ds(row, 1), :], (ZP, LANES))
        return jnp.where(high == row + base, lane_pick(line, low), acc)

    return lax.fori_loop(0, count, step, jnp.zeros((ZP, LANES), F32), unroll=8)


def two_phase(tile_out, tile_in, rows_out, rows_in, sems):
    me = lax.axis_index("lon")
    my = lax.axis_index("lat")
    s1, r1, s2, r2 = sems
    first = lambda device, slot: push(
        tile_out.at[device], tile_in.at[slot], s1.at[device], r1.at[slot], "lon", device
    )
    second = lambda device, slot: push(
        rows_out.at[device], rows_in.at[slot], s2.at[device], r2.at[slot], "lat", device
    )

    def begin():
        over_lon(lambda device: first(device, me).start())
        tile_in[me] = tile_out[me]

    def middle():
        over_lon(lambda device: first(0, device).wait_recv())
        for lat in range(N_LAT):
            rows_out[lat] = tile_in[:, lat, :]
        over_lat(lambda device: second(device, my).start())
        rows_in[my] = rows_out[my]

    def end():
        over_lat(lambda device: second(0, device).wait_recv())

    def sent():
        over_lon(lambda device: first(device, me).wait_send())
        over_lat(lambda device: second(device, my).wait_send())

    return begin, middle, end, sent


def prepare_kernel(
    ints_ref, floats_ref, north_ref,
    out_ref, zs_ref, zr_ref, zco_out, ms_ref, mr_ref, mss_ref, mrr_ref, mco_out, vert_ref,
    alpha, gamma, minv, sums_ref, row_ref, *rest
):
    grids, rest = rest[:GRIDS], rest[GRIDS:]
    prepare_body(
        ints_ref, floats_ref, north_ref, out_ref, zs_ref, zr_ref, zco_out, ms_ref, mr_ref, mss_ref,
        mrr_ref, mco_out, vert_ref, alpha, gamma, minv, sums_ref, row_ref, grids, *rest,
    )


def prepare_body(
    ints_ref, floats_ref, north_ref,
    out_ref, zs_ref, zr_ref, zco_out, ms_ref, mr_ref, mss_ref, mrr_ref, mco_out, vert_ref,
    alpha, gamma, minv, sums_ref, row_ref, grids,
    iw_ref, st_ref, rt_ref, miw_ref, prod_ref,
    tile_out, tile_in, rows_out, rows_in, zco_ref, zco_all, mco_ref, mco_all,
    o1s, o1r, o2s, o2r, zco_s, zco_r, mco_s, mco_r,
):
    me = lax.axis_index("lon")
    my = lax.axis_index("lat")
    greet()
    index = ints_ref[0:CAP, :]
    picked = gather_lines(floats_ref, CAP, index >> 7, index & 127, 0)
    picked = jnp.transpose(
        jnp.concatenate([picked, jnp.zeros((LANES - CAP, LANES), F32)], axis=0)
    )
    for device in range(N_LON):
        tile_out[device, 0:4, :] = picked[4 * device : 4 * device + 4]
        tile_out[device, 4:8, :] = jnp.zeros((4, LANES), F32)

    begin, middle, end, sent = two_phase(tile_out, tile_in, rows_out, rows_in, (o1s, o1r, o2s, o2r))
    zco_copy = lambda device, slot: push(
        zco_ref, zco_all.at[slot], zco_s.at[device], zco_r.at[slot], "lon", device
    )
    mco_copy = lambda device, slot: push(
        mco_ref, mco_all.at[slot], mco_s.at[device], mco_r.at[slot], "lat", device
    )
    greeted()
    begin()
    zero = north_ref[...] * 0.0
    zonal_coefs(floats_ref, zs_ref, zr_ref, zco_ref, iw_ref, st_ref, rt_ref, zero)
    over_lon(lambda device: zco_copy(device, me).start())
    zco_all[me] = zco_ref[...]
    merid_coefs(floats_ref, ms_ref, mr_ref, mss_ref, mrr_ref, mco_ref, miw_ref, north_ref[...], zero)
    over_lat(lambda device: mco_copy(device, my).start())
    mco_all[my] = mco_ref[...]
    middle()
    for field in range(NF):
        zco_out[field] = to_field(zco_ref[...], field)
    cell = ints_ref[CAP : 2 * CAP, :]
    line = cell >> 7
    plane = line // NLAT
    second_field = (plane >= NZ).astype(jnp.int32)
    live_row = (second_field * NLAT + line - plane * NLAT) * ZP + plane - second_field * NZ
    dead_row = lax.broadcasted_iota(jnp.int32, (CAP, LANES), 0) * ZP + NZ
    row_ref[...] = jnp.where(cell >= 0, live_row, dead_row)
    prod_ref[...] = jnp.zeros((ZP, LANES), F32)
    for field in range(NF):
        matrix = floats_ref[pl.ds(VERT_AT + field, NZ, stride=NF), :]
        prod_ref[:NZ, :NZ] = lax.dot_general(
            matrix, matrix, (((1,), (1,)), ((), ())),
            precision=lax.Precision.HIGHEST, preferred_element_type=F32,
        )
        high, low = split(prod_ref[:, :ZP])
        vert_ref[field] = jnp.concatenate([high, low, high], axis=1)
    source = lax.broadcasted_iota(jnp.int32, (2 * LANES, 2 * LANES), 0) & 127
    target = lax.broadcasted_iota(jnp.int32, (2 * LANES, 2 * LANES), 1)
    sums_ref[...] = jnp.where(source <= target, 1.0, 0.0).astype(BF16)
    def clear(step, _):
        at = pl.ds(pl.multiple_of(step * 64, 64), 64)
        for grid in grids:
            grid[at, :] = jnp.zeros((64, LANES), F32)
        return 0

    lax.fori_loop(0, ROWS // 64, clear, 0)
    end()
    for lat in range(N_LAT):
        out_ref[N_LON * lat : N_LON * lat + N_LON, :] = rows_in[lat]
    over_lon(lambda device: zco_copy(0, device).wait_recv())
    zonal_factor(zco_all, alpha, gamma, minv)
    over_lat(lambda device: mco_copy(0, device).wait_recv())
    mco_out[...] = mco_all[...]
    sent()
    over_lon(lambda device: zco_copy(device, me).wait_send())
    over_lat(lambda device: mco_copy(device, my).wait_send())


def prepare(ints, floats, north):
    shape = lambda *dims: jax.ShapeDtypeStruct(dims, F32)
    vmem = lambda *dims: pltpu.VMEM(dims, F32)
    dma = pltpu.SemaphoreType.DMA
    return pl.pallas_call(
        prepare_kernel,
        out_shape=(
            shape(RANKS, LANES), shape(80, LANES), shape(80, LANES), shape(NF, 8, LANES),
            shape(NF, NLAT, LANES), shape(NF, NLAT, LANES),
            shape(NF, NLAT, LANES), shape(NF, NLAT, LANES), shape(N_LAT, NF, 8, LANES),
            jax.ShapeDtypeStruct((NF, ZP, 3 * ZP), BF16),
            shape(NF, 5, N_LON, LANES), shape(NF, 5, N_LON, LANES), shape(NF, N_LON, LANES),
            jax.ShapeDtypeStruct((2 * LANES, 2 * LANES), BF16),
            jax.ShapeDtypeStruct((CAP, LANES), jnp.int32),
        )
        + (shape(ROWS, LANES),) * GRIDS,
        in_specs=[VMEM_SPEC] * 3,
        out_specs=(VMEM_SPEC,) * (15 + GRIDS),
        scratch_shapes=[
            vmem(LANES, LANES), vmem(LANES, LANES), vmem(LANES, LANES), vmem(NF, NLAT, LANES),
            vmem(ZP, LANES),
            vmem(N_LON, 8, LANES), vmem(N_LON, 8, LANES),
            vmem(N_LAT, N_LON, LANES), vmem(N_LAT, N_LON, LANES),
            vmem(8, LANES), vmem(N_LON, 8, LANES), vmem(NF, 8, LANES), vmem(N_LAT, NF, 8, LANES),
            dma((N_LON,)), dma((N_LON,)), dma((N_LAT,)), dma((N_LAT,)),
            dma((N_LON,)), dma((N_LON,)), dma((N_LAT,)), dma((N_LAT,)),
        ],
        compiler_params=pltpu.CompilerParams(
            collective_id=0, has_side_effects=True, vmem_limit_bytes=6 << 20
        ),
        cost_estimate=cost(15),
        name="prepare",
    )(ints, floats, north)


def scatter_kernel(rows_ref, ints_ref, in_ref, norm_ref, *refs):
    grids = refs[GRIDS : 2 * GRIDS]
    norm_buf, norm_sem, value_ref, even_ref, odd_ref = refs[2 * GRIDS :]

    def norm_copy(field, row):
        return pltpu.make_async_copy(
            norm_ref.at[field, :, row, :],
            norm_buf.at[field, row, pl.ds(0, NZ), :],
            norm_sem.at[field, row],
        )

    def over_rows(action):
        for field in range(NF):

            def body(row, _, field=field):
                action(norm_copy(field, row))
                return 0

            lax.fori_loop(0, NLAT, body, 0)

    over_rows(lambda copy: copy.start())
    value_ref[...] = jnp.transpose(in_ref[...])
    iota = lane_iota(CAP)

    def spread(q):
        index = jnp.full((CAP, LANES), q, jnp.int32)
        place = jnp.full((CAP, LANES), (q % N_LAT) * N_LON + q // N_LAT, jnp.int32)
        lane = lane_pick(ints_ref[CAP : 2 * CAP, :] & 127, index)
        return jnp.where(iota == lane, lane_pick(value_ref[:CAP, :], place), 0.0)

    def add(q, source):
        for k in range(CAP):
            at = pl.ds(rows_ref[k * RANKS + q], 1)
            grid = grids[k % GRIDS]
            grid[at, :] = grid[at, :] + source[k : k + 1, :]

    even_ref[...] = spread(0)

    def senders(pair, _):
        q = 2 * pair
        odd_ref[...] = spread(q + 1)
        add(q, even_ref)
        even_ref[...] = spread(jnp.minimum(q + 2, RANKS - 1))
        add(q + 1, odd_ref)
        return 0

    lax.fori_loop(0, RANKS // 2, senders, 0)
    over_rows(lambda copy: copy.wait())


def scatter(rows, ints, incoming, norm, grids):
    grid = jax.ShapeDtypeStruct((ROWS, LANES), F32)
    return pl.pallas_call(
        scatter_kernel,
        out_shape=(grid,) * GRIDS + (jax.ShapeDtypeStruct((NF, NLAT, ZP, LANES), F32),),
        in_specs=[SMEM_SPEC] + [VMEM_SPEC] * 2 + [ANY_SPEC] + [VMEM_SPEC] * GRIDS,
        out_specs=(VMEM_SPEC,) * (GRIDS + 1),
        input_output_aliases={4 + index: index for index in range(GRIDS)},
        scratch_shapes=[
            pltpu.SemaphoreType.DMA((NF, NLAT)),
            pltpu.VMEM((LANES, LANES), F32), pltpu.VMEM((CAP, LANES), F32), pltpu.VMEM((CAP, LANES), F32),
        ],
        compiler_params=pltpu.CompilerParams(vmem_limit_bytes=6 << 20),
        cost_estimate=cost(12),
        name="scatter",
    )(rows, ints, incoming, norm, *grids)


def solve_kernel(*refs):
    solve_body(refs[:GRIDS], *refs[GRIDS:])


def solve_body(
    grids, norm_ref, ints_ref, zs_ref, zr_ref, zco_ref, ms_ref, mr_ref, mss_ref, mrr_ref, mco_all,
    vert_ref, alpha, gamma, minv, sums_ref,
    x_ref,
    zsend, zrecv, zret, zres, msend, mrecv, mret, mres,
    acc_a, acc_b, ubuf, gbuf, mtot, mbuf,
    z1s, z1r, z2s, z2r, m1s, m1r, m2s, m2r,
):
    me = lax.axis_index("lon")
    my = lax.axis_index("lat")
    iota = lane_iota(ZP)
    half = N_LON // NF
    my_field = me // half
    is_solver = me % half < GROUPS
    nothing = jnp.zeros((ZP, LANES), F32)
    greet()


    def zonal_out(turn, field, group, slot):
        return push(
            zsend.at[turn, field, group], zrecv.at[turn, slot],
            z1s.at[turn, field, group], z1r.at[turn, slot], "lon", field * half + group,
        )

    def zonal_back(turn, device, field, group):
        return push(
            zret.at[turn, device], zres.at[turn, field, group],
            z2s.at[turn, device], z2r.at[turn, field, group], "lon", device,
        )

    def others(field, action):
        for group in range(GROUPS):
            pl.when(me != field * half + group)(lambda group=group: action(group))

    def zonal_pass(turn, field, load):
        def chunk_pass(chunk, _):
            lines, left = [], []
            for step in range(CHUNK):
                row = chunk * CHUNK + step
                at = pl.ds(field * NLAT + row, 1)
                s_row, r_row = zs_ref[at, :], zr_ref[at, :]
                value = load(row)
                for coef in (s_row, r_row):
                    high, low = split(coef * value)
                    left.append(jnp.concatenate([high, low], axis=1))
                lines.append((row, s_row, r_row))
            sums = jnp.dot(
                jnp.concatenate(left, axis=0), sums_ref[...], preferred_element_type=F32
            )
            tot_a, tot_b = acc_a[...], acc_b[field]
            for step, (row, s_row, r_row) in enumerate(lines):
                a_part = sums[2 * step * ZP : (2 * step + 1) * ZP]
                b_part = sums[(2 * step + 1) * ZP : (2 * step + 2) * ZP]
                x_ref[field, row] = r_row * a_part[:, :LANES] - s_row * b_part[:, :LANES]
                mine = iota == row
                tot_a = jnp.where(mine, a_part[:, LANES:], tot_a)
                tot_b = jnp.where(mine, b_part[:, LANES:], tot_b)
            acc_a[...] = tot_a
            acc_b[field] = tot_b
            return 0

        acc_a[...] = nothing
        acc_b[field] = nothing
        lax.fori_loop(0, NLAT // CHUNK, chunk_pass, 0)
        acc_a[...] = acc_b[field] + pltpu.roll(acc_a[...] * zco_ref[field, 0:1, :], HALF, 1)
        for group in range(GROUPS):
            at = slice(GROUP * group, GROUP * group + GROUP)
            zsend[turn, field, group, 0:GROUP, :] = acc_a[at, :]

    def zonal_send(turn, field):
        others(field, lambda group: zonal_out(turn, field, group, me).start())

        @pl.when(is_solver & (my_field == field))
        def _():
            zrecv[turn, me] = zsend[turn, field, me % half]

    def zonal_reduced(turn):
        mine = me % half
        over_lon(lambda device: zonal_out(turn, 0, 0, device).wait_recv())
        right_side = [
            zrecv[turn, k] + pltpu.roll(zrecv[turn, (k - 1) % N_LON], HALF, 1) for k in range(N_LON)
        ]
        for bit in range(5):
            stride = 1 << bit
            right_side = [
                right_side[k]
                + alpha[my_field, bit, k : k + 1, :] * right_side[(k - stride) % N_LON]
                + gamma[my_field, bit, k : k + 1, :] * right_side[(k + stride) % N_LON]
                for k in range(N_LON)
            ]
        values = [right_side[k] * minv[my_field, k : k + 1, :] for k in range(N_LON)]
        for k in range(N_LON):
            zret[turn, k] = jnp.where(
                iota[0:8] < HALF, values[k], pltpu.roll(values[(k + 1) % N_LON], HALF, 1)
            )
        over_lon(lambda device: zonal_back(turn, device, my_field, mine).start())
        zres[turn, my_field, mine] = zret[turn, me]

    def zonal_receive(turn, field):
        others(field, lambda group: zonal_back(turn, 0, field, group).wait_recv())
        ubuf[72:80, :] = jnp.zeros((8, LANES), F32)
        for group in range(GROUPS):
            at = slice(GROUP * group, GROUP * group + GROUP)
            ubuf[at, :] = zres[turn, field, group, 0:GROUP, :]
        gbuf[...] = pltpu.roll(ubuf[...], HALF, 1) * zco_ref[field, 0:1, :] + acc_b[field]

    def zonal_values(field, chunk):
        u_all, g_all = ubuf[...], gbuf[...]
        found = []
        for step in range(CHUNK):
            row = chunk * CHUNK + step
            at = pl.ds(field * NLAT + row, 1)
            found.append(
                x_ref[field, row]
                + zr_ref[at, :] * jnp.broadcast_to(u_all[:, step : step + 1], (ZP, LANES))
                + zs_ref[at, :] * jnp.broadcast_to(g_all[:, step : step + 1], (ZP, LANES))
            )
        ubuf[...] = pltpu.roll(u_all, LANES - CHUNK, 1)
        gbuf[...] = pltpu.roll(g_all, LANES - CHUNK, 1)
        return found


    def vertical(field, value):
        high, low = split(value)
        return jnp.dot(
            vert_ref[field], jnp.concatenate([high, high, low], axis=0), preferred_element_type=F32
        )

    def vertical_field(field):
        def body(step, _):
            row = step * VERT_CHUNK
            value = jnp.concatenate([x_ref[field, row + k] for k in range(VERT_CHUNK)], axis=1)
            value = vertical(field, value)
            for k in range(VERT_CHUNK):
                x_ref[field, row + k] = value[:, k * LANES : (k + 1) * LANES]
            return 0

        lax.fori_loop(0, NLAT // VERT_CHUNK, body, 0)


    def merid_out(field, device, slot):
        return push(
            msend.at[field, device], mrecv.at[field, slot],
            m1s.at[field, device], m1r.at[field, slot], "lat", device,
        )

    def merid_back(field, device, slot):
        return push(
            mret.at[field, device], mres.at[field, slot],
            m2s.at[field, device], m2r.at[field, slot], "lat", device,
        )

    def merid_pass(field):
        def one(chunk, carry):
            tot_a, tot_b = carry
            found = zonal_values(field, chunk)
            for step in range(CHUNK):
                row = chunk * CHUNK + step
                s_row, r_row = ms_ref[field, pl.ds(row, 1), :], mr_ref[field, pl.ds(row, 1), :]
                tot_a = tot_a + s_row * found[step]
                tot_b = tot_b + r_row * found[step]
                x_ref[field, row] = r_row * tot_a - s_row * tot_b
            return tot_a, tot_b

        a_one, b_one = lax.fori_loop(0, NLAT // CHUNK, one, (nothing, nothing))
        ubuf[...] = b_one

        def two(row, carry):
            tot_a, tot_b = carry
            s_row, r_row = ms_ref[field, pl.ds(row, 1), :], mr_ref[field, pl.ds(row, 1), :]
            value = x_ref[field, row] + s_row * ubuf[...]
            tot_a = tot_a + s_row * value
            tot_b = tot_b + r_row * value
            x_ref[field, row] = r_row * tot_a - s_row * tot_b
            return tot_a, tot_b

        a_two, b_two = lax.fori_loop(0, NLAT, two, (nothing, nothing), unroll=4)
        mtot[field] = b_two
        coupling = mco_all[my, field, 0:1, :]
        for part, value in enumerate((b_one, a_one * coupling, b_two, a_two * coupling)):
            for solver in range(N_LAT):
                count = min(SPLIT, ZP - SPLIT * solver)
                msend[field, solver, part, 0:count, :] = value[SPLIT * solver : SPLIT * solver + count]
                if count < SPLIT:
                    msend[field, solver, part, count:SPLIT, :] = jnp.zeros(
                        (SPLIT - count, LANES), F32
                    )
        over_lat(lambda device: merid_out(field, device, my).start())
        mrecv[field, my] = msend[field, my]

    def merid_reduced(field):
        over_lat(lambda device: merid_out(field, 0, device).wait_recv())
        coef = lambda k, row: mco_all[k, field, row : row + 1, :]
        part = lambda k, index: mrecv[field, k, index]

        def solve_four(right_side):
            mass = 1.0 + coef(0, 1)
            reduced = right_side[0]
            kept, inverses, values = [], [], [None] * N_LAT
            for k in range(N_LAT):
                inverse = 1.0 / (mass + coef(k, 0))
                kept.append(reduced)
                inverses.append(inverse)
                if k + 1 < N_LAT:
                    factor = coef(k, 0) * inverse
                    mass = 1.0 + coef(k + 1, 1) + coef(k, 2) + factor * mass
                    reduced = right_side[k + 1] + factor * reduced
            values[-1] = kept[-1] * inverses[-1]
            for k in range(N_LAT - 2, -1, -1):
                values[k] = (kept[k] + coef(k, 0) * values[k + 1]) * inverses[k]
            return values

        none = jnp.zeros((SPLIT, LANES), F32)
        u = solve_four([part(k, 0) + (part(k - 1, 1) if k else none) for k in range(N_LAT)]) + [none]
        second = []
        for k in range(N_LAT):
            value = part(k, 2) + coef(k, 3) * u[k] + coef(k, 4) * u[k + 1]
            if k:
                value = value + part(k - 1, 3) + coef(k - 1, 4) * u[k - 1] + coef(k - 1, 5) * u[k]
            second.append(value)
        v = solve_four(second) + [none]
        for k in range(N_LAT):
            for index, value in enumerate((u[k], u[k + 1], v[k], v[k + 1])):
                mret[field, k, index] = value
        over_lat(lambda device: merid_back(field, device, my).start())
        mres[field, my] = mret[field, my]

    def merid_receive(field):
        over_lat(lambda device: merid_back(field, 0, device).wait_recv())
        for index in range(4):
            for solver in range(N_LAT):
                count = min(SPLIT, ZP - SPLIT * solver)
                mbuf[index, SPLIT * solver : SPLIT * solver + count, :] = mres[
                    field, solver, index, 0:count, :
                ]
        coupling = mco_all[my, field, 0:1, :]
        mbuf[1] = mbuf[1] * coupling
        mbuf[3] = mbuf[3] * coupling + mtot[field]

    def merid_value(field, row):
        at = pl.ds(row, 1)
        return (
            x_ref[field, row]
            + mrr_ref[field, at, :] * mbuf[0]
            + mss_ref[field, at, :] * mbuf[1]
            + mr_ref[field, at, :] * mbuf[2]
            + ms_ref[field, at, :] * mbuf[3]
        )

    level = lax.broadcasted_iota(jnp.int32, (ZP, LANES), 0)

    def scale(field, row):
        wet = level < ints_ref[pl.ds(DEPTH_AT + row, 1), :]
        return jnp.where(wet, norm_ref[field, row], 0.0)

    def scaled_grid(field):
        def load(row):
            at = pl.ds(pl.multiple_of((field * NLAT + row) * ZP, ZP), ZP)
            total = [grid[at, :] for grid in grids]
            while len(total) > 1:
                total = [one + two for one, two in zip(total[::2], total[1::2])]
            return scale(field, row) * total[0]

        return load

    zonal_pass(0, 0, scaled_grid(0))
    greeted()
    zonal_send(0, 0)
    zonal_pass(0, 1, scaled_grid(1))
    zonal_send(0, 1)
    vertical_field(0)
    pl.when(is_solver & (my_field == 0))(lambda: zonal_reduced(0))
    vertical_field(1)
    pl.when(is_solver & (my_field == 1))(lambda: zonal_reduced(0))

    for field in range(NF):
        zonal_receive(0, field)
        both = vertical(field, jnp.concatenate([ubuf[...], gbuf[...]], axis=1))
        ubuf[...] = both[:, :LANES]
        gbuf[...] = both[:, LANES:]
        merid_pass(field)
    for field in range(NF):
        merid_reduced(field)

    for field in range(NF):
        merid_receive(field)
        zonal_pass(1, field, lambda row, field=field: merid_value(field, row))
        zonal_send(1, field)
    pl.when(is_solver)(lambda: zonal_reduced(1))
    for field in range(NF):
        zonal_receive(1, field)

        def last_pass(chunk, _, field=field):
            found = zonal_values(field, chunk)
            for step in range(CHUNK):
                row = chunk * CHUNK + step
                x_ref[field, row] = found[step] * scale(field, row)
            return 0

        lax.fori_loop(0, NLAT // CHUNK, last_pass, 0)

    for field in range(NF):
        over_lat(lambda device, field=field: merid_out(field, device, my).wait_send())
        over_lat(lambda device, field=field: merid_back(field, device, my).wait_send())
        for turn in range(2):
            others(
                field,
                lambda group, turn=turn, field=field: zonal_out(turn, field, group, me).wait_send(),
            )

    @pl.when(is_solver)
    def _():
        for turn in range(2):
            over_lon(lambda device, turn=turn: zonal_back(turn, device, 0, 0).wait_send())


def solve(grids, norm, ints, coefs):
    dma = pltpu.SemaphoreType.DMA
    vmem = lambda *dims: pltpu.VMEM(dims, F32)
    return pl.pallas_call(
        solve_kernel,
        out_shape=jax.ShapeDtypeStruct((NF, NLAT, ZP, LANES), F32),
        in_specs=[VMEM_SPEC] * (15 + GRIDS),
        out_specs=VMEM_SPEC,
        scratch_shapes=[
            vmem(2, NF, GROUPS, 8, LANES), vmem(2, N_LON, 8, LANES),
            vmem(2, N_LON, 8, LANES), vmem(2, NF, GROUPS, 8, LANES),
            vmem(NF, N_LAT, 4, SPLIT, LANES), vmem(NF, N_LAT, 4, SPLIT, LANES),
            vmem(NF, N_LAT, 4, SPLIT, LANES), vmem(NF, N_LAT, 4, SPLIT, LANES),
            vmem(ZP, LANES), vmem(NF, ZP, LANES), vmem(ZP, LANES), vmem(ZP, LANES),
            vmem(NF, ZP, LANES), vmem(4, ZP, LANES),
            dma((2, NF, GROUPS)), dma((2, N_LON)), dma((2, N_LON)), dma((2, NF, GROUPS)),
            dma((NF, N_LAT)), dma((NF, N_LAT)), dma((NF, N_LAT)), dma((NF, N_LAT)),
        ],
        compiler_params=pltpu.CompilerParams(
            collective_id=1, has_side_effects=True, vmem_limit_bytes=10 << 20
        ),
        cost_estimate=cost(40),
        name="solve",
    )(*grids, norm, ints, *coefs)


def pick_kernel(rows_ref, ints_ref, x_ref, out_ref, inc_ref, inc_sem, *copies):
    iota = lane_iota(8)

    def inc_copy(field, row):
        return pltpu.make_async_copy(
            x_ref.at[pl.ds(pl.multiple_of((field * NLAT + row) * ZP, ZP), NZ), :],
            inc_ref.at[field, :, row, :],
            inc_sem.at[field, row],
        )

    def over_rows(action):
        for field in range(NF):

            def body(row, _, field=field):
                action(inc_copy(field, row))
                return 0

            lax.fori_loop(0, NLAT, body, 0)

    over_rows(lambda copy: copy.start())
    group = len(copies)

    def senders(step, acc):
        acc = list(acc)
        for part in range(group):
            q = step * group + part
            for k in range(CAP):
                copies[part][k : k + 1, :] = x_ref[pl.ds(rows_ref[k * RANKS + q], 1), :]
        for part in range(group):
            q = step * group + part
            for tile in range(CAP // 8):
                at = slice(8 * tile, 8 * tile + 8)
                found = lane_pick(
                    copies[part][at, :], ints_ref[CAP + 8 * tile : CAP + 8 * tile + 8, :] & 127
                )
                acc[tile] = jnp.where(iota == q, found, acc[tile])
        return tuple(acc)

    acc = lax.fori_loop(0, RANKS // group, senders, (jnp.zeros((8, LANES), F32),) * (CAP // 8))
    whole = jnp.concatenate(list(acc) + [jnp.zeros((LANES - CAP, LANES), F32)], axis=0)
    whole = jnp.transpose(whole)
    for device in range(N_LON):
        out_ref[device, 0:4, :] = whole[4 * device : 4 * device + 4]
        out_ref[device, 4:8, :] = jnp.zeros((4, LANES), F32)
    over_rows(lambda copy: copy.wait())


def pick(rows, ints, increment):
    return pl.pallas_call(
        pick_kernel,
        out_shape=(
            jax.ShapeDtypeStruct((N_LON, 8, LANES), F32),
            jax.ShapeDtypeStruct((NF, NZ, NLAT, LANES), F32),
        ),
        in_specs=[SMEM_SPEC, VMEM_SPEC, VMEM_SPEC],
        out_specs=(VMEM_SPEC, ANY_SPEC),
        scratch_shapes=[pltpu.SemaphoreType.DMA((NF, NLAT))] + [pltpu.VMEM((CAP, LANES), F32)] * 16,
        compiler_params=pltpu.CompilerParams(vmem_limit_bytes=8 << 20),
        cost_estimate=cost(14),
        name="pick",
    )(rows, ints, increment.reshape(ROWS, LANES))


def place_kernel(
    tile_out, ints_ref, out_ref,
    idx_ref, val_ref, rows_oh, cols_oh, tile_in, rows_out, rows_in, b1s, b1r, b2s, b2r,
):
    greet()
    none = jnp.full((LANES - CAP, LANES), -1, jnp.int32)
    idx_ref[...] = jnp.transpose(jnp.concatenate([ints_ref[0:CAP, :], none], axis=0))
    begin, middle, end, sent = two_phase(tile_out, tile_in, rows_out, rows_in, (b1s, b1r, b2s, b2r))
    row_iota = lax.broadcasted_iota(jnp.int32, (CAP, 2 * LANES), 0)
    col_iota = lax.broadcasted_iota(jnp.int32, (LANES, 2 * LANES), 0)

    def build(step, _):
        lat = step // (N_LON // 2)
        left = (step % (N_LON // 2)) * 2 * N_LAT + lat
        index = jnp.concatenate(
            [idx_ref[pl.ds(left, 1), :], idx_ref[pl.ds(left + N_LAT, 1), :]], axis=1
        )
        rows_oh[step] = jnp.where(row_iota == (index >> 7), 1.0, 0.0).astype(BF16)
        cols_oh[step] = jnp.where(col_iota == (index & 127), 1.0, 0.0).astype(BF16)
        return 0

    def add(step, acc):
        value = jnp.concatenate(
            [val_ref[pl.ds(2 * step, 1), :], val_ref[pl.ds(2 * step + 1, 1), :]], axis=1
        )
        high, low = split(value)
        rows = rows_oh[step]
        return acc + lax.dot_general(
            jnp.concatenate([rows * high, rows * low], axis=0), cols_oh[step],
            (((1,), (1,)), ((), ())), preferred_element_type=F32,
        )

    greeted()
    begin()
    lax.fori_loop(0, RANKS // 4, build, 0, unroll=2)
    middle()
    lax.fori_loop(RANKS // 4, RANKS // 2, build, 0, unroll=2)
    end()
    for lat in range(N_LAT):
        val_ref[N_LON * lat : N_LON * lat + N_LON, :] = rows_in[lat]
    acc = lax.fori_loop(0, RANKS // 2, add, jnp.zeros((2 * CAP, LANES), F32), unroll=8)
    out_ref[...] = acc[:CAP] + acc[CAP:]
    sent()


def place(tiles, ints):
    vmem = lambda *dims: pltpu.VMEM(dims, F32)
    dma = pltpu.SemaphoreType.DMA
    return pl.pallas_call(
        place_kernel,
        out_shape=jax.ShapeDtypeStruct((CAP, LANES), F32),
        in_specs=[VMEM_SPEC] * 2,
        out_specs=VMEM_SPEC,
        scratch_shapes=[
            pltpu.VMEM((RANKS, LANES), jnp.int32), vmem(RANKS, LANES),
            pltpu.VMEM((RANKS // 2, CAP, 2 * LANES), BF16),
            pltpu.VMEM((RANKS // 2, LANES, 2 * LANES), BF16),
            vmem(N_LON, 8, LANES), vmem(N_LAT, N_LON, LANES), vmem(N_LAT, N_LON, LANES),
            dma((N_LON,)), dma((N_LON,)), dma((N_LAT,)), dma((N_LAT,)),
        ],
        compiler_params=pltpu.CompilerParams(
            collective_id=2, has_side_effects=True, vmem_limit_bytes=10 << 20
        ),
        cost_estimate=cost(15),
        name="place",
    )(tiles, ints)


def local(
    obs_value, send_list, recv_cell, column_depth, zonal_weight, merid_weight, vert_inverse, norm_scale
):
    is_north = lax.axis_index("lat") == N_LAT - 1
    north = jnp.full((8, LANES), jnp.where(is_north, 1.0, 0.0), F32)
    ints = jnp.concatenate(
        [jnp.transpose(send_list), jnp.transpose(recv_cell), column_depth], axis=0
    )
    vert = jnp.transpose(vert_inverse, (1, 0, 2)).reshape(NF * NZ, NZ)
    floats = jnp.concatenate(
        [
            obs_value.reshape(CAP, LANES),
            zonal_weight.reshape(NF * NLAT, LANES),
            merid_weight.reshape(NF * NLAT, LANES),
            jnp.pad(vert, ((0, 0), (0, LANES - NZ))),
        ],
        axis=0,
    )
    made = prepare(ints, floats, north)
    incoming, coefs, rows, grids = made[0], made[1:14], made[14].reshape(-1), made[15:]
    *grids, norm = scatter(rows, ints, incoming, norm_scale, grids)
    whole = solve(grids, norm, ints, coefs)
    tiles, increment = pick(rows, ints, whole)
    return increment, place(tiles, ints).reshape(-1)


def solution(mesh):
    in_specs = (
        P(("lon", "lat")),
        P(("lon", "lat"), None),
        P(("lon", "lat"), None),
        P("lat", "lon"),
        P(None, "lat", "lon"),
        P(None, "lat", "lon"),
        P(),
        P(None, None, "lat", "lon"),
    )
    out_specs = (P(None, None, "lat", "lon"), P(("lon", "lat")))
    return jax.shard_map(local, mesh=mesh, in_specs=in_specs, out_specs=out_specs, check_vma=False)
```

```python
import jax
import jax.numpy as jnp
from jax import lax
from jax.experimental import pallas as pl
from jax.experimental.pallas import tpu as pltpu
from jax.sharding import PartitionSpec as P

F32 = jnp.float32
BF16 = jnp.bfloat16
MESH = pl.DeviceIdType.MESH
NF, NZ, NLAT, NLON = 2, 75, 40, 128
ZP = 80
RANKS, CAP = 128, 80
N_LON, N_LAT = 32, 4
GROUPS = 15
GROUP = 5
LANES = 128
CHUNK = 20
HALF = 64
SPLIT = 24
VERT_CHUNK = 10
GRIDS = 8
ROWS = NF * NLAT * ZP
ZW_AT, MW_AT, VERT_AT = 80, 160, 240
DEPTH_AT = 160
VMEM_SPEC = pl.BlockSpec(memory_space=pltpu.VMEM)
SMEM_SPEC = pl.BlockSpec(memory_space=pltpu.SMEM)
ANY_SPEC = pl.BlockSpec(memory_space=pl.ANY)


def cost(micros):
    return pl.CostEstimate(flops=0, bytes_accessed=int(micros * 3.6e6), transcendentals=0)


def lane_iota(rows):
    return lax.broadcasted_iota(jnp.int32, (rows, LANES), 1)


def split(value):
    high = value.astype(BF16)
    return high, (value - high.astype(F32)).astype(BF16)


def lane_pick(table, index):
    return jnp.take_along_axis(table, index, axis=1, mode="promise_in_bounds")


def push(source, target, send_sem, recv_sem, axis, device):
    return pltpu.make_async_remote_copy(
        src_ref=source, dst_ref=target, send_sem=send_sem, recv_sem=recv_sem,
        device_id={axis: device}, device_id_type=MESH,
    )


def over(axis, count, action):
    mine = lax.axis_index(axis)

    def body(step, _):
        action((mine + step) % count)
        return 0

    lax.fori_loop(1, count, body, 0)


def over_lon(action):
    over("lon", N_LON, action)


def over_lat(action):
    over("lat", N_LAT, action)


def greet():
    barrier = pltpu.get_barrier_semaphore()
    over_lon(
        lambda device: pl.semaphore_signal(
            barrier, inc=1, device_id={"lon": device}, device_id_type=MESH
        )
    )
    over_lat(
        lambda device: pl.semaphore_signal(
            barrier, inc=1, device_id={"lat": device}, device_id_type=MESH
        )
    )


def greeted():
    pl.semaphore_wait(pltpu.get_barrier_semaphore(), N_LON - 1 + N_LAT - 1)


def zonal_coefs(floats_ref, zs_ref, zr_ref, zco_ref, iw_ref, st_ref, rt_ref, zero):
    one = zero + 1.0
    iw_ref[...] = jnp.full((LANES, LANES), 1e-3, F32)
    iw_ref[: NF * NLAT, :] = 1.0 / floats_ref[ZW_AT : ZW_AT + NF * NLAT, :]
    iw_ref[...] = jnp.transpose(iw_ref[...])

    def zonal_step(step, carry):
        s_val, s_flux, s_sum, r_val, r_flux, r_sum = carry
        back = LANES - 1 - step
        st_ref[pl.ds(step, 1), :] = s_val[0:1]
        s_sum = s_sum + s_val
        s_val = s_val + s_flux * iw_ref[pl.ds(step, 1), :]
        s_flux = s_flux + s_val
        r_sum = r_sum + r_val
        r_val = r_val + r_flux * iw_ref[pl.ds(back, 1), :]
        rt_ref[pl.ds(back, 1), :] = r_val[0:1]
        r_flux = r_flux + r_val
        return s_val, s_flux, s_sum, r_val, r_flux, r_sum

    _, _, s_sum, r_first, _, r_sum = lax.fori_loop(
        0, LANES, zonal_step, (zero, one, zero, zero, one, zero), unroll=8
    )
    coupling = 1.0 / r_first[0:1]
    zco_ref[...] = jnp.zeros((8, LANES), F32)
    zco_ref[0:1, :] = coupling
    zco_ref[1:2, :] = r_sum[0:1] * coupling
    zco_ref[2:3, :] = s_sum[0:1] * coupling
    zs_ref[...] = jnp.transpose(st_ref[...])[: NF * NLAT, :]
    zr_ref[...] = jnp.transpose(rt_ref[...] * coupling)[: NF * NLAT, :]


def merid_coefs(floats_ref, ms_ref, mr_ref, mss_ref, mrr_ref, mco_ref, miw_ref, north, zero):
    one = zero + 1.0
    for field in range(NF):
        at = MW_AT + field * NLAT
        miw_ref[field] = 1.0 / floats_ref[at : at + NLAT, :]
    mco_ref[...] = jnp.zeros((NF, 8, LANES), F32)
    for field in range(NF):
        s_val, s_flux, s_sum = zero, one, zero
        for row in range(NLAT):
            ms_ref[field, row : row + 1, :] = s_val[0:1]
            s_sum = s_sum + s_val
            s_val = s_val + s_flux * miw_ref[field, row : row + 1, :]
            s_flux = s_flux + s_val
        r_val = jnp.where(north > 0.5, 1.0, miw_ref[field, NLAT - 1 : NLAT, :] + zero)
        r_flux = jnp.where(north > 0.5, 0.0, one)
        r_sum = zero
        mr_ref[field, NLAT - 1 : NLAT, :] = r_val[0:1]
        for row in range(NLAT - 2, -1, -1):
            r_sum = r_sum + r_val
            r_flux = r_flux + r_val
            r_val = r_val + r_flux * miw_ref[field, row : row + 1, :]
            mr_ref[field, row : row + 1, :] = r_val[0:1]
        inverse = 1.0 / r_val[0:1]
        coupling = jnp.where(north[0:1] > 0.5, 0.0, inverse)
        mr_ref[field] = mr_ref[field] * inverse
        sum_rr, sum_rs = zero, zero
        for row in range(NLAT - 1, -1, -1):
            at = slice(row, row + 1)
            s_row, r_row = ms_ref[field, at, :], mr_ref[field, at, :]
            mrr_ref[field, at, :] = s_row * sum_rr[0:1]
            mss_ref[field, at, :] = s_row * sum_rs[0:1]
            sum_rr = sum_rr + r_row * r_row
            sum_rs = sum_rs + r_row * s_row
        sum_sr, sum_ss = zero, zero
        for row in range(NLAT):
            at = slice(row, row + 1)
            s_row, r_row = ms_ref[field, at, :], mr_ref[field, at, :]
            sum_sr = sum_sr + s_row * r_row
            sum_ss = sum_ss + s_row * s_row
            mrr_ref[field, at, :] = mrr_ref[field, at, :] + r_row * sum_sr[0:1]
            mss_ref[field, at, :] = mss_ref[field, at, :] + r_row * sum_ss[0:1]
        mco_ref[field, 0:1, :] = coupling
        mco_ref[field, 1:2, :] = r_sum[0:1] * inverse
        mco_ref[field, 2:3, :] = s_sum[0:1] * coupling
        mco_ref[field, 3:4, :] = sum_rr[0:1]
        mco_ref[field, 4:5, :] = sum_rs[0:1] * coupling
        mco_ref[field, 5:6, :] = sum_ss[0:1] * coupling * coupling


def zonal_factor(zco_all, alpha, gamma, minv):
    coupling = zco_all[:, 0, :]
    west = jnp.concatenate([coupling[-1:], coupling[:-1]], axis=0)
    spill = zco_all[:, 2, :]
    mass = 1.0 + zco_all[:, 1, :] + jnp.concatenate([spill[-1:], spill[:-1]], axis=0)
    east = coupling
    for bit in range(5):
        stride = 1 << bit
        down = lambda v: jnp.concatenate([v[-stride:], v[:-stride]], axis=0)
        up = lambda v: jnp.concatenate([v[stride:], v[:stride]], axis=0)
        inverse = 1.0 / (mass + west + east)
        left = west * down(inverse)
        right = east * up(inverse)
        for field in range(NF):
            alpha[field, bit] = to_field(left, field)
            gamma[field, bit] = to_field(right, field)
        mass = mass + left * down(mass) + right * up(mass)
        west, east = left * down(west), right * up(east)
    for field in range(NF):
        minv[field] = to_field(1.0 / mass, field)


def to_field(rows, field):
    return rows if field == 0 else pltpu.roll(rows, LANES - field * NLAT, 1)


def gather_lines(table_ref, count, high, low, beside):
    def step(row, acc):
        beside(row)
        line = jnp.broadcast_to(table_ref[pl.ds(row, 1), :], (ZP, LANES))
        return jnp.where(high == row, lane_pick(line, low), acc)

    return lax.fori_loop(0, count, step, jnp.zeros((ZP, LANES), F32), unroll=8)


def two_phase(tile_out, tile_in, rows_out, rows_in, sems):
    me = lax.axis_index("lon")
    my = lax.axis_index("lat")
    s1, r1, s2, r2 = sems
    first = lambda device, slot: push(
        tile_out.at[device], tile_in.at[slot], s1.at[device], r1.at[slot], "lon", device
    )
    second = lambda device, slot: push(
        rows_out.at[device], rows_in.at[slot], s2.at[device], r2.at[slot], "lat", device
    )

    def begin():
        over_lon(lambda device: first(device, me).start())
        tile_in[me] = tile_out[me]

    def middle():
        over_lon(lambda device: first(0, device).wait_recv())
        for lat in range(N_LAT):
            rows_out[lat] = tile_in[:, lat, :]
        over_lat(lambda device: second(device, my).start())
        rows_in[my] = rows_out[my]

    def end():
        over_lat(lambda device: second(0, device).wait_recv())

    def sent():
        over_lon(lambda device: first(device, me).wait_send())
        over_lat(lambda device: second(device, my).wait_send())

    return begin, middle, end, sent


def prepare_kernel(
    ints_ref, floats_ref, north_ref, norm_ref,
    out_ref, zs_ref, zr_ref, zco_out, ms_ref, mr_ref, mss_ref, mrr_ref, mco_out, vert_ref,
    alpha, gamma, minv, sums_ref, row_ref, norm_buf, *rest
):
    grids, rest = rest[:GRIDS], rest[GRIDS:]
    prepare_body(
        ints_ref, floats_ref, north_ref, norm_ref, out_ref, zs_ref, zr_ref, zco_out, ms_ref, mr_ref, mss_ref,
        mrr_ref, mco_out, vert_ref, alpha, gamma, minv, sums_ref, row_ref, norm_buf,
        grids, *rest,
    )


def prepare_body(
    ints_ref, floats_ref, north_ref, norm_ref,
    out_ref, zs_ref, zr_ref, zco_out, ms_ref, mr_ref, mss_ref, mrr_ref, mco_out, vert_ref,
    alpha, gamma, minv, sums_ref, row_ref, norm_buf, grids,
    iw_ref, st_ref, rt_ref, miw_ref, prod_ref,
    tile_out, tile_in, rows_out, rows_in, zco_ref, zco_all, mco_ref, mco_all,
    o1s, o1r, o2s, o2r, zco_s, zco_r, mco_s, mco_r, norm_sem,
):
    me = lax.axis_index("lon")
    my = lax.axis_index("lat")
    greet()
    index = ints_ref[0:CAP, :]

    def norm_copy(line):
        field, row = line // NLAT, line % NLAT
        pltpu.make_async_copy(
            norm_ref.at[field, :, row, :], norm_buf.at[field, row, pl.ds(0, NZ), :], norm_sem
        ).start()

    picked = gather_lines(floats_ref, CAP, index >> 7, index & 127, norm_copy)
    picked = jnp.transpose(
        jnp.concatenate([picked, jnp.zeros((LANES - CAP, LANES), F32)], axis=0)
    )
    for device in range(N_LON):
        tile_out[device, 0:4, :] = picked[4 * device : 4 * device + 4]
        tile_out[device, 4:8, :] = jnp.zeros((4, LANES), F32)

    begin, middle, end, sent = two_phase(tile_out, tile_in, rows_out, rows_in, (o1s, o1r, o2s, o2r))
    zco_copy = lambda device, slot: push(
        zco_ref, zco_all.at[slot], zco_s.at[device], zco_r.at[slot], "lon", device
    )
    mco_copy = lambda device, slot: push(
        mco_ref, mco_all.at[slot], mco_s.at[device], mco_r.at[slot], "lat", device
    )
    greeted()
    begin()
    zero = north_ref[...] * 0.0
    zonal_coefs(floats_ref, zs_ref, zr_ref, zco_ref, iw_ref, st_ref, rt_ref, zero)
    over_lon(lambda device: zco_copy(device, me).start())
    zco_all[me] = zco_ref[...]
    merid_coefs(floats_ref, ms_ref, mr_ref, mss_ref, mrr_ref, mco_ref, miw_ref, north_ref[...], zero)
    over_lat(lambda device: mco_copy(device, my).start())
    mco_all[my] = mco_ref[...]
    middle()
    for field in range(NF):
        zco_out[field] = to_field(zco_ref[...], field)
    cell = ints_ref[CAP : 2 * CAP, :]
    line = cell >> 7
    plane = line // NLAT
    second_field = (plane >= NZ).astype(jnp.int32)
    live_row = (second_field * NLAT + line - plane * NLAT) * ZP + plane - second_field * NZ
    dead_row = lax.broadcasted_iota(jnp.int32, (CAP, LANES), 0) * ZP + NZ
    row_ref[...] = jnp.where(cell >= 0, live_row, dead_row)
    prod_ref[...] = jnp.zeros((ZP, LANES), F32)
    for field in range(NF):
        matrix = floats_ref[pl.ds(VERT_AT + field, NZ, stride=NF), :]
        prod_ref[:NZ, :NZ] = lax.dot_general(
            matrix, matrix, (((1,), (1,)), ((), ())),
            precision=lax.Precision.HIGHEST, preferred_element_type=F32,
        )
        high, low = split(prod_ref[:, :ZP])
        vert_ref[field] = jnp.concatenate([high, low, high], axis=1)
    source = lax.broadcasted_iota(jnp.int32, (2 * LANES, 2 * LANES), 0) & 127
    target = lax.broadcasted_iota(jnp.int32, (2 * LANES, 2 * LANES), 1)
    sums_ref[...] = jnp.where(source <= target, 1.0, 0.0).astype(BF16)
    def clear(step, _):
        at = pl.ds(pl.multiple_of(step * 64, 64), 64)
        for grid in grids:
            grid[at, :] = jnp.zeros((64, LANES), F32)
        return 0

    lax.fori_loop(0, ROWS // 64, clear, 0)
    end()
    for lat in range(N_LAT):
        out_ref[N_LON * lat : N_LON * lat + N_LON, :] = rows_in[lat]
    over_lon(lambda device: zco_copy(0, device).wait_recv())
    zonal_factor(zco_all, alpha, gamma, minv)
    over_lat(lambda device: mco_copy(0, device).wait_recv())
    mco_out[...] = mco_all[...]
    whole = norm_buf.at[:, :, pl.ds(0, NZ), :]
    pltpu.make_async_copy(whole, whole, norm_sem).wait()
    sent()
    over_lon(lambda device: zco_copy(device, me).wait_send())
    over_lat(lambda device: mco_copy(device, my).wait_send())


def prepare(ints, floats, north, norm):
    shape = lambda *dims: jax.ShapeDtypeStruct(dims, F32)
    vmem = lambda *dims: pltpu.VMEM(dims, F32)
    dma = pltpu.SemaphoreType.DMA
    return pl.pallas_call(
        prepare_kernel,
        out_shape=(
            shape(RANKS, LANES), shape(80, LANES), shape(80, LANES), shape(NF, 8, LANES),
            shape(NF, NLAT, LANES), shape(NF, NLAT, LANES),
            shape(NF, NLAT, LANES), shape(NF, NLAT, LANES), shape(N_LAT, NF, 8, LANES),
            jax.ShapeDtypeStruct((NF, ZP, 3 * ZP), BF16),
            shape(NF, 5, N_LON, LANES), shape(NF, 5, N_LON, LANES), shape(NF, N_LON, LANES),
            jax.ShapeDtypeStruct((2 * LANES, 2 * LANES), BF16),
            jax.ShapeDtypeStruct((CAP, LANES), jnp.int32),
            shape(NF, NLAT, ZP, LANES),
        )
        + (shape(ROWS, LANES),) * GRIDS,
        in_specs=[VMEM_SPEC] * 3 + [ANY_SPEC],
        out_specs=(VMEM_SPEC,) * (16 + GRIDS),
        scratch_shapes=[
            vmem(LANES, LANES), vmem(LANES, LANES), vmem(LANES, LANES), vmem(NF, NLAT, LANES),
            vmem(ZP, LANES),
            vmem(N_LON, 8, LANES), vmem(N_LON, 8, LANES),
            vmem(N_LAT, N_LON, LANES), vmem(N_LAT, N_LON, LANES),
            vmem(8, LANES), vmem(N_LON, 8, LANES), vmem(NF, 8, LANES), vmem(N_LAT, NF, 8, LANES),
            dma((N_LON,)), dma((N_LON,)), dma((N_LAT,)), dma((N_LAT,)),
            dma((N_LON,)), dma((N_LON,)), dma((N_LAT,)), dma((N_LAT,)), dma,
        ],
        compiler_params=pltpu.CompilerParams(
            collective_id=0, has_side_effects=True, vmem_limit_bytes=6 << 20
        ),
        cost_estimate=cost(15),
        name="prepare",
    )(ints, floats, north, norm)


def scatter_kernel(rows_ref, ints_ref, in_ref, *refs):
    grids = refs[GRIDS : 2 * GRIDS]
    value_ref, even_ref, odd_ref = refs[2 * GRIDS :]
    value_ref[...] = jnp.transpose(in_ref[...])
    iota = lane_iota(CAP)

    def spread(q):
        index = jnp.full((CAP, LANES), q, jnp.int32)
        place = jnp.full((CAP, LANES), (q % N_LAT) * N_LON + q // N_LAT, jnp.int32)
        lane = lane_pick(ints_ref[CAP : 2 * CAP, :] & 127, index)
        return jnp.where(iota == lane, lane_pick(value_ref[:CAP, :], place), 0.0)

    def add(q, source):
        for k in range(CAP):
            at = pl.ds(rows_ref[k * RANKS + q], 1)
            grid = grids[k % GRIDS]
            grid[at, :] = grid[at, :] + source[k : k + 1, :]

    even_ref[...] = spread(0)

    def senders(pair, _):
        q = 2 * pair
        odd_ref[...] = spread(q + 1)
        add(q, even_ref)
        even_ref[...] = spread(jnp.minimum(q + 2, RANKS - 1))
        add(q + 1, odd_ref)
        return 0

    lax.fori_loop(0, RANKS // 2, senders, 0)


def scatter(rows, ints, incoming, grids):
    grid = jax.ShapeDtypeStruct((ROWS, LANES), F32)
    return pl.pallas_call(
        scatter_kernel,
        out_shape=(grid,) * GRIDS,
        in_specs=[SMEM_SPEC] + [VMEM_SPEC] * (2 + GRIDS),
        out_specs=(VMEM_SPEC,) * GRIDS,
        input_output_aliases={3 + index: index for index in range(GRIDS)},
        scratch_shapes=[
            pltpu.VMEM((LANES, LANES), F32), pltpu.VMEM((CAP, LANES), F32), pltpu.VMEM((CAP, LANES), F32),
        ],
        compiler_params=pltpu.CompilerParams(vmem_limit_bytes=6 << 20),
        cost_estimate=cost(12),
        name="scatter",
    )(rows, ints, incoming, *grids)


def solve_kernel(*refs):
    solve_body(refs[:GRIDS], *refs[GRIDS:])


def solve_body(
    grids, norm_ref, ints_ref, zs_ref, zr_ref, zco_ref, ms_ref, mr_ref, mss_ref, mrr_ref, mco_all,
    vert_ref, alpha, gamma, minv, sums_ref,
    x_ref,
    zsend, zrecv, zret, zres, msend, mrecv, mret, mres,
    acc_a, acc_b, ubuf, gbuf, mtot, mbuf,
    z1s, z1r, z2s, z2r, m1s, m1r, m2s, m2r,
):
    me = lax.axis_index("lon")
    my = lax.axis_index("lat")
    iota = lane_iota(ZP)
    half = N_LON // NF
    my_field = me // half
    is_solver = me % half < GROUPS
    nothing = jnp.zeros((ZP, LANES), F32)
    greet()


    def zonal_out(turn, field, group, slot):
        return push(
            zsend.at[turn, field, group], zrecv.at[turn, slot],
            z1s.at[turn, field, group], z1r.at[turn, slot], "lon", field * half + group,
        )

    def zonal_back(turn, device, field, group):
        return push(
            zret.at[turn, device], zres.at[turn, field, group],
            z2s.at[turn, device], z2r.at[turn, field, group], "lon", device,
        )

    def others(field, action):
        for group in range(GROUPS):
            pl.when(me != field * half + group)(lambda group=group: action(group))

    def zonal_pass(turn, field, load):
        def chunk_pass(chunk, _):
            lines, left = [], []
            for step in range(CHUNK):
                row = chunk * CHUNK + step
                at = pl.ds(field * NLAT + row, 1)
                s_row, r_row = zs_ref[at, :], zr_ref[at, :]
                value = load(row)
                for coef in (s_row, r_row):
                    high, low = split(coef * value)
                    left.append(jnp.concatenate([high, low], axis=1))
                lines.append((row, s_row, r_row))
            sums = jnp.dot(
                jnp.concatenate(left, axis=0), sums_ref[...], preferred_element_type=F32
            )
            tot_a, tot_b = acc_a[...], acc_b[field]
            for step, (row, s_row, r_row) in enumerate(lines):
                a_part = sums[2 * step * ZP : (2 * step + 1) * ZP]
                b_part = sums[(2 * step + 1) * ZP : (2 * step + 2) * ZP]
                x_ref[field, row] = r_row * a_part[:, :LANES] - s_row * b_part[:, :LANES]
                mine = iota == row
                tot_a = jnp.where(mine, a_part[:, LANES:], tot_a)
                tot_b = jnp.where(mine, b_part[:, LANES:], tot_b)
            acc_a[...] = tot_a
            acc_b[field] = tot_b
            return 0

        acc_a[...] = nothing
        acc_b[field] = nothing
        lax.fori_loop(0, NLAT // CHUNK, chunk_pass, 0)
        acc_a[...] = acc_b[field] + pltpu.roll(acc_a[...] * zco_ref[field, 0:1, :], HALF, 1)
        for group in range(GROUPS):
            at = slice(GROUP * group, GROUP * group + GROUP)
            zsend[turn, field, group, 0:GROUP, :] = acc_a[at, :]

    def zonal_send(turn, field):
        others(field, lambda group: zonal_out(turn, field, group, me).start())

        @pl.when(is_solver & (my_field == field))
        def _():
            zrecv[turn, me] = zsend[turn, field, me % half]

    def zonal_reduced(turn):
        mine = me % half
        over_lon(lambda device: zonal_out(turn, 0, 0, device).wait_recv())
        right_side = [
            zrecv[turn, k] + pltpu.roll(zrecv[turn, (k - 1) % N_LON], HALF, 1) for k in range(N_LON)
        ]
        for bit in range(5):
            stride = 1 << bit
            right_side = [
                right_side[k]
                + alpha[my_field, bit, k : k + 1, :] * right_side[(k - stride) % N_LON]
                + gamma[my_field, bit, k : k + 1, :] * right_side[(k + stride) % N_LON]
                for k in range(N_LON)
            ]
        values = [right_side[k] * minv[my_field, k : k + 1, :] for k in range(N_LON)]
        for k in range(N_LON):
            zret[turn, k] = jnp.where(
                iota[0:8] < HALF, values[k], pltpu.roll(values[(k + 1) % N_LON], HALF, 1)
            )
        over_lon(lambda device: zonal_back(turn, device, my_field, mine).start())
        zres[turn, my_field, mine] = zret[turn, me]

    def zonal_receive(turn, field):
        others(field, lambda group: zonal_back(turn, 0, field, group).wait_recv())
        ubuf[72:80, :] = jnp.zeros((8, LANES), F32)
        for group in range(GROUPS):
            at = slice(GROUP * group, GROUP * group + GROUP)
            ubuf[at, :] = zres[turn, field, group, 0:GROUP, :]
        gbuf[...] = pltpu.roll(ubuf[...], HALF, 1) * zco_ref[field, 0:1, :] + acc_b[field]

    def zonal_values(field, chunk):
        u_all, g_all = ubuf[...], gbuf[...]
        found = []
        for step in range(CHUNK):
            row = chunk * CHUNK + step
            at = pl.ds(field * NLAT + row, 1)
            found.append(
                x_ref[field, row]
                + zr_ref[at, :] * jnp.broadcast_to(u_all[:, step : step + 1], (ZP, LANES))
                + zs_ref[at, :] * jnp.broadcast_to(g_all[:, step : step + 1], (ZP, LANES))
            )
        ubuf[...] = pltpu.roll(u_all, LANES - CHUNK, 1)
        gbuf[...] = pltpu.roll(g_all, LANES - CHUNK, 1)
        return found


    def vertical(field, value):
        high, low = split(value)
        return jnp.dot(
            vert_ref[field], jnp.concatenate([high, high, low], axis=0), preferred_element_type=F32
        )

    def vertical_field(field):
        def body(step, _):
            row = step * VERT_CHUNK
            value = jnp.concatenate([x_ref[field, row + k] for k in range(VERT_CHUNK)], axis=1)
            value = vertical(field, value)
            for k in range(VERT_CHUNK):
                x_ref[field, row + k] = value[:, k * LANES : (k + 1) * LANES]
            return 0

        lax.fori_loop(0, NLAT // VERT_CHUNK, body, 0)


    def merid_out(field, device, slot):
        return push(
            msend.at[field, device], mrecv.at[field, slot],
            m1s.at[field, device], m1r.at[field, slot], "lat", device,
        )

    def merid_back(field, device, slot):
        return push(
            mret.at[field, device], mres.at[field, slot],
            m2s.at[field, device], m2r.at[field, slot], "lat", device,
        )

    def merid_pass(field):
        def one(chunk, carry):
            tot_a, tot_b = carry
            found = zonal_values(field, chunk)
            for step in range(CHUNK):
                row = chunk * CHUNK + step
                s_row, r_row = ms_ref[field, pl.ds(row, 1), :], mr_ref[field, pl.ds(row, 1), :]
                tot_a = tot_a + s_row * found[step]
                tot_b = tot_b + r_row * found[step]
                x_ref[field, row] = r_row * tot_a - s_row * tot_b
            return tot_a, tot_b

        a_one, b_one = lax.fori_loop(0, NLAT // CHUNK, one, (nothing, nothing))
        ubuf[...] = b_one

        def two(row, carry):
            tot_a, tot_b = carry
            s_row, r_row = ms_ref[field, pl.ds(row, 1), :], mr_ref[field, pl.ds(row, 1), :]
            value = x_ref[field, row] + s_row * ubuf[...]
            tot_a = tot_a + s_row * value
            tot_b = tot_b + r_row * value
            x_ref[field, row] = r_row * tot_a - s_row * tot_b
            return tot_a, tot_b

        a_two, b_two = lax.fori_loop(0, NLAT, two, (nothing, nothing), unroll=4)
        mtot[field] = b_two
        coupling = mco_all[my, field, 0:1, :]
        for part, value in enumerate((b_one, a_one * coupling, b_two, a_two * coupling)):
            for solver in range(N_LAT):
                count = min(SPLIT, ZP - SPLIT * solver)
                msend[field, solver, part, 0:count, :] = value[SPLIT * solver : SPLIT * solver + count]
                if count < SPLIT:
                    msend[field, solver, part, count:SPLIT, :] = jnp.zeros(
                        (SPLIT - count, LANES), F32
                    )
        over_lat(lambda device: merid_out(field, device, my).start())
        mrecv[field, my] = msend[field, my]

    def merid_reduced(field):
        over_lat(lambda device: merid_out(field, 0, device).wait_recv())
        coef = lambda k, row: mco_all[k, field, row : row + 1, :]
        part = lambda k, index: mrecv[field, k, index]

        def solve_four(right_side):
            mass = 1.0 + coef(0, 1)
            reduced = right_side[0]
            kept, inverses, values = [], [], [None] * N_LAT
            for k in range(N_LAT):
                inverse = 1.0 / (mass + coef(k, 0))
                kept.append(reduced)
                inverses.append(inverse)
                if k + 1 < N_LAT:
                    factor = coef(k, 0) * inverse
                    mass = 1.0 + coef(k + 1, 1) + coef(k, 2) + factor * mass
                    reduced = right_side[k + 1] + factor * reduced
            values[-1] = kept[-1] * inverses[-1]
            for k in range(N_LAT - 2, -1, -1):
                values[k] = (kept[k] + coef(k, 0) * values[k + 1]) * inverses[k]
            return values

        none = jnp.zeros((SPLIT, LANES), F32)
        u = solve_four([part(k, 0) + (part(k - 1, 1) if k else none) for k in range(N_LAT)]) + [none]
        second = []
        for k in range(N_LAT):
            value = part(k, 2) + coef(k, 3) * u[k] + coef(k, 4) * u[k + 1]
            if k:
                value = value + part(k - 1, 3) + coef(k - 1, 4) * u[k - 1] + coef(k - 1, 5) * u[k]
            second.append(value)
        v = solve_four(second) + [none]
        for k in range(N_LAT):
            for index, value in enumerate((u[k], u[k + 1], v[k], v[k + 1])):
                mret[field, k, index] = value
        over_lat(lambda device: merid_back(field, device, my).start())
        mres[field, my] = mret[field, my]

    def merid_receive(field):
        over_lat(lambda device: merid_back(field, 0, device).wait_recv())
        for index in range(4):
            for solver in range(N_LAT):
                count = min(SPLIT, ZP - SPLIT * solver)
                mbuf[index, SPLIT * solver : SPLIT * solver + count, :] = mres[
                    field, solver, index, 0:count, :
                ]
        coupling = mco_all[my, field, 0:1, :]
        mbuf[1] = mbuf[1] * coupling
        mbuf[3] = mbuf[3] * coupling + mtot[field]

    def merid_value(field, row):
        at = pl.ds(row, 1)
        return (
            x_ref[field, row]
            + mrr_ref[field, at, :] * mbuf[0]
            + mss_ref[field, at, :] * mbuf[1]
            + mr_ref[field, at, :] * mbuf[2]
            + ms_ref[field, at, :] * mbuf[3]
        )

    level = lax.broadcasted_iota(jnp.int32, (ZP, LANES), 0)

    def scale(field, row):
        wet = level < ints_ref[pl.ds(DEPTH_AT + row, 1), :]
        return jnp.where(wet, norm_ref[field, row], 0.0)

    def scaled_grid(field):
        def load(row):
            at = pl.ds(pl.multiple_of((field * NLAT + row) * ZP, ZP), ZP)
            total = [grid[at, :] for grid in grids]
            while len(total) > 1:
                total = [one + two for one, two in zip(total[::2], total[1::2])]
            return scale(field, row) * total[0]

        return load

    zonal_pass(0, 0, scaled_grid(0))
    greeted()
    zonal_send(0, 0)
    zonal_pass(0, 1, scaled_grid(1))
    zonal_send(0, 1)
    vertical_field(0)
    pl.when(is_solver & (my_field == 0))(lambda: zonal_reduced(0))
    vertical_field(1)
    pl.when(is_solver & (my_field == 1))(lambda: zonal_reduced(0))

    for field in range(NF):
        zonal_receive(0, field)
        both = vertical(field, jnp.concatenate([ubuf[...], gbuf[...]], axis=1))
        ubuf[...] = both[:, :LANES]
        gbuf[...] = both[:, LANES:]
        merid_pass(field)
    for field in range(NF):
        merid_reduced(field)

    for field in range(NF):
        merid_receive(field)
        zonal_pass(1, field, lambda row, field=field: merid_value(field, row))
        zonal_send(1, field)
    pl.when(is_solver)(lambda: zonal_reduced(1))
    for field in range(NF):
        zonal_receive(1, field)

        def last_pass(chunk, _, field=field):
            found = zonal_values(field, chunk)
            for step in range(CHUNK):
                row = chunk * CHUNK + step
                x_ref[field, row] = found[step] * scale(field, row)
            return 0

        lax.fori_loop(0, NLAT // CHUNK, last_pass, 0)

    for field in range(NF):
        over_lat(lambda device, field=field: merid_out(field, device, my).wait_send())
        over_lat(lambda device, field=field: merid_back(field, device, my).wait_send())
        for turn in range(2):
            others(
                field,
                lambda group, turn=turn, field=field: zonal_out(turn, field, group, me).wait_send(),
            )

    @pl.when(is_solver)
    def _():
        for turn in range(2):
            over_lon(lambda device, turn=turn: zonal_back(turn, device, 0, 0).wait_send())


def solve(grids, norm, ints, coefs):
    dma = pltpu.SemaphoreType.DMA
    vmem = lambda *dims: pltpu.VMEM(dims, F32)
    return pl.pallas_call(
        solve_kernel,
        out_shape=jax.ShapeDtypeStruct((NF, NLAT, ZP, LANES), F32),
        in_specs=[VMEM_SPEC] * (15 + GRIDS),
        out_specs=VMEM_SPEC,
        scratch_shapes=[
            vmem(2, NF, GROUPS, 8, LANES), vmem(2, N_LON, 8, LANES),
            vmem(2, N_LON, 8, LANES), vmem(2, NF, GROUPS, 8, LANES),
            vmem(NF, N_LAT, 4, SPLIT, LANES), vmem(NF, N_LAT, 4, SPLIT, LANES),
            vmem(NF, N_LAT, 4, SPLIT, LANES), vmem(NF, N_LAT, 4, SPLIT, LANES),
            vmem(ZP, LANES), vmem(NF, ZP, LANES), vmem(ZP, LANES), vmem(ZP, LANES),
            vmem(NF, ZP, LANES), vmem(4, ZP, LANES),
            dma((2, NF, GROUPS)), dma((2, N_LON)), dma((2, N_LON)), dma((2, NF, GROUPS)),
            dma((NF, N_LAT)), dma((NF, N_LAT)), dma((NF, N_LAT)), dma((NF, N_LAT)),
        ],
        compiler_params=pltpu.CompilerParams(
            collective_id=1, has_side_effects=True, vmem_limit_bytes=10 << 20
        ),
        cost_estimate=cost(40),
        name="solve",
    )(*grids, norm, ints, *coefs)


def pick_kernel(rows_ref, ints_ref, x_ref, out_ref, inc_ref, inc_sem):
    iota = lane_iota(8)
    group = 16
    for field in range(NF):

        def begin(row, _, field=field):
            at = pl.ds(pl.multiple_of((field * NLAT + row) * ZP, ZP), NZ)
            pltpu.make_async_copy(x_ref.at[at, :], inc_ref.at[field, :, row, :], inc_sem).start()
            return 0

        lax.fori_loop(0, NLAT, begin, 0)

    def senders(step, acc):
        acc = list(acc)
        for part in range(group):
            q = step * group + part
            for tile in range(CAP // 8):
                lines = [
                    x_ref[pl.ds(rows_ref[k * RANKS + q], 1), :] for k in range(8 * tile, 8 * tile + 8)
                ]
                lane = ints_ref[CAP + 8 * tile : CAP + 8 * tile + 8, :] & 127
                found = lane_pick(jnp.concatenate(lines, axis=0), lane)
                acc[tile] = jnp.where(iota == q, found, acc[tile])
        return tuple(acc)

    acc = lax.fori_loop(0, RANKS // group, senders, (jnp.zeros((8, LANES), F32),) * (CAP // 8))
    whole = jnp.concatenate(list(acc) + [jnp.zeros((LANES - CAP, LANES), F32)], axis=0)
    whole = jnp.transpose(whole)
    for device in range(N_LON):
        out_ref[device, 0:4, :] = whole[4 * device : 4 * device + 4]
        out_ref[device, 4:8, :] = jnp.zeros((4, LANES), F32)
    pltpu.make_async_copy(inc_ref, inc_ref, inc_sem).wait()


def pick(rows, ints, increment):
    return pl.pallas_call(
        pick_kernel,
        out_shape=(
            jax.ShapeDtypeStruct((N_LON, 8, LANES), F32),
            jax.ShapeDtypeStruct((NF, NZ, NLAT, LANES), F32),
        ),
        in_specs=[SMEM_SPEC, VMEM_SPEC, VMEM_SPEC],
        out_specs=(VMEM_SPEC, ANY_SPEC),
        scratch_shapes=[pltpu.SemaphoreType.DMA],
        compiler_params=pltpu.CompilerParams(vmem_limit_bytes=8 << 20),
        cost_estimate=cost(14),
        name="pick",
    )(rows, ints, increment.reshape(ROWS, LANES))


def place_kernel(
    tile_out, ints_ref, out_ref,
    idx_ref, val_ref, rows_oh, cols_oh, tile_in, rows_out, rows_in, b1s, b1r, b2s, b2r,
):
    greet()
    none = jnp.full((LANES - CAP, LANES), -1, jnp.int32)
    idx_ref[...] = jnp.transpose(jnp.concatenate([ints_ref[0:CAP, :], none], axis=0))
    begin, middle, end, sent = two_phase(tile_out, tile_in, rows_out, rows_in, (b1s, b1r, b2s, b2r))
    row_iota = lax.broadcasted_iota(jnp.int32, (CAP, 2 * LANES), 0)
    col_iota = lax.broadcasted_iota(jnp.int32, (LANES, 2 * LANES), 0)

    def build(step, _):
        lat = step // (N_LON // 2)
        left = (step % (N_LON // 2)) * 2 * N_LAT + lat
        index = jnp.concatenate(
            [idx_ref[pl.ds(left, 1), :], idx_ref[pl.ds(left + N_LAT, 1), :]], axis=1
        )
        rows_oh[step] = jnp.where(row_iota == (index >> 7), 1.0, 0.0).astype(BF16)
        cols_oh[step] = jnp.where(col_iota == (index & 127), 1.0, 0.0).astype(BF16)
        return 0

    def add(step, acc):
        value = jnp.concatenate(
            [val_ref[pl.ds(2 * step, 1), :], val_ref[pl.ds(2 * step + 1, 1), :]], axis=1
        )
        high, low = split(value)
        rows = rows_oh[step]
        return acc + lax.dot_general(
            jnp.concatenate([rows * high, rows * low], axis=0), cols_oh[step],
            (((1,), (1,)), ((), ())), preferred_element_type=F32,
        )

    greeted()
    begin()
    lax.fori_loop(0, RANKS // 4, build, 0, unroll=2)
    middle()
    lax.fori_loop(RANKS // 4, RANKS // 2, build, 0, unroll=2)
    end()
    for lat in range(N_LAT):
        val_ref[N_LON * lat : N_LON * lat + N_LON, :] = rows_in[lat]
    acc = lax.fori_loop(0, RANKS // 2, add, jnp.zeros((2 * CAP, LANES), F32), unroll=8)
    out_ref[...] = acc[:CAP] + acc[CAP:]
    sent()


def place(tiles, ints):
    vmem = lambda *dims: pltpu.VMEM(dims, F32)
    dma = pltpu.SemaphoreType.DMA
    return pl.pallas_call(
        place_kernel,
        out_shape=jax.ShapeDtypeStruct((CAP, LANES), F32),
        in_specs=[VMEM_SPEC] * 2,
        out_specs=VMEM_SPEC,
        scratch_shapes=[
            pltpu.VMEM((RANKS, LANES), jnp.int32), vmem(RANKS, LANES),
            pltpu.VMEM((RANKS // 2, CAP, 2 * LANES), BF16),
            pltpu.VMEM((RANKS // 2, LANES, 2 * LANES), BF16),
            vmem(N_LON, 8, LANES), vmem(N_LAT, N_LON, LANES), vmem(N_LAT, N_LON, LANES),
            dma((N_LON,)), dma((N_LON,)), dma((N_LAT,)), dma((N_LAT,)),
        ],
        compiler_params=pltpu.CompilerParams(
            collective_id=2, has_side_effects=True, vmem_limit_bytes=10 << 20
        ),
        cost_estimate=cost(15),
        name="place",
    )(tiles, ints)


def local(
    obs_value, send_list, recv_cell, column_depth, zonal_weight, merid_weight, vert_inverse, norm_scale
):
    is_north = lax.axis_index("lat") == N_LAT - 1
    north = jnp.full((8, LANES), jnp.where(is_north, 1.0, 0.0), F32)
    ints = jnp.concatenate(
        [jnp.transpose(send_list), jnp.transpose(recv_cell), column_depth], axis=0
    )
    vert = jnp.transpose(vert_inverse, (1, 0, 2)).reshape(NF * NZ, NZ)
    floats = jnp.concatenate(
        [
            obs_value.reshape(CAP, LANES),
            zonal_weight.reshape(NF * NLAT, LANES),
            merid_weight.reshape(NF * NLAT, LANES),
            jnp.pad(vert, ((0, 0), (0, LANES - NZ))),
        ],
        axis=0,
    )
    made = prepare(ints, floats, north, norm_scale)
    incoming, coefs, rows, norm = made[0], made[1:14], made[14].reshape(-1), made[15]
    grids = scatter(rows, ints, incoming, made[16:])
    whole = solve(grids, norm, ints, coefs)
    tiles, increment = pick(rows, ints, whole)
    return increment, place(tiles, ints).reshape(-1)


def solution(mesh):
    in_specs = (
        P(("lon", "lat")),
        P(("lon", "lat"), None),
        P(("lon", "lat"), None),
        P("lat", "lon"),
        P(None, "lat", "lon"),
        P(None, "lat", "lon"),
        P(),
        P(None, None, "lat", "lon"),
    )
    out_specs = (P(None, None, "lat", "lon"), P(("lon", "lat")))
    return jax.shard_map(local, mesh=mesh, in_specs=in_specs, out_specs=out_specs, check_vma=False)
```

```python
import jax
import jax.numpy as jnp
from jax import lax
from jax.experimental import pallas as pl
from jax.experimental.pallas import tpu as pltpu
from jax.sharding import PartitionSpec as P

F32 = jnp.float32
BF16 = jnp.bfloat16
MESH = pl.DeviceIdType.MESH
NF, NZ, NLAT, NLON = 2, 75, 40, 128
ZP = 80
RANKS, CAP = 128, 80
N_LON, N_LAT = 32, 4
GROUPS = 15
GROUP = 5
LANES = 128
CHUNK = 20
HALF = 64
SPLIT = 24
VERT_CHUNK = 10
GRIDS = 8
ROWS = NF * NLAT * ZP
ZW_AT, MW_AT, VERT_AT = 80, 160, 240
DEPTH_AT = 160
VMEM_SPEC = pl.BlockSpec(memory_space=pltpu.VMEM)
SMEM_SPEC = pl.BlockSpec(memory_space=pltpu.SMEM)
ANY_SPEC = pl.BlockSpec(memory_space=pl.ANY)


def cost(micros):
    return pl.CostEstimate(flops=0, bytes_accessed=int(micros * 3.6e6), transcendentals=0)


def lane_iota(rows):
    return lax.broadcasted_iota(jnp.int32, (rows, LANES), 1)


def split(value):
    high = value.astype(BF16)
    return high, (value - high.astype(F32)).astype(BF16)


def lane_pick(table, index):
    return jnp.take_along_axis(table, index, axis=1, mode="promise_in_bounds")


def push(source, target, send_sem, recv_sem, axis, device):
    return pltpu.make_async_remote_copy(
        src_ref=source, dst_ref=target, send_sem=send_sem, recv_sem=recv_sem,
        device_id={axis: device}, device_id_type=MESH,
    )


def over(axis, count, action):
    mine = lax.axis_index(axis)

    def body(step, _):
        action((mine + step) % count)
        return 0

    lax.fori_loop(1, count, body, 0)


def over_lon(action):
    over("lon", N_LON, action)


def over_lat(action):
    over("lat", N_LAT, action)


def greet():
    barrier = pltpu.get_barrier_semaphore()
    over_lon(
        lambda device: pl.semaphore_signal(
            barrier, inc=1, device_id={"lon": device}, device_id_type=MESH
        )
    )
    over_lat(
        lambda device: pl.semaphore_signal(
            barrier, inc=1, device_id={"lat": device}, device_id_type=MESH
        )
    )


def greeted():
    pl.semaphore_wait(pltpu.get_barrier_semaphore(), N_LON - 1 + N_LAT - 1)


def zonal_coefs(floats_ref, zs_ref, zr_ref, zco_ref, iw_ref, st_ref, rt_ref, zero):
    one = zero + 1.0
    iw_ref[...] = jnp.full((LANES, LANES), 1e-3, F32)
    iw_ref[: NF * NLAT, :] = 1.0 / floats_ref[ZW_AT : ZW_AT + NF * NLAT, :]
    iw_ref[...] = jnp.transpose(iw_ref[...])

    def zonal_step(step, carry):
        s_val, s_flux, s_sum, r_val, r_flux, r_sum = carry
        back = LANES - 1 - step
        st_ref[pl.ds(step, 1), :] = s_val[0:1]
        s_sum = s_sum + s_val
        s_val = s_val + s_flux * iw_ref[pl.ds(step, 1), :]
        s_flux = s_flux + s_val
        r_sum = r_sum + r_val
        r_val = r_val + r_flux * iw_ref[pl.ds(back, 1), :]
        rt_ref[pl.ds(back, 1), :] = r_val[0:1]
        r_flux = r_flux + r_val
        return s_val, s_flux, s_sum, r_val, r_flux, r_sum

    _, _, s_sum, r_first, _, r_sum = lax.fori_loop(
        0, LANES, zonal_step, (zero, one, zero, zero, one, zero), unroll=8
    )
    coupling = 1.0 / r_first[0:1]
    zco_ref[...] = jnp.zeros((8, LANES), F32)
    zco_ref[0:1, :] = coupling
    zco_ref[1:2, :] = r_sum[0:1] * coupling
    zco_ref[2:3, :] = s_sum[0:1] * coupling
    zs_ref[...] = jnp.transpose(st_ref[...])[: NF * NLAT, :]
    zr_ref[...] = jnp.transpose(rt_ref[...] * coupling)[: NF * NLAT, :]


def merid_coefs(floats_ref, ms_ref, mr_ref, mss_ref, mrr_ref, mco_ref, miw_ref, north, zero):
    one = zero + 1.0
    for field in range(NF):
        at = MW_AT + field * NLAT
        miw_ref[field] = 1.0 / floats_ref[at : at + NLAT, :]
    mco_ref[...] = jnp.zeros((NF, 8, LANES), F32)
    for field in range(NF):
        s_val, s_flux, s_sum = zero, one, zero
        for row in range(NLAT):
            ms_ref[field, row : row + 1, :] = s_val[0:1]
            s_sum = s_sum + s_val
            s_val = s_val + s_flux * miw_ref[field, row : row + 1, :]
            s_flux = s_flux + s_val
        r_val = jnp.where(north > 0.5, 1.0, miw_ref[field, NLAT - 1 : NLAT, :] + zero)
        r_flux = jnp.where(north > 0.5, 0.0, one)
        r_sum = zero
        mr_ref[field, NLAT - 1 : NLAT, :] = r_val[0:1]
        for row in range(NLAT - 2, -1, -1):
            r_sum = r_sum + r_val
            r_flux = r_flux + r_val
            r_val = r_val + r_flux * miw_ref[field, row : row + 1, :]
            mr_ref[field, row : row + 1, :] = r_val[0:1]
        inverse = 1.0 / r_val[0:1]
        coupling = jnp.where(north[0:1] > 0.5, 0.0, inverse)
        mr_ref[field] = mr_ref[field] * inverse
        sum_rr, sum_rs = zero, zero
        for row in range(NLAT - 1, -1, -1):
            at = slice(row, row + 1)
            s_row, r_row = ms_ref[field, at, :], mr_ref[field, at, :]
            mrr_ref[field, at, :] = s_row * sum_rr[0:1]
            mss_ref[field, at, :] = s_row * sum_rs[0:1]
            sum_rr = sum_rr + r_row * r_row
            sum_rs = sum_rs + r_row * s_row
        sum_sr, sum_ss = zero, zero
        for row in range(NLAT):
            at = slice(row, row + 1)
            s_row, r_row = ms_ref[field, at, :], mr_ref[field, at, :]
            sum_sr = sum_sr + s_row * r_row
            sum_ss = sum_ss + s_row * s_row
            mrr_ref[field, at, :] = mrr_ref[field, at, :] + r_row * sum_sr[0:1]
            mss_ref[field, at, :] = mss_ref[field, at, :] + r_row * sum_ss[0:1]
        mco_ref[field, 0:1, :] = coupling
        mco_ref[field, 1:2, :] = r_sum[0:1] * inverse
        mco_ref[field, 2:3, :] = s_sum[0:1] * coupling
        mco_ref[field, 3:4, :] = sum_rr[0:1]
        mco_ref[field, 4:5, :] = sum_rs[0:1] * coupling
        mco_ref[field, 5:6, :] = sum_ss[0:1] * coupling * coupling


def zonal_factor(zco_all, alpha, gamma, minv):
    coupling = zco_all[:, 0, :]
    west = jnp.concatenate([coupling[-1:], coupling[:-1]], axis=0)
    spill = zco_all[:, 2, :]
    mass = 1.0 + zco_all[:, 1, :] + jnp.concatenate([spill[-1:], spill[:-1]], axis=0)
    east = coupling
    for bit in range(5):
        stride = 1 << bit
        down = lambda v: jnp.concatenate([v[-stride:], v[:-stride]], axis=0)
        up = lambda v: jnp.concatenate([v[stride:], v[:stride]], axis=0)
        inverse = 1.0 / (mass + west + east)
        left = west * down(inverse)
        right = east * up(inverse)
        for field in range(NF):
            alpha[field, bit] = to_field(left, field)
            gamma[field, bit] = to_field(right, field)
        mass = mass + left * down(mass) + right * up(mass)
        west, east = left * down(west), right * up(east)
    for field in range(NF):
        minv[field] = to_field(1.0 / mass, field)


def to_field(rows, field):
    return rows if field == 0 else pltpu.roll(rows, LANES - field * NLAT, 1)


def gather_lines(table_ref, count, high, low, beside):
    def step(row, acc):
        beside(row)
        line = jnp.broadcast_to(table_ref[pl.ds(row, 1), :], (ZP, LANES))
        return jnp.where(high == row, lane_pick(line, low), acc)

    return lax.fori_loop(0, count, step, jnp.zeros((ZP, LANES), F32), unroll=8)


def two_phase(tile_out, tile_in, rows_out, rows_in, sems):
    me = lax.axis_index("lon")
    my = lax.axis_index("lat")
    s1, r1, s2, r2 = sems
    first = lambda device, slot: push(
        tile_out.at[device], tile_in.at[slot], s1.at[device], r1.at[slot], "lon", device
    )
    second = lambda device, slot: push(
        rows_out.at[device], rows_in.at[slot], s2.at[device], r2.at[slot], "lat", device
    )

    def begin():
        over_lon(lambda device: first(device, me).start())
        tile_in[me] = tile_out[me]

    def middle():
        over_lon(lambda device: first(0, device).wait_recv())
        for lat in range(N_LAT):
            rows_out[lat] = tile_in[:, lat, :]
        over_lat(lambda device: second(device, my).start())
        rows_in[my] = rows_out[my]

    def end():
        over_lat(lambda device: second(0, device).wait_recv())

    def sent():
        over_lon(lambda device: first(device, me).wait_send())
        over_lat(lambda device: second(device, my).wait_send())

    return begin, middle, end, sent


def prepare_kernel(
    ints_ref, floats_ref, north_ref,
    out_ref, zs_ref, zr_ref, zco_out, ms_ref, mr_ref, mss_ref, mrr_ref, mco_out, vert_ref,
    alpha, gamma, minv, sums_ref, row_ref, *rest
):
    grids, rest = rest[:GRIDS], rest[GRIDS:]
    prepare_body(
        ints_ref, floats_ref, north_ref, out_ref, zs_ref, zr_ref, zco_out, ms_ref, mr_ref, mss_ref,
        mrr_ref, mco_out, vert_ref, alpha, gamma, minv, sums_ref, row_ref, grids, *rest,
    )


def prepare_body(
    ints_ref, floats_ref, north_ref,
    out_ref, zs_ref, zr_ref, zco_out, ms_ref, mr_ref, mss_ref, mrr_ref, mco_out, vert_ref,
    alpha, gamma, minv, sums_ref, row_ref, grids,
    iw_ref, st_ref, rt_ref, miw_ref, prod_ref,
    tile_out, tile_in, rows_out, rows_in, zco_ref, zco_all, mco_ref, mco_all,
    o1s, o1r, o2s, o2r, zco_s, zco_r, mco_s, mco_r,
):
    me = lax.axis_index("lon")
    my = lax.axis_index("lat")
    greet()
    index = ints_ref[0:CAP, :]

    def clear(line):
        at = pl.ds(pl.multiple_of(line * ZP, ZP), ZP)
        for grid in grids:
            grid[at, :] = jnp.zeros((ZP, LANES), F32)

    picked = gather_lines(floats_ref, CAP, index >> 7, index & 127, clear)
    picked = jnp.transpose(
        jnp.concatenate([picked, jnp.zeros((LANES - CAP, LANES), F32)], axis=0)
    )
    for device in range(N_LON):
        tile_out[device, 0:4, :] = picked[4 * device : 4 * device + 4]
        tile_out[device, 4:8, :] = jnp.zeros((4, LANES), F32)

    begin, middle, end, sent = two_phase(tile_out, tile_in, rows_out, rows_in, (o1s, o1r, o2s, o2r))
    zco_copy = lambda device, slot: push(
        zco_ref, zco_all.at[slot], zco_s.at[device], zco_r.at[slot], "lon", device
    )
    mco_copy = lambda device, slot: push(
        mco_ref, mco_all.at[slot], mco_s.at[device], mco_r.at[slot], "lat", device
    )
    greeted()
    begin()
    zero = north_ref[...] * 0.0
    zonal_coefs(floats_ref, zs_ref, zr_ref, zco_ref, iw_ref, st_ref, rt_ref, zero)
    over_lon(lambda device: zco_copy(device, me).start())
    zco_all[me] = zco_ref[...]
    merid_coefs(floats_ref, ms_ref, mr_ref, mss_ref, mrr_ref, mco_ref, miw_ref, north_ref[...], zero)
    over_lat(lambda device: mco_copy(device, my).start())
    mco_all[my] = mco_ref[...]
    middle()
    for field in range(NF):
        zco_out[field] = to_field(zco_ref[...], field)
    cell = ints_ref[CAP : 2 * CAP, :]
    line = cell >> 7
    plane = line // NLAT
    second_field = (plane >= NZ).astype(jnp.int32)
    live_row = (second_field * NLAT + line - plane * NLAT) * ZP + plane - second_field * NZ
    dead_row = lax.broadcasted_iota(jnp.int32, (CAP, LANES), 0) * ZP + NZ
    row_ref[...] = jnp.where(cell >= 0, live_row, dead_row)
    prod_ref[...] = jnp.zeros((ZP, LANES), F32)
    for field in range(NF):
        matrix = floats_ref[pl.ds(VERT_AT + field, NZ, stride=NF), :]
        prod_ref[:NZ, :NZ] = lax.dot_general(
            matrix, matrix, (((1,), (1,)), ((), ())),
            precision=lax.Precision.HIGHEST, preferred_element_type=F32,
        )
        high, low = split(prod_ref[:, :ZP])
        vert_ref[field] = jnp.concatenate([high, low, high], axis=1)
    source = lax.broadcasted_iota(jnp.int32, (2 * LANES, 2 * LANES), 0) & 127
    target = lax.broadcasted_iota(jnp.int32, (2 * LANES, 2 * LANES), 1)
    sums_ref[...] = jnp.where(source <= target, 1.0, 0.0).astype(BF16)
    end()
    for lat in range(N_LAT):
        out_ref[N_LON * lat : N_LON * lat + N_LON, :] = rows_in[lat]
    over_lon(lambda device: zco_copy(0, device).wait_recv())
    zonal_factor(zco_all, alpha, gamma, minv)
    over_lat(lambda device: mco_copy(0, device).wait_recv())
    mco_out[...] = mco_all[...]
    sent()
    over_lon(lambda device: zco_copy(device, me).wait_send())
    over_lat(lambda device: mco_copy(device, my).wait_send())


def prepare(ints, floats, north):
    shape = lambda *dims: jax.ShapeDtypeStruct(dims, F32)
    vmem = lambda *dims: pltpu.VMEM(dims, F32)
    dma = pltpu.SemaphoreType.DMA
    return pl.pallas_call(
        prepare_kernel,
        out_shape=(
            shape(RANKS, LANES), shape(80, LANES), shape(80, LANES), shape(NF, 8, LANES),
            shape(NF, NLAT, LANES), shape(NF, NLAT, LANES),
            shape(NF, NLAT, LANES), shape(NF, NLAT, LANES), shape(N_LAT, NF, 8, LANES),
            jax.ShapeDtypeStruct((NF, ZP, 3 * ZP), BF16),
            shape(NF, 5, N_LON, LANES), shape(NF, 5, N_LON, LANES), shape(NF, N_LON, LANES),
            jax.ShapeDtypeStruct((2 * LANES, 2 * LANES), BF16),
            jax.ShapeDtypeStruct((CAP, LANES), jnp.int32),
        )
        + (shape(ROWS, LANES),) * GRIDS,
        in_specs=[VMEM_SPEC] * 3,
        out_specs=(VMEM_SPEC,) * (15 + GRIDS),
        scratch_shapes=[
            vmem(LANES, LANES), vmem(LANES, LANES), vmem(LANES, LANES), vmem(NF, NLAT, LANES),
            vmem(ZP, LANES),
            vmem(N_LON, 8, LANES), vmem(N_LON, 8, LANES),
            vmem(N_LAT, N_LON, LANES), vmem(N_LAT, N_LON, LANES),
            vmem(8, LANES), vmem(N_LON, 8, LANES), vmem(NF, 8, LANES), vmem(N_LAT, NF, 8, LANES),
            dma((N_LON,)), dma((N_LON,)), dma((N_LAT,)), dma((N_LAT,)),
            dma((N_LON,)), dma((N_LON,)), dma((N_LAT,)), dma((N_LAT,)),
        ],
        compiler_params=pltpu.CompilerParams(
            collective_id=0, has_side_effects=True, vmem_limit_bytes=6 << 20
        ),
        cost_estimate=cost(15),
        name="prepare",
    )(ints, floats, north)


def scatter_kernel(rows_ref, ints_ref, in_ref, *refs):
    grids = refs[GRIDS : 2 * GRIDS]
    value_ref, even_ref, odd_ref = refs[2 * GRIDS :]
    value_ref[...] = jnp.transpose(in_ref[...])
    iota = lane_iota(CAP)

    def spread(q):
        index = jnp.full((CAP, LANES), q, jnp.int32)
        place = jnp.full((CAP, LANES), (q % N_LAT) * N_LON + q // N_LAT, jnp.int32)
        lane = lane_pick(ints_ref[CAP : 2 * CAP, :] & 127, index)
        return jnp.where(iota == lane, lane_pick(value_ref[:CAP, :], place), 0.0)

    def add(q, source):
        for k in range(CAP):
            at = pl.ds(rows_ref[k * RANKS + q], 1)
            grid = grids[k % GRIDS]
            grid[at, :] = grid[at, :] + source[k : k + 1, :]

    even_ref[...] = spread(0)

    def senders(pair, _):
        q = 2 * pair
        odd_ref[...] = spread(q + 1)
        add(q, even_ref)
        even_ref[...] = spread(jnp.minimum(q + 2, RANKS - 1))
        add(q + 1, odd_ref)
        return 0

    lax.fori_loop(0, RANKS // 2, senders, 0)


def scatter(rows, ints, incoming, grids):
    grid = jax.ShapeDtypeStruct((ROWS, LANES), F32)
    return pl.pallas_call(
        scatter_kernel,
        out_shape=(grid,) * GRIDS,
        in_specs=[SMEM_SPEC] + [VMEM_SPEC] * (2 + GRIDS),
        out_specs=(VMEM_SPEC,) * GRIDS,
        input_output_aliases={3 + index: index for index in range(GRIDS)},
        scratch_shapes=[
            pltpu.VMEM((LANES, LANES), F32), pltpu.VMEM((CAP, LANES), F32), pltpu.VMEM((CAP, LANES), F32),
        ],
        compiler_params=pltpu.CompilerParams(vmem_limit_bytes=6 << 20),
        cost_estimate=cost(12),
        name="scatter",
    )(rows, ints, incoming, *grids)


def solve_kernel(*refs):
    solve_body(refs[:GRIDS], *refs[GRIDS:])


def solve_body(
    grids, norm_ref, ints_ref, zs_ref, zr_ref, zco_ref, ms_ref, mr_ref, mss_ref, mrr_ref, mco_all,
    vert_ref, alpha, gamma, minv, sums_ref,
    x_ref,
    zsend, zrecv, zret, zres, msend, mrecv, mret, mres,
    acc_a, acc_b, ubuf, gbuf, mtot, mbuf,
    z1s, z1r, z2s, z2r, m1s, m1r, m2s, m2r,
):
    me = lax.axis_index("lon")
    my = lax.axis_index("lat")
    iota = lane_iota(ZP)
    half = N_LON // NF
    my_field = me // half
    is_solver = me % half < GROUPS
    nothing = jnp.zeros((ZP, LANES), F32)
    greet()


    def zonal_out(turn, field, group, slot):
        return push(
            zsend.at[turn, field, group], zrecv.at[turn, slot],
            z1s.at[turn, field, group], z1r.at[turn, slot], "lon", field * half + group,
        )

    def zonal_back(turn, device, field, group):
        return push(
            zret.at[turn, device], zres.at[turn, field, group],
            z2s.at[turn, device], z2r.at[turn, field, group], "lon", device,
        )

    def others(field, action):
        for group in range(GROUPS):
            pl.when(me != field * half + group)(lambda group=group: action(group))

    def zonal_pass(turn, field, load):
        def chunk_pass(chunk, _):
            lines, left = [], []
            for step in range(CHUNK):
                row = chunk * CHUNK + step
                at = pl.ds(field * NLAT + row, 1)
                s_row, r_row = zs_ref[at, :], zr_ref[at, :]
                value = load(row)
                for coef in (s_row, r_row):
                    high, low = split(coef * value)
                    left.append(jnp.concatenate([high, low], axis=1))
                lines.append((row, s_row, r_row))
            sums = jnp.dot(
                jnp.concatenate(left, axis=0), sums_ref[...], preferred_element_type=F32
            )
            tot_a, tot_b = acc_a[...], acc_b[field]
            for step, (row, s_row, r_row) in enumerate(lines):
                a_part = sums[2 * step * ZP : (2 * step + 1) * ZP]
                b_part = sums[(2 * step + 1) * ZP : (2 * step + 2) * ZP]
                x_ref[field, row] = r_row * a_part[:, :LANES] - s_row * b_part[:, :LANES]
                mine = iota == row
                tot_a = jnp.where(mine, a_part[:, LANES:], tot_a)
                tot_b = jnp.where(mine, b_part[:, LANES:], tot_b)
            acc_a[...] = tot_a
            acc_b[field] = tot_b
            return 0

        acc_a[...] = nothing
        acc_b[field] = nothing
        lax.fori_loop(0, NLAT // CHUNK, chunk_pass, 0)
        acc_a[...] = acc_b[field] + pltpu.roll(acc_a[...] * zco_ref[field, 0:1, :], HALF, 1)
        for group in range(GROUPS):
            at = slice(GROUP * group, GROUP * group + GROUP)
            zsend[turn, field, group, 0:GROUP, :] = acc_a[at, :]

    def zonal_send(turn, field):
        others(field, lambda group: zonal_out(turn, field, group, me).start())

        @pl.when(is_solver & (my_field == field))
        def _():
            zrecv[turn, me] = zsend[turn, field, me % half]

    def zonal_reduced(turn):
        mine = me % half
        over_lon(lambda device: zonal_out(turn, 0, 0, device).wait_recv())
        right_side = [
            zrecv[turn, k] + pltpu.roll(zrecv[turn, (k - 1) % N_LON], HALF, 1) for k in range(N_LON)
        ]
        for bit in range(5):
            stride = 1 << bit
            right_side = [
                right_side[k]
                + alpha[my_field, bit, k : k + 1, :] * right_side[(k - stride) % N_LON]
                + gamma[my_field, bit, k : k + 1, :] * right_side[(k + stride) % N_LON]
                for k in range(N_LON)
            ]
        values = [right_side[k] * minv[my_field, k : k + 1, :] for k in range(N_LON)]
        for k in range(N_LON):
            zret[turn, k] = jnp.where(
                iota[0:8] < HALF, values[k], pltpu.roll(values[(k + 1) % N_LON], HALF, 1)
            )
        over_lon(lambda device: zonal_back(turn, device, my_field, mine).start())
        zres[turn, my_field, mine] = zret[turn, me]

    def zonal_receive(turn, field):
        others(field, lambda group: zonal_back(turn, 0, field, group).wait_recv())
        ubuf[72:80, :] = jnp.zeros((8, LANES), F32)
        for group in range(GROUPS):
            at = slice(GROUP * group, GROUP * group + GROUP)
            ubuf[at, :] = zres[turn, field, group, 0:GROUP, :]
        gbuf[...] = pltpu.roll(ubuf[...], HALF, 1) * zco_ref[field, 0:1, :] + acc_b[field]

    def zonal_values(field, chunk):
        u_all, g_all = ubuf[...], gbuf[...]
        found = []
        for step in range(CHUNK):
            row = chunk * CHUNK + step
            at = pl.ds(field * NLAT + row, 1)
            found.append(
                x_ref[field, row]
                + zr_ref[at, :] * jnp.broadcast_to(u_all[:, step : step + 1], (ZP, LANES))
                + zs_ref[at, :] * jnp.broadcast_to(g_all[:, step : step + 1], (ZP, LANES))
            )
        ubuf[...] = pltpu.roll(u_all, LANES - CHUNK, 1)
        gbuf[...] = pltpu.roll(g_all, LANES - CHUNK, 1)
        return found


    def vertical(field, value):
        high, low = split(value)
        return jnp.dot(
            vert_ref[field], jnp.concatenate([high, high, low], axis=0), preferred_element_type=F32
        )

    def vertical_field(field):
        def body(step, _):
            row = step * VERT_CHUNK
            value = jnp.concatenate([x_ref[field, row + k] for k in range(VERT_CHUNK)], axis=1)
            value = vertical(field, value)
            for k in range(VERT_CHUNK):
                x_ref[field, row + k] = value[:, k * LANES : (k + 1) * LANES]
            return 0

        lax.fori_loop(0, NLAT // VERT_CHUNK, body, 0)


    def merid_out(field, device, slot):
        return push(
            msend.at[field, device], mrecv.at[field, slot],
            m1s.at[field, device], m1r.at[field, slot], "lat", device,
        )

    def merid_back(field, device, slot):
        return push(
            mret.at[field, device], mres.at[field, slot],
            m2s.at[field, device], m2r.at[field, slot], "lat", device,
        )

    def merid_pass(field):
        def one(chunk, carry):
            tot_a, tot_b = carry
            found = zonal_values(field, chunk)
            for step in range(CHUNK):
                row = chunk * CHUNK + step
                s_row, r_row = ms_ref[field, pl.ds(row, 1), :], mr_ref[field, pl.ds(row, 1), :]
                tot_a = tot_a + s_row * found[step]
                tot_b = tot_b + r_row * found[step]
                x_ref[field, row] = r_row * tot_a - s_row * tot_b
            return tot_a, tot_b

        a_one, b_one = lax.fori_loop(0, NLAT // CHUNK, one, (nothing, nothing))
        ubuf[...] = b_one

        def two(row, carry):
            tot_a, tot_b = carry
            s_row, r_row = ms_ref[field, pl.ds(row, 1), :], mr_ref[field, pl.ds(row, 1), :]
            value = x_ref[field, row] + s_row * ubuf[...]
            tot_a = tot_a + s_row * value
            tot_b = tot_b + r_row * value
            x_ref[field, row] = r_row * tot_a - s_row * tot_b
            return tot_a, tot_b

        a_two, b_two = lax.fori_loop(0, NLAT, two, (nothing, nothing), unroll=4)
        mtot[field] = b_two
        coupling = mco_all[my, field, 0:1, :]
        for part, value in enumerate((b_one, a_one * coupling, b_two, a_two * coupling)):
            for solver in range(N_LAT):
                count = min(SPLIT, ZP - SPLIT * solver)
                msend[field, solver, part, 0:count, :] = value[SPLIT * solver : SPLIT * solver + count]
                if count < SPLIT:
                    msend[field, solver, part, count:SPLIT, :] = jnp.zeros(
                        (SPLIT - count, LANES), F32
                    )
        over_lat(lambda device: merid_out(field, device, my).start())
        mrecv[field, my] = msend[field, my]

    def merid_reduced(field):
        over_lat(lambda device: merid_out(field, 0, device).wait_recv())
        coef = lambda k, row: mco_all[k, field, row : row + 1, :]
        part = lambda k, index: mrecv[field, k, index]

        def solve_four(right_side):
            mass = 1.0 + coef(0, 1)
            reduced = right_side[0]
            kept, inverses, values = [], [], [None] * N_LAT
            for k in range(N_LAT):
                inverse = 1.0 / (mass + coef(k, 0))
                kept.append(reduced)
                inverses.append(inverse)
                if k + 1 < N_LAT:
                    factor = coef(k, 0) * inverse
                    mass = 1.0 + coef(k + 1, 1) + coef(k, 2) + factor * mass
                    reduced = right_side[k + 1] + factor * reduced
            values[-1] = kept[-1] * inverses[-1]
            for k in range(N_LAT - 2, -1, -1):
                values[k] = (kept[k] + coef(k, 0) * values[k + 1]) * inverses[k]
            return values

        none = jnp.zeros((SPLIT, LANES), F32)
        u = solve_four([part(k, 0) + (part(k - 1, 1) if k else none) for k in range(N_LAT)]) + [none]
        second = []
        for k in range(N_LAT):
            value = part(k, 2) + coef(k, 3) * u[k] + coef(k, 4) * u[k + 1]
            if k:
                value = value + part(k - 1, 3) + coef(k - 1, 4) * u[k - 1] + coef(k - 1, 5) * u[k]
            second.append(value)
        v = solve_four(second) + [none]
        for k in range(N_LAT):
            for index, value in enumerate((u[k], u[k + 1], v[k], v[k + 1])):
                mret[field, k, index] = value
        over_lat(lambda device: merid_back(field, device, my).start())
        mres[field, my] = mret[field, my]

    def merid_receive(field):
        over_lat(lambda device: merid_back(field, 0, device).wait_recv())
        for index in range(4):
            for solver in range(N_LAT):
                count = min(SPLIT, ZP - SPLIT * solver)
                mbuf[index, SPLIT * solver : SPLIT * solver + count, :] = mres[
                    field, solver, index, 0:count, :
                ]
        coupling = mco_all[my, field, 0:1, :]
        mbuf[1] = mbuf[1] * coupling
        mbuf[3] = mbuf[3] * coupling + mtot[field]

    def merid_value(field, row):
        at = pl.ds(row, 1)
        return (
            x_ref[field, row]
            + mrr_ref[field, at, :] * mbuf[0]
            + mss_ref[field, at, :] * mbuf[1]
            + mr_ref[field, at, :] * mbuf[2]
            + ms_ref[field, at, :] * mbuf[3]
        )

    level = lax.broadcasted_iota(jnp.int32, (ZP, LANES), 0)

    def scale(field, row):
        wet = level < ints_ref[pl.ds(DEPTH_AT + row, 1), :]
        line = jnp.concatenate([norm_ref[field, row], jnp.zeros((ZP - NZ, LANES), F32)], axis=0)
        return jnp.where(wet, line, 0.0)

    def scaled_grid(field):
        def load(row):
            at = pl.ds(pl.multiple_of((field * NLAT + row) * ZP, ZP), ZP)
            total = [grid[at, :] for grid in grids]
            while len(total) > 1:
                total = [one + two for one, two in zip(total[::2], total[1::2])]
            return scale(field, row) * total[0]

        return load

    zonal_pass(0, 0, scaled_grid(0))
    greeted()
    zonal_send(0, 0)
    zonal_pass(0, 1, scaled_grid(1))
    zonal_send(0, 1)
    vertical_field(0)
    pl.when(is_solver & (my_field == 0))(lambda: zonal_reduced(0))
    vertical_field(1)
    pl.when(is_solver & (my_field == 1))(lambda: zonal_reduced(0))

    for field in range(NF):
        zonal_receive(0, field)
        both = vertical(field, jnp.concatenate([ubuf[...], gbuf[...]], axis=1))
        ubuf[...] = both[:, :LANES]
        gbuf[...] = both[:, LANES:]
        merid_pass(field)
    for field in range(NF):
        merid_reduced(field)

    for field in range(NF):
        merid_receive(field)
        zonal_pass(1, field, lambda row, field=field: merid_value(field, row))
        zonal_send(1, field)
    pl.when(is_solver)(lambda: zonal_reduced(1))
    for field in range(NF):
        zonal_receive(1, field)

        def last_pass(chunk, _, field=field):
            found = zonal_values(field, chunk)
            for step in range(CHUNK):
                row = chunk * CHUNK + step
                x_ref[field, row] = found[step] * scale(field, row)
            return 0

        lax.fori_loop(0, NLAT // CHUNK, last_pass, 0)

    for field in range(NF):
        over_lat(lambda device, field=field: merid_out(field, device, my).wait_send())
        over_lat(lambda device, field=field: merid_back(field, device, my).wait_send())
        for turn in range(2):
            others(
                field,
                lambda group, turn=turn, field=field: zonal_out(turn, field, group, me).wait_send(),
            )

    @pl.when(is_solver)
    def _():
        for turn in range(2):
            over_lon(lambda device, turn=turn: zonal_back(turn, device, 0, 0).wait_send())


def solve(grids, norm, ints, coefs):
    dma = pltpu.SemaphoreType.DMA
    vmem = lambda *dims: pltpu.VMEM(dims, F32)
    return pl.pallas_call(
        solve_kernel,
        out_shape=jax.ShapeDtypeStruct((NF, NLAT, ZP, LANES), F32),
        in_specs=[VMEM_SPEC] * (15 + GRIDS),
        out_specs=VMEM_SPEC,
        scratch_shapes=[
            vmem(2, NF, GROUPS, 8, LANES), vmem(2, N_LON, 8, LANES),
            vmem(2, N_LON, 8, LANES), vmem(2, NF, GROUPS, 8, LANES),
            vmem(NF, N_LAT, 4, SPLIT, LANES), vmem(NF, N_LAT, 4, SPLIT, LANES),
            vmem(NF, N_LAT, 4, SPLIT, LANES), vmem(NF, N_LAT, 4, SPLIT, LANES),
            vmem(ZP, LANES), vmem(NF, ZP, LANES), vmem(ZP, LANES), vmem(ZP, LANES),
            vmem(NF, ZP, LANES), vmem(4, ZP, LANES),
            dma((2, NF, GROUPS)), dma((2, N_LON)), dma((2, N_LON)), dma((2, NF, GROUPS)),
            dma((NF, N_LAT)), dma((NF, N_LAT)), dma((NF, N_LAT)), dma((NF, N_LAT)),
        ],
        compiler_params=pltpu.CompilerParams(
            collective_id=1, has_side_effects=True, vmem_limit_bytes=10 << 20
        ),
        cost_estimate=cost(40),
        name="solve",
    )(*grids, norm, ints, *coefs)


def pick_kernel(rows_ref, ints_ref, x_ref, out_ref, inc_ref, inc_sem):
    iota = lane_iota(8)
    group = 16
    for field in range(NF):

        def begin(row, _, field=field):
            at = pl.ds(pl.multiple_of((field * NLAT + row) * ZP, ZP), NZ)
            pltpu.make_async_copy(x_ref.at[at, :], inc_ref.at[field, :, row, :], inc_sem).start()
            return 0

        lax.fori_loop(0, NLAT, begin, 0)

    def senders(step, acc):
        acc = list(acc)
        for part in range(group):
            q = step * group + part
            for tile in range(CAP // 8):
                lines = [
                    x_ref[pl.ds(rows_ref[k * RANKS + q], 1), :] for k in range(8 * tile, 8 * tile + 8)
                ]
                lane = ints_ref[CAP + 8 * tile : CAP + 8 * tile + 8, :] & 127
                found = lane_pick(jnp.concatenate(lines, axis=0), lane)
                acc[tile] = jnp.where(iota == q, found, acc[tile])
        return tuple(acc)

    acc = lax.fori_loop(0, RANKS // group, senders, (jnp.zeros((8, LANES), F32),) * (CAP // 8))
    whole = jnp.concatenate(list(acc) + [jnp.zeros((LANES - CAP, LANES), F32)], axis=0)
    whole = jnp.transpose(whole)
    for device in range(N_LON):
        out_ref[device, 0:4, :] = whole[4 * device : 4 * device + 4]
        out_ref[device, 4:8, :] = jnp.zeros((4, LANES), F32)
    pltpu.make_async_copy(inc_ref, inc_ref, inc_sem).wait()


def pick(rows, ints, increment):
    return pl.pallas_call(
        pick_kernel,
        out_shape=(
            jax.ShapeDtypeStruct((N_LON, 8, LANES), F32),
            jax.ShapeDtypeStruct((NF, NZ, NLAT, LANES), F32),
        ),
        in_specs=[SMEM_SPEC, VMEM_SPEC, VMEM_SPEC],
        out_specs=(VMEM_SPEC, ANY_SPEC),
        scratch_shapes=[pltpu.SemaphoreType.DMA],
        compiler_params=pltpu.CompilerParams(vmem_limit_bytes=8 << 20),
        cost_estimate=cost(14),
        name="pick",
    )(rows, ints, increment.reshape(ROWS, LANES))


def place_kernel(
    tile_out, ints_ref, out_ref,
    idx_ref, val_ref, rows_oh, cols_oh, tile_in, rows_out, rows_in, b1s, b1r, b2s, b2r,
):
    greet()
    none = jnp.full((LANES - CAP, LANES), -1, jnp.int32)
    idx_ref[...] = jnp.transpose(jnp.concatenate([ints_ref[0:CAP, :], none], axis=0))
    begin, middle, end, sent = two_phase(tile_out, tile_in, rows_out, rows_in, (b1s, b1r, b2s, b2r))
    row_iota = lax.broadcasted_iota(jnp.int32, (CAP, 2 * LANES), 0)
    col_iota = lax.broadcasted_iota(jnp.int32, (LANES, 2 * LANES), 0)

    def build(step, _):
        lat = step // (N_LON // 2)
        left = (step % (N_LON // 2)) * 2 * N_LAT + lat
        index = jnp.concatenate(
            [idx_ref[pl.ds(left, 1), :], idx_ref[pl.ds(left + N_LAT, 1), :]], axis=1
        )
        rows_oh[step] = jnp.where(row_iota == (index >> 7), 1.0, 0.0).astype(BF16)
        cols_oh[step] = jnp.where(col_iota == (index & 127), 1.0, 0.0).astype(BF16)
        return 0

    def add(step, acc):
        value = jnp.concatenate(
            [val_ref[pl.ds(2 * step, 1), :], val_ref[pl.ds(2 * step + 1, 1), :]], axis=1
        )
        high, low = split(value)
        rows = rows_oh[step]
        return acc + lax.dot_general(
            jnp.concatenate([rows * high, rows * low], axis=0), cols_oh[step],
            (((1,), (1,)), ((), ())), preferred_element_type=F32,
        )

    greeted()
    begin()
    lax.fori_loop(0, RANKS // 4, build, 0, unroll=2)
    middle()
    lax.fori_loop(RANKS // 4, RANKS // 2, build, 0, unroll=2)
    end()
    for lat in range(N_LAT):
        val_ref[N_LON * lat : N_LON * lat + N_LON, :] = rows_in[lat]
    acc = lax.fori_loop(0, RANKS // 2, add, jnp.zeros((2 * CAP, LANES), F32), unroll=8)
    out_ref[...] = acc[:CAP] + acc[CAP:]
    sent()


def place(tiles, ints):
    vmem = lambda *dims: pltpu.VMEM(dims, F32)
    dma = pltpu.SemaphoreType.DMA
    return pl.pallas_call(
        place_kernel,
        out_shape=jax.ShapeDtypeStruct((CAP, LANES), F32),
        in_specs=[VMEM_SPEC] * 2,
        out_specs=VMEM_SPEC,
        scratch_shapes=[
            pltpu.VMEM((RANKS, LANES), jnp.int32), vmem(RANKS, LANES),
            pltpu.VMEM((RANKS // 2, CAP, 2 * LANES), BF16),
            pltpu.VMEM((RANKS // 2, LANES, 2 * LANES), BF16),
            vmem(N_LON, 8, LANES), vmem(N_LAT, N_LON, LANES), vmem(N_LAT, N_LON, LANES),
            dma((N_LON,)), dma((N_LON,)), dma((N_LAT,)), dma((N_LAT,)),
        ],
        compiler_params=pltpu.CompilerParams(
            collective_id=2, has_side_effects=True, vmem_limit_bytes=10 << 20
        ),
        cost_estimate=cost(15),
        name="place",
    )(tiles, ints)


def local(
    obs_value, send_list, recv_cell, column_depth, zonal_weight, merid_weight, vert_inverse, norm_scale
):
    is_north = lax.axis_index("lat") == N_LAT - 1
    north = jnp.full((8, LANES), jnp.where(is_north, 1.0, 0.0), F32)
    ints = jnp.concatenate(
        [jnp.transpose(send_list), jnp.transpose(recv_cell), column_depth], axis=0
    )
    vert = jnp.transpose(vert_inverse, (1, 0, 2)).reshape(NF * NZ, NZ)
    floats = jnp.concatenate(
        [
            obs_value.reshape(CAP, LANES),
            zonal_weight.reshape(NF * NLAT, LANES),
            merid_weight.reshape(NF * NLAT, LANES),
            jnp.pad(vert, ((0, 0), (0, LANES - NZ))),
        ],
        axis=0,
    )
    made = prepare(ints, floats, north)
    incoming, coefs, rows = made[0], made[1:14], made[14].reshape(-1)
    grids = scatter(rows, ints, incoming, made[15:])
    norm = jnp.transpose(norm_scale, (0, 2, 1, 3))
    whole = solve(grids, norm, ints, coefs)
    tiles, increment = pick(rows, ints, whole)
    return increment, place(tiles, ints).reshape(-1)


def solution(mesh):
    in_specs = (
        P(("lon", "lat")),
        P(("lon", "lat"), None),
        P(("lon", "lat"), None),
        P("lat", "lon"),
        P(None, "lat", "lon"),
        P(None, "lat", "lon"),
        P(),
        P(None, None, "lat", "lon"),
    )
    out_specs = (P(None, None, "lat", "lon"), P(("lon", "lat")))
    return jax.shard_map(local, mesh=mesh, in_specs=in_specs, out_specs=out_specs, check_vma=False)
```

```python
import jax
import jax.numpy as jnp
from jax import lax
from jax.experimental import pallas as pl
from jax.experimental.pallas import tpu as pltpu
from jax.sharding import PartitionSpec as P

F32 = jnp.float32
BF16 = jnp.bfloat16
MESH = pl.DeviceIdType.MESH
NF, NZ, NLAT, NLON = 2, 75, 40, 128
ZP = 80
RANKS, CAP = 128, 80
N_LON, N_LAT = 32, 4
GROUPS = 15
GROUP = 5
LANES = 128
CHUNK = 20
HALF = 64
SPLIT = 24
VERT_CHUNK = 10
GRIDS = 8
ROWS = NF * NLAT * ZP
ZW_AT, MW_AT, VERT_AT = 80, 160, 240
DEPTH_AT = 160
VMEM_SPEC = pl.BlockSpec(memory_space=pltpu.VMEM)
SMEM_SPEC = pl.BlockSpec(memory_space=pltpu.SMEM)
ANY_SPEC = pl.BlockSpec(memory_space=pl.ANY)


def cost(micros):
    return pl.CostEstimate(flops=0, bytes_accessed=int(micros * 3.6e6), transcendentals=0)


def lane_iota(rows):
    return lax.broadcasted_iota(jnp.int32, (rows, LANES), 1)


def split(value):
    high = value.astype(BF16)
    return high, (value - high.astype(F32)).astype(BF16)


def lane_pick(table, index):
    return jnp.take_along_axis(table, index, axis=1, mode="promise_in_bounds")


def push(source, target, send_sem, recv_sem, axis, device):
    return pltpu.make_async_remote_copy(
        src_ref=source, dst_ref=target, send_sem=send_sem, recv_sem=recv_sem,
        device_id={axis: device}, device_id_type=MESH,
    )


def over(axis, count, action):
    mine = lax.axis_index(axis)

    def body(step, _):
        action((mine + step) % count)
        return 0

    lax.fori_loop(1, count, body, 0)


def over_lon(action):
    over("lon", N_LON, action)


def each_lon(action):
    mine = lax.axis_index("lon")
    for step in range(1, N_LON):
        action((mine + step) % N_LON)


def over_lat(action):
    over("lat", N_LAT, action)


def greet():
    barrier = pltpu.get_barrier_semaphore()
    over_lon(
        lambda device: pl.semaphore_signal(
            barrier, inc=1, device_id={"lon": device}, device_id_type=MESH
        )
    )
    over_lat(
        lambda device: pl.semaphore_signal(
            barrier, inc=1, device_id={"lat": device}, device_id_type=MESH
        )
    )


def greeted():
    pl.semaphore_wait(pltpu.get_barrier_semaphore(), N_LON - 1 + N_LAT - 1)


def zonal_coefs(floats_ref, zs_ref, zr_ref, zco_ref, iw_ref, st_ref, rt_ref, zero):
    one = zero + 1.0
    iw_ref[...] = jnp.full((LANES, LANES), 1e-3, F32)
    iw_ref[: NF * NLAT, :] = 1.0 / floats_ref[ZW_AT : ZW_AT + NF * NLAT, :]
    iw_ref[...] = jnp.transpose(iw_ref[...])

    def zonal_step(step, carry):
        s_val, s_flux, s_sum, r_val, r_flux, r_sum = carry
        back = LANES - 1 - step
        st_ref[pl.ds(step, 1), :] = s_val[0:1]
        s_sum = s_sum + s_val
        s_val = s_val + s_flux * iw_ref[pl.ds(step, 1), :]
        s_flux = s_flux + s_val
        r_sum = r_sum + r_val
        r_val = r_val + r_flux * iw_ref[pl.ds(back, 1), :]
        rt_ref[pl.ds(back, 1), :] = r_val[0:1]
        r_flux = r_flux + r_val
        return s_val, s_flux, s_sum, r_val, r_flux, r_sum

    _, _, s_sum, r_first, _, r_sum = lax.fori_loop(
        0, LANES, zonal_step, (zero, one, zero, zero, one, zero), unroll=8
    )
    coupling = 1.0 / r_first[0:1]
    zco_ref[...] = jnp.zeros((8, LANES), F32)
    zco_ref[0:1, :] = coupling
    zco_ref[1:2, :] = r_sum[0:1] * coupling
    zco_ref[2:3, :] = s_sum[0:1] * coupling
    zs_ref[...] = jnp.transpose(st_ref[...])[: NF * NLAT, :]
    zr_ref[...] = jnp.transpose(rt_ref[...] * coupling)[: NF * NLAT, :]


def merid_coefs(floats_ref, ms_ref, mr_ref, mss_ref, mrr_ref, mco_ref, miw_ref, north, zero):
    one = zero + 1.0
    for field in range(NF):
        at = MW_AT + field * NLAT
        miw_ref[field] = 1.0 / floats_ref[at : at + NLAT, :]
    mco_ref[...] = jnp.zeros((NF, 8, LANES), F32)
    for field in range(NF):
        s_val, s_flux, s_sum = zero, one, zero
        for row in range(NLAT):
            ms_ref[field, row : row + 1, :] = s_val[0:1]
            s_sum = s_sum + s_val
            s_val = s_val + s_flux * miw_ref[field, row : row + 1, :]
            s_flux = s_flux + s_val
        r_val = jnp.where(north > 0.5, 1.0, miw_ref[field, NLAT - 1 : NLAT, :] + zero)
        r_flux = jnp.where(north > 0.5, 0.0, one)
        r_sum = zero
        mr_ref[field, NLAT - 1 : NLAT, :] = r_val[0:1]
        for row in range(NLAT - 2, -1, -1):
            r_sum = r_sum + r_val
            r_flux = r_flux + r_val
            r_val = r_val + r_flux * miw_ref[field, row : row + 1, :]
            mr_ref[field, row : row + 1, :] = r_val[0:1]
        inverse = 1.0 / r_val[0:1]
        coupling = jnp.where(north[0:1] > 0.5, 0.0, inverse)
        mr_ref[field] = mr_ref[field] * inverse
        sum_rr, sum_rs = zero, zero
        for row in range(NLAT - 1, -1, -1):
            at = slice(row, row + 1)
            s_row, r_row = ms_ref[field, at, :], mr_ref[field, at, :]
            mrr_ref[field, at, :] = s_row * sum_rr[0:1]
            mss_ref[field, at, :] = s_row * sum_rs[0:1]
            sum_rr = sum_rr + r_row * r_row
            sum_rs = sum_rs + r_row * s_row
        sum_sr, sum_ss = zero, zero
        for row in range(NLAT):
            at = slice(row, row + 1)
            s_row, r_row = ms_ref[field, at, :], mr_ref[field, at, :]
            sum_sr = sum_sr + s_row * r_row
            sum_ss = sum_ss + s_row * s_row
            mrr_ref[field, at, :] = mrr_ref[field, at, :] + r_row * sum_sr[0:1]
            mss_ref[field, at, :] = mss_ref[field, at, :] + r_row * sum_ss[0:1]
        mco_ref[field, 0:1, :] = coupling
        mco_ref[field, 1:2, :] = r_sum[0:1] * inverse
        mco_ref[field, 2:3, :] = s_sum[0:1] * coupling
        mco_ref[field, 3:4, :] = sum_rr[0:1]
        mco_ref[field, 4:5, :] = sum_rs[0:1] * coupling
        mco_ref[field, 5:6, :] = sum_ss[0:1] * coupling * coupling


def zonal_factor(zco_all, alpha, gamma, minv):
    coupling = zco_all[:, 0, :]
    west = jnp.concatenate([coupling[-1:], coupling[:-1]], axis=0)
    spill = zco_all[:, 2, :]
    mass = 1.0 + zco_all[:, 1, :] + jnp.concatenate([spill[-1:], spill[:-1]], axis=0)
    east = coupling
    for bit in range(5):
        stride = 1 << bit
        down = lambda v: jnp.concatenate([v[-stride:], v[:-stride]], axis=0)
        up = lambda v: jnp.concatenate([v[stride:], v[:stride]], axis=0)
        inverse = 1.0 / (mass + west + east)
        left = west * down(inverse)
        right = east * up(inverse)
        for field in range(NF):
            alpha[field, bit] = to_field(left, field)
            gamma[field, bit] = to_field(right, field)
        mass = mass + left * down(mass) + right * up(mass)
        west, east = left * down(west), right * up(east)
    for field in range(NF):
        minv[field] = to_field(1.0 / mass, field)


def to_field(rows, field):
    return rows if field == 0 else pltpu.roll(rows, LANES - field * NLAT, 1)


def gather_lines(table_ref, count, high, low, beside):
    def step(row, acc):
        beside(row)
        line = jnp.broadcast_to(table_ref[pl.ds(row, 1), :], (ZP, LANES))
        return jnp.where(high == row, lane_pick(line, low), acc)

    return lax.fori_loop(0, count, step, jnp.zeros((ZP, LANES), F32), unroll=8)


def two_phase(tile_out, tile_in, rows_out, rows_in, sems):
    me = lax.axis_index("lon")
    my = lax.axis_index("lat")
    s1, r1, s2, r2 = sems
    first = lambda device, slot: push(
        tile_out.at[device], tile_in.at[slot], s1.at[device], r1.at[slot], "lon", device
    )
    second = lambda device, slot: push(
        rows_out.at[device], rows_in.at[slot], s2.at[device], r2.at[slot], "lat", device
    )

    def begin():
        each_lon(lambda device: first(device, me).start())
        tile_in[me] = tile_out[me]

    def middle():
        each_lon(lambda device: first(0, device).wait_recv())
        for lat in range(N_LAT):
            rows_out[lat] = tile_in[:, lat, :]
        over_lat(lambda device: second(device, my).start())
        rows_in[my] = rows_out[my]

    def end():
        over_lat(lambda device: second(0, device).wait_recv())

    def sent():
        over_lon(lambda device: first(device, me).wait_send())
        over_lat(lambda device: second(device, my).wait_send())

    return begin, middle, end, sent


def prepare_kernel(
    ints_ref, floats_ref, north_ref,
    out_ref, zs_ref, zr_ref, zco_out, ms_ref, mr_ref, mss_ref, mrr_ref, mco_out, vert_ref,
    alpha, gamma, minv, sums_ref, row_ref, *rest
):
    grids, rest = rest[:GRIDS], rest[GRIDS:]
    prepare_body(
        ints_ref, floats_ref, north_ref, out_ref, zs_ref, zr_ref, zco_out, ms_ref, mr_ref, mss_ref,
        mrr_ref, mco_out, vert_ref, alpha, gamma, minv, sums_ref, row_ref, grids, *rest,
    )


def prepare_body(
    ints_ref, floats_ref, north_ref,
    out_ref, zs_ref, zr_ref, zco_out, ms_ref, mr_ref, mss_ref, mrr_ref, mco_out, vert_ref,
    alpha, gamma, minv, sums_ref, row_ref, grids,
    iw_ref, st_ref, rt_ref, miw_ref, prod_ref,
    tile_out, tile_in, rows_out, rows_in, zco_ref, zco_all, mco_ref, mco_all,
    o1s, o1r, o2s, o2r, zco_s, zco_r, mco_s, mco_r,
):
    me = lax.axis_index("lon")
    my = lax.axis_index("lat")
    greet()
    index = ints_ref[0:CAP, :]

    def clear(line):
        at = pl.ds(pl.multiple_of(line * ZP, ZP), ZP)
        for grid in grids:
            grid[at, :] = jnp.zeros((ZP, LANES), F32)

    picked = gather_lines(floats_ref, CAP, index >> 7, index & 127, clear)
    picked = jnp.transpose(
        jnp.concatenate([picked, jnp.zeros((LANES - CAP, LANES), F32)], axis=0)
    )
    for device in range(N_LON):
        tile_out[device] = picked[4 * device : 4 * device + 4]

    begin, middle, end, sent = two_phase(tile_out, tile_in, rows_out, rows_in, (o1s, o1r, o2s, o2r))
    zco_copy = lambda device, slot: push(
        zco_ref, zco_all.at[slot], zco_s.at[device], zco_r.at[slot], "lon", device
    )
    mco_copy = lambda device, slot: push(
        mco_ref, mco_all.at[slot], mco_s.at[device], mco_r.at[slot], "lat", device
    )
    greeted()
    begin()
    zero = north_ref[...] * 0.0
    zonal_coefs(floats_ref, zs_ref, zr_ref, zco_ref, iw_ref, st_ref, rt_ref, zero)
    over_lon(lambda device: zco_copy(device, me).start())
    zco_all[me] = zco_ref[...]
    merid_coefs(floats_ref, ms_ref, mr_ref, mss_ref, mrr_ref, mco_ref, miw_ref, north_ref[...], zero)
    over_lat(lambda device: mco_copy(device, my).start())
    mco_all[my] = mco_ref[...]
    middle()
    for field in range(NF):
        zco_out[field] = to_field(zco_ref[...], field)
    cell = ints_ref[CAP : 2 * CAP, :]
    line = cell >> 7
    plane = line // NLAT
    second_field = (plane >= NZ).astype(jnp.int32)
    live_row = (second_field * NLAT + line - plane * NLAT) * ZP + plane - second_field * NZ
    dead_row = lax.broadcasted_iota(jnp.int32, (CAP, LANES), 0) * ZP + NZ
    row_ref[...] = jnp.where(cell >= 0, live_row, dead_row)
    prod_ref[...] = jnp.zeros((ZP, LANES), F32)
    for field in range(NF):
        matrix = floats_ref[pl.ds(VERT_AT + field, NZ, stride=NF), :]
        prod_ref[:NZ, :NZ] = lax.dot_general(
            matrix, matrix, (((1,), (1,)), ((), ())),
            precision=lax.Precision.HIGHEST, preferred_element_type=F32,
        )
        high, low = split(prod_ref[:, :ZP])
        vert_ref[field] = jnp.concatenate([high, low, high], axis=1)
    source = lax.broadcasted_iota(jnp.int32, (2 * LANES, 2 * LANES), 0) & 127
    target = lax.broadcasted_iota(jnp.int32, (2 * LANES, 2 * LANES), 1)
    sums_ref[...] = jnp.where(source <= target, 1.0, 0.0).astype(BF16)
    end()
    for lat in range(N_LAT):
        out_ref[N_LON * lat : N_LON * lat + N_LON, :] = rows_in[lat]
    over_lon(lambda device: zco_copy(0, device).wait_recv())
    zonal_factor(zco_all, alpha, gamma, minv)
    over_lat(lambda device: mco_copy(0, device).wait_recv())
    mco_out[...] = mco_all[...]
    sent()
    over_lon(lambda device: zco_copy(device, me).wait_send())
    over_lat(lambda device: mco_copy(device, my).wait_send())


def prepare(ints, floats, north):
    shape = lambda *dims: jax.ShapeDtypeStruct(dims, F32)
    vmem = lambda *dims: pltpu.VMEM(dims, F32)
    dma = pltpu.SemaphoreType.DMA
    return pl.pallas_call(
        prepare_kernel,
        out_shape=(
            shape(RANKS, LANES), shape(80, LANES), shape(80, LANES), shape(NF, 8, LANES),
            shape(NF, NLAT, LANES), shape(NF, NLAT, LANES),
            shape(NF, NLAT, LANES), shape(NF, NLAT, LANES), shape(N_LAT, NF, 8, LANES),
            jax.ShapeDtypeStruct((NF, ZP, 3 * ZP), BF16),
            shape(NF, 5, N_LON, LANES), shape(NF, 5, N_LON, LANES), shape(NF, N_LON, LANES),
            jax.ShapeDtypeStruct((2 * LANES, 2 * LANES), BF16),
            jax.ShapeDtypeStruct((CAP, LANES), jnp.int32),
        )
        + (shape(ROWS, LANES),) * GRIDS,
        in_specs=[VMEM_SPEC] * 3,
        out_specs=(VMEM_SPEC,) * (15 + GRIDS),
        scratch_shapes=[
            vmem(LANES, LANES), vmem(LANES, LANES), vmem(LANES, LANES), vmem(NF, NLAT, LANES),
            vmem(ZP, LANES),
            vmem(N_LON, 4, LANES), vmem(N_LON, 4, LANES),
            vmem(N_LAT, N_LON, LANES), vmem(N_LAT, N_LON, LANES),
            vmem(8, LANES), vmem(N_LON, 8, LANES), vmem(NF, 8, LANES), vmem(N_LAT, NF, 8, LANES),
            dma((N_LON,)), dma((N_LON,)), dma((N_LAT,)), dma((N_LAT,)),
            dma((N_LON,)), dma((N_LON,)), dma((N_LAT,)), dma((N_LAT,)),
        ],
        compiler_params=pltpu.CompilerParams(
            collective_id=0, has_side_effects=True, vmem_limit_bytes=6 << 20
        ),
        cost_estimate=cost(15),
        name="prepare",
    )(ints, floats, north)


def scatter_kernel(rows_ref, ints_ref, in_ref, *refs):
    grids = refs[GRIDS : 2 * GRIDS]
    value_ref, even_ref, odd_ref = refs[2 * GRIDS :]
    value_ref[...] = jnp.transpose(in_ref[...])
    iota = lane_iota(CAP)

    def spread(q):
        index = jnp.full((CAP, LANES), q, jnp.int32)
        place = jnp.full((CAP, LANES), (q % N_LAT) * N_LON + q // N_LAT, jnp.int32)
        lane = lane_pick(ints_ref[CAP : 2 * CAP, :] & 127, index)
        return jnp.where(iota == lane, lane_pick(value_ref[:CAP, :], place), 0.0)

    def add(q, source):
        for k in range(CAP):
            at = pl.ds(rows_ref[k * RANKS + q], 1)
            grid = grids[k % GRIDS]
            grid[at, :] = grid[at, :] + source[k : k + 1, :]

    even_ref[...] = spread(0)

    def senders(pair, _):
        q = 2 * pair
        odd_ref[...] = spread(q + 1)
        add(q, even_ref)
        even_ref[...] = spread(jnp.minimum(q + 2, RANKS - 1))
        add(q + 1, odd_ref)
        return 0

    lax.fori_loop(0, RANKS // 2, senders, 0)


def scatter(rows, ints, incoming, grids):
    grid = jax.ShapeDtypeStruct((ROWS, LANES), F32)
    return pl.pallas_call(
        scatter_kernel,
        out_shape=(grid,) * GRIDS,
        in_specs=[SMEM_SPEC] + [VMEM_SPEC] * (2 + GRIDS),
        out_specs=(VMEM_SPEC,) * GRIDS,
        input_output_aliases={3 + index: index for index in range(GRIDS)},
        scratch_shapes=[
            pltpu.VMEM((LANES, LANES), F32), pltpu.VMEM((CAP, LANES), F32), pltpu.VMEM((CAP, LANES), F32),
        ],
        compiler_params=pltpu.CompilerParams(vmem_limit_bytes=6 << 20),
        cost_estimate=cost(12),
        name="scatter",
    )(rows, ints, incoming, *grids)


def solve_kernel(*refs):
    solve_body(refs[:GRIDS], *refs[GRIDS:])


def solve_body(
    grids, norm_ref, ints_ref, zs_ref, zr_ref, zco_ref, ms_ref, mr_ref, mss_ref, mrr_ref, mco_all,
    vert_ref, alpha, gamma, minv, sums_ref,
    x_ref,
    zsend, zrecv, zret, zres, msend, mrecv, mret, mres,
    acc_a, acc_b, ubuf, gbuf, mtot, mbuf,
    z1s, z1r, z2s, z2r, m1s, m1r, m2s, m2r,
):
    me = lax.axis_index("lon")
    my = lax.axis_index("lat")
    iota = lane_iota(ZP)
    half = N_LON // NF
    my_field = me // half
    is_solver = me % half < GROUPS
    nothing = jnp.zeros((ZP, LANES), F32)
    greet()


    def zonal_out(turn, field, group, slot):
        return push(
            zsend.at[turn, field, group], zrecv.at[turn, slot],
            z1s.at[turn, field, group], z1r.at[turn, slot], "lon", field * half + group,
        )

    def zonal_back(turn, device, field, group):
        return push(
            zret.at[turn, device], zres.at[turn, field, group],
            z2s.at[turn, device], z2r.at[turn, field, group], "lon", device,
        )

    def others(field, action):
        for group in range(GROUPS):
            pl.when(me != field * half + group)(lambda group=group: action(group))

    def zonal_pass(turn, field, load):
        def chunk_pass(chunk, _):
            lines, left = [], []
            for step in range(CHUNK):
                row = chunk * CHUNK + step
                at = pl.ds(field * NLAT + row, 1)
                s_row, r_row = zs_ref[at, :], zr_ref[at, :]
                value = load(row)
                for coef in (s_row, r_row):
                    high, low = split(coef * value)
                    left.append(jnp.concatenate([high, low], axis=1))
                lines.append((row, s_row, r_row))
            sums = jnp.dot(
                jnp.concatenate(left, axis=0), sums_ref[...], preferred_element_type=F32
            )
            tot_a, tot_b = acc_a[...], acc_b[field]
            for step, (row, s_row, r_row) in enumerate(lines):
                a_part = sums[2 * step * ZP : (2 * step + 1) * ZP]
                b_part = sums[(2 * step + 1) * ZP : (2 * step + 2) * ZP]
                x_ref[field, row] = r_row * a_part[:, :LANES] - s_row * b_part[:, :LANES]
                mine = iota == row
                tot_a = jnp.where(mine, a_part[:, LANES:], tot_a)
                tot_b = jnp.where(mine, b_part[:, LANES:], tot_b)
            acc_a[...] = tot_a
            acc_b[field] = tot_b
            return 0

        acc_a[...] = nothing
        acc_b[field] = nothing
        lax.fori_loop(0, NLAT // CHUNK, chunk_pass, 0)
        acc_a[...] = acc_b[field] + pltpu.roll(acc_a[...] * zco_ref[field, 0:1, :], HALF, 1)
        for group in range(GROUPS):
            at = slice(GROUP * group, GROUP * group + GROUP)
            zsend[turn, field, group, 0:GROUP, :] = acc_a[at, :]

    def zonal_send(turn, field):
        others(field, lambda group: zonal_out(turn, field, group, me).start())

        @pl.when(is_solver & (my_field == field))
        def _():
            zrecv[turn, me] = zsend[turn, field, me % half]

    def zonal_reduced(turn):
        mine = me % half
        each_lon(lambda device: zonal_out(turn, 0, 0, device).wait_recv())
        right_side = [
            zrecv[turn, k] + pltpu.roll(zrecv[turn, (k - 1) % N_LON], HALF, 1) for k in range(N_LON)
        ]
        for bit in range(5):
            stride = 1 << bit
            right_side = [
                right_side[k]
                + alpha[my_field, bit, k : k + 1, :] * right_side[(k - stride) % N_LON]
                + gamma[my_field, bit, k : k + 1, :] * right_side[(k + stride) % N_LON]
                for k in range(N_LON)
            ]
        values = [right_side[k] * minv[my_field, k : k + 1, :] for k in range(N_LON)]
        for k in range(N_LON):
            zret[turn, k] = jnp.where(
                iota[0:8] < HALF, values[k], pltpu.roll(values[(k + 1) % N_LON], HALF, 1)
            )
        each_lon(lambda device: zonal_back(turn, device, my_field, mine).start())
        zres[turn, my_field, mine] = zret[turn, me]

    def zonal_receive(turn, field):
        others(field, lambda group: zonal_back(turn, 0, field, group).wait_recv())
        ubuf[72:80, :] = jnp.zeros((8, LANES), F32)
        for group in range(GROUPS):
            at = slice(GROUP * group, GROUP * group + GROUP)
            ubuf[at, :] = zres[turn, field, group, 0:GROUP, :]
        gbuf[...] = pltpu.roll(ubuf[...], HALF, 1) * zco_ref[field, 0:1, :] + acc_b[field]

    def zonal_values(field, chunk):
        u_all, g_all = ubuf[...], gbuf[...]
        found = []
        for step in range(CHUNK):
            row = chunk * CHUNK + step
            at = pl.ds(field * NLAT + row, 1)
            found.append(
                x_ref[field, row]
                + zr_ref[at, :] * jnp.broadcast_to(u_all[:, step : step + 1], (ZP, LANES))
                + zs_ref[at, :] * jnp.broadcast_to(g_all[:, step : step + 1], (ZP, LANES))
            )
        ubuf[...] = pltpu.roll(u_all, LANES - CHUNK, 1)
        gbuf[...] = pltpu.roll(g_all, LANES - CHUNK, 1)
        return found


    def vertical(field, value):
        high, low = split(value)
        return jnp.dot(
            vert_ref[field], jnp.concatenate([high, high, low], axis=0), preferred_element_type=F32
        )

    def vertical_field(field):
        def body(step, _):
            row = step * VERT_CHUNK
            value = jnp.concatenate([x_ref[field, row + k] for k in range(VERT_CHUNK)], axis=1)
            value = vertical(field, value)
            for k in range(VERT_CHUNK):
                x_ref[field, row + k] = value[:, k * LANES : (k + 1) * LANES]
            return 0

        lax.fori_loop(0, NLAT // VERT_CHUNK, body, 0)


    def merid_out(field, device, slot):
        return push(
            msend.at[field, device], mrecv.at[field, slot],
            m1s.at[field, device], m1r.at[field, slot], "lat", device,
        )

    def merid_back(field, device, slot):
        return push(
            mret.at[field, device], mres.at[field, slot],
            m2s.at[field, device], m2r.at[field, slot], "lat", device,
        )

    def merid_pass(field):
        def one(chunk, carry):
            tot_a, tot_b = carry
            found = zonal_values(field, chunk)
            for step in range(CHUNK):
                row = chunk * CHUNK + step
                s_row, r_row = ms_ref[field, pl.ds(row, 1), :], mr_ref[field, pl.ds(row, 1), :]
                tot_a = tot_a + s_row * found[step]
                tot_b = tot_b + r_row * found[step]
                x_ref[field, row] = r_row * tot_a - s_row * tot_b
            return tot_a, tot_b

        a_one, b_one = lax.fori_loop(0, NLAT // CHUNK, one, (nothing, nothing))
        ubuf[...] = b_one

        def two(row, carry):
            tot_a, tot_b = carry
            s_row, r_row = ms_ref[field, pl.ds(row, 1), :], mr_ref[field, pl.ds(row, 1), :]
            value = x_ref[field, row] + s_row * ubuf[...]
            tot_a = tot_a + s_row * value
            tot_b = tot_b + r_row * value
            x_ref[field, row] = r_row * tot_a - s_row * tot_b
            return tot_a, tot_b

        a_two, b_two = lax.fori_loop(0, NLAT, two, (nothing, nothing), unroll=4)
        mtot[field] = b_two
        coupling = mco_all[my, field, 0:1, :]
        for part, value in enumerate((b_one, a_one * coupling, b_two, a_two * coupling)):
            for solver in range(N_LAT):
                count = min(SPLIT, ZP - SPLIT * solver)
                msend[field, solver, part, 0:count, :] = value[SPLIT * solver : SPLIT * solver + count]
                if count < SPLIT:
                    msend[field, solver, part, count:SPLIT, :] = jnp.zeros(
                        (SPLIT - count, LANES), F32
                    )
        over_lat(lambda device: merid_out(field, device, my).start())
        mrecv[field, my] = msend[field, my]

    def merid_reduced(field):
        over_lat(lambda device: merid_out(field, 0, device).wait_recv())
        coef = lambda k, row: mco_all[k, field, row : row + 1, :]
        part = lambda k, index: mrecv[field, k, index]

        def solve_four(right_side):
            mass = 1.0 + coef(0, 1)
            reduced = right_side[0]
            kept, inverses, values = [], [], [None] * N_LAT
            for k in range(N_LAT):
                inverse = 1.0 / (mass + coef(k, 0))
                kept.append(reduced)
                inverses.append(inverse)
                if k + 1 < N_LAT:
                    factor = coef(k, 0) * inverse
                    mass = 1.0 + coef(k + 1, 1) + coef(k, 2) + factor * mass
                    reduced = right_side[k + 1] + factor * reduced
            values[-1] = kept[-1] * inverses[-1]
            for k in range(N_LAT - 2, -1, -1):
                values[k] = (kept[k] + coef(k, 0) * values[k + 1]) * inverses[k]
            return values

        none = jnp.zeros((SPLIT, LANES), F32)
        u = solve_four([part(k, 0) + (part(k - 1, 1) if k else none) for k in range(N_LAT)]) + [none]
        second = []
        for k in range(N_LAT):
            value = part(k, 2) + coef(k, 3) * u[k] + coef(k, 4) * u[k + 1]
            if k:
                value = value + part(k - 1, 3) + coef(k - 1, 4) * u[k - 1] + coef(k - 1, 5) * u[k]
            second.append(value)
        v = solve_four(second) + [none]
        for k in range(N_LAT):
            for index, value in enumerate((u[k], u[k + 1], v[k], v[k + 1])):
                mret[field, k, index] = value
        over_lat(lambda device: merid_back(field, device, my).start())
        mres[field, my] = mret[field, my]

    def merid_receive(field):
        over_lat(lambda device: merid_back(field, 0, device).wait_recv())
        for index in range(4):
            for solver in range(N_LAT):
                count = min(SPLIT, ZP - SPLIT * solver)
                mbuf[index, SPLIT * solver : SPLIT * solver + count, :] = mres[
                    field, solver, index, 0:count, :
                ]
        coupling = mco_all[my, field, 0:1, :]
        mbuf[1] = mbuf[1] * coupling
        mbuf[3] = mbuf[3] * coupling + mtot[field]

    def merid_value(field, row):
        at = pl.ds(row, 1)
        return (
            x_ref[field, row]
            + mrr_ref[field, at, :] * mbuf[0]
            + mss_ref[field, at, :] * mbuf[1]
            + mr_ref[field, at, :] * mbuf[2]
            + ms_ref[field, at, :] * mbuf[3]
        )

    level = lax.broadcasted_iota(jnp.int32, (ZP, LANES), 0)

    def scale(field, row):
        wet = level < ints_ref[pl.ds(DEPTH_AT + row, 1), :]
        line = jnp.concatenate([norm_ref[field, row], jnp.zeros((ZP - NZ, LANES), F32)], axis=0)
        return jnp.where(wet, line, 0.0)

    def scaled_grid(field):
        def load(row):
            at = pl.ds(pl.multiple_of((field * NLAT + row) * ZP, ZP), ZP)
            total = [grid[at, :] for grid in grids]
            while len(total) > 1:
                total = [one + two for one, two in zip(total[::2], total[1::2])]
            return scale(field, row) * total[0]

        return load

    zonal_pass(0, 0, scaled_grid(0))
    greeted()
    zonal_send(0, 0)
    zonal_pass(0, 1, scaled_grid(1))
    zonal_send(0, 1)
    vertical_field(0)
    pl.when(is_solver & (my_field == 0))(lambda: zonal_reduced(0))
    vertical_field(1)
    pl.when(is_solver & (my_field == 1))(lambda: zonal_reduced(0))

    for field in range(NF):
        zonal_receive(0, field)
        both = vertical(field, jnp.concatenate([ubuf[...], gbuf[...]], axis=1))
        ubuf[...] = both[:, :LANES]
        gbuf[...] = both[:, LANES:]
        merid_pass(field)
    for field in range(NF):
        merid_reduced(field)

    for field in range(NF):
        merid_receive(field)
        zonal_pass(1, field, lambda row, field=field: merid_value(field, row))
        zonal_send(1, field)
    pl.when(is_solver)(lambda: zonal_reduced(1))
    for field in range(NF):
        zonal_receive(1, field)

        def last_pass(chunk, _, field=field):
            found = zonal_values(field, chunk)
            for step in range(CHUNK):
                row = chunk * CHUNK + step
                x_ref[field, row] = found[step] * scale(field, row)
            return 0

        lax.fori_loop(0, NLAT // CHUNK, last_pass, 0)

    for field in range(NF):
        over_lat(lambda device, field=field: merid_out(field, device, my).wait_send())
        over_lat(lambda device, field=field: merid_back(field, device, my).wait_send())
        for turn in range(2):
            others(
                field,
                lambda group, turn=turn, field=field: zonal_out(turn, field, group, me).wait_send(),
            )

    @pl.when(is_solver)
    def _():
        for turn in range(2):
            over_lon(lambda device, turn=turn: zonal_back(turn, device, 0, 0).wait_send())


def solve(grids, norm, ints, coefs):
    dma = pltpu.SemaphoreType.DMA
    vmem = lambda *dims: pltpu.VMEM(dims, F32)
    return pl.pallas_call(
        solve_kernel,
        out_shape=jax.ShapeDtypeStruct((NF, NLAT, ZP, LANES), F32),
        in_specs=[VMEM_SPEC] * (15 + GRIDS),
        out_specs=VMEM_SPEC,
        scratch_shapes=[
            vmem(2, NF, GROUPS, 8, LANES), vmem(2, N_LON, 8, LANES),
            vmem(2, N_LON, 8, LANES), vmem(2, NF, GROUPS, 8, LANES),
            vmem(NF, N_LAT, 4, SPLIT, LANES), vmem(NF, N_LAT, 4, SPLIT, LANES),
            vmem(NF, N_LAT, 4, SPLIT, LANES), vmem(NF, N_LAT, 4, SPLIT, LANES),
            vmem(ZP, LANES), vmem(NF, ZP, LANES), vmem(ZP, LANES), vmem(ZP, LANES),
            vmem(NF, ZP, LANES), vmem(4, ZP, LANES),
            dma((2, NF, GROUPS)), dma((2, N_LON)), dma((2, N_LON)), dma((2, NF, GROUPS)),
            dma((NF, N_LAT)), dma((NF, N_LAT)), dma((NF, N_LAT)), dma((NF, N_LAT)),
        ],
        compiler_params=pltpu.CompilerParams(
            collective_id=1, has_side_effects=True, vmem_limit_bytes=10 << 20
        ),
        cost_estimate=cost(40),
        name="solve",
    )(*grids, norm, ints, *coefs)


def pick_kernel(rows_ref, ints_ref, x_ref, out_ref, inc_ref, inc_sem):
    iota = lane_iota(8)
    group = 16
    for field in range(NF):

        def begin(row, _, field=field):
            at = pl.ds(pl.multiple_of((field * NLAT + row) * ZP, ZP), NZ)
            pltpu.make_async_copy(x_ref.at[at, :], inc_ref.at[field, :, row, :], inc_sem).start()
            return 0

        lax.fori_loop(0, NLAT, begin, 0)

    def senders(step, acc):
        acc = list(acc)
        for part in range(group):
            q = step * group + part
            for tile in range(CAP // 8):
                lines = [
                    x_ref[pl.ds(rows_ref[k * RANKS + q], 1), :] for k in range(8 * tile, 8 * tile + 8)
                ]
                lane = ints_ref[CAP + 8 * tile : CAP + 8 * tile + 8, :] & 127
                found = lane_pick(jnp.concatenate(lines, axis=0), lane)
                acc[tile] = jnp.where(iota == q, found, acc[tile])
        return tuple(acc)

    acc = lax.fori_loop(0, RANKS // group, senders, (jnp.zeros((8, LANES), F32),) * (CAP // 8))
    whole = jnp.concatenate(list(acc) + [jnp.zeros((LANES - CAP, LANES), F32)], axis=0)
    whole = jnp.transpose(whole)
    for device in range(N_LON):
        out_ref[device] = whole[4 * device : 4 * device + 4]
    pltpu.make_async_copy(inc_ref, inc_ref, inc_sem).wait()


def pick(rows, ints, increment):
    return pl.pallas_call(
        pick_kernel,
        out_shape=(
            jax.ShapeDtypeStruct((N_LON, 4, LANES), F32),
            jax.ShapeDtypeStruct((NF, NZ, NLAT, LANES), F32),
        ),
        in_specs=[SMEM_SPEC, VMEM_SPEC, VMEM_SPEC],
        out_specs=(VMEM_SPEC, ANY_SPEC),
        scratch_shapes=[pltpu.SemaphoreType.DMA],
        compiler_params=pltpu.CompilerParams(vmem_limit_bytes=8 << 20),
        cost_estimate=cost(14),
        name="pick",
    )(rows, ints, increment.reshape(ROWS, LANES))


def place_kernel(
    tile_out, ints_ref, out_ref,
    idx_ref, val_ref, rows_oh, cols_oh, tile_in, rows_out, rows_in, b1s, b1r, b2s, b2r,
):
    greet()
    none = jnp.full((LANES - CAP, LANES), -1, jnp.int32)
    idx_ref[...] = jnp.transpose(jnp.concatenate([ints_ref[0:CAP, :], none], axis=0))
    begin, middle, end, sent = two_phase(tile_out, tile_in, rows_out, rows_in, (b1s, b1r, b2s, b2r))
    row_iota = lax.broadcasted_iota(jnp.int32, (CAP, 2 * LANES), 0)
    col_iota = lax.broadcasted_iota(jnp.int32, (LANES, 2 * LANES), 0)

    def build(step, _):
        lat = step // (N_LON // 2)
        left = (step % (N_LON // 2)) * 2 * N_LAT + lat
        index = jnp.concatenate(
            [idx_ref[pl.ds(left, 1), :], idx_ref[pl.ds(left + N_LAT, 1), :]], axis=1
        )
        rows_oh[step] = jnp.where(row_iota == (index >> 7), 1.0, 0.0).astype(BF16)
        cols_oh[step] = jnp.where(col_iota == (index & 127), 1.0, 0.0).astype(BF16)
        return 0

    def add(step, acc):
        value = jnp.concatenate(
            [val_ref[pl.ds(2 * step, 1), :], val_ref[pl.ds(2 * step + 1, 1), :]], axis=1
        )
        high, low = split(value)
        rows = rows_oh[step]
        return acc + lax.dot_general(
            jnp.concatenate([rows * high, rows * low], axis=0), cols_oh[step],
            (((1,), (1,)), ((), ())), preferred_element_type=F32,
        )

    greeted()
    begin()
    lax.fori_loop(0, RANKS // 4, build, 0, unroll=2)
    middle()
    lax.fori_loop(RANKS // 4, RANKS // 2, build, 0, unroll=2)
    end()
    for lat in range(N_LAT):
        val_ref[N_LON * lat : N_LON * lat + N_LON, :] = rows_in[lat]
    acc = lax.fori_loop(0, RANKS // 2, add, jnp.zeros((2 * CAP, LANES), F32), unroll=8)
    out_ref[...] = acc[:CAP] + acc[CAP:]
    sent()


def place(tiles, ints):
    vmem = lambda *dims: pltpu.VMEM(dims, F32)
    dma = pltpu.SemaphoreType.DMA
    return pl.pallas_call(
        place_kernel,
        out_shape=jax.ShapeDtypeStruct((CAP, LANES), F32),
        in_specs=[VMEM_SPEC] * 2,
        out_specs=VMEM_SPEC,
        scratch_shapes=[
            pltpu.VMEM((RANKS, LANES), jnp.int32), vmem(RANKS, LANES),
            pltpu.VMEM((RANKS // 2, CAP, 2 * LANES), BF16),
            pltpu.VMEM((RANKS // 2, LANES, 2 * LANES), BF16),
            vmem(N_LON, 4, LANES), vmem(N_LAT, N_LON, LANES), vmem(N_LAT, N_LON, LANES),
            dma((N_LON,)), dma((N_LON,)), dma((N_LAT,)), dma((N_LAT,)),
        ],
        compiler_params=pltpu.CompilerParams(
            collective_id=2, has_side_effects=True, vmem_limit_bytes=10 << 20
        ),
        cost_estimate=cost(15),
        name="place",
    )(tiles, ints)


def local(
    obs_value, send_list, recv_cell, column_depth, zonal_weight, merid_weight, vert_inverse, norm_scale
):
    is_north = lax.axis_index("lat") == N_LAT - 1
    north = jnp.full((8, LANES), jnp.where(is_north, 1.0, 0.0), F32)
    ints = jnp.concatenate(
        [jnp.transpose(send_list), jnp.transpose(recv_cell), column_depth], axis=0
    )
    vert = jnp.transpose(vert_inverse, (1, 0, 2)).reshape(NF * NZ, NZ)
    floats = jnp.concatenate(
        [
            obs_value.reshape(CAP, LANES),
            zonal_weight.reshape(NF * NLAT, LANES),
            merid_weight.reshape(NF * NLAT, LANES),
            jnp.pad(vert, ((0, 0), (0, LANES - NZ))),
        ],
        axis=0,
    )
    made = prepare(ints, floats, north)
    incoming, coefs, rows = made[0], made[1:14], made[14].reshape(-1)
    grids = scatter(rows, ints, incoming, made[15:])
    norm = jnp.transpose(norm_scale, (0, 2, 1, 3))
    whole = solve(grids, norm, ints, coefs)
    tiles, increment = pick(rows, ints, whole)
    return increment, place(tiles, ints).reshape(-1)


def solution(mesh):
    in_specs = (
        P(("lon", "lat")),
        P(("lon", "lat"), None),
        P(("lon", "lat"), None),
        P("lat", "lon"),
        P(None, "lat", "lon"),
        P(None, "lat", "lon"),
        P(),
        P(None, None, "lat", "lon"),
    )
    out_specs = (P(None, None, "lat", "lon"), P(("lon", "lat")))
    return jax.shard_map(local, mesh=mesh, in_specs=in_specs, out_specs=out_specs, check_vma=False)
```

```python
import jax
import jax.numpy as jnp
from jax import lax
from jax.experimental import pallas as pl
from jax.experimental.pallas import tpu as pltpu
from jax.sharding import PartitionSpec as P

F32 = jnp.float32
BF16 = jnp.bfloat16
MESH = pl.DeviceIdType.MESH
NF, NZ, NLAT, NLON = 2, 75, 40, 128
ZP = 80
RANKS, CAP = 128, 80
N_LON, N_LAT = 32, 4
GROUPS = 15
GROUP = 5
LANES = 128
CHUNK = 20
HALF = 64
SPLIT = 24
VERT_CHUNK = 10
GRIDS = 8
ROWS = NF * NLAT * ZP
ZW_AT, MW_AT, VERT_AT = 80, 160, 240
DEPTH_AT = 160
VMEM_SPEC = pl.BlockSpec(memory_space=pltpu.VMEM)
SMEM_SPEC = pl.BlockSpec(memory_space=pltpu.SMEM)
ANY_SPEC = pl.BlockSpec(memory_space=pl.ANY)


def cost(micros):
    return pl.CostEstimate(flops=0, bytes_accessed=int(micros * 3.6e6), transcendentals=0)


def lane_iota(rows):
    return lax.broadcasted_iota(jnp.int32, (rows, LANES), 1)


def split(value):
    high = value.astype(BF16)
    return high, (value - high.astype(F32)).astype(BF16)


def lane_pick(table, index):
    return jnp.take_along_axis(table, index, axis=1, mode="promise_in_bounds")


def push(source, target, send_sem, recv_sem, axis, device):
    return pltpu.make_async_remote_copy(
        src_ref=source, dst_ref=target, send_sem=send_sem, recv_sem=recv_sem,
        device_id={axis: device}, device_id_type=MESH,
    )


def over(axis, count, action):
    mine = lax.axis_index(axis)

    def body(step, _):
        action((mine + step) % count)
        return 0

    lax.fori_loop(1, count, body, 0)


def over_lon(action):
    over("lon", N_LON, action)


def each_lon(action):
    mine = lax.axis_index("lon")
    for step in range(1, N_LON):
        action((mine + step) % N_LON)


def over_lat(action):
    over("lat", N_LAT, action)


def greet():
    barrier = pltpu.get_barrier_semaphore()
    over_lon(
        lambda device: pl.semaphore_signal(
            barrier, inc=1, device_id={"lon": device}, device_id_type=MESH
        )
    )
    over_lat(
        lambda device: pl.semaphore_signal(
            barrier, inc=1, device_id={"lat": device}, device_id_type=MESH
        )
    )


def greeted():
    pl.semaphore_wait(pltpu.get_barrier_semaphore(), N_LON - 1 + N_LAT - 1)


def zonal_coefs(floats_ref, zs_ref, zr_ref, zco_ref, iw_ref, st_ref, rt_ref, zero):
    one = zero + 1.0
    iw_ref[...] = jnp.full((LANES, LANES), 1e-3, F32)
    iw_ref[: NF * NLAT, :] = 1.0 / floats_ref[ZW_AT : ZW_AT + NF * NLAT, :]
    iw_ref[...] = jnp.transpose(iw_ref[...])

    def zonal_step(step, carry):
        s_val, s_flux, s_sum, r_val, r_flux, r_sum = carry
        back = LANES - 1 - step
        st_ref[pl.ds(step, 1), :] = s_val[0:1]
        s_sum = s_sum + s_val
        s_val = s_val + s_flux * iw_ref[pl.ds(step, 1), :]
        s_flux = s_flux + s_val
        r_sum = r_sum + r_val
        r_val = r_val + r_flux * iw_ref[pl.ds(back, 1), :]
        rt_ref[pl.ds(back, 1), :] = r_val[0:1]
        r_flux = r_flux + r_val
        return s_val, s_flux, s_sum, r_val, r_flux, r_sum

    _, _, s_sum, r_first, _, r_sum = lax.fori_loop(
        0, LANES, zonal_step, (zero, one, zero, zero, one, zero), unroll=8
    )
    coupling = 1.0 / r_first[0:1]
    zco_ref[...] = jnp.zeros((8, LANES), F32)
    zco_ref[0:1, :] = coupling
    zco_ref[1:2, :] = r_sum[0:1] * coupling
    zco_ref[2:3, :] = s_sum[0:1] * coupling
    zs_ref[...] = jnp.transpose(st_ref[...])[: NF * NLAT, :]
    zr_ref[...] = jnp.transpose(rt_ref[...] * coupling)[: NF * NLAT, :]


def merid_coefs(floats_ref, ms_ref, mr_ref, mss_ref, mrr_ref, mco_ref, miw_ref, north, zero):
    one = zero + 1.0
    for field in range(NF):
        at = MW_AT + field * NLAT
        miw_ref[field] = 1.0 / floats_ref[at : at + NLAT, :]
    mco_ref[...] = jnp.zeros((NF, 8, LANES), F32)
    for field in range(NF):
        s_val, s_flux, s_sum = zero, one, zero
        for row in range(NLAT):
            ms_ref[field, row : row + 1, :] = s_val[0:1]
            s_sum = s_sum + s_val
            s_val = s_val + s_flux * miw_ref[field, row : row + 1, :]
            s_flux = s_flux + s_val
        r_val = jnp.where(north > 0.5, 1.0, miw_ref[field, NLAT - 1 : NLAT, :] + zero)
        r_flux = jnp.where(north > 0.5, 0.0, one)
        r_sum = zero
        mr_ref[field, NLAT - 1 : NLAT, :] = r_val[0:1]
        for row in range(NLAT - 2, -1, -1):
            r_sum = r_sum + r_val
            r_flux = r_flux + r_val
            r_val = r_val + r_flux * miw_ref[field, row : row + 1, :]
            mr_ref[field, row : row + 1, :] = r_val[0:1]
        inverse = 1.0 / r_val[0:1]
        coupling = jnp.where(north[0:1] > 0.5, 0.0, inverse)
        mr_ref[field] = mr_ref[field] * inverse
        sum_rr, sum_rs = zero, zero
        for row in range(NLAT - 1, -1, -1):
            at = slice(row, row + 1)
            s_row, r_row = ms_ref[field, at, :], mr_ref[field, at, :]
            mrr_ref[field, at, :] = s_row * sum_rr[0:1]
            mss_ref[field, at, :] = s_row * sum_rs[0:1]
            sum_rr = sum_rr + r_row * r_row
            sum_rs = sum_rs + r_row * s_row
        sum_sr, sum_ss = zero, zero
        for row in range(NLAT):
            at = slice(row, row + 1)
            s_row, r_row = ms_ref[field, at, :], mr_ref[field, at, :]
            sum_sr = sum_sr + s_row * r_row
            sum_ss = sum_ss + s_row * s_row
            mrr_ref[field, at, :] = mrr_ref[field, at, :] + r_row * sum_sr[0:1]
            mss_ref[field, at, :] = mss_ref[field, at, :] + r_row * sum_ss[0:1]
        mco_ref[field, 0:1, :] = coupling
        mco_ref[field, 1:2, :] = r_sum[0:1] * inverse
        mco_ref[field, 2:3, :] = s_sum[0:1] * coupling
        mco_ref[field, 3:4, :] = sum_rr[0:1]
        mco_ref[field, 4:5, :] = sum_rs[0:1] * coupling
        mco_ref[field, 5:6, :] = sum_ss[0:1] * coupling * coupling


def zonal_factor(zco_all, alpha, gamma, minv):
    coupling = zco_all[:, 0, :]
    west = jnp.concatenate([coupling[-1:], coupling[:-1]], axis=0)
    spill = zco_all[:, 2, :]
    mass = 1.0 + zco_all[:, 1, :] + jnp.concatenate([spill[-1:], spill[:-1]], axis=0)
    east = coupling
    for bit in range(5):
        stride = 1 << bit
        down = lambda v: jnp.concatenate([v[-stride:], v[:-stride]], axis=0)
        up = lambda v: jnp.concatenate([v[stride:], v[:stride]], axis=0)
        inverse = 1.0 / (mass + west + east)
        left = west * down(inverse)
        right = east * up(inverse)
        for field in range(NF):
            alpha[field, bit] = to_field(left, field)
            gamma[field, bit] = to_field(right, field)
        mass = mass + left * down(mass) + right * up(mass)
        west, east = left * down(west), right * up(east)
    for field in range(NF):
        minv[field] = to_field(1.0 / mass, field)


def to_field(rows, field):
    return rows if field == 0 else pltpu.roll(rows, LANES - field * NLAT, 1)


def gather_lines(table_ref, count, high, low, beside):
    def step(row, acc):
        beside(row)
        line = jnp.broadcast_to(table_ref[pl.ds(row, 1), :], (ZP, LANES))
        return jnp.where(high == row, lane_pick(line, low), acc)

    return lax.fori_loop(0, count, step, jnp.zeros((ZP, LANES), F32), unroll=8)


def two_phase(tile_out, tile_in, rows_out, rows_in, sems):
    me = lax.axis_index("lon")
    my = lax.axis_index("lat")
    s1, r1, s2, r2 = sems
    first = lambda device, slot: push(
        tile_out.at[device], tile_in.at[slot], s1.at[device], r1.at[slot], "lon", device
    )
    second = lambda device, slot: push(
        rows_out.at[device], rows_in.at[slot], s2.at[device], r2.at[slot], "lat", device
    )

    def begin():
        each_lon(lambda device: first(device, me).start())
        tile_in[me] = tile_out[me]

    def middle():
        each_lon(lambda device: first(0, device).wait_recv())
        for lat in range(N_LAT):
            rows_out[lat] = tile_in[:, lat, :]
        over_lat(lambda device: second(device, my).start())
        rows_in[my] = rows_out[my]

    def end():
        over_lat(lambda device: second(0, device).wait_recv())

    def sent_first():
        over_lon(lambda device: first(device, me).wait_send())

    def sent_second():
        over_lat(lambda device: second(device, my).wait_send())

    return begin, middle, end, sent_first, sent_second


def prepare_kernel(
    ints_ref, floats_ref, north_ref,
    out_ref, zs_ref, zr_ref, zco_out, ms_ref, mr_ref, mss_ref, mrr_ref, mco_out, vert_ref,
    alpha, gamma, minv, sums_ref, row_ref, *rest
):
    grids, rest = rest[:GRIDS], rest[GRIDS:]
    prepare_body(
        ints_ref, floats_ref, north_ref, out_ref, zs_ref, zr_ref, zco_out, ms_ref, mr_ref, mss_ref,
        mrr_ref, mco_out, vert_ref, alpha, gamma, minv, sums_ref, row_ref, grids, *rest,
    )


def prepare_body(
    ints_ref, floats_ref, north_ref,
    out_ref, zs_ref, zr_ref, zco_out, ms_ref, mr_ref, mss_ref, mrr_ref, mco_out, vert_ref,
    alpha, gamma, minv, sums_ref, row_ref, grids,
    iw_ref, st_ref, rt_ref, miw_ref, prod_ref,
    tile_out, tile_in, rows_out, rows_in, zco_ref, zco_all, mco_ref, mco_all,
    o1s, o1r, o2s, o2r, zco_s, zco_r, mco_s, mco_r,
):
    me = lax.axis_index("lon")
    my = lax.axis_index("lat")
    greet()
    index = ints_ref[0:CAP, :]

    def clear(line):
        at = pl.ds(pl.multiple_of(line * ZP, ZP), ZP)
        for grid in grids:
            grid[at, :] = jnp.zeros((ZP, LANES), F32)

    picked = gather_lines(floats_ref, CAP, index >> 7, index & 127, clear)
    picked = jnp.transpose(
        jnp.concatenate([picked, jnp.zeros((LANES - CAP, LANES), F32)], axis=0)
    )
    for device in range(N_LON):
        tile_out[device] = picked[4 * device : 4 * device + 4]

    begin, middle, end, sent_first, sent_second = two_phase(
        tile_out, tile_in, rows_out, rows_in, (o1s, o1r, o2s, o2r)
    )
    zco_copy = lambda device, slot: push(
        zco_ref, zco_all.at[slot], zco_s.at[device], zco_r.at[slot], "lon", device
    )
    mco_copy = lambda device, slot: push(
        mco_ref, mco_all.at[slot], mco_s.at[device], mco_r.at[slot], "lat", device
    )
    greeted()
    begin()
    zero = north_ref[...] * 0.0
    zonal_coefs(floats_ref, zs_ref, zr_ref, zco_ref, iw_ref, st_ref, rt_ref, zero)
    over_lon(lambda device: zco_copy(device, me).start())
    zco_all[me] = zco_ref[...]
    merid_coefs(floats_ref, ms_ref, mr_ref, mss_ref, mrr_ref, mco_ref, miw_ref, north_ref[...], zero)
    over_lat(lambda device: mco_copy(device, my).start())
    mco_all[my] = mco_ref[...]
    middle()
    for field in range(NF):
        zco_out[field] = to_field(zco_ref[...], field)
    cell = ints_ref[CAP : 2 * CAP, :]
    line = cell >> 7
    plane = line // NLAT
    second_field = (plane >= NZ).astype(jnp.int32)
    live_row = (second_field * NLAT + line - plane * NLAT) * ZP + plane - second_field * NZ
    dead_row = lax.broadcasted_iota(jnp.int32, (CAP, LANES), 0) * ZP + NZ
    row_ref[...] = jnp.where(cell >= 0, live_row, dead_row)
    prod_ref[...] = jnp.zeros((ZP, LANES), F32)
    for field in range(NF):
        matrix = floats_ref[pl.ds(VERT_AT + field, NZ, stride=NF), :]
        prod_ref[:NZ, :NZ] = lax.dot_general(
            matrix, matrix, (((1,), (1,)), ((), ())),
            precision=lax.Precision.HIGHEST, preferred_element_type=F32,
        )
        high, low = split(prod_ref[:, :ZP])
        vert_ref[field] = jnp.concatenate([high, low, high], axis=1)
    source = lax.broadcasted_iota(jnp.int32, (2 * LANES, 2 * LANES), 0) & 127
    target = lax.broadcasted_iota(jnp.int32, (2 * LANES, 2 * LANES), 1)
    sums_ref[...] = jnp.where(source <= target, 1.0, 0.0).astype(BF16)
    sent_first()
    over_lon(lambda device: zco_copy(device, me).wait_send())
    end()
    for lat in range(N_LAT):
        out_ref[N_LON * lat : N_LON * lat + N_LON, :] = rows_in[lat]
    over_lon(lambda device: zco_copy(0, device).wait_recv())
    zonal_factor(zco_all, alpha, gamma, minv)
    over_lat(lambda device: mco_copy(0, device).wait_recv())
    mco_out[...] = mco_all[...]
    sent_second()
    over_lat(lambda device: mco_copy(device, my).wait_send())


def prepare(ints, floats, north):
    shape = lambda *dims: jax.ShapeDtypeStruct(dims, F32)
    vmem = lambda *dims: pltpu.VMEM(dims, F32)
    dma = pltpu.SemaphoreType.DMA
    return pl.pallas_call(
        prepare_kernel,
        out_shape=(
            shape(RANKS, LANES), shape(80, LANES), shape(80, LANES), shape(NF, 8, LANES),
            shape(NF, NLAT, LANES), shape(NF, NLAT, LANES),
            shape(NF, NLAT, LANES), shape(NF, NLAT, LANES), shape(N_LAT, NF, 8, LANES),
            jax.ShapeDtypeStruct((NF, ZP, 3 * ZP), BF16),
            shape(NF, 5, N_LON, LANES), shape(NF, 5, N_LON, LANES), shape(NF, N_LON, LANES),
            jax.ShapeDtypeStruct((2 * LANES, 2 * LANES), BF16),
            jax.ShapeDtypeStruct((CAP, LANES), jnp.int32),
        )
        + (shape(ROWS, LANES),) * GRIDS,
        in_specs=[VMEM_SPEC] * 3,
        out_specs=(VMEM_SPEC,) * (15 + GRIDS),
        scratch_shapes=[
            vmem(LANES, LANES), vmem(LANES, LANES), vmem(LANES, LANES), vmem(NF, NLAT, LANES),
            vmem(ZP, LANES),
            vmem(N_LON, 4, LANES), vmem(N_LON, 4, LANES),
            vmem(N_LAT, N_LON, LANES), vmem(N_LAT, N_LON, LANES),
            vmem(8, LANES), vmem(N_LON, 8, LANES), vmem(NF, 8, LANES), vmem(N_LAT, NF, 8, LANES),
            dma((N_LON,)), dma((N_LON,)), dma((N_LAT,)), dma((N_LAT,)),
            dma((N_LON,)), dma((N_LON,)), dma((N_LAT,)), dma((N_LAT,)),
        ],
        compiler_params=pltpu.CompilerParams(
            collective_id=0, has_side_effects=True, vmem_limit_bytes=6 << 20
        ),
        cost_estimate=cost(15),
        name="prepare",
    )(ints, floats, north)


def scatter_kernel(rows_ref, ints_ref, in_ref, *refs):
    grids = refs[GRIDS : 2 * GRIDS]
    value_ref, even_ref, odd_ref = refs[2 * GRIDS :]
    value_ref[...] = jnp.transpose(in_ref[...])
    iota = lane_iota(CAP)

    def spread(q):
        index = jnp.full((CAP, LANES), q, jnp.int32)
        place = jnp.full((CAP, LANES), (q % N_LAT) * N_LON + q // N_LAT, jnp.int32)
        lane = lane_pick(ints_ref[CAP : 2 * CAP, :] & 127, index)
        return jnp.where(iota == lane, lane_pick(value_ref[:CAP, :], place), 0.0)

    def add(q, source):
        for k in range(CAP):
            at = pl.ds(rows_ref[k * RANKS + q], 1)
            grid = grids[k % GRIDS]
            grid[at, :] = grid[at, :] + source[k : k + 1, :]

    even_ref[...] = spread(0)

    def senders(pair, _):
        q = 2 * pair
        odd_ref[...] = spread(q + 1)
        add(q, even_ref)
        even_ref[...] = spread(jnp.minimum(q + 2, RANKS - 1))
        add(q + 1, odd_ref)
        return 0

    lax.fori_loop(0, RANKS // 2, senders, 0)


def scatter(rows, ints, incoming, grids):
    grid = jax.ShapeDtypeStruct((ROWS, LANES), F32)
    return pl.pallas_call(
        scatter_kernel,
        out_shape=(grid,) * GRIDS,
        in_specs=[SMEM_SPEC] + [VMEM_SPEC] * (2 + GRIDS),
        out_specs=(VMEM_SPEC,) * GRIDS,
        input_output_aliases={3 + index: index for index in range(GRIDS)},
        scratch_shapes=[
            pltpu.VMEM((LANES, LANES), F32), pltpu.VMEM((CAP, LANES), F32), pltpu.VMEM((CAP, LANES), F32),
        ],
        compiler_params=pltpu.CompilerParams(vmem_limit_bytes=6 << 20),
        cost_estimate=cost(12),
        name="scatter",
    )(rows, ints, incoming, *grids)


def solve_kernel(*refs):
    solve_body(refs[:GRIDS], *refs[GRIDS:])


def solve_body(
    grids, norm_ref, ints_ref, zs_ref, zr_ref, zco_ref, ms_ref, mr_ref, mss_ref, mrr_ref, mco_all,
    vert_ref, alpha, gamma, minv, sums_ref,
    x_ref,
    zsend, zrecv, zret, zres, msend, mrecv, mret, mres,
    acc_a, acc_b, ubuf, gbuf, mtot, mbuf,
    z1s, z1r, z2s, z2r, m1s, m1r, m2s, m2r,
):
    me = lax.axis_index("lon")
    my = lax.axis_index("lat")
    iota = lane_iota(ZP)
    half = N_LON // NF
    my_field = me // half
    is_solver = me % half < GROUPS
    nothing = jnp.zeros((ZP, LANES), F32)
    greet()


    def zonal_out(turn, field, group, slot):
        return push(
            zsend.at[turn, field, group], zrecv.at[turn, slot],
            z1s.at[turn, field, group], z1r.at[turn, slot], "lon", field * half + group,
        )

    def zonal_back(turn, device, field, group):
        return push(
            zret.at[turn, device], zres.at[turn, field, group],
            z2s.at[turn, device], z2r.at[turn, field, group], "lon", device,
        )

    def others(field, action):
        for group in range(GROUPS):
            pl.when(me != field * half + group)(lambda group=group: action(group))

    def zonal_pass(turn, field, load):
        def chunk_pass(chunk, _):
            lines, left = [], []
            for step in range(CHUNK):
                row = chunk * CHUNK + step
                at = pl.ds(field * NLAT + row, 1)
                s_row, r_row = zs_ref[at, :], zr_ref[at, :]
                value = load(row)
                for coef in (s_row, r_row):
                    high, low = split(coef * value)
                    left.append(jnp.concatenate([high, low], axis=1))
                lines.append((row, s_row, r_row))
            sums = jnp.dot(
                jnp.concatenate(left, axis=0), sums_ref[...], preferred_element_type=F32
            )
            tot_a, tot_b = acc_a[...], acc_b[field]
            for step, (row, s_row, r_row) in enumerate(lines):
                a_part = sums[2 * step * ZP : (2 * step + 1) * ZP]
                b_part = sums[(2 * step + 1) * ZP : (2 * step + 2) * ZP]
                x_ref[field, row] = r_row * a_part[:, :LANES] - s_row * b_part[:, :LANES]
                mine = iota == row
                tot_a = jnp.where(mine, a_part[:, LANES:], tot_a)
                tot_b = jnp.where(mine, b_part[:, LANES:], tot_b)
            acc_a[...] = tot_a
            acc_b[field] = tot_b
            return 0

        acc_a[...] = nothing
        acc_b[field] = nothing
        lax.fori_loop(0, NLAT // CHUNK, chunk_pass, 0)
        acc_a[...] = acc_b[field] + pltpu.roll(acc_a[...] * zco_ref[field, 0:1, :], HALF, 1)
        for group in range(GROUPS):
            at = slice(GROUP * group, GROUP * group + GROUP)
            zsend[turn, field, group, 0:GROUP, :] = acc_a[at, :]

    def zonal_send(turn, field):
        others(field, lambda group: zonal_out(turn, field, group, me).start())

        @pl.when(is_solver & (my_field == field))
        def _():
            zrecv[turn, me] = zsend[turn, field, me % half]

    def zonal_reduced(turn):
        mine = me % half
        each_lon(lambda device: zonal_out(turn, 0, 0, device).wait_recv())
        right_side = [
            zrecv[turn, k] + pltpu.roll(zrecv[turn, (k - 1) % N_LON], HALF, 1) for k in range(N_LON)
        ]
        for bit in range(5):
            stride = 1 << bit
            right_side = [
                right_side[k]
                + alpha[my_field, bit, k : k + 1, :] * right_side[(k - stride) % N_LON]
                + gamma[my_field, bit, k : k + 1, :] * right_side[(k + stride) % N_LON]
                for k in range(N_LON)
            ]
        values = [right_side[k] * minv[my_field, k : k + 1, :] for k in range(N_LON)]
        for k in range(N_LON):
            zret[turn, k] = jnp.where(
                iota[0:8] < HALF, values[k], pltpu.roll(values[(k + 1) % N_LON], HALF, 1)
            )
        each_lon(lambda device: zonal_back(turn, device, my_field, mine).start())
        zres[turn, my_field, mine] = zret[turn, me]

    def zonal_receive(turn, field):
        others(field, lambda group: zonal_back(turn, 0, field, group).wait_recv())
        ubuf[72:80, :] = jnp.zeros((8, LANES), F32)
        for group in range(GROUPS):
            at = slice(GROUP * group, GROUP * group + GROUP)
            ubuf[at, :] = zres[turn, field, group, 0:GROUP, :]
        gbuf[...] = pltpu.roll(ubuf[...], HALF, 1) * zco_ref[field, 0:1, :] + acc_b[field]

    def zonal_values(field, chunk):
        u_all, g_all = ubuf[...], gbuf[...]
        found = []
        for step in range(CHUNK):
            row = chunk * CHUNK + step
            at = pl.ds(field * NLAT + row, 1)
            found.append(
                x_ref[field, row]
                + zr_ref[at, :] * jnp.broadcast_to(u_all[:, step : step + 1], (ZP, LANES))
                + zs_ref[at, :] * jnp.broadcast_to(g_all[:, step : step + 1], (ZP, LANES))
            )
        ubuf[...] = pltpu.roll(u_all, LANES - CHUNK, 1)
        gbuf[...] = pltpu.roll(g_all, LANES - CHUNK, 1)
        return found


    def vertical(field, value):
        high, low = split(value)
        return jnp.dot(
            vert_ref[field], jnp.concatenate([high, high, low], axis=0), preferred_element_type=F32
        )

    def vertical_field(field):
        def body(step, _):
            row = step * VERT_CHUNK
            value = jnp.concatenate([x_ref[field, row + k] for k in range(VERT_CHUNK)], axis=1)
            value = vertical(field, value)
            for k in range(VERT_CHUNK):
                x_ref[field, row + k] = value[:, k * LANES : (k + 1) * LANES]
            return 0

        lax.fori_loop(0, NLAT // VERT_CHUNK, body, 0)


    def merid_out(field, device, slot):
        return push(
            msend.at[field, device], mrecv.at[field, slot],
            m1s.at[field, device], m1r.at[field, slot], "lat", device,
        )

    def merid_back(field, device, slot):
        return push(
            mret.at[field, device], mres.at[field, slot],
            m2s.at[field, device], m2r.at[field, slot], "lat", device,
        )

    def merid_pass(field):
        def one(chunk, carry):
            tot_a, tot_b = carry
            found = zonal_values(field, chunk)
            for step in range(CHUNK):
                row = chunk * CHUNK + step
                s_row, r_row = ms_ref[field, pl.ds(row, 1), :], mr_ref[field, pl.ds(row, 1), :]
                tot_a = tot_a + s_row * found[step]
                tot_b = tot_b + r_row * found[step]
                x_ref[field, row] = r_row * tot_a - s_row * tot_b
            return tot_a, tot_b

        a_one, b_one = lax.fori_loop(0, NLAT // CHUNK, one, (nothing, nothing))
        ubuf[...] = b_one

        def two(row, carry):
            tot_a, tot_b = carry
            s_row, r_row = ms_ref[field, pl.ds(row, 1), :], mr_ref[field, pl.ds(row, 1), :]
            value = x_ref[field, row] + s_row * ubuf[...]
            tot_a = tot_a + s_row * value
            tot_b = tot_b + r_row * value
            x_ref[field, row] = r_row * tot_a - s_row * tot_b
            return tot_a, tot_b

        a_two, b_two = lax.fori_loop(0, NLAT, two, (nothing, nothing), unroll=4)
        mtot[field] = b_two
        coupling = mco_all[my, field, 0:1, :]
        for part, value in enumerate((b_one, a_one * coupling, b_two, a_two * coupling)):
            for solver in range(N_LAT):
                count = min(SPLIT, ZP - SPLIT * solver)
                msend[field, solver, part, 0:count, :] = value[SPLIT * solver : SPLIT * solver + count]
                if count < SPLIT:
                    msend[field, solver, part, count:SPLIT, :] = jnp.zeros(
                        (SPLIT - count, LANES), F32
                    )
        over_lat(lambda device: merid_out(field, device, my).start())
        mrecv[field, my] = msend[field, my]

    def merid_reduced(field):
        over_lat(lambda device: merid_out(field, 0, device).wait_recv())
        coef = lambda k, row: mco_all[k, field, row : row + 1, :]
        part = lambda k, index: mrecv[field, k, index]

        def solve_four(right_side):
            mass = 1.0 + coef(0, 1)
            reduced = right_side[0]
            kept, inverses, values = [], [], [None] * N_LAT
            for k in range(N_LAT):
                inverse = 1.0 / (mass + coef(k, 0))
                kept.append(reduced)
                inverses.append(inverse)
                if k + 1 < N_LAT:
                    factor = coef(k, 0) * inverse
                    mass = 1.0 + coef(k + 1, 1) + coef(k, 2) + factor * mass
                    reduced = right_side[k + 1] + factor * reduced
            values[-1] = kept[-1] * inverses[-1]
            for k in range(N_LAT - 2, -1, -1):
                values[k] = (kept[k] + coef(k, 0) * values[k + 1]) * inverses[k]
            return values

        none = jnp.zeros((SPLIT, LANES), F32)
        u = solve_four([part(k, 0) + (part(k - 1, 1) if k else none) for k in range(N_LAT)]) + [none]
        second = []
        for k in range(N_LAT):
            value = part(k, 2) + coef(k, 3) * u[k] + coef(k, 4) * u[k + 1]
            if k:
                value = value + part(k - 1, 3) + coef(k - 1, 4) * u[k - 1] + coef(k - 1, 5) * u[k]
            second.append(value)
        v = solve_four(second) + [none]
        for k in range(N_LAT):
            for index, value in enumerate((u[k], u[k + 1], v[k], v[k + 1])):
                mret[field, k, index] = value
        over_lat(lambda device: merid_back(field, device, my).start())
        mres[field, my] = mret[field, my]

    def merid_receive(field):
        over_lat(lambda device: merid_back(field, 0, device).wait_recv())
        for index in range(4):
            for solver in range(N_LAT):
                count = min(SPLIT, ZP - SPLIT * solver)
                mbuf[index, SPLIT * solver : SPLIT * solver + count, :] = mres[
                    field, solver, index, 0:count, :
                ]
        coupling = mco_all[my, field, 0:1, :]
        mbuf[1] = mbuf[1] * coupling
        mbuf[3] = mbuf[3] * coupling + mtot[field]

    def merid_value(field, row):
        at = pl.ds(row, 1)
        return (
            x_ref[field, row]
            + mrr_ref[field, at, :] * mbuf[0]
            + mss_ref[field, at, :] * mbuf[1]
            + mr_ref[field, at, :] * mbuf[2]
            + ms_ref[field, at, :] * mbuf[3]
        )

    level = lax.broadcasted_iota(jnp.int32, (ZP, LANES), 0)

    def scale(field, row):
        wet = level < ints_ref[pl.ds(DEPTH_AT + row, 1), :]
        line = jnp.concatenate([norm_ref[field, row], jnp.zeros((ZP - NZ, LANES), F32)], axis=0)
        return jnp.where(wet, line, 0.0)

    def scaled_grid(field):
        def load(row):
            at = pl.ds(pl.multiple_of((field * NLAT + row) * ZP, ZP), ZP)
            total = [grid[at, :] for grid in grids]
            while len(total) > 1:
                total = [one + two for one, two in zip(total[::2], total[1::2])]
            return scale(field, row) * total[0]

        return load

    zonal_pass(0, 0, scaled_grid(0))
    greeted()
    zonal_send(0, 0)
    zonal_pass(0, 1, scaled_grid(1))
    zonal_send(0, 1)
    vertical_field(0)
    pl.when(is_solver & (my_field == 0))(lambda: zonal_reduced(0))
    vertical_field(1)
    pl.when(is_solver & (my_field == 1))(lambda: zonal_reduced(0))

    for field in range(NF):
        zonal_receive(0, field)
        both = vertical(field, jnp.concatenate([ubuf[...], gbuf[...]], axis=1))
        ubuf[...] = both[:, :LANES]
        gbuf[...] = both[:, LANES:]
        merid_pass(field)
    for field in range(NF):
        merid_reduced(field)

    for field in range(NF):
        merid_receive(field)
        zonal_pass(1, field, lambda row, field=field: merid_value(field, row))
        zonal_send(1, field)
    pl.when(is_solver)(lambda: zonal_reduced(1))

    for field in range(NF):
        over_lat(lambda device, field=field: merid_out(field, device, my).wait_send())
        over_lat(lambda device, field=field: merid_back(field, device, my).wait_send())
        for turn in range(2):
            others(
                field,
                lambda group, turn=turn, field=field: zonal_out(turn, field, group, me).wait_send(),
            )

    @pl.when(is_solver)
    def _():
        for turn in range(2):
            over_lon(lambda device, turn=turn: zonal_back(turn, device, 0, 0).wait_send())

    for field in range(NF):
        zonal_receive(1, field)

        def last_pass(chunk, _, field=field):
            found = zonal_values(field, chunk)
            for step in range(CHUNK):
                row = chunk * CHUNK + step
                x_ref[field, row] = found[step] * scale(field, row)
            return 0

        lax.fori_loop(0, NLAT // CHUNK, last_pass, 0)


def solve(grids, norm, ints, coefs):
    dma = pltpu.SemaphoreType.DMA
    vmem = lambda *dims: pltpu.VMEM(dims, F32)
    return pl.pallas_call(
        solve_kernel,
        out_shape=jax.ShapeDtypeStruct((NF, NLAT, ZP, LANES), F32),
        in_specs=[VMEM_SPEC] * (15 + GRIDS),
        out_specs=VMEM_SPEC,
        scratch_shapes=[
            vmem(2, NF, GROUPS, 8, LANES), vmem(2, N_LON, 8, LANES),
            vmem(2, N_LON, 8, LANES), vmem(2, NF, GROUPS, 8, LANES),
            vmem(NF, N_LAT, 4, SPLIT, LANES), vmem(NF, N_LAT, 4, SPLIT, LANES),
            vmem(NF, N_LAT, 4, SPLIT, LANES), vmem(NF, N_LAT, 4, SPLIT, LANES),
            vmem(ZP, LANES), vmem(NF, ZP, LANES), vmem(ZP, LANES), vmem(ZP, LANES),
            vmem(NF, ZP, LANES), vmem(4, ZP, LANES),
            dma((2, NF, GROUPS)), dma((2, N_LON)), dma((2, N_LON)), dma((2, NF, GROUPS)),
            dma((NF, N_LAT)), dma((NF, N_LAT)), dma((NF, N_LAT)), dma((NF, N_LAT)),
        ],
        compiler_params=pltpu.CompilerParams(
            collective_id=1, has_side_effects=True, vmem_limit_bytes=10 << 20
        ),
        cost_estimate=cost(40),
        name="solve",
    )(*grids, norm, ints, *coefs)


def pick_kernel(rows_ref, ints_ref, x_ref, out_ref, inc_ref, inc_sem):
    iota = lane_iota(8)
    group = 16
    for field in range(NF):

        def begin(row, _, field=field):
            at = pl.ds(pl.multiple_of((field * NLAT + row) * ZP, ZP), NZ)
            pltpu.make_async_copy(x_ref.at[at, :], inc_ref.at[field, :, row, :], inc_sem).start()
            return 0

        lax.fori_loop(0, NLAT, begin, 0)

    def senders(step, acc):
        acc = list(acc)
        for part in range(group):
            q = step * group + part
            for tile in range(CAP // 8):
                lines = [
                    x_ref[pl.ds(rows_ref[k * RANKS + q], 1), :] for k in range(8 * tile, 8 * tile + 8)
                ]
                lane = ints_ref[CAP + 8 * tile : CAP + 8 * tile + 8, :] & 127
                found = lane_pick(jnp.concatenate(lines, axis=0), lane)
                acc[tile] = jnp.where(iota == q, found, acc[tile])
        return tuple(acc)

    acc = lax.fori_loop(0, RANKS // group, senders, (jnp.zeros((8, LANES), F32),) * (CAP // 8))
    whole = jnp.concatenate(list(acc) + [jnp.zeros((LANES - CAP, LANES), F32)], axis=0)
    whole = jnp.transpose(whole)
    for device in range(N_LON):
        out_ref[device] = whole[4 * device : 4 * device + 4]
    pltpu.make_async_copy(inc_ref, inc_ref, inc_sem).wait()


def pick(rows, ints, increment):
    return pl.pallas_call(
        pick_kernel,
        out_shape=(
            jax.ShapeDtypeStruct((N_LON, 4, LANES), F32),
            jax.ShapeDtypeStruct((NF, NZ, NLAT, LANES), F32),
        ),
        in_specs=[SMEM_SPEC, VMEM_SPEC, VMEM_SPEC],
        out_specs=(VMEM_SPEC, ANY_SPEC),
        scratch_shapes=[pltpu.SemaphoreType.DMA],
        compiler_params=pltpu.CompilerParams(vmem_limit_bytes=8 << 20),
        cost_estimate=cost(14),
        name="pick",
    )(rows, ints, increment.reshape(ROWS, LANES))


def place_kernel(
    tile_out, ints_ref, out_ref,
    idx_ref, val_ref, rows_oh, cols_oh, tile_in, rows_out, rows_in, b1s, b1r, b2s, b2r,
):
    greet()
    none = jnp.full((LANES - CAP, LANES), -1, jnp.int32)
    idx_ref[...] = jnp.transpose(jnp.concatenate([ints_ref[0:CAP, :], none], axis=0))
    begin, middle, end, sent_first, sent_second = two_phase(
        tile_out, tile_in, rows_out, rows_in, (b1s, b1r, b2s, b2r)
    )
    row_iota = lax.broadcasted_iota(jnp.int32, (CAP, 2 * LANES), 0)
    col_iota = lax.broadcasted_iota(jnp.int32, (LANES, 2 * LANES), 0)

    def build(step, _):
        lat = step // (N_LON // 2)
        left = (step % (N_LON // 2)) * 2 * N_LAT + lat
        index = jnp.concatenate(
            [idx_ref[pl.ds(left, 1), :], idx_ref[pl.ds(left + N_LAT, 1), :]], axis=1
        )
        rows_oh[step] = jnp.where(row_iota == (index >> 7), 1.0, 0.0).astype(BF16)
        cols_oh[step] = jnp.where(col_iota == (index & 127), 1.0, 0.0).astype(BF16)
        return 0

    def add(step, acc):
        value = jnp.concatenate(
            [val_ref[pl.ds(2 * step, 1), :], val_ref[pl.ds(2 * step + 1, 1), :]], axis=1
        )
        high, low = split(value)
        rows = rows_oh[step]
        return acc + lax.dot_general(
            jnp.concatenate([rows * high, rows * low], axis=0), cols_oh[step],
            (((1,), (1,)), ((), ())), preferred_element_type=F32,
        )

    greeted()
    begin()
    lax.fori_loop(0, RANKS // 4, build, 0, unroll=2)
    middle()
    lax.fori_loop(RANKS // 4, RANKS // 2, build, 0, unroll=2)
    sent_first()
    end()
    for lat in range(N_LAT):
        val_ref[N_LON * lat : N_LON * lat + N_LON, :] = rows_in[lat]
    acc = lax.fori_loop(0, RANKS // 2, add, jnp.zeros((2 * CAP, LANES), F32), unroll=8)
    out_ref[...] = acc[:CAP] + acc[CAP:]
    sent_second()


def place(tiles, ints):
    vmem = lambda *dims: pltpu.VMEM(dims, F32)
    dma = pltpu.SemaphoreType.DMA
    return pl.pallas_call(
        place_kernel,
        out_shape=jax.ShapeDtypeStruct((CAP, LANES), F32),
        in_specs=[VMEM_SPEC] * 2,
        out_specs=VMEM_SPEC,
        scratch_shapes=[
            pltpu.VMEM((RANKS, LANES), jnp.int32), vmem(RANKS, LANES),
            pltpu.VMEM((RANKS // 2, CAP, 2 * LANES), BF16),
            pltpu.VMEM((RANKS // 2, LANES, 2 * LANES), BF16),
            vmem(N_LON, 4, LANES), vmem(N_LAT, N_LON, LANES), vmem(N_LAT, N_LON, LANES),
            dma((N_LON,)), dma((N_LON,)), dma((N_LAT,)), dma((N_LAT,)),
        ],
        compiler_params=pltpu.CompilerParams(
            collective_id=2, has_side_effects=True, vmem_limit_bytes=10 << 20
        ),
        cost_estimate=cost(15),
        name="place",
    )(tiles, ints)


def local(
    obs_value, send_list, recv_cell, column_depth, zonal_weight, merid_weight, vert_inverse, norm_scale
):
    is_north = lax.axis_index("lat") == N_LAT - 1
    north = jnp.full((8, LANES), jnp.where(is_north, 1.0, 0.0), F32)
    ints = jnp.concatenate(
        [jnp.transpose(send_list), jnp.transpose(recv_cell), column_depth], axis=0
    )
    vert = jnp.transpose(vert_inverse, (1, 0, 2)).reshape(NF * NZ, NZ)
    floats = jnp.concatenate(
        [
            obs_value.reshape(CAP, LANES),
            zonal_weight.reshape(NF * NLAT, LANES),
            merid_weight.reshape(NF * NLAT, LANES),
            jnp.pad(vert, ((0, 0), (0, LANES - NZ))),
        ],
        axis=0,
    )
    made = prepare(ints, floats, north)
    incoming, coefs, rows = made[0], made[1:14], made[14].reshape(-1)
    grids = scatter(rows, ints, incoming, made[15:])
    norm = jnp.transpose(norm_scale, (0, 2, 1, 3))
    whole = solve(grids, norm, ints, coefs)
    tiles, increment = pick(rows, ints, whole)
    return increment, place(tiles, ints).reshape(-1)


def solution(mesh):
    in_specs = (
        P(("lon", "lat")),
        P(("lon", "lat"), None),
        P(("lon", "lat"), None),
        P("lat", "lon"),
        P(None, "lat", "lon"),
        P(None, "lat", "lon"),
        P(),
        P(None, None, "lat", "lon"),
    )
    out_specs = (P(None, None, "lat", "lon"), P(("lon", "lat")))
    return jax.shard_map(local, mesh=mesh, in_specs=in_specs, out_specs=out_specs, check_vma=False)
```
